32 devices in a mesh: group: 4 (over z), expert: 8 (over y, x, core).
Axes of the slice: x: 2, y: 2, z: 4, core: 2. Of those that a mesh axis runs over, the one named last changes fastest.
Arguments:
- tokens: bfloat16 [16384, 768], P(('group', 'expert')), may hold values from -6 to 6
- gain_first: float32 [768], replicated, may hold values from 0.5 to 1.5
- w_qkv: bfloat16 [768, 2304], replicated, may hold values from -0.21875 to 0.21875
- w_proj: bfloat16 [768, 768], replicated, may hold values from -1.25 to 1.25
- bias_table: float32 [32, 12], replicated, may hold values from -4 to 4
- gain_second: float32 [768], replicated, may hold values from 0.5 to 1.5
- w_router: bfloat16 [768, 8], replicated, may hold values from -0.109375 to 0.109375
- w_in: bfloat16 [8, 768, 3072], P('expert'), may hold values from -0.21875 to 0.21875
- w_out: bfloat16 [8, 3072, 768], P('expert'), may hold values from -0.21875 to 0.21875
- routes: int32 [16384, 2], P(('group', 'expert')), may hold values from 0 to 7, all different within a row; in each aligned block of 512 rows (0 to 511, 512 to 1023, ...) at most 256 rows name the same one
- priority: int32 [32, 512], P(('group', 'expert')), may hold values from 0 to 511, each once within a row
- span_start: int32 [32], P(('group', 'expert')), may hold values from 0 to 256
- cotangent: bfloat16 [16384, 768], P(('group', 'expert')), may hold values from -6 to 6
Outputs:
- block_out: bfloat16 [16384, 768], P(('group', 'expert'))
- grad_tokens: bfloat16 [16384, 768], P(('group', 'expert'))
- grad_gain_first: float32 [768], P('expert')
- grad_qkv: float32 [768, 2304], P('expert')
- grad_proj: float32 [768, 768], P('expert')
- grad_table: float32 [32, 12], P('expert')
- grad_gain_second: float32 [768], P('expert')
- grad_router: float32 [768, 8], P('expert')
- grad_in: float32 [8, 768, 3072], P('expert', 'group')
- grad_out: float32 [8, 3072, 768], P('expert', 'group')
The draws below stay inside these ranges and needn't reach their ends.
Inputs may be any that keep to these rules, and one draw needn't show every extreme that they name: `routes`: each token names two different experts; among the 512 rows of one device no expert is named by more than 256 rows. `priority`: each row is a permutation of the ranks of one sequence's tokens.
All inputs are finite; a program needn't handle non-finite values.
Results may differ from the reference program's by a relative error of at most 0.02.
Values may be sent and summed in bfloat16 or wider, within the bound.
A program may use at most 192 MiB of HBM per device.

```python
import math
import jax
import jax.numpy as jnp
import numpy as np
from jax import lax

D = 768
HEADS = 12
HEAD_DIM = 64
FF = 3072
BUCKETS = 32
PIC = 256
TOK_DEV = 512
EXPERTS = 8
SEQS = 32
TOKENS = 16384
MOST = 256
CAP = 1280
N_GROUP = 4
N_EXPERT = 8


def touch_ends(entries, stream_key, least, top_value):
    extent = entries.shape
    spot = [jax.random.randint(jax.random.fold_in(stream_key, axis), (), 0, extent[axis]) for axis in range(len(extent))]
    entries = entries.at[tuple(spot)].set(least)
    longest = extent.index(max(extent))
    spot[longest] = (spot[longest] + 1) % extent[longest]
    return entries.at[tuple(spot)].set(top_value)


def levels(own_key, dims, cuts, smallest, largest):
    factor_of, own = 1.0, jax.random.fold_in(own_key, 6)
    for axis_at, parts in cuts:
        steps = jnp.exp(jax.random.uniform(jax.random.fold_in(own, axis_at), (parts,), jnp.float32, smallest / len(cuts), largest / len(cuts)))
        factor_of = factor_of * jnp.repeat(steps, dims[axis_at] // parts).reshape([-1 if axis == axis_at else 1 for axis in range(len(dims))])
    return factor_of


def shared_out(rng, own, number, rows, number_of, top, reach, slope):
    ranking = jax.random.permutation(rng, number_of)
    crowded, common = shares(number_of, rows * top, reach, slope, True), shares(number_of, rows * top, reach, slope, False)
    places = jnp.arange(number_of)

    def named(tallies, turn):
        used = int((tallies > 0).sum())
        fixed = max(1, used // 4)
        shifted = fixed + (places - fixed + turn * (used - fixed)) % max(1, number_of - fixed)
        return jnp.zeros((number_of,), jnp.int32).at[ranking[jnp.where(places < fixed, places, shifted)]].set(jnp.asarray(tallies, jnp.int32))

    tallies = jnp.where(number % 4 == 0, named(crowded, number // 4), named(common, number - number // 4 - 1))
    mixed = jax.random.permutation(jax.random.fold_in(own, 3), number_of)
    donor, taker = mixed[0:number_of // 2 * 2:2], mixed[1:number_of // 2 * 2:2]
    slack = jnp.minimum(tallies[donor] - 1, reach - tallies[taker]) // 2
    slack = jnp.where((donor == ranking[0]) | (taker == ranking[0]) | (tallies[taker] == 0), 0, jnp.maximum(slack, 0))
    shifted = jax.random.randint(jax.random.fold_in(own, 4), (number_of // 2,), 0, 1 << 20) % (slack + 1)
    tallies = tallies.at[donor].add(-shifted).at[taker].add(shifted)
    labels = jnp.searchsorted(jnp.cumsum(tallies), jnp.arange(rows * top), side="right").astype(jnp.int32)
    grid = labels.reshape(top, rows).T
    grid = grid[jax.random.permutation(jax.random.fold_in(own, 1), rows)]
    turn = jax.random.randint(jax.random.fold_in(own, 2), (rows, 1), 0, top)
    return jnp.take_along_axis(grid, (jnp.arange(top)[None, :] + turn) % top, axis=1)


def shares(amount, total, most, lean, full):
    portions = [(1 << 20) // math.isqrt(grade ** lean) + 1 for grade in range(1, amount + 1)]
    largest = most if full else min(most, max(-(-total // amount), total * portions[0] // sum(portions)))
    least = 1 if total - largest >= amount - 1 else 0
    holding, surplus = [largest] + [least] * (amount - 1), total - largest - least * (amount - 1)
    while surplus > 0:
        free = [i for i in range(1, amount) if holding[i] < largest] or [i for i in range(1, amount) if holding[i] < most]
        pool, left = sum([portions[i] for i in free]), surplus
        for i in free:
            extra = min(most - holding[i], max(1, left * portions[i] // pool), surplus)
            holding[i] = holding[i] + extra
            surplus = surplus - extra
    return np.array(holding)


def bell_draw(stream_key, extent, scale, limit, cuts=(), kind=jnp.bfloat16):
    array = scale * jax.random.normal(stream_key, extent, jnp.float32)
    if cuts:
        array = array * levels(stream_key, extent, cuts, -0.22, 0.18)
    return jnp.clip(array, -limit, limit).astype(kind)


def setup_inputs(seed: int = 0) -> dict:
    streams_of = jax.random.split(jax.random.key(seed), 14)
    tokens = bell_draw(streams_of[0], (TOKENS, D), 1.0, 6.0, ((0, 32),))
    gain_first = jnp.clip(1.0 + 0.1 * jax.random.normal(streams_of[1], (D,), jnp.float32), 0.5, 1.5)
    w_qkv = bell_draw(streams_of[2], (D, 3 * D), D ** -0.5, 0.21875)
    w_proj = bell_draw(streams_of[3], (D, D), (D // 32) ** -0.5, 1.25)
    bias_table = bell_draw(streams_of[4], (BUCKETS, HEADS), 1.0, 4.0, (), jnp.float32)
    gain_second = jnp.clip(1.0 + 0.1 * jax.random.normal(streams_of[5], (D,), jnp.float32), 0.5, 1.5)
    w_router = bell_draw(streams_of[6], (D, EXPERTS), (4 * D) ** -0.5, 0.109375)
    w_in = bell_draw(streams_of[7], (EXPERTS, D, FF), D ** -0.5, 0.21875, ((0, 8),))
    w_out = bell_draw(streams_of[8], (EXPERTS, FF, D), (FF // 4) ** -0.5, 0.21875, ((0, 8),))
    routes_keys = jax.random.split(jax.random.fold_in(streams_of[9], 1), TOKENS // TOK_DEV)
    routes_turns = jax.random.permutation(jax.random.fold_in(streams_of[9], 3), TOKENS // TOK_DEV)
    routes = jax.vmap(lambda own, number: shared_out(jax.random.fold_in(streams_of[9], 2), own, number, TOK_DEV, EXPERTS, 2, MOST, 1))(routes_keys, routes_turns).reshape((TOKENS, 2))
    priority = jax.vmap(lambda own: jax.random.permutation(own, TOK_DEV))(jax.random.split(streams_of[10], SEQS)).reshape((SEQS, TOK_DEV)).astype(jnp.int32)
    span_start = touch_ends(jax.random.randint(streams_of[11], (SEQS,), 0, TOK_DEV - PIC + 1), jax.random.fold_in(streams_of[11], 1), 0, TOK_DEV - PIC).astype(jnp.int32)
    cotangent = bell_draw(streams_of[12], (TOKENS, D), 1.0, 6.0, ((0, 32),))
    return {"tokens": tokens, "gain_first": gain_first, "w_qkv": w_qkv, "w_proj": w_proj, "bias_table": bias_table, "gain_second": gain_second, "w_router": w_router, "w_in": w_in, "w_out": w_out, "routes": routes, "priority": priority, "span_start": span_start, "cotangent": cotangent}


@jax.custom_vjp
def low(v):
    return lax.optimization_barrier(v.astype(jnp.bfloat16)).astype(jnp.float32)

@jax.custom_vjp
def low_back(v):
    return v

def low_keep(v):
    return (low(v), None)

def low_pass(kept, grad):
    return (grad,)

def back_keep(v):
    return (v, None)

def back_low(kept, grad):
    return (low(grad),)
low.defvjp(low_keep, low_pass)
low_back.defvjp(back_keep, back_low)

def bucket_table(seq_len, buckets):
    half_count = buckets // 2
    exact_count = half_count // 2
    offsets = np.arange(-(seq_len - 1), seq_len)
    upper_half = (offsets > 0).astype(np.int64) * half_count
    distance = np.abs(offsets)
    scaled = np.log(np.maximum(distance, 1) / float(exact_count)) / np.log(128.0 / exact_count) * (half_count - exact_count)
    larger = np.minimum(exact_count + np.floor(np.maximum(scaled, 0.0)).astype(np.int64), half_count - 1)
    bucket = upper_half + np.where(distance < exact_count, distance, larger)
    places = np.arange(seq_len)
    return bucket[places[None, :] - places[:, None] + seq_len - 1].astype(np.int32)

def allowed_pairs(seq_len, span_begin, span_len):
    places = jnp.arange(seq_len, dtype=jnp.int32)
    causal = places[None, :] <= places[:, None]
    inside = (places >= span_begin) & (places < span_begin + span_len)
    return causal | inside[:, None] & inside[None, :]

def rms_norm(values, norm_gain):
    return values * lax.rsqrt(lax.optimization_barrier(jnp.mean(values * values, axis=-1, keepdims=True)) + 1e-06) * norm_gain

def gate_values(logits, routes, experts):
    probabilities = jax.nn.softmax(logits, axis=-1)
    chosen = (routes[..., None] == jnp.arange(experts, dtype=jnp.int32)).astype(jnp.float32)
    picked = lax.optimization_barrier(jnp.sum(probabilities[:, None, :] * chosen, axis=-1))
    return picked / lax.optimization_barrier(jnp.sum(picked, axis=1, keepdims=True))

def local_ranks(choice_hits, priority):
    token_count = priority.shape[0]
    token_order = jnp.zeros((token_count,), jnp.int32).at[priority].set(jnp.arange(token_count, dtype=jnp.int32))
    ordered = choice_hits[token_order]
    running = (jnp.cumsum(ordered, axis=0) - ordered).astype(jnp.int32)
    return lax.optimization_barrier(jnp.sum(running[priority] * choice_hits, axis=-1)).astype(jnp.int32)

def pair_positions(group_routes, group_priority, experts, capacity):
    choice_hits = (group_routes[..., None] == jnp.arange(experts, dtype=jnp.int32)).astype(jnp.int32)
    counts = lax.optimization_barrier(jnp.sum(choice_hits, axis=1)).astype(jnp.int32)
    earlier = (jnp.cumsum(counts, axis=0) - counts).astype(jnp.int32)
    first_total = lax.optimization_barrier(jnp.sum(counts[:, 0], axis=0)).astype(jnp.int32)
    pair_ranks = jax.vmap(local_ranks)(choice_hits, group_priority)
    base_rows = lax.optimization_barrier(jnp.sum(choice_hits * earlier[:, None], axis=-1)).astype(jnp.int32)
    second_shift = lax.optimization_barrier(jnp.sum(choice_hits[:, :, 1] * first_total, axis=-1)).astype(jnp.int32)
    positions = pair_ranks + base_rows + jnp.stack([jnp.zeros_like(second_shift), second_shift], axis=-1)
    return jnp.where(positions < capacity, positions, capacity).astype(jnp.int32)

def attend_block(block_tokens, block_starts, gain_one, qkv_weight, proj_weight, table_f, bucket_index):
    batch_size, seq_len, model_width = block_tokens.shape
    highest = lax.Precision.HIGHEST
    normed = low(rms_norm(block_tokens, gain_one))
    qkv_rows = low(low_back(jnp.einsum('bld,de->ble', normed, qkv_weight, precision=highest)))
    qkv_rows = qkv_rows.reshape(batch_size, seq_len, 3, HEADS, HEAD_DIM)
    queries, key_rows, value_rows = (qkv_rows[:, :, 0], qkv_rows[:, :, 1], qkv_rows[:, :, 2])
    rel_bias = jnp.transpose(table_f[bucket_index], (2, 0, 1))
    scores = jnp.einsum('bqhc,bkhc->bhqk', queries, key_rows, precision=highest) * (1.0 / math.sqrt(HEAD_DIM)) + rel_bias[None]
    allowed = jax.vmap(lambda span_begin: allowed_pairs(seq_len, span_begin, PIC))(block_starts)
    scores = jnp.where(allowed[:, None], scores, -1e+30)
    scores = low_back(scores)
    attn_probs = low(jax.nn.softmax(scores, axis=-1))
    mixed_heads = jnp.einsum('bhqk,bkhc->bqhc', attn_probs, value_rows, precision=highest).reshape(batch_size, seq_len, model_width)
    mixed_heads = low(low_back(mixed_heads))
    branch = low_back(jnp.einsum('bld,de->ble', mixed_heads, proj_weight, precision=highest))
    return block_tokens + branch

def expert_group(group_hidden, group_routes, group_priority, gain_two, router_weight, inner_weight, outer_weight):
    highest = lax.Precision.HIGHEST
    normed = low(rms_norm(group_hidden, gain_two))
    logits = low_back(jnp.dot(normed, router_weight, precision=highest))
    flat_routes = group_routes.reshape(-1, 2)
    gate_weights = gate_values(logits, flat_routes, EXPERTS)
    destination = pair_positions(group_routes, group_priority, EXPERTS, CAP).reshape(-1)
    pair_experts = flat_routes.reshape(-1)
    filled = jnp.zeros((EXPERTS, CAP + 1, D), jnp.float32).at[pair_experts, destination].add(jnp.repeat(normed, 2, axis=0))
    expert_rows = low_back(filled[:, :CAP])
    inner_pre = low_back(jnp.einsum('ecd,edf->ecf', expert_rows, inner_weight, precision=highest))
    active = low(jax.nn.gelu(inner_pre))
    result = low(low_back(jnp.einsum('ecf,efd->ecd', active, outer_weight, precision=highest)))
    padded = jnp.concatenate([result, jnp.zeros((EXPERTS, 1, D), jnp.float32)], axis=1)
    returned = padded[pair_experts, destination].reshape(-1, 2, D)
    return group_hidden + lax.optimization_barrier(jnp.sum(gate_weights[..., None] * returned, axis=1))

def reference(tokens, gain_first, w_qkv, w_proj, bias_table, gain_second, w_router, w_in, w_out, routes, priority, span_start, cotangent):
    bucket_index = jnp.asarray(bucket_table(TOK_DEV, BUCKETS))
    per_block = math.gcd(SEQS, max(1, 4096 // TOK_DEV))

    def forward(tokens_f, gain_one, qkv_weight, proj_weight, table_f, gain_two, router_weight, inner_weight, outer_weight):
        blocks = tokens_f.reshape(SEQS // per_block, per_block, TOK_DEV, D)
        block_spans = span_start.reshape(SEQS // per_block, per_block)
        attend = jax.checkpoint(lambda pieces: attend_block(pieces[0], pieces[1], gain_one, qkv_weight, proj_weight, table_f, bucket_index))
        hidden = lax.map(attend, (blocks, block_spans)).reshape(N_GROUP, N_EXPERT * TOK_DEV, D)
        group_routes = routes.reshape(N_GROUP, N_EXPERT, TOK_DEV, 2)
        group_priority = priority.reshape(N_GROUP, N_EXPERT, TOK_DEV)
        mixture = jax.checkpoint(lambda pieces: expert_group(pieces[0], pieces[1], pieces[2], gain_two, router_weight, inner_weight, outer_weight))
        return lax.map(mixture, (hidden, group_routes, group_priority)).reshape(TOKENS, D)
    block_out, pullback = jax.vjp(forward, tokens.astype(jnp.float32), gain_first.astype(jnp.float32), w_qkv.astype(jnp.float32), w_proj.astype(jnp.float32), bias_table.astype(jnp.float32), gain_second.astype(jnp.float32), w_router.astype(jnp.float32), w_in.astype(jnp.float32), w_out.astype(jnp.float32))
    grads = pullback(cotangent.astype(jnp.float32))
    return (block_out.astype(jnp.bfloat16), grads[0].astype(jnp.bfloat16), grads[1], grads[2], grads[3], grads[4], grads[5], grads[6], grads[7], grads[8])
```

```python
import functools
import math

import jax
import jax.numpy as jnp
import numpy as np
from jax import lax
from jax.experimental import pallas as pl
from jax.experimental.pallas import tpu as pltpu
from jax.sharding import PartitionSpec as P

PIC = 256
EPS = 1e-6
LOW = jnp.bfloat16
FULL = jnp.float32
VM = pl.BlockSpec(memory_space=pltpu.VMEM)
SM = pl.BlockSpec(memory_space=pltpu.SMEM)
HBM = pl.BlockSpec(memory_space=pl.ANY)
MIB = 1 << 20
ATT_ROWS = 256
ATT_UNROLL = 2
MESH = pl.DeviceIdType.MESH
SECOND = 512.0
SLOTS = 256
ROW_TILE = 256
FF_TILE = 512


def offset_bucket(offsets, buckets):
    half_count = buckets // 2
    exact_count = half_count // 2
    upper_half = (offsets > 0).astype(np.int64) * half_count
    distance = np.abs(offsets)
    scaled = (
        np.log(np.maximum(distance, 1) / float(exact_count))
        / np.log(128.0 / exact_count)
        * (half_count - exact_count)
    )
    larger = np.minimum(
        exact_count + np.floor(np.maximum(scaled, 0.0)).astype(np.int64), half_count - 1
    )
    return upper_half + np.where(distance < exact_count, distance, larger)


def near_onehot(buckets):
    bucket = offset_bucket(np.arange(512) - 256, buckets)
    return (np.arange(buckets)[:, None] == bucket[None, :]).astype(np.float32)


def dot_nn(a, b):
    return lax.dot_general(a, b, (((1,), (0,)), ((), ())), preferred_element_type=FULL)


def dot_nt(a, b):
    return lax.dot_general(a, b, (((1,), (1,)), ((), ())), preferred_element_type=FULL)


def dot_tn(a, b):
    return lax.dot_general(a, b, (((0,), (0,)), ((), ())), preferred_element_type=FULL)


def exact_nn(a, b):
    return lax.dot_general(
        a, b, (((1,), (0,)), ((), ())), precision=lax.Precision.HIGHEST, preferred_element_type=FULL
    )


def exact_nt(a, b):
    return lax.dot_general(
        a, b, (((1,), (1,)), ((), ())), precision=lax.Precision.HIGHEST, preferred_element_type=FULL
    )


def split3(x):
    hi = x.astype(LOW)
    rest = x - hi.astype(FULL)
    mid = rest.astype(LOW)
    low = (rest - mid.astype(FULL)).astype(LOW)
    return hi, mid, low


def half_mask(sub, value, shape=(1, 128)):
    lane = lax.broadcasted_iota(jnp.int32, shape, 1)
    keep = (lane < 64) if sub == 0 else (lane >= 64)
    return jnp.where(keep, value, 0.0).astype(FULL)


def attn_setup(span_ref, table_ref, onehot_ref, near_ref, mask_ref):
    seq_len = mask_ref.shape[0]
    heads = near_ref.shape[0]
    start = span_ref[0]
    qi = lax.broadcasted_iota(jnp.int32, (seq_len, seq_len), 0)
    kj = lax.broadcasted_iota(jnp.int32, (seq_len, seq_len), 1)
    q_in = (qi >= start) & (qi < start + PIC)
    k_in = (kj >= start) & (kj < start + PIC)
    mask_ref[...] = jnp.where((kj <= qi) | (q_in & k_in), 0.0, -1e30).astype(FULL)
    vecs = exact_nn(table_ref[...], onehot_ref[...])
    for h in range(heads):
        rows = jnp.broadcast_to(vecs[h : h + 1, :], (128, 512))
        rolled = pltpu.roll(rows, 0, 1, stride=1, stride_axis=0)
        near_ref[h] = rolled[:, 128:]


def bias_rows(block, blocks, near):
    far_neg = jnp.broadcast_to(near[127:128, 0:1], (128, 128))
    far_pos = jnp.broadcast_to(near[0:1, 383:384], (128, 128))
    pieces = []
    for other in range(blocks):
        d = other - block
        if d <= -2:
            pieces.append(far_neg)
        elif d >= 2:
            pieces.append(far_pos)
        else:
            pieces.append(near[:, (d + 1) * 128 : (d + 2) * 128])
    return jnp.concatenate(pieces, axis=1)


def attn_block(row0, count, qkv_ref, near_ref, mask_ref, prob_ref, mixed_ref):
    seq_len, width3 = qkv_ref.shape
    width = width3 // 3
    blocks = seq_len // 128
    rows = slice(row0, row0 + count)

    @pl.loop(0, width // 128, unroll=ATT_UNROLL)
    def _(pair):
        col = pl.multiple_of(pair * 128, 128)
        qp = qkv_ref[rows, pl.ds(col, 128)].astype(FULL)
        kp = qkv_ref[:, pl.ds(width + col, 128)]
        vp = qkv_ref[:, pl.ds(2 * width + col, 128)]
        qs = jnp.concatenate([qp * half_mask(sub, 0.125) for sub in range(2)], axis=0)
        scores = dot_nt(qs.astype(LOW), kp)
        probs = []
        for sub in range(2):
            h = 2 * pair + sub
            for part in range(count // 128):
                first = sub * count + part * 128
                here = slice(row0 + part * 128, row0 + part * 128 + 128)
                s = scores[first : first + 128]
                bias = bias_rows(row0 // 128 + part, blocks, near_ref[h])
                s = s + bias + mask_ref[here, :]
                top = jnp.max(s, axis=1, keepdims=True)
                e = jnp.exp(s - top)
                total = jnp.sum(e, axis=1, keepdims=True)
                p = (e * (1.0 / total)).astype(LOW)
                prob_ref[h, here, :] = p
                probs.append(p)
        outs = dot_nn(jnp.concatenate(probs, axis=0), vp)
        lane = lax.broadcasted_iota(jnp.int32, (count, 128), 1)
        mixed_ref[rows, pl.ds(col, 128)] = jnp.where(
            lane < 64, outs[:count], outs[count:]
        ).astype(LOW)


def choice_hits(routes, experts):
    who = lax.broadcasted_iota(jnp.int32, (experts, routes.shape[1]), 0)
    return [who == routes[k : k + 1, :] for k in range(2)]


def to_column(row, width):
    return jnp.transpose(jnp.broadcast_to(row, (8, width)))[:, 0:1]


def ranks_by_priority(hits, priority):
    tokens = priority.shape[1]
    prio = priority.astype(FULL)
    less = jnp.where(to_column(prio, tokens) < prio, 1.0, 0.0).astype(LOW)
    return [dot_nn(jnp.where(hit, 1.0, 0.0).astype(LOW), less) for hit in hits]


def attn_dispatch_kernel(
    tokens_ref,
    cot_ref,
    gain1_ref,
    wqkv_ref,
    wproj_ref,
    table_ref,
    onehot_ref,
    gain2_ref,
    wrouter_ref,
    routes_ref,
    prio_ref,
    span_ref,
    qkv_out,
    prob_out,
    mixed_out,
    hidden_out,
    normed2_out,
    rows_ref,
    cotrows_ref,
    resg_ref,
    gatecol_ref,
    token_ref,
    info_ref,
    qkv_ref,
    prob_ref,
    mixed_ref,
    hidden_ref,
    normed2_ref,
    near_ref,
    mask_ref,
    meta_ref,
    gate_ref,
    meta_all,
    gate_all,
    gat_c,
    gat_n,
    acc_c,
    acc_n,
    acc_g,
    pos_ref,
    send_sem,
    recv_sem,
    small_send,
    small_recv,
    out_sem,
):
    g = lax.axis_index("group")
    me = lax.axis_index("expert")
    experts = wrouter_ref.shape[0]
    seq_len, width = tokens_ref.shape
    half = seq_len // 2

    def device(mask):
        return (g, lax.bitwise_xor(me, mask))

    barrier = pltpu.get_barrier_semaphore()
    for mask in range(1, experts):
        pl.semaphore_signal(barrier, inc=1, device_id=device(mask), device_id_type=MESH)
    pl.semaphore_wait(barrier, experts - 1)

    gats = (gat_c, gat_n)
    owns = (cot_ref, normed2_ref)

    def send(which, kind, chunk, held, target):
        rows = pl.ds(chunk * half, half)
        slot = lax.bitwise_xor(me, held)
        src = owns[which].at[rows, :] if held == 0 else gats[which].at[slot, rows, :]
        return pltpu.make_async_remote_copy(
            src_ref=src,
            dst_ref=gats[which].at[slot, rows, :],
            send_sem=send_sem.at[which, kind, chunk],
            recv_sem=recv_sem.at[which, held ^ target, chunk],
            device_id=device(target),
            device_id_type=MESH,
        )

    started = []

    def go(*args):
        copy = send(*args)
        copy.start()
        started.append(copy)

    def arrived(which, mask, chunk):
        rows = pl.ds(chunk * half, half)
        here = gats[which].at[lax.bitwise_xor(me, mask), rows, :]
        pltpu.make_async_remote_copy(
            src_ref=here,
            dst_ref=here,
            send_sem=send_sem.at[which, 0, chunk],
            recv_sem=recv_sem.at[which, mask, chunk],
            device_id=device(1),
            device_id_type=MESH,
        ).wait_recv()

    def own_out(which, chunk):
        go(which, 0, chunk, 0, 2)
        go(which, 1, chunk, 0, 4)
        go(which, 2, chunk, 0, 1)

    def relay(which):
        arrived(which, 2, 0)
        go(which, 3, 0, 2, 4)
        arrived(which, 4, 1)
        go(which, 3, 1, 4, 2)

    def small(src, dst, index):
        for mask in range(1, experts):
            copy = pltpu.make_async_remote_copy(
                src_ref=src,
                dst_ref=dst.at[me],
                send_sem=small_send.at[index, mask],
                recv_sem=small_recv.at[index, mask],
                device_id=device(mask),
                device_id_type=MESH,
            )
            copy.start()
            started.append(copy)

    def small_arrived(dst, index):
        for mask in range(1, experts):
            here = dst.at[lax.bitwise_xor(me, mask)]
            pltpu.make_async_remote_copy(
                src_ref=here,
                dst_ref=here,
                send_sem=small_send.at[index, mask],
                recv_sem=small_recv.at[index, mask],
                device_id=device(1),
                device_id_type=MESH,
            ).wait_recv()

    own_out(0, 0)
    own_out(0, 1)

    hits = choice_hits(routes_ref[...], experts)
    ranks = ranks_by_priority(hits, prio_ref[...])
    meta = jnp.where(hits[0], ranks[0], jnp.where(hits[1], ranks[1] + SECOND, -1.0))
    meta_ref[...] = meta
    meta_all[me] = meta
    small(meta_ref, meta_all, 0)

    attn_setup(span_ref, table_ref, onehot_ref, near_ref, mask_ref)
    for row0 in range(0, seq_len, 128):
        rows = slice(row0, row0 + 128)
        x = tokens_ref[rows, :].astype(FULL)
        inv = lax.rsqrt(jnp.mean(x * x, axis=1, keepdims=True) + EPS)
        n1 = (x * inv * gain1_ref[...][None, :]).astype(LOW)
        qkv_ref[rows, :] = dot_nn(n1, wqkv_ref[...]).astype(LOW)
    outs = [pltpu.make_async_copy(qkv_ref, qkv_out, out_sem.at[0])]
    outs[0].start()

    logits = []
    for chunk in range(2):
        row0 = chunk * half
        rows = slice(row0, row0 + half)
        attn_block(row0, half, qkv_ref, near_ref, mask_ref, prob_ref, mixed_ref)
        hidden = tokens_ref[rows, :].astype(FULL) + dot_nn(mixed_ref[rows, :], wproj_ref[...])
        hidden_ref[rows, :] = hidden
        inv = lax.rsqrt(jnp.mean(hidden * hidden, axis=1, keepdims=True) + EPS)
        n2 = (hidden * inv * gain2_ref[...][None, :]).astype(LOW)
        normed2_ref[rows, :] = n2
        own_out(1, chunk)
        logits.append(dot_nt(wrouter_ref[...], n2))
        if chunk == 0:
            relay(0)
    for index, (src, dst) in enumerate(
        ((prob_ref, prob_out), (mixed_ref, mixed_out), (hidden_ref, hidden_out), (normed2_ref, normed2_out))
    ):
        copy = pltpu.make_async_copy(src, dst, out_sem.at[index + 1])
        copy.start()
        outs.append(copy)

    logits = jnp.concatenate(logits, axis=1)
    unnormed = jnp.exp(logits - jnp.max(logits, axis=0, keepdims=True))
    probabilities = unnormed / jnp.sum(unnormed, axis=0, keepdims=True)
    picked = [jnp.sum(jnp.where(hit, probabilities, 0.0), axis=0, keepdims=True) for hit in hits]
    both = picked[0] + picked[1]
    gates = [p / both for p in picked]
    gate = jnp.where(hits[0], gates[0], jnp.where(hits[1], gates[1], 0.0))
    gate_ref[...] = gate
    gate_all[me] = gate
    small(gate_ref, gate_all, 1)

    first_count = jnp.sum(jnp.where(hits[0], 1.0, 0.0), axis=1, keepdims=True)
    who = lax.broadcasted_iota(jnp.int32, hits[0].shape, 0).astype(FULL)
    slots = [
        jnp.sum(jnp.where(hits[0], ranks[0] + who * SLOTS, 0.0), axis=0, keepdims=True),
        jnp.sum(
            jnp.where(hits[1], ranks[1] + first_count + who * SLOTS, 0.0), axis=0, keepdims=True
        ),
    ]
    routes_f = routes_ref[...].astype(FULL)
    token_rows = jnp.concatenate(slots + gates + [routes_f[0:1], routes_f[1:2]] + slots, axis=0)
    token_ref[...] = jnp.transpose(token_rows)

    small_arrived(meta_all, 0)
    value = meta_all[:, me, :]
    is_first = (value >= 0.0) & (value < SECOND)
    is_second = value >= SECOND
    counts = [
        jnp.sum(jnp.where(hit, 1.0, 0.0), axis=1, keepdims=True) for hit in (is_first, is_second)
    ]
    row = lax.broadcasted_iota(jnp.int32, (experts, 128), 0)
    lane = lax.broadcasted_iota(jnp.int32, (experts, 128), 1)
    count_mat = jnp.where(lane == 0, counts[0], jnp.where(lane == 1, counts[1], 0.0))
    before = jnp.zeros((experts, 128), FULL)
    for s in range(experts):
        before = before + jnp.where(row > s, count_mat[s : s + 1, :], 0.0)
    first_total = jnp.sum(counts[0], axis=0, keepdims=True)
    base = [before[:, 0:1], before[:, 1:2] + first_total]
    pos_ref[...] = jnp.where(
        is_first, value + base[0], jnp.where(is_second, value - SECOND + base[1], -1.0)
    )
    info_ref[...] = jnp.where(
        lane == 0,
        counts[0],
        jnp.where(lane == 1, counts[1], jnp.where(lane == 2, base[0], base[1])),
    )

    acc_c[...] = jnp.zeros_like(acc_c)
    acc_n[...] = jnp.zeros_like(acc_n)
    acc_g[...] = jnp.zeros_like(acc_g)

    def compact(which, mask, chunk):
        slot = lax.bitwise_xor(me, mask)
        cols = slice(chunk * half, chunk * half + half)
        acc = (acc_c, acc_n)[which]

        @pl.loop(0, acc.shape[0] // ROW_TILE)
        def _(tile):
            row0 = pl.multiple_of(tile * ROW_TILE, ROW_TILE)
            place = pos_ref[pl.ds(slot, 1), :][:, cols] - row0.astype(FULL)
            at = lax.broadcasted_iota(jnp.int32, (ROW_TILE, half), 0).astype(FULL)
            pick = jnp.where(at == place, 1.0, 0.0).astype(LOW)
            if mask == 0:
                data = owns[which][cols, :]
            else:
                data = gats[which][slot, cols, :]
            acc[pl.ds(row0, ROW_TILE), :] += dot_nn(pick, data)
            if which == 1:
                g_row = gate_all[slot, pl.ds(me, 1), :][:, cols]
                terms = [jnp.broadcast_to(t.astype(FULL), (8, half)) for t in split3(g_row)]
                third = lax.broadcasted_iota(jnp.int32, (8, half), 0)
                mat = jnp.where(
                    third == 0, terms[0], jnp.where(third == 1, terms[1], jnp.where(third == 2, terms[2], 0.0))
                ).astype(LOW)
                acc_g[pl.ds(row0, ROW_TILE), :] += dot_nt(pick, mat)

    def take(which, mask):
        for chunk in range(2):
            if mask:
                arrived(which, mask, chunk)
        if mask in (2, 4, 6):
            for chunk in range(2):
                go(which, 2 + mask // 2 + 0 * chunk + 1, chunk, mask, 1)
        for chunk in range(2):
            compact(which, mask, chunk)

    def take_relayed(which, mask, chunk_done):
        arrived(which, mask, 1 - chunk_done)
        for chunk in range(2):
            go(which, 3 + mask // 2, chunk, mask, 1)
        for chunk in range(2):
            compact(which, mask, chunk)

    take(0, 0)
    take(0, 1)
    take_relayed(0, 2, 0)
    take_relayed(0, 4, 1)
    take(0, 6)
    take(0, 3)
    take(0, 5)
    relay(1)
    take(0, 7)
    small_arrived(gate_all, 1)
    take(1, 0)
    take(1, 1)
    take_relayed(1, 2, 0)
    take_relayed(1, 4, 1)
    take(1, 3)
    take(1, 5)
    take(1, 6)
    take(1, 7)

    @pl.loop(0, acc_n.shape[0] // ROW_TILE)
    def _(tile):
        rows = pl.ds(pl.multiple_of(tile * ROW_TILE, ROW_TILE), ROW_TILE)
        cot_rows = acc_c[rows, :]
        gate_col = jnp.sum(acc_g[rows, :], axis=1, keepdims=True)
        rows_ref[rows, :] = acc_n[rows, :].astype(LOW)
        cotrows_ref[rows, :] = cot_rows.astype(LOW)
        resg_ref[rows, :] = (gate_col * cot_rows).astype(LOW)
        gatecol_ref[rows, :] = jnp.broadcast_to(gate_col, (ROW_TILE, 128))

    for copy in outs:
        copy.wait()
    for copy in started:
        copy.wait_send()


def attn_dispatch(
    tokens, cot, gain1, wqkv, wproj, table, gain2, wrouter, routes, priority, span
):
    seq_len, width = tokens.shape
    buckets, heads = table.shape
    experts = wrouter.shape[1]
    capacity = 5 * seq_len // 2
    sds = jax.ShapeDtypeStruct
    dma = pltpu.SemaphoreType.DMA
    return pl.pallas_call(
        attn_dispatch_kernel,
        out_shape=(
            sds((seq_len, 3 * width), LOW),
            sds((heads, seq_len, seq_len), LOW),
            sds((seq_len, width), LOW),
            sds((seq_len, width), FULL),
            sds((seq_len, width), LOW),
            sds((capacity, width), LOW),
            sds((capacity, width), LOW),
            sds((capacity, width), LOW),
            sds((capacity, 128), FULL),
            sds((seq_len, 8), FULL),
            sds((experts, 128), FULL),
        ),
        in_specs=[VM] * 11 + [SM],
        out_specs=[HBM] * 5 + [VM] * 6,
        scratch_shapes=[
            pltpu.VMEM((seq_len, 3 * width), LOW),
            pltpu.VMEM((heads, seq_len, seq_len), LOW),
            pltpu.VMEM((seq_len, width), LOW),
            pltpu.VMEM((seq_len, width), FULL),
            pltpu.VMEM((seq_len, width), LOW),
            pltpu.VMEM((heads, 128, 384), FULL),
            pltpu.VMEM((seq_len, seq_len), FULL),
            pltpu.VMEM((experts, seq_len), FULL),
            pltpu.VMEM((experts, seq_len), FULL),
            pltpu.VMEM((experts, experts, seq_len), FULL),
            pltpu.VMEM((experts, experts, seq_len), FULL),
            pltpu.VMEM((experts, seq_len, width), LOW),
            pltpu.VMEM((experts, seq_len, width), LOW),
            pltpu.VMEM((capacity, width), FULL),
            pltpu.VMEM((capacity, width), FULL),
            pltpu.VMEM((capacity, 8), FULL),
            pltpu.VMEM((experts, seq_len), FULL),
            dma((2, 7, 2)),
            dma((2, 8, 2)),
            dma((2, 8)),
            dma((2, 8)),
            dma((5,)),
        ],
        compiler_params=pltpu.CompilerParams(
            vmem_limit_bytes=60 * MIB, collective_id=0, has_side_effects=True
        ),
    )(
        tokens,
        cot,
        gain1,
        wqkv,
        wproj,
        table.T,
        jnp.asarray(near_onehot(buckets)),
        gain2,
        wrouter.T,
        routes.T,
        priority,
        span,
    )


def expert_first_kernel(rows_ref, resg_ref, win_ref, act_ref, slope_ref, gout_ref):
    pre = dot_nn(rows_ref[...], win_ref[...])
    act, slope = gelu_and_slope(pre)
    act_ref[...] = act.astype(LOW)
    slope_ref[...] = slope.astype(LOW)
    gout_ref[...] = dot_tn(act_ref[...], resg_ref[...]).astype(LOW)


def gelu_and_slope(x):
    c = math.sqrt(2.0 / math.pi)
    square = x * x
    t = jnp.tanh(x * (c + (c * 0.044715) * square))
    cdf = 0.5 + 0.5 * t
    slope = cdf + (0.5 * x) * (1.0 - t * t) * (c + (3.0 * c * 0.044715) * square)
    return x * cdf, slope


def expert_first(rows, resg, w_in):
    capacity, width = rows.shape
    ff = w_in.shape[1]
    sds = jax.ShapeDtypeStruct
    return pl.pallas_call(
        expert_first_kernel,
        grid=(ff // FF_TILE,),
        out_shape=(
            sds((capacity, ff), LOW),
            sds((capacity, ff), LOW),
            sds((ff, width), LOW),
        ),
        in_specs=[
            pl.BlockSpec((capacity, width), lambda f: (0, 0)),
            pl.BlockSpec((capacity, width), lambda f: (0, 0)),
            pl.BlockSpec((width, FF_TILE), lambda f: (0, f)),
        ],
        out_specs=[
            pl.BlockSpec((capacity, FF_TILE), lambda f: (0, f)),
            pl.BlockSpec((capacity, FF_TILE), lambda f: (0, f)),
            pl.BlockSpec((FF_TILE, width), lambda f: (f, 0)),
        ],
        compiler_params=pltpu.CompilerParams(vmem_limit_bytes=56 * MIB),
        cost_estimate=pl.CostEstimate(
            flops=4 * capacity * width * ff, bytes_accessed=40 * MIB, transcendentals=capacity * ff
        ),
    )(rows, resg, w_in)


def pack_rows(source, info_ref, data, out_ref, slots):
    info = info_ref[source : source + 1, :]
    slot = lax.broadcasted_iota(jnp.int32, (slots, 1), 0).astype(FULL)
    n0, n1, b0, b1 = [info[:, i : i + 1] for i in range(4)]
    place = jnp.where(slot < n0, b0 + slot, jnp.where(slot < n0 + n1, b1 + slot - n0, -1.0))
    at = lax.broadcasted_iota(jnp.int32, (slots, data.shape[0]), 1).astype(FULL)
    pick = jnp.where(at == place, 1.0, 0.0).astype(LOW)
    out_ref[source] = dot_nn(pick, data[...]).astype(LOW)


def expert_second_kernel(
    cot_ref, gate_ref, act_ref, slope_ref, wout_ref, win_ref, info_ref, ig_ref, packed_ref, acc_ref, gg_ref, data_ref
):
    step = pl.program_id(0)
    width = cot_ref.shape[1]

    @pl.when(step == 0)
    def _():
        acc_ref[...] = jnp.zeros_like(acc_ref)
        gg_ref[...] = jnp.zeros_like(gg_ref)

    back = dot_nt(cot_ref[...], wout_ref[...])
    part = act_ref[...].astype(FULL) * back
    total = part[:, 0:128]
    for i in range(1, part.shape[1] // 128):
        total = total + part[:, i * 128 : i * 128 + 128]
    gg_ref[...] += total
    ig = (slope_ref[...].astype(FULL) * (gate_ref[:, 0:1] * back)).astype(LOW)
    ig_ref[...] = ig
    acc_ref[...] += dot_nt(ig, win_ref[...])

    @pl.when(step == pl.num_programs(0) - 1)
    def _():
        data_ref[:, :width] = acc_ref[...].astype(LOW)
        gg = jnp.sum(gg_ref[...], axis=1, keepdims=True)
        hi, mid, low = [t.astype(FULL) for t in split3(gg)]
        lane = lax.broadcasted_iota(jnp.int32, (gg.shape[0], 128), 1)
        data_ref[:, width:] = jnp.where(
            lane == 0, hi, jnp.where(lane == 1, mid, jnp.where(lane == 2, low, 0.0))
        ).astype(LOW)
        for source in range(packed_ref.shape[0]):
            pack_rows(source, info_ref, data_ref, packed_ref, packed_ref.shape[1])


def expert_second(cot_rows, gate_col, act, slope, w_out, w_in, info):
    capacity, width = cot_rows.shape
    ff = w_in.shape[1]
    experts = info.shape[0]
    sds = jax.ShapeDtypeStruct
    return pl.pallas_call(
        expert_second_kernel,
        grid=(ff // FF_TILE,),
        out_shape=(
            sds((capacity, ff), LOW),
            sds((experts, SLOTS, width + 128), LOW),
        ),
        in_specs=[
            pl.BlockSpec((capacity, width), lambda f: (0, 0)),
            pl.BlockSpec((capacity, 128), lambda f: (0, 0)),
            pl.BlockSpec((capacity, FF_TILE), lambda f: (0, f)),
            pl.BlockSpec((capacity, FF_TILE), lambda f: (0, f)),
            pl.BlockSpec((FF_TILE, width), lambda f: (f, 0)),
            pl.BlockSpec((width, FF_TILE), lambda f: (0, f)),
            pl.BlockSpec((experts, 128), lambda f: (0, 0)),
        ],
        out_specs=[
            pl.BlockSpec((capacity, FF_TILE), lambda f: (0, f)),
            pl.BlockSpec((experts, SLOTS, width + 128), lambda f: (0, 0, 0)),
        ],
        scratch_shapes=[
            pltpu.VMEM((capacity, width), FULL),
            pltpu.VMEM((capacity, 128), FULL),
            pltpu.VMEM((capacity, width + 128), LOW),
        ],
        compiler_params=pltpu.CompilerParams(vmem_limit_bytes=56 * MIB),
        cost_estimate=pl.CostEstimate(
            flops=4 * capacity * width * ff, bytes_accessed=50 * MIB, transcendentals=0
        ),
    )(cot_rows, gate_col, act, slope, w_out, w_in, info)


def expert_inner_kernel(rows_ref, ig_ref, gin_ref, rows_t):
    @pl.when(pl.program_id(0) == 0)
    def _():
        rows_t[...] = jnp.transpose(rows_ref[...])

    gin_ref[...] = dot_nn(rows_t[...], ig_ref[...]).astype(LOW)


def expert_inner(rows, ig):
    capacity, width = rows.shape
    ff = ig.shape[1]
    return pl.pallas_call(
        expert_inner_kernel,
        grid=(ff // FF_TILE,),
        out_shape=jax.ShapeDtypeStruct((width, ff), LOW),
        in_specs=[
            pl.BlockSpec((capacity, width), lambda f: (0, 0)),
            pl.BlockSpec((capacity, FF_TILE), lambda f: (0, f)),
        ],
        out_specs=pl.BlockSpec((width, FF_TILE), lambda f: (0, f)),
        scratch_shapes=[pltpu.VMEM((width, capacity), LOW)],
        compiler_params=pltpu.CompilerParams(vmem_limit_bytes=56 * MIB),
        cost_estimate=pl.CostEstimate(
            flops=2 * capacity * width * ff, bytes_accessed=15 * MIB, transcendentals=0
        ),
    )(rows, ig)


def expert_result_kernel(act_ref, wout_ref, info_ref, packed_ref, acc_ref, data_ref):
    step = pl.program_id(0)

    @pl.when(step == 0)
    def _():
        acc_ref[...] = jnp.zeros_like(acc_ref)

    acc_ref[...] += dot_nn(act_ref[...], wout_ref[...])

    @pl.when(step == pl.num_programs(0) - 1)
    def _():
        data_ref[...] = acc_ref[...].astype(LOW)
        for source in range(packed_ref.shape[0]):
            pack_rows(source, info_ref, data_ref, packed_ref, packed_ref.shape[1])


def expert_result(act, w_out, info):
    capacity, ff = act.shape
    width = w_out.shape[1]
    experts = info.shape[0]
    return pl.pallas_call(
        expert_result_kernel,
        grid=(ff // FF_TILE,),
        out_shape=jax.ShapeDtypeStruct((experts, SLOTS, width), LOW),
        in_specs=[
            pl.BlockSpec((capacity, FF_TILE), lambda f: (0, f)),
            pl.BlockSpec((FF_TILE, width), lambda f: (f, 0)),
            pl.BlockSpec((experts, 128), lambda f: (0, 0)),
        ],
        out_specs=pl.BlockSpec((experts, SLOTS, width), lambda f: (0, 0, 0)),
        scratch_shapes=[pltpu.VMEM((capacity, width), FULL), pltpu.VMEM((capacity, width), LOW)],
        compiler_params=pltpu.CompilerParams(vmem_limit_bytes=56 * MIB),
        cost_estimate=pl.CostEstimate(
            flops=2 * capacity * width * ff, bytes_accessed=20 * MIB, transcendentals=0
        ),
    )(act, w_out, info)


def slot_picks(token_ref, slots):
    at = lax.broadcasted_iota(jnp.int32, (token_ref.shape[0], slots), 1).astype(FULL)
    return [jnp.where(at == token_ref[:, k : k + 1], 1.0, 0.0) for k in range(2)]


def combine_kernel(hidden_ref, token_ref, back_ref, out_ref):
    rows = 128
    width = hidden_ref.shape[1]
    for row0 in range(0, hidden_ref.shape[0], rows):
        here = slice(row0, row0 + rows)
        token = token_ref[here, :]
        at = lax.broadcasted_iota(jnp.int32, (rows, back_ref.shape[0]), 1).astype(FULL)
        picks = [jnp.where(at == token[:, k : k + 1], 1.0, 0.0).astype(LOW) for k in range(2)]
        got = dot_nn(jnp.concatenate(picks, axis=0), back_ref[...])
        out = hidden_ref[here, :] + token[:, 2:3] * got[:rows] + token[:, 3:4] * got[rows:]
        out_ref[here, :] = out.astype(LOW)


def combine(hidden, token, back):
    return pl.pallas_call(
        combine_kernel,
        out_shape=jax.ShapeDtypeStruct(hidden.shape, LOW),
        in_specs=[VM] * 3,
        out_specs=VM,
        compiler_params=pltpu.CompilerParams(vmem_limit_bytes=56 * MIB),
        cost_estimate=pl.CostEstimate(
            flops=4 * hidden.shape[0] * hidden.shape[1] * back.shape[0],
            bytes_accessed=6 * MIB,
            transcendentals=0,
        ),
    )(hidden, token, back)


def attn_back_kernel(
    tokens_ref,
    cot_ref,
    hidden_ref,
    normed2_ref,
    mixed_ref,
    qkv_ref,
    prob_ref,
    recv_ref,
    token_ref,
    gain1_ref,
    gain2_ref,
    wqkv_ref,
    wproj_ref,
    wrouter_ref,
    onehot_ref,
    gtok_ref,
    ggain1_ref,
    gqkv_ref,
    gproj_ref,
    gtable_ref,
    ggain2_ref,
    grouter_ref,
    hgrad_ref,
    mgrad_ref,
    mgrad_t,
    q_t,
    ds_ref,
    diag_ref,
    dk_t,
    dv_t,
    dqkv_ref,
):
    seq_len, width = tokens_ref.shape
    experts = wrouter_ref.shape[0]
    heads = prob_ref.shape[0]
    tile = 128
    ggain2 = jnp.zeros((8, width), FULL)
    lg_t = []
    for row0 in range(0, seq_len, tile):
        rows = slice(row0, row0 + tile)
        token = token_ref[rows, :]
        at = lax.broadcasted_iota(jnp.int32, (tile, recv_ref.shape[0]), 1).astype(FULL)
        picks = [jnp.where(at == token[:, k : k + 1], 1.0, 0.0).astype(LOW) for k in range(2)]
        got = dot_nn(jnp.concatenate(picks, axis=0), recv_ref[...])
        gg = [
            jnp.sum(got[k * tile : k * tile + tile, width:], axis=1, keepdims=True) for k in range(2)
        ]
        pull = token[:, 2:3] * token[:, 3:4] * (gg[0] - gg[1])
        expert = lax.broadcasted_iota(jnp.int32, (tile, 128), 1).astype(FULL)
        lg = jnp.where(expert == token[:, 4:5], pull, jnp.where(expert == token[:, 5:6], -pull, 0.0))
        lg_t.append(jnp.transpose(lg)[:experts])
        ngrad = (
            got[:tile, :width]
            + got[tile:, :width]
            + dot_nn(lg[:, :experts].astype(LOW), wrouter_ref[...])
        )
        hidden = hidden_ref[rows, :]
        inv = lax.rsqrt(jnp.mean(hidden * hidden, axis=1, keepdims=True) + EPS)
        unit = hidden * inv
        ng = ngrad * unit
        for i in range(tile // 8):
            ggain2 = ggain2 + ng[i * 8 : i * 8 + 8]
        scaled = ngrad * gain2_ref[...][None, :]
        proj = jnp.mean(scaled * unit, axis=1, keepdims=True)
        hgrad_ref[rows, :] = cot_ref[rows, :].astype(FULL) + inv * (scaled - unit * proj)
        mgrad_ref[rows, :] = dot_nt(hgrad_ref[rows, :].astype(LOW), wproj_ref[...]).astype(LOW)
    ggain2_ref[...] = jnp.sum(ggain2, axis=0, keepdims=True)
    logit_grad_t = jnp.concatenate(lg_t, axis=1).astype(LOW)
    grouter_ref[...] = dot_nn(logit_grad_t, normed2_ref[...])
    gproj_ref[...] = dot_nn(
        jnp.transpose(mixed_ref[...]), hgrad_ref[...].astype(LOW)
    ).astype(LOW)
    mgrad_t[...] = jnp.transpose(mgrad_ref[...])
    q_t[...] = jnp.transpose(qkv_ref[:, :width])
    up = lax.broadcasted_iota(jnp.int32, (128, 128), 0)
    across = lax.broadcasted_iota(jnp.int32, (128, 128), 1)
    flip = jnp.where(up + across == 127, 1.0, 0.0).astype(FULL)

    @pl.loop(0, width // 128)
    def _(pair):
        col = pl.multiple_of(pair * 128, 128)
        kp = qkv_ref[:, pl.ds(width + col, 128)]
        vp = qkv_ref[:, pl.ds(2 * width + col, 128)]
        op = mgrad_ref[:, pl.ds(col, 128)].astype(FULL)
        os = jnp.concatenate([(op * half_mask(sub, 1.0)).astype(LOW) for sub in range(2)], axis=0)
        dp = dot_nt(os, vp)
        for sub in range(2):
            h = 2 * pair + sub
            near = jnp.zeros((128, 384), FULL)
            far_neg = jnp.zeros((128, 128), FULL)
            far_pos = jnp.zeros((128, 128), FULL)
            blocks = seq_len // 128
            for block in range(blocks):
                first = sub * seq_len + block * 128
                here = slice(block * 128, block * 128 + 128)
                p = prob_ref[h, here, :].astype(FULL)
                weighted = p * dp[first : first + 128]
                ds = weighted - p * jnp.sum(weighted, axis=1, keepdims=True)
                low = ds.astype(LOW)
                ds_ref[sub, here, :] = low
                ds = low.astype(FULL)
                strip = []
                for d in range(-1, 2):
                    other = block + d
                    if 0 <= other < blocks:
                        strip.append(ds[:, other * 128 : other * 128 + 128])
                    else:
                        strip.append(jnp.zeros((128, 128), FULL))
                near = near + jnp.concatenate(strip, axis=1)
                for other in range(blocks):
                    piece = ds[:, other * 128 : other * 128 + 128]
                    if other - block <= -2:
                        far_neg = far_neg + piece
                    elif other - block >= 2:
                        far_pos = far_pos + piece
            low_sum = jnp.sum(far_neg)
            high_sum = jnp.sum(far_pos)
            padded = jnp.concatenate([exact_nn(flip, near), jnp.zeros((128, 128), FULL)], axis=1)
            turned = pltpu.roll(padded, 1, 1, stride=1, stride_axis=0)
            sums = jnp.sum(turned, axis=0, keepdims=True)
            lane = lax.broadcasted_iota(jnp.int32, (1, 512), 1)
            sums = sums + jnp.where(lane == 1, low_sum, jnp.where(lane == 511, high_sum, 0.0))
            diag_ref[pl.ds(h, 1), :] = sums
        lane = lax.broadcasted_iota(jnp.int32, (seq_len, 128), 1)
        dq = dot_nn(jnp.concatenate([ds_ref[0], ds_ref[1]], axis=0), kp)
        dqkv_ref[:, pl.ds(col, 128)] = (
            jnp.where(lane < 64, dq[:seq_len], dq[seq_len:]) * 0.125
        ).astype(LOW)
        for sub in range(2):
            part = pl.ds(pl.multiple_of(col + sub * 64, 64), 64)
            dk_t[part, :] = (dot_nn(q_t[part, :], ds_ref[sub]) * 0.125).astype(LOW)
            dv_t[part, :] = dot_nn(mgrad_t[part, :], prob_ref[2 * pair + sub]).astype(LOW)

    gtable_ref[...] = exact_nt(onehot_ref[...], diag_ref[...])
    dqkv_ref[:, width : 2 * width] = jnp.transpose(dk_t[...])
    dqkv_ref[:, 2 * width :] = jnp.transpose(dv_t[...])

    ggain1 = jnp.zeros((8, width), FULL)
    for row0 in range(0, seq_len, tile):
        rows = slice(row0, row0 + tile)
        x = tokens_ref[rows, :].astype(FULL)
        inv = lax.rsqrt(jnp.mean(x * x, axis=1, keepdims=True) + EPS)
        unit = x * inv
        mgrad_ref[rows, :] = (unit * gain1_ref[...][None, :]).astype(LOW)
        ngrad = dot_nt(dqkv_ref[rows, :], wqkv_ref[...])
        ng = ngrad * unit
        for i in range(tile // 8):
            ggain1 = ggain1 + ng[i * 8 : i * 8 + 8]
        scaled = ngrad * gain1_ref[...][None, :]
        proj = jnp.mean(scaled * unit, axis=1, keepdims=True)
        gtok_ref[rows, :] = (hgrad_ref[rows, :] + inv * (scaled - unit * proj)).astype(LOW)
    ggain1_ref[...] = jnp.sum(ggain1, axis=0, keepdims=True)
    mgrad_t[...] = jnp.transpose(mgrad_ref[...])
    gqkv_ref[...] = dot_nn(mgrad_t[...], dqkv_ref[...]).astype(LOW)


def attn_back(
    tokens, cot, hidden, normed2, mixed, qkv, prob, recv, token, gain1, gain2, wqkv, wproj, wrouter, table
):
    seq_len, width = tokens.shape
    buckets, heads = table.shape
    experts = wrouter.shape[1]
    sds = jax.ShapeDtypeStruct
    return pl.pallas_call(
        attn_back_kernel,
        out_shape=(
            sds((seq_len, width), LOW),
            sds((1, width), FULL),
            sds((width, 3 * width), LOW),
            sds((width, width), LOW),
            sds((buckets, heads), FULL),
            sds((1, width), FULL),
            sds((experts, width), FULL),
        ),
        in_specs=[VM] * 15,
        out_specs=[VM] * 7,
        scratch_shapes=[
            pltpu.VMEM((seq_len, width), FULL),
            pltpu.VMEM((seq_len, width), LOW),
            pltpu.VMEM((width, seq_len), LOW),
            pltpu.VMEM((width, seq_len), LOW),
            pltpu.VMEM((2, seq_len, seq_len), LOW),
            pltpu.VMEM((heads, 512), FULL),
            pltpu.VMEM((width, seq_len), LOW),
            pltpu.VMEM((width, seq_len), LOW),
            pltpu.VMEM((seq_len, 3 * width), LOW),
        ],
        compiler_params=pltpu.CompilerParams(vmem_limit_bytes=56 * MIB),
        cost_estimate=pl.CostEstimate(
            flops=20_000_000_000, bytes_accessed=30 * MIB, transcendentals=0
        ),
    )(
        tokens,
        cot,
        hidden,
        normed2,
        mixed,
        qkv,
        prob,
        recv,
        token,
        gain1,
        gain2,
        wqkv,
        wproj,
        wrouter.T,
        jnp.asarray(near_onehot(buckets)),
    )


def on_device_fast(
    tokens,
    gain_first,
    w_qkv,
    w_proj,
    bias_table,
    gain_second,
    w_router,
    w_in,
    w_out,
    routes,
    priority,
    span_start,
    cotangent,
):
    experts = w_router.shape[1]
    width = tokens.shape[1]
    qkv, prob, mixed, hidden, normed2, rows, cot_rows, resg, gate_col, token, info = attn_dispatch(
        tokens,
        cotangent,
        gain_first,
        w_qkv,
        w_proj,
        bias_table,
        gain_second,
        w_router,
        routes,
        priority,
        span_start,
    )
    act, slope, grad_outer = expert_first(rows, resg, w_in[0])
    grad_out = lax.psum_scatter(
        grad_outer[None], "group", scatter_dimension=1, tiled=True
    ).astype(FULL)
    ig, packed = expert_second(cot_rows, gate_col, act, slope, w_out[0], w_in[0], info)
    recv = lax.all_to_all(packed, "expert", split_axis=0, concat_axis=0, tiled=True)
    grad_inner = expert_inner(rows, ig)
    grad_in = lax.psum_scatter(
        grad_inner[None], "group", scatter_dimension=1, tiled=True
    ).astype(FULL)
    packed_out = expert_result(act, w_out[0], info)
    back = lax.all_to_all(packed_out, "expert", split_axis=0, concat_axis=0, tiled=True)
    gtok, ggain1, gqkv, gproj, gtable, ggain2, grouter = attn_back(
        tokens,
        cotangent,
        hidden,
        normed2,
        mixed,
        qkv,
        prob,
        recv.reshape(-1, width + 128),
        token,
        gain_first,
        gain_second,
        w_qkv,
        w_proj,
        w_router,
        bias_table,
    )
    block_out = combine(hidden, token, back.reshape(-1, width))

    def reduce(x):
        share = lax.psum_scatter(x.astype(LOW), "expert", scatter_dimension=0, tiled=True)
        return lax.psum(share, "group").astype(FULL)

    return (
        block_out,
        gtok,
        reduce(ggain1[0]),
        reduce(gqkv),
        reduce(gproj),
        reduce(gtable),
        reduce(ggain2[0]),
        reduce(grouter.T),
        grad_in,
        grad_out,
    )


def bucket_table(seq_len, buckets):
    half_count = buckets // 2
    exact_count = half_count // 2
    offsets = np.arange(-(seq_len - 1), seq_len)
    upper_half = (offsets > 0).astype(np.int64) * half_count
    distance = np.abs(offsets)
    scaled = (
        np.log(np.maximum(distance, 1) / float(exact_count))
        / np.log(128.0 / exact_count)
        * (half_count - exact_count)
    )
    larger = np.minimum(
        exact_count + np.floor(np.maximum(scaled, 0.0)).astype(np.int64), half_count - 1
    )
    bucket = upper_half + np.where(distance < exact_count, distance, larger)
    places = np.arange(seq_len)
    return bucket[places[None, :] - places[:, None] + seq_len - 1].astype(np.int32)


def allowed_pairs(seq_len, span_begin, span_len):
    places = jnp.arange(seq_len, dtype=jnp.int32)
    causal = places[None, :] <= places[:, None]
    inside = (places >= span_begin) & (places < span_begin + span_len)
    return causal | inside[:, None] & inside[None, :]


def rms_norm(values, norm_gain):
    return values * lax.rsqrt(jnp.mean(values * values, axis=-1, keepdims=True) + 1e-06) * norm_gain


def gate_values(logits, routes, experts):
    probabilities = jax.nn.softmax(logits, axis=-1)
    chosen = (routes[..., None] == jnp.arange(experts, dtype=jnp.int32)).astype(jnp.float32)
    picked = jnp.sum(probabilities[:, None, :] * chosen, axis=-1)
    return picked / jnp.sum(picked, axis=1, keepdims=True)


def local_ranks(choice_hits, priority):
    token_count = priority.shape[0]
    token_order = (
        jnp.zeros((token_count,), jnp.int32)
        .at[priority]
        .set(jnp.arange(token_count, dtype=jnp.int32))
    )
    ordered = choice_hits[token_order]
    running = jnp.cumsum(ordered, axis=0) - ordered
    return jnp.sum(running[priority] * choice_hits, axis=-1)


def contract_rows(left, right):
    return lax.dot_general(
        left, right, (((0,), (0,)), ((), ())), preferred_element_type=jnp.float32
    )


def on_device(
    tokens,
    gain_first,
    w_qkv,
    w_proj,
    bias_table,
    gain_second,
    w_router,
    w_in,
    w_out,
    routes,
    priority,
    span_start,
    cotangent,
):
    seq_len, model_width = tokens.shape
    buckets, head_count = bias_table.shape
    head_dim = model_width // head_count
    experts = w_router.shape[1]
    slot_count = 4 * seq_len // experts
    capacity = 5 * seq_len // 2
    score_scale = 1.0 / math.sqrt(head_dim)
    highest = lax.Precision.HIGHEST
    lowtype = jnp.bfloat16
    fulltype = jnp.float32
    tokens_f = tokens.astype(fulltype)
    normed_one = rms_norm(tokens_f, gain_first).astype(lowtype)
    qkv_rows = jnp.dot(normed_one, w_qkv, preferred_element_type=fulltype).astype(lowtype)
    qkv_rows = qkv_rows.reshape(seq_len, 3, head_count, head_dim)
    queries, key_rows, value_rows = (qkv_rows[:, 0], qkv_rows[:, 1], qkv_rows[:, 2])
    bucket_index = jnp.asarray(bucket_table(seq_len, buckets))
    onehot_table = (bucket_index[:, :, None] == jnp.arange(buckets, dtype=jnp.int32)).astype(
        fulltype
    )
    rel_bias = jnp.einsum("qkb,bh->hqk", onehot_table, bias_table, precision=highest)
    allowed = allowed_pairs(seq_len, span_start[0], PIC)

    def masked_scores():
        raw_scores = (
            jnp.einsum("qhc,khc->hqk", queries, key_rows, preferred_element_type=fulltype)
            * score_scale
            + rel_bias
        )
        return jnp.where(allowed[None], raw_scores, -1e30)

    scores = masked_scores()
    log_total = jax.nn.logsumexp(scores, axis=-1)
    attn_probs = jnp.exp(scores - log_total[..., None]).astype(lowtype)
    mixed_heads = jnp.einsum(
        "hqk,khc->qhc", attn_probs, value_rows, preferred_element_type=fulltype
    )
    mixed_heads = mixed_heads.astype(lowtype).reshape(seq_len, model_width)
    hidden = tokens_f + jnp.dot(mixed_heads, w_proj, preferred_element_type=fulltype)
    normed_two = rms_norm(hidden, gain_second).astype(lowtype)
    logits = jnp.dot(normed_two, w_router, preferred_element_type=fulltype)
    gate_weights = gate_values(logits, routes, experts)
    choice_hits = (routes[..., None] == jnp.arange(experts, dtype=jnp.int32)).astype(jnp.int32)
    counts = jnp.sum(choice_hits, axis=0)
    every_count = lax.all_gather(counts[None], "expert", axis=0, tiled=True)
    pair_ranks = local_ranks(choice_hits, priority[0])
    second_shift = jnp.sum(choice_hits[:, 1] * counts[0], axis=-1)
    slot_index = pair_ranks + jnp.stack([jnp.zeros_like(second_shift), second_shift], axis=-1)
    flat_slot = (routes * slot_count + slot_index).reshape(-1)
    own_expert = (jnp.arange(experts, dtype=jnp.int32) == lax.axis_index("expert")).astype(
        jnp.int32
    )
    own_counts = jnp.sum(every_count * own_expert, axis=-1)
    first_rows, second_rows = (own_counts[:, 0], own_counts[:, 1])
    first_before = jnp.cumsum(first_rows) - first_rows
    second_before = jnp.cumsum(second_rows) - second_rows
    first_total = jnp.sum(first_rows)
    column = jnp.arange(slot_count, dtype=jnp.int32)[None, :]
    position = jnp.where(
        column < first_rows[:, None],
        first_before[:, None] + column,
        first_total + second_before[:, None] + column - first_rows[:, None],
    )
    usable = (column < (first_rows + second_rows)[:, None]) & (position < capacity)
    destination = jnp.where(usable, position, capacity).reshape(-1)

    def pack_pairs(pair_rows):
        packed = jnp.zeros((experts * slot_count, model_width), lowtype)
        packed = packed.at[flat_slot].set(pair_rows.reshape(-1, model_width))
        return packed.reshape(experts, slot_count, model_width)

    def compact_rows(arrived):
        gathered_rows = jnp.zeros((capacity + 1, model_width), lowtype)
        return gathered_rows.at[destination].add(arrived.reshape(-1, model_width))[:capacity]

    def spread_rows(expert_out):
        padded = jnp.concatenate([expert_out, jnp.zeros((1, model_width), lowtype)], axis=0)
        return padded[destination].reshape(-1, slot_count, model_width)

    def unpack_pairs(received):
        return (
            received.reshape(-1, model_width)[flat_slot]
            .reshape(seq_len, 2, model_width)
            .astype(fulltype)
        )

    pair_rows = jnp.broadcast_to(normed_two[:, None, :], (seq_len, 2, model_width))
    arrived = lax.all_to_all(
        pack_pairs(pair_rows), "expert", split_axis=0, concat_axis=0, tiled=True
    )
    expert_rows = compact_rows(arrived)
    inner_pre = jnp.dot(expert_rows, w_in[0], preferred_element_type=fulltype)
    active = jax.nn.gelu(inner_pre).astype(lowtype)
    result = jnp.dot(active, w_out[0], preferred_element_type=fulltype).astype(lowtype)
    returned = unpack_pairs(
        lax.all_to_all(spread_rows(result), "expert", split_axis=0, concat_axis=0, tiled=True)
    )
    block_out = hidden + jnp.sum(gate_weights[..., None] * returned, axis=1)
    upstream = cotangent.astype(fulltype)
    gate_grad = jnp.sum(upstream[:, None, :] * returned, axis=-1)
    result_grad = (gate_weights[..., None] * upstream[:, None, :]).astype(lowtype)
    result_rows = compact_rows(
        lax.all_to_all(pack_pairs(result_grad), "expert", split_axis=0, concat_axis=0, tiled=True)
    )
    grad_outer = contract_rows(active, result_rows)
    hidden_pre_grad = jnp.dot(result_rows, w_out[0].T, preferred_element_type=fulltype)
    inner_grad = jax.vjp(jax.nn.gelu, inner_pre)[1](hidden_pre_grad)[0].astype(lowtype)
    grad_inner = contract_rows(expert_rows, inner_grad)
    rows_grad = jnp.dot(inner_grad, w_in[0].T, preferred_element_type=fulltype).astype(lowtype)
    pair_grad = unpack_pairs(
        lax.all_to_all(spread_rows(rows_grad), "expert", split_axis=0, concat_axis=0, tiled=True)
    )
    logit_grad = jax.vjp(lambda values: gate_values(values, routes, experts), logits)[1](gate_grad)[
        0
    ].astype(lowtype)
    grad_router = contract_rows(normed_two, logit_grad)
    normed_grad = jnp.sum(pair_grad, axis=1) + jnp.dot(
        logit_grad, w_router.T, preferred_element_type=fulltype
    )
    second_back = jax.vjp(rms_norm, hidden, gain_second)[1](normed_grad)
    hidden_grad = upstream + second_back[0]
    branch_grad = hidden_grad.astype(lowtype)
    grad_proj = contract_rows(mixed_heads, branch_grad)
    mixed_grad = jnp.dot(branch_grad, w_proj.T, preferred_element_type=fulltype).astype(lowtype)
    mixed_grad = mixed_grad.reshape(seq_len, head_count, head_dim)
    scores = masked_scores()
    probs_full = jnp.exp(scores - log_total[..., None])
    probs_low = probs_full.astype(lowtype)
    prob_grad = jnp.einsum("qhc,khc->hqk", mixed_grad, value_rows, preferred_element_type=fulltype)
    value_grad = jnp.einsum("hqk,qhc->khc", probs_low, mixed_grad, preferred_element_type=fulltype)
    row_dot = jnp.sum(probs_full * prob_grad, axis=-1, keepdims=True)
    score_grad = (probs_full * (prob_grad - row_dot)).astype(lowtype)
    query_grad = (
        jnp.einsum("hqk,khc->qhc", score_grad, key_rows, preferred_element_type=fulltype)
        * score_scale
    )
    key_grad = (
        jnp.einsum("hqk,qhc->khc", score_grad, queries, preferred_element_type=fulltype)
        * score_scale
    )
    grad_table = jnp.einsum(
        "hqk,qkb->bh", score_grad.astype(fulltype), onehot_table, precision=highest
    )
    qkv_grad = (
        jnp.stack([query_grad, key_grad, value_grad], axis=1)
        .astype(lowtype)
        .reshape(seq_len, 3 * model_width)
    )
    grad_qkv = contract_rows(normed_one, qkv_grad)
    normed_one_grad = jnp.dot(qkv_grad, w_qkv.T, preferred_element_type=fulltype)
    first_back = jax.vjp(rms_norm, tokens_f, gain_first)[1](normed_one_grad)
    grad_tokens = (hidden_grad + first_back[0]).astype(lowtype)
    dense_grads = (first_back[1], grad_qkv, grad_proj, grad_table, second_back[1], grad_router)
    shares = (
        lax.psum_scatter(
            dense_grads[0].astype(jnp.bfloat16), "expert", scatter_dimension=0, tiled=True
        ).astype(jnp.float32),
        lax.psum_scatter(
            dense_grads[1].astype(jnp.bfloat16), "expert", scatter_dimension=0, tiled=True
        ).astype(jnp.float32),
        lax.psum_scatter(
            dense_grads[2].astype(jnp.bfloat16), "expert", scatter_dimension=0, tiled=True
        ).astype(jnp.float32),
        lax.psum_scatter(
            dense_grads[3].astype(jnp.bfloat16), "expert", scatter_dimension=0, tiled=True
        ).astype(jnp.float32),
        lax.psum_scatter(
            dense_grads[4].astype(jnp.bfloat16), "expert", scatter_dimension=0, tiled=True
        ).astype(jnp.float32),
        lax.psum_scatter(
            dense_grads[5].astype(jnp.bfloat16), "expert", scatter_dimension=0, tiled=True
        ).astype(jnp.float32),
    )
    totals = (
        lax.psum(shares[0].astype(jnp.bfloat16), "group").astype(jnp.float32),
        lax.psum(shares[1].astype(jnp.bfloat16), "group").astype(jnp.float32),
        lax.psum(shares[2].astype(jnp.bfloat16), "group").astype(jnp.float32),
        lax.psum(shares[3].astype(jnp.bfloat16), "group").astype(jnp.float32),
        lax.psum(shares[4].astype(jnp.bfloat16), "group").astype(jnp.float32),
        lax.psum(shares[5].astype(jnp.bfloat16), "group").astype(jnp.float32),
    )
    grad_in, grad_out = (
        lax.psum_scatter(
            grad_inner[None].astype(jnp.bfloat16), "group", scatter_dimension=1, tiled=True
        ).astype(jnp.float32),
        lax.psum_scatter(
            grad_outer[None].astype(jnp.bfloat16), "group", scatter_dimension=1, tiled=True
        ).astype(jnp.float32),
    )
    return (
        block_out.astype(lowtype),
        grad_tokens,
        totals[0],
        totals[1],
        totals[2],
        totals[3],
        totals[4],
        totals[5],
        grad_in,
        grad_out,
    )


def solution(mesh):
    step = on_device_fast if mesh.shape["expert"] == 8 else on_device
    return jax.shard_map(
        step,
        mesh=mesh,
        in_specs=(
            P(("group", "expert"), None),
            P(),
            P(),
            P(),
            P(),
            P(),
            P(),
            P("expert", None, None),
            P("expert", None, None),
            P(("group", "expert"), None),
            P(("group", "expert"), None),
            P(("group", "expert")),
            P(("group", "expert"), None),
        ),
        out_specs=(
            P(("group", "expert"), None),
            P(("group", "expert"), None),
            P("expert"),
            P("expert", None),
            P("expert", None),
            P("expert", None),
            P("expert"),
            P("expert", None),
            P("expert", "group", None),
            P("expert", "group", None),
        ),
        check_vma=False,
    )
```

```python
import functools
import math

import jax
import jax.numpy as jnp
import numpy as np
from jax import lax
from jax.experimental import pallas as pl
from jax.experimental.pallas import tpu as pltpu
from jax.sharding import PartitionSpec as P

PIC = 256
EPS = 1e-6
LOW = jnp.bfloat16
FULL = jnp.float32
VM = pl.BlockSpec(memory_space=pltpu.VMEM)
SM = pl.BlockSpec(memory_space=pltpu.SMEM)
HBM = pl.BlockSpec(memory_space=pl.ANY)
MIB = 1 << 20
ATT_ROWS = 256
ATT_UNROLL = 2
MESH = pl.DeviceIdType.MESH
SECOND = 512.0
SLOTS = 256
ROW_TILE = 256
FF_TILE = 512


def offset_bucket(offsets, buckets):
    half_count = buckets // 2
    exact_count = half_count // 2
    upper_half = (offsets > 0).astype(np.int64) * half_count
    distance = np.abs(offsets)
    scaled = (
        np.log(np.maximum(distance, 1) / float(exact_count))
        / np.log(128.0 / exact_count)
        * (half_count - exact_count)
    )
    larger = np.minimum(
        exact_count + np.floor(np.maximum(scaled, 0.0)).astype(np.int64), half_count - 1
    )
    return upper_half + np.where(distance < exact_count, distance, larger)


def near_onehot(buckets):
    bucket = offset_bucket(np.arange(512) - 256, buckets)
    return (np.arange(buckets)[:, None] == bucket[None, :]).astype(np.float32)


def dot_nn(a, b):
    return lax.dot_general(a, b, (((1,), (0,)), ((), ())), preferred_element_type=FULL)


def dot_nt(a, b):
    return lax.dot_general(a, b, (((1,), (1,)), ((), ())), preferred_element_type=FULL)


def dot_tn(a, b):
    return lax.dot_general(a, b, (((0,), (0,)), ((), ())), preferred_element_type=FULL)


def exact_nn(a, b):
    return lax.dot_general(
        a, b, (((1,), (0,)), ((), ())), precision=lax.Precision.HIGHEST, preferred_element_type=FULL
    )


def exact_nt(a, b):
    return lax.dot_general(
        a, b, (((1,), (1,)), ((), ())), precision=lax.Precision.HIGHEST, preferred_element_type=FULL
    )


def split3(x):
    hi = x.astype(LOW)
    rest = x - hi.astype(FULL)
    mid = rest.astype(LOW)
    low = (rest - mid.astype(FULL)).astype(LOW)
    return hi, mid, low


def half_mask(sub, value, shape=(1, 128)):
    lane = lax.broadcasted_iota(jnp.int32, shape, 1)
    keep = (lane < 64) if sub == 0 else (lane >= 64)
    return jnp.where(keep, value, 0.0).astype(FULL)


def attn_setup(span_ref, table_ref, onehot_ref, near_ref, mask_ref):
    seq_len = mask_ref.shape[0]
    heads = near_ref.shape[0]
    start = span_ref[0]
    qi = lax.broadcasted_iota(jnp.int32, (seq_len, seq_len), 0)
    kj = lax.broadcasted_iota(jnp.int32, (seq_len, seq_len), 1)
    q_in = (qi >= start) & (qi < start + PIC)
    k_in = (kj >= start) & (kj < start + PIC)
    mask_ref[...] = jnp.where((kj <= qi) | (q_in & k_in), 0.0, -1e30).astype(FULL)
    vecs = exact_nn(table_ref[...], onehot_ref[...])
    for h in range(heads):
        rows = jnp.broadcast_to(vecs[h : h + 1, :], (128, 512))
        rolled = pltpu.roll(rows, 0, 1, stride=1, stride_axis=0)
        near_ref[h] = rolled[:, 128:]


def bias_rows(block, blocks, near):
    far_neg = jnp.broadcast_to(near[127:128, 0:1], (128, 128))
    far_pos = jnp.broadcast_to(near[0:1, 383:384], (128, 128))
    pieces = []
    for other in range(blocks):
        d = other - block
        if d <= -2:
            pieces.append(far_neg)
        elif d >= 2:
            pieces.append(far_pos)
        else:
            pieces.append(near[:, (d + 1) * 128 : (d + 2) * 128])
    return jnp.concatenate(pieces, axis=1)


def attn_block(row0, count, qkv_ref, near_ref, mask_ref, prob_ref, mixed_ref):
    seq_len, width3 = qkv_ref.shape
    width = width3 // 3
    blocks = seq_len // 128
    rows = slice(row0, row0 + count)

    @pl.loop(0, width // 128, unroll=ATT_UNROLL)
    def _(pair):
        col = pl.multiple_of(pair * 128, 128)
        qp = qkv_ref[rows, pl.ds(col, 128)].astype(FULL)
        kp = qkv_ref[:, pl.ds(width + col, 128)]
        vp = qkv_ref[:, pl.ds(2 * width + col, 128)]
        qs = jnp.concatenate([qp * half_mask(sub, 0.125) for sub in range(2)], axis=0)
        scores = dot_nt(qs.astype(LOW), kp)
        probs = []
        for sub in range(2):
            h = 2 * pair + sub
            for part in range(count // 128):
                first = sub * count + part * 128
                here = slice(row0 + part * 128, row0 + part * 128 + 128)
                s = scores[first : first + 128]
                bias = bias_rows(row0 // 128 + part, blocks, near_ref[h])
                s = s + bias + mask_ref[here, :]
                top = jnp.max(s, axis=1, keepdims=True)
                e = jnp.exp(s - top)
                total = jnp.sum(e, axis=1, keepdims=True)
                p = (e * (1.0 / total)).astype(LOW)
                prob_ref[h, here, :] = p
                probs.append(p)
        outs = dot_nn(jnp.concatenate(probs, axis=0), vp)
        lane = lax.broadcasted_iota(jnp.int32, (count, 128), 1)
        mixed_ref[rows, pl.ds(col, 128)] = jnp.where(
            lane < 64, outs[:count], outs[count:]
        ).astype(LOW)


def choice_hits(routes, experts):
    who = lax.broadcasted_iota(jnp.int32, (experts, routes.shape[1]), 0)
    return [who == routes[k : k + 1, :] for k in range(2)]


def to_column(row, width):
    return jnp.transpose(jnp.broadcast_to(row, (8, width)))[:, 0:1]


def ranks_by_priority(hits, priority):
    tokens = priority.shape[1]
    prio = priority.astype(FULL)
    less = jnp.where(to_column(prio, tokens) < prio, 1.0, 0.0).astype(LOW)
    return [dot_nn(jnp.where(hit, 1.0, 0.0).astype(LOW), less) for hit in hits]


def attn_dispatch_kernel(
    tokens_ref,
    cot_ref,
    gain1_ref,
    wqkv_ref,
    wproj_ref,
    table_ref,
    onehot_ref,
    gain2_ref,
    wrouter_ref,
    routes_ref,
    prio_ref,
    span_ref,
    qkv_out,
    prob_out,
    mixed_out,
    hidden_out,
    normed2_out,
    rows_ref,
    cotrows_ref,
    resg_ref,
    gatecol_ref,
    token_ref,
    info_ref,
    qkv_ref,
    prob_ref,
    mixed_ref,
    hidden_ref,
    normed2_ref,
    near_ref,
    mask_ref,
    meta_ref,
    gate_ref,
    meta_all,
    gate_all,
    gat_c,
    gat_n,
    acc_c,
    acc_n,
    acc_g,
    pos_ref,
    send_sem,
    recv_sem,
    small_send,
    small_recv,
    out_sem,
):
    g = lax.axis_index("group")
    me = lax.axis_index("expert")
    experts = wrouter_ref.shape[0]
    seq_len, width = tokens_ref.shape
    half = seq_len // 2

    def device(mask):
        return (g, lax.bitwise_xor(me, mask))

    barrier = pltpu.get_barrier_semaphore()
    for mask in range(1, experts):
        pl.semaphore_signal(barrier, inc=1, device_id=device(mask), device_id_type=MESH)
    pl.semaphore_wait(barrier, experts - 1)

    gats = (gat_c, gat_n)
    owns = (cot_ref, normed2_ref)

    def send(which, kind, chunk, held, target):
        rows = pl.ds(chunk * half, half)
        slot = lax.bitwise_xor(me, held)
        src = owns[which].at[rows, :] if held == 0 else gats[which].at[slot, rows, :]
        return pltpu.make_async_remote_copy(
            src_ref=src,
            dst_ref=gats[which].at[slot, rows, :],
            send_sem=send_sem.at[which, kind, chunk],
            recv_sem=recv_sem.at[which, held ^ target, chunk],
            device_id=device(target),
            device_id_type=MESH,
        )

    started = []

    def go(*args):
        copy = send(*args)
        copy.start()
        started.append(copy)

    def arrived(which, mask, chunk):
        rows = pl.ds(chunk * half, half)
        here = gats[which].at[lax.bitwise_xor(me, mask), rows, :]
        pltpu.make_async_remote_copy(
            src_ref=here,
            dst_ref=here,
            send_sem=send_sem.at[which, 0, chunk],
            recv_sem=recv_sem.at[which, mask, chunk],
            device_id=device(1),
            device_id_type=MESH,
        ).wait_recv()

    def own_out(which, chunk):
        go(which, 0, chunk, 0, 2)
        go(which, 1, chunk, 0, 4)
        go(which, 2, chunk, 0, 1)

    def relay(which):
        arrived(which, 2, 0)
        go(which, 3, 0, 2, 4)
        arrived(which, 4, 1)
        go(which, 3, 1, 4, 2)

    def small(src, dst, index):
        for mask in range(1, experts):
            copy = pltpu.make_async_remote_copy(
                src_ref=src,
                dst_ref=dst.at[me],
                send_sem=small_send.at[index, mask],
                recv_sem=small_recv.at[index, mask],
                device_id=device(mask),
                device_id_type=MESH,
            )
            copy.start()
            started.append(copy)

    def small_arrived(dst, index):
        for mask in range(1, experts):
            here = dst.at[lax.bitwise_xor(me, mask)]
            pltpu.make_async_remote_copy(
                src_ref=here,
                dst_ref=here,
                send_sem=small_send.at[index, mask],
                recv_sem=small_recv.at[index, mask],
                device_id=device(1),
                device_id_type=MESH,
            ).wait_recv()

    own_out(0, 0)
    own_out(0, 1)

    hits = choice_hits(routes_ref[...], experts)
    ranks = ranks_by_priority(hits, prio_ref[...])
    meta = jnp.where(hits[0], ranks[0], jnp.where(hits[1], ranks[1] + SECOND, -1.0))
    meta_ref[...] = meta
    meta_all[me] = meta
    small(meta_ref, meta_all, 0)

    attn_setup(span_ref, table_ref, onehot_ref, near_ref, mask_ref)
    for row0 in range(0, seq_len, 128):
        rows = slice(row0, row0 + 128)
        x = tokens_ref[rows, :].astype(FULL)
        inv = lax.rsqrt(jnp.mean(x * x, axis=1, keepdims=True) + EPS)
        n1 = (x * inv * gain1_ref[...][None, :]).astype(LOW)
        qkv_ref[rows, :] = dot_nn(n1, wqkv_ref[...]).astype(LOW)
    outs = [pltpu.make_async_copy(qkv_ref, qkv_out, out_sem.at[0])]
    outs[0].start()

    logits = []
    for chunk in range(2):
        row0 = chunk * half
        rows = slice(row0, row0 + half)
        attn_block(row0, half, qkv_ref, near_ref, mask_ref, prob_ref, mixed_ref)
        hidden = tokens_ref[rows, :].astype(FULL) + dot_nn(mixed_ref[rows, :], wproj_ref[...])
        hidden_ref[rows, :] = hidden
        inv = lax.rsqrt(jnp.mean(hidden * hidden, axis=1, keepdims=True) + EPS)
        n2 = (hidden * inv * gain2_ref[...][None, :]).astype(LOW)
        normed2_ref[rows, :] = n2
        own_out(1, chunk)
        logits.append(dot_nt(wrouter_ref[...], n2))
        if chunk == 0:
            relay(0)
    for index, (src, dst) in enumerate(
        ((prob_ref, prob_out), (mixed_ref, mixed_out), (hidden_ref, hidden_out), (normed2_ref, normed2_out))
    ):
        copy = pltpu.make_async_copy(src, dst, out_sem.at[index + 1])
        copy.start()
        outs.append(copy)

    logits = jnp.concatenate(logits, axis=1)
    unnormed = jnp.exp(logits - jnp.max(logits, axis=0, keepdims=True))
    probabilities = unnormed / jnp.sum(unnormed, axis=0, keepdims=True)
    picked = [jnp.sum(jnp.where(hit, probabilities, 0.0), axis=0, keepdims=True) for hit in hits]
    both = picked[0] + picked[1]
    gates = [p / both for p in picked]
    gate = jnp.where(hits[0], gates[0], jnp.where(hits[1], gates[1], 0.0))
    gate_ref[...] = gate
    gate_all[me] = gate
    small(gate_ref, gate_all, 1)

    first_count = jnp.sum(jnp.where(hits[0], 1.0, 0.0), axis=1, keepdims=True)
    who = lax.broadcasted_iota(jnp.int32, hits[0].shape, 0).astype(FULL)
    slots = [
        jnp.sum(jnp.where(hits[0], ranks[0] + who * SLOTS, 0.0), axis=0, keepdims=True),
        jnp.sum(
            jnp.where(hits[1], ranks[1] + first_count + who * SLOTS, 0.0), axis=0, keepdims=True
        ),
    ]
    routes_f = routes_ref[...].astype(FULL)
    token_rows = jnp.concatenate(slots + gates + [routes_f[0:1], routes_f[1:2]] + slots, axis=0)
    token_ref[...] = jnp.transpose(token_rows)

    small_arrived(meta_all, 0)
    value = meta_all[:, me, :]
    is_first = (value >= 0.0) & (value < SECOND)
    is_second = value >= SECOND
    counts = [
        jnp.sum(jnp.where(hit, 1.0, 0.0), axis=1, keepdims=True) for hit in (is_first, is_second)
    ]
    row = lax.broadcasted_iota(jnp.int32, (experts, 128), 0)
    lane = lax.broadcasted_iota(jnp.int32, (experts, 128), 1)
    count_mat = jnp.where(lane == 0, counts[0], jnp.where(lane == 1, counts[1], 0.0))
    before = jnp.zeros((experts, 128), FULL)
    for s in range(experts):
        before = before + jnp.where(row > s, count_mat[s : s + 1, :], 0.0)
    first_total = jnp.sum(counts[0], axis=0, keepdims=True)
    base = [before[:, 0:1], before[:, 1:2] + first_total]
    pos_ref[...] = jnp.where(
        is_first, value + base[0], jnp.where(is_second, value - SECOND + base[1], -1.0)
    )
    info_ref[...] = jnp.where(
        lane == 0,
        counts[0],
        jnp.where(lane == 1, counts[1], jnp.where(lane == 2, base[0], base[1])),
    )

    acc_c[...] = jnp.zeros_like(acc_c)
    acc_n[...] = jnp.zeros_like(acc_n)
    acc_g[...] = jnp.zeros_like(acc_g)

    def compact(which, mask, chunk):
        slot = lax.bitwise_xor(me, mask)
        cols = slice(chunk * half, chunk * half + half)
        acc = (acc_c, acc_n)[which]

        @pl.loop(0, acc.shape[0] // ROW_TILE)
        def _(tile):
            row0 = pl.multiple_of(tile * ROW_TILE, ROW_TILE)
            place = pos_ref[pl.ds(slot, 1), :][:, cols] - row0.astype(FULL)
            at = lax.broadcasted_iota(jnp.int32, (ROW_TILE, half), 0).astype(FULL)
            pick = jnp.where(at == place, 1.0, 0.0).astype(LOW)
            if mask == 0:
                data = owns[which][cols, :]
            else:
                data = gats[which][slot, cols, :]
            acc[pl.ds(row0, ROW_TILE), :] += dot_nn(pick, data)
            if which == 1:
                g_row = gate_all[slot, pl.ds(me, 1), :][:, cols]
                terms = [jnp.broadcast_to(t.astype(FULL), (8, half)) for t in split3(g_row)]
                third = lax.broadcasted_iota(jnp.int32, (8, half), 0)
                mat = jnp.where(
                    third == 0, terms[0], jnp.where(third == 1, terms[1], jnp.where(third == 2, terms[2], 0.0))
                ).astype(LOW)
                acc_g[pl.ds(row0, ROW_TILE), :] += dot_nt(pick, mat)

    def take(which, mask):
        for chunk in range(2):
            if mask:
                arrived(which, mask, chunk)
        if mask in (2, 4, 6):
            for chunk in range(2):
                go(which, 2 + mask // 2 + 0 * chunk + 1, chunk, mask, 1)
        for chunk in range(2):
            compact(which, mask, chunk)

    def take_relayed(which, mask, chunk_done):
        arrived(which, mask, 1 - chunk_done)
        for chunk in range(2):
            go(which, 3 + mask // 2, chunk, mask, 1)
        for chunk in range(2):
            compact(which, mask, chunk)

    take(0, 0)
    take(0, 1)
    take_relayed(0, 2, 0)
    take_relayed(0, 4, 1)
    take(0, 6)
    take(0, 3)
    take(0, 5)
    relay(1)
    take(0, 7)
    small_arrived(gate_all, 1)
    take(1, 0)
    take(1, 1)
    take_relayed(1, 2, 0)
    take_relayed(1, 4, 1)
    take(1, 3)
    take(1, 5)
    take(1, 6)
    take(1, 7)

    @pl.loop(0, acc_n.shape[0] // ROW_TILE)
    def _(tile):
        rows = pl.ds(pl.multiple_of(tile * ROW_TILE, ROW_TILE), ROW_TILE)
        cot_rows = acc_c[rows, :]
        gate_col = jnp.sum(acc_g[rows, :], axis=1, keepdims=True)
        rows_ref[rows, :] = acc_n[rows, :].astype(LOW)
        cotrows_ref[rows, :] = cot_rows.astype(LOW)
        resg_ref[rows, :] = (gate_col * cot_rows).astype(LOW)
        gatecol_ref[rows, :] = jnp.broadcast_to(gate_col, (ROW_TILE, 128))

    for copy in outs:
        copy.wait()
    for copy in started:
        copy.wait_send()


def attn_dispatch(
    tokens, cot, gain1, wqkv, wproj, table, gain2, wrouter, routes, priority, span
):
    seq_len, width = tokens.shape
    buckets, heads = table.shape
    experts = wrouter.shape[1]
    capacity = 5 * seq_len // 2
    sds = jax.ShapeDtypeStruct
    dma = pltpu.SemaphoreType.DMA
    return pl.pallas_call(
        attn_dispatch_kernel,
        out_shape=(
            sds((seq_len, 3 * width), LOW),
            sds((heads, seq_len, seq_len), LOW),
            sds((seq_len, width), LOW),
            sds((seq_len, width), FULL),
            sds((seq_len, width), LOW),
            sds((capacity, width), LOW),
            sds((capacity, width), LOW),
            sds((capacity, width), LOW),
            sds((capacity, 128), FULL),
            sds((seq_len, 8), FULL),
            sds((experts, 128), FULL),
        ),
        in_specs=[VM] * 11 + [SM],
        out_specs=[HBM] * 5 + [VM] * 6,
        scratch_shapes=[
            pltpu.VMEM((seq_len, 3 * width), LOW),
            pltpu.VMEM((heads, seq_len, seq_len), LOW),
            pltpu.VMEM((seq_len, width), LOW),
            pltpu.VMEM((seq_len, width), FULL),
            pltpu.VMEM((seq_len, width), LOW),
            pltpu.VMEM((heads, 128, 384), FULL),
            pltpu.VMEM((seq_len, seq_len), FULL),
            pltpu.VMEM((experts, seq_len), FULL),
            pltpu.VMEM((experts, seq_len), FULL),
            pltpu.VMEM((experts, experts, seq_len), FULL),
            pltpu.VMEM((experts, experts, seq_len), FULL),
            pltpu.VMEM((experts, seq_len, width), LOW),
            pltpu.VMEM((experts, seq_len, width), LOW),
            pltpu.VMEM((capacity, width), FULL),
            pltpu.VMEM((capacity, width), FULL),
            pltpu.VMEM((capacity, 8), FULL),
            pltpu.VMEM((experts, seq_len), FULL),
            dma((2, 7, 2)),
            dma((2, 8, 2)),
            dma((2, 8)),
            dma((2, 8)),
            dma((5,)),
        ],
        compiler_params=pltpu.CompilerParams(
            vmem_limit_bytes=60 * MIB, collective_id=0, has_side_effects=True
        ),
    )(
        tokens,
        cot,
        gain1,
        wqkv,
        wproj,
        table.T,
        jnp.asarray(near_onehot(buckets)),
        gain2,
        wrouter.T,
        routes.T,
        priority,
        span,
    )


def expert_first_kernel(rows_ref, resg_ref, win_ref, act_ref, slope_ref, gout_ref):
    pre = dot_nn(rows_ref[...], win_ref[...])
    act, slope = gelu_and_slope(pre)
    act_ref[...] = act.astype(LOW)
    slope_ref[...] = slope.astype(LOW)
    gout_ref[...] = dot_tn(act_ref[...], resg_ref[...]).astype(LOW)


def gelu_and_slope(x):
    c = math.sqrt(2.0 / math.pi)
    square = x * x
    t = jnp.tanh(x * (c + (c * 0.044715) * square))
    cdf = 0.5 + 0.5 * t
    slope = cdf + (0.5 * x) * (1.0 - t * t) * (c + (3.0 * c * 0.044715) * square)
    return x * cdf, slope


def expert_first(rows, resg, w_in):
    capacity, width = rows.shape
    ff = w_in.shape[1]
    sds = jax.ShapeDtypeStruct
    return pl.pallas_call(
        expert_first_kernel,
        grid=(ff // FF_TILE,),
        out_shape=(
            sds((capacity, ff), LOW),
            sds((capacity, ff), LOW),
            sds((ff, width), LOW),
        ),
        in_specs=[
            pl.BlockSpec((capacity, width), lambda f: (0, 0)),
            pl.BlockSpec((capacity, width), lambda f: (0, 0)),
            pl.BlockSpec((width, FF_TILE), lambda f: (0, f)),
        ],
        out_specs=[
            pl.BlockSpec((capacity, FF_TILE), lambda f: (0, f)),
            pl.BlockSpec((capacity, FF_TILE), lambda f: (0, f)),
            pl.BlockSpec((FF_TILE, width), lambda f: (f, 0)),
        ],
        compiler_params=pltpu.CompilerParams(vmem_limit_bytes=56 * MIB),
        cost_estimate=pl.CostEstimate(
            flops=4 * capacity * width * ff, bytes_accessed=40 * MIB, transcendentals=capacity * ff
        ),
    )(rows, resg, w_in)


def pack_rows(source, info_ref, data, out_ref, slots):
    info = info_ref[source : source + 1, :]
    slot = lax.broadcasted_iota(jnp.int32, (slots, 1), 0).astype(FULL)
    n0, n1, b0, b1 = [info[:, i : i + 1] for i in range(4)]
    place = jnp.where(slot < n0, b0 + slot, jnp.where(slot < n0 + n1, b1 + slot - n0, -1.0))
    at = lax.broadcasted_iota(jnp.int32, (slots, data.shape[0]), 1).astype(FULL)
    pick = jnp.where(at == place, 1.0, 0.0).astype(LOW)
    out_ref[source] = dot_nn(pick, data[...]).astype(LOW)


def expert_second_kernel(
    cot_ref, gate_ref, act_ref, slope_ref, wout_ref, win_ref, info_ref, ig_ref, packed_ref, acc_ref, gg_ref, data_ref
):
    step = pl.program_id(0)
    width = cot_ref.shape[1]

    @pl.when(step == 0)
    def _():
        acc_ref[...] = jnp.zeros_like(acc_ref)
        gg_ref[...] = jnp.zeros_like(gg_ref)

    back = dot_nt(cot_ref[...], wout_ref[...])
    part = act_ref[...].astype(FULL) * back
    total = part[:, 0:128]
    for i in range(1, part.shape[1] // 128):
        total = total + part[:, i * 128 : i * 128 + 128]
    gg_ref[...] += total
    ig = (slope_ref[...].astype(FULL) * (gate_ref[:, 0:1] * back)).astype(LOW)
    ig_ref[...] = ig
    acc_ref[...] += dot_nt(ig, win_ref[...])

    @pl.when(step == pl.num_programs(0) - 1)
    def _():
        data_ref[:, :width] = acc_ref[...].astype(LOW)
        gg = jnp.sum(gg_ref[...], axis=1, keepdims=True)
        hi, mid, low = [t.astype(FULL) for t in split3(gg)]
        lane = lax.broadcasted_iota(jnp.int32, (gg.shape[0], 128), 1)
        data_ref[:, width:] = jnp.where(
            lane == 0, hi, jnp.where(lane == 1, mid, jnp.where(lane == 2, low, 0.0))
        ).astype(LOW)
        for source in range(packed_ref.shape[0]):
            pack_rows(source, info_ref, data_ref, packed_ref, packed_ref.shape[1])


def expert_second(cot_rows, gate_col, act, slope, w_out, w_in, info):
    capacity, width = cot_rows.shape
    ff = w_in.shape[1]
    experts = info.shape[0]
    sds = jax.ShapeDtypeStruct
    return pl.pallas_call(
        expert_second_kernel,
        grid=(ff // FF_TILE,),
        out_shape=(
            sds((capacity, ff), LOW),
            sds((experts, SLOTS, width + 128), LOW),
        ),
        in_specs=[
            pl.BlockSpec((capacity, width), lambda f: (0, 0)),
            pl.BlockSpec((capacity, 128), lambda f: (0, 0)),
            pl.BlockSpec((capacity, FF_TILE), lambda f: (0, f)),
            pl.BlockSpec((capacity, FF_TILE), lambda f: (0, f)),
            pl.BlockSpec((FF_TILE, width), lambda f: (f, 0)),
            pl.BlockSpec((width, FF_TILE), lambda f: (0, f)),
            pl.BlockSpec((experts, 128), lambda f: (0, 0)),
        ],
        out_specs=[
            pl.BlockSpec((capacity, FF_TILE), lambda f: (0, f)),
            pl.BlockSpec((experts, SLOTS, width + 128), lambda f: (0, 0, 0)),
        ],
        scratch_shapes=[
            pltpu.VMEM((capacity, width), FULL),
            pltpu.VMEM((capacity, 128), FULL),
            pltpu.VMEM((capacity, width + 128), LOW),
        ],
        compiler_params=pltpu.CompilerParams(vmem_limit_bytes=56 * MIB),
        cost_estimate=pl.CostEstimate(
            flops=4 * capacity * width * ff, bytes_accessed=50 * MIB, transcendentals=0
        ),
    )(cot_rows, gate_col, act, slope, w_out, w_in, info)


def expert_inner_kernel(rows_ref, ig_ref, gin_ref, rows_t):
    @pl.when(pl.program_id(0) == 0)
    def _():
        rows_t[...] = jnp.transpose(rows_ref[...])

    gin_ref[...] = dot_nn(rows_t[...], ig_ref[...]).astype(LOW)


def expert_inner(rows, ig):
    capacity, width = rows.shape
    ff = ig.shape[1]
    return pl.pallas_call(
        expert_inner_kernel,
        grid=(ff // FF_TILE,),
        out_shape=jax.ShapeDtypeStruct((width, ff), LOW),
        in_specs=[
            pl.BlockSpec((capacity, width), lambda f: (0, 0)),
            pl.BlockSpec((capacity, FF_TILE), lambda f: (0, f)),
        ],
        out_specs=pl.BlockSpec((width, FF_TILE), lambda f: (0, f)),
        scratch_shapes=[pltpu.VMEM((width, capacity), LOW)],
        compiler_params=pltpu.CompilerParams(vmem_limit_bytes=56 * MIB),
        cost_estimate=pl.CostEstimate(
            flops=2 * capacity * width * ff, bytes_accessed=15 * MIB, transcendentals=0
        ),
    )(rows, ig)


def expert_result_kernel(act_ref, wout_ref, info_ref, packed_ref, acc_ref, data_ref):
    step = pl.program_id(0)

    @pl.when(step == 0)
    def _():
        acc_ref[...] = jnp.zeros_like(acc_ref)

    acc_ref[...] += dot_nn(act_ref[...], wout_ref[...])

    @pl.when(step == pl.num_programs(0) - 1)
    def _():
        data_ref[...] = acc_ref[...].astype(LOW)
        for source in range(packed_ref.shape[0]):
            pack_rows(source, info_ref, data_ref, packed_ref, packed_ref.shape[1])


def expert_result(act, w_out, info):
    capacity, ff = act.shape
    width = w_out.shape[1]
    experts = info.shape[0]
    return pl.pallas_call(
        expert_result_kernel,
        grid=(ff // FF_TILE,),
        out_shape=jax.ShapeDtypeStruct((experts, SLOTS, width), LOW),
        in_specs=[
            pl.BlockSpec((capacity, FF_TILE), lambda f: (0, f)),
            pl.BlockSpec((FF_TILE, width), lambda f: (f, 0)),
            pl.BlockSpec((experts, 128), lambda f: (0, 0)),
        ],
        out_specs=pl.BlockSpec((experts, SLOTS, width), lambda f: (0, 0, 0)),
        scratch_shapes=[pltpu.VMEM((capacity, width), FULL), pltpu.VMEM((capacity, width), LOW)],
        compiler_params=pltpu.CompilerParams(vmem_limit_bytes=56 * MIB),
        cost_estimate=pl.CostEstimate(
            flops=2 * capacity * width * ff, bytes_accessed=20 * MIB, transcendentals=0
        ),
    )(act, w_out, info)


def slot_picks(token_ref, slots):
    at = lax.broadcasted_iota(jnp.int32, (token_ref.shape[0], slots), 1).astype(FULL)
    return [jnp.where(at == token_ref[:, k : k + 1], 1.0, 0.0) for k in range(2)]


def combine_kernel(hidden_ref, token_ref, back_ref, out_ref):
    rows = 128
    width = hidden_ref.shape[1]
    for row0 in range(0, hidden_ref.shape[0], rows):
        here = slice(row0, row0 + rows)
        token = token_ref[here, :]
        at = lax.broadcasted_iota(jnp.int32, (rows, back_ref.shape[0]), 1).astype(FULL)
        picks = [jnp.where(at == token[:, k : k + 1], 1.0, 0.0).astype(LOW) for k in range(2)]
        got = dot_nn(jnp.concatenate(picks, axis=0), back_ref[...])
        out = hidden_ref[here, :] + token[:, 2:3] * got[:rows] + token[:, 3:4] * got[rows:]
        out_ref[here, :] = out.astype(LOW)


def combine(hidden, token, back):
    return pl.pallas_call(
        combine_kernel,
        out_shape=jax.ShapeDtypeStruct(hidden.shape, LOW),
        in_specs=[VM] * 3,
        out_specs=VM,
        compiler_params=pltpu.CompilerParams(vmem_limit_bytes=56 * MIB),
        cost_estimate=pl.CostEstimate(
            flops=4 * hidden.shape[0] * hidden.shape[1] * back.shape[0],
            bytes_accessed=6 * MIB,
            transcendentals=0,
        ),
    )(hidden, token, back)


def attn_back_kernel(
    tokens_ref,
    cot_ref,
    hidden_ref,
    normed2_ref,
    mixed_ref,
    qkv_ref,
    prob_ref,
    recv_ref,
    token_ref,
    gain1_ref,
    gain2_ref,
    wqkv_ref,
    wproj_ref,
    wrouter_ref,
    onehot_ref,
    gtok_ref,
    dense_out,
    small_out,
    hgrad_ref,
    mgrad_ref,
    mgrad_t,
    normed_t,
    q_t,
    ds_ref,
    diag_ref,
    dk_t,
    dv_t,
    dqkv_ref,
    part_ref,
    pair_in,
    chip_ref,
    plane_in,
    plane_ref,
    group_in,
    small_ref,
    small_in,
    small_plane,
    small_group,
    pair_sems,
    plane_sems,
    group_sems,
    final_sems,
    small_sems,
    smallz_sems,
):
    seq_len, width = tokens_ref.shape
    experts = wrouter_ref.shape[0]
    chunks = part_ref.shape[0]
    groups = group_in.shape[0]
    tile = 128
    g = lax.axis_index("group")
    me = lax.axis_index("expert")
    parity = lax.rem(me, 2)
    mine = lax.div(me, 2)
    summer = [(c * (groups - 1)) % groups for c in range(chunks)]

    def device(mask):
        return (g, lax.bitwise_xor(me, mask))

    barrier = pltpu.get_barrier_semaphore()
    for mask in range(1, experts):
        pl.semaphore_signal(barrier, inc=1, device_id=device(mask), device_id_type=MESH)
    for step in range(1, groups):
        pl.semaphore_signal(
            barrier, inc=1, device_id=(lax.rem(g + step, groups), me), device_id_type=MESH
        )
    pl.semaphore_wait(barrier, experts - 1 + groups - 1)

    def remote(src, dst, sems, at, where):
        return pltpu.make_async_remote_copy(
            src_ref=src,
            dst_ref=dst,
            send_sem=sems.at[(0, *at)],
            recv_sem=sems.at[(1, *at)],
            device_id=where,
            device_id_type=MESH,
        )

    started = []

    def go(copy):
        copy.start()
        started.append(copy)

    def pair_send(c):
        for chip in range(experts // 2):
            other = 2 * chip + 1 - parity
            go(remote(part_ref.at[c, other], pair_in.at[c, chip], pair_sems, (c, chip), device(1)))

    def plane_send(c):
        for chip in range(experts // 2):
            remote(
                part_ref.at[c, 0], pair_in.at[c, chip], pair_sems, (c, chip), device(1)
            ).wait_recv()
            total = part_ref[c, 2 * chip + parity].astype(FULL) + pair_in[c, chip].astype(FULL)
            chip_ref[c, chip] = total.astype(LOW)
        for other in range(1, experts // 2):
            go(
                remote(
                    chip_ref.at[c, lax.bitwise_xor(mine, other)],
                    plane_in.at[c, other - 1],
                    plane_sems,
                    (c, other - 1),
                    device(2 * other),
                )
            )

    def group_send(c):
        total = chip_ref[c, mine].astype(FULL)
        for other in range(1, experts // 2):
            remote(
                chip_ref.at[c, 0],
                plane_in.at[c, other - 1],
                plane_sems,
                (c, other - 1),
                device(2 * other),
            ).wait_recv()
            total = total + plane_in[c, other - 1].astype(FULL)
        plane_ref[c] = total.astype(LOW)

        @pl.when(g != summer[c])
        def _():
            remote(
                plane_ref.at[c], group_in.at[g], group_sems, (g,), (jnp.int32(summer[c]), me)
            ).start()

    def final_send(c):
        @pl.when(g == summer[c])
        def _():
            total = plane_ref[c].astype(FULL)
            for step in range(1, groups):
                src = lax.rem(g + step, groups)
                remote(
                    plane_ref.at[c], group_in.at[src], group_sems, (src,), (src, me)
                ).wait_recv()
                total = total + group_in[src].astype(FULL)
            dense_out[c] = total.astype(LOW)
            for step in range(1, groups):
                where = (lax.rem(g + step, groups), me)
                remote(dense_out.at[c], dense_out.at[c], final_sems, (c, step - 1), where).start()

    def finish(c):
        where = (lax.rem(g + 1, groups), me)
        for step in range(1, groups):
            copy = remote(dense_out.at[c], dense_out.at[c], final_sems, (c, step - 1), where)

            @pl.when(g == summer[c])
            def _():
                copy.wait_send()

            @pl.when(lax.rem(summer[c] + step, groups) == g)
            def _():
                copy.wait_recv()

        @pl.when(g != summer[c])
        def _():
            remote(plane_ref.at[c], group_in.at[g], group_sems, (g,), where).wait_send()

    ggain2 = jnp.zeros((8, width), FULL)
    lg_t = []
    for row0 in range(0, seq_len, tile):
        rows = slice(row0, row0 + tile)
        token = token_ref[rows, :]
        at = lax.broadcasted_iota(jnp.int32, (tile, recv_ref.shape[0]), 1).astype(FULL)
        picks = [jnp.where(at == token[:, k : k + 1], 1.0, 0.0).astype(LOW) for k in range(2)]
        got = dot_nn(jnp.concatenate(picks, axis=0), recv_ref[...])
        gg = [
            jnp.sum(got[k * tile : k * tile + tile, width:], axis=1, keepdims=True) for k in range(2)
        ]
        pull = token[:, 2:3] * token[:, 3:4] * (gg[0] - gg[1])
        expert = lax.broadcasted_iota(jnp.int32, (tile, 128), 1).astype(FULL)
        lg = jnp.where(expert == token[:, 4:5], pull, jnp.where(expert == token[:, 5:6], -pull, 0.0))
        lg_t.append(jnp.transpose(lg)[:experts])
        ngrad = (
            got[:tile, :width]
            + got[tile:, :width]
            + dot_nn(lg[:, :experts].astype(LOW), wrouter_ref[...])
        )
        hidden = hidden_ref[rows, :]
        inv = lax.rsqrt(jnp.mean(hidden * hidden, axis=1, keepdims=True) + EPS)
        unit = hidden * inv
        ng = ngrad * unit
        for i in range(tile // 8):
            ggain2 = ggain2 + ng[i * 8 : i * 8 + 8]
        scaled = ngrad * gain2_ref[...][None, :]
        proj = jnp.mean(scaled * unit, axis=1, keepdims=True)
        hgrad = cot_ref[rows, :].astype(FULL) + inv * (scaled - unit * proj)
        hgrad_ref[rows, :] = hgrad
        mgrad_ref[rows, :] = dot_nt(hgrad.astype(LOW), wproj_ref[...]).astype(LOW)
        x = tokens_ref[rows, :].astype(FULL)
        inv = lax.rsqrt(jnp.mean(x * x, axis=1, keepdims=True) + EPS)
        dqkv_ref[rows, :width] = (x * inv * gain1_ref[...][None, :]).astype(LOW)
    ggain2 = jnp.sum(ggain2, axis=0, keepdims=True)
    logit_grad_t = jnp.concatenate(lg_t, axis=1).astype(LOW)
    grouter = dot_nn(logit_grad_t, normed2_ref[...])
    normed_t[...] = jnp.transpose(dqkv_ref[:, :width])
    part_ref[0] = (
        dot_nn(jnp.transpose(mixed_ref[...]), hgrad_ref[...].astype(LOW))
        .astype(LOW)
        .reshape(experts, width // experts, width)
    )
    pair_send(0)
    mgrad_t[...] = jnp.transpose(mgrad_ref[...])
    q_t[...] = jnp.transpose(qkv_ref[:, :width])
    up = lax.broadcasted_iota(jnp.int32, (128, 128), 0)
    across = lax.broadcasted_iota(jnp.int32, (128, 128), 1)
    flip = jnp.where(up + across == 127, 1.0, 0.0).astype(FULL)

    def heads_back(pair):
        col = pl.multiple_of(pair * 128, 128)
        kp = qkv_ref[:, pl.ds(width + col, 128)]
        vp = qkv_ref[:, pl.ds(2 * width + col, 128)]
        op = mgrad_ref[:, pl.ds(col, 128)].astype(FULL)
        os = jnp.concatenate([(op * half_mask(sub, 1.0)).astype(LOW) for sub in range(2)], axis=0)
        dp = dot_nt(os, vp)
        for sub in range(2):
            h = 2 * pair + sub
            near = jnp.zeros((128, 384), FULL)
            far_neg = jnp.zeros((128, 128), FULL)
            far_pos = jnp.zeros((128, 128), FULL)
            blocks = seq_len // 128
            for block in range(blocks):
                first = sub * seq_len + block * 128
                here = slice(block * 128, block * 128 + 128)
                p = prob_ref[h, here, :].astype(FULL)
                weighted = p * dp[first : first + 128]
                ds = weighted - p * jnp.sum(weighted, axis=1, keepdims=True)
                low = ds.astype(LOW)
                ds_ref[sub, here, :] = low
                ds = low.astype(FULL)
                strip = []
                for d in range(-1, 2):
                    other = block + d
                    if 0 <= other < blocks:
                        strip.append(ds[:, other * 128 : other * 128 + 128])
                    else:
                        strip.append(jnp.zeros((128, 128), FULL))
                near = near + jnp.concatenate(strip, axis=1)
                for other in range(blocks):
                    piece = ds[:, other * 128 : other * 128 + 128]
                    if other - block <= -2:
                        far_neg = far_neg + piece
                    elif other - block >= 2:
                        far_pos = far_pos + piece
            low_sum = jnp.sum(far_neg)
            high_sum = jnp.sum(far_pos)
            padded = jnp.concatenate([exact_nn(flip, near), jnp.zeros((128, 128), FULL)], axis=1)
            turned = pltpu.roll(padded, 1, 1, stride=1, stride_axis=0)
            sums = jnp.sum(turned, axis=0, keepdims=True)
            lane = lax.broadcasted_iota(jnp.int32, (1, 512), 1)
            sums = sums + jnp.where(lane == 1, low_sum, jnp.where(lane == 511, high_sum, 0.0))
            diag_ref[pl.ds(h, 1), :] = sums
        lane = lax.broadcasted_iota(jnp.int32, (seq_len, 128), 1)
        dq = dot_nn(jnp.concatenate([ds_ref[0], ds_ref[1]], axis=0), kp)
        dqkv_ref[:, pl.ds(col, 128)] = (
            jnp.where(lane < 64, dq[:seq_len], dq[seq_len:]) * 0.125
        ).astype(LOW)
        for sub in range(2):
            part = pl.ds(pl.multiple_of(col + sub * 64, 64), 64)
            dk_t[part, :] = (dot_nn(q_t[part, :], ds_ref[sub]) * 0.125).astype(LOW)
            dv_t[part, :] = dot_nn(mgrad_t[part, :], prob_ref[2 * pair + sub]).astype(LOW)

    stripe = width // (chunks - 1)
    for c in range(1, chunks):
        pairs = stripe // 128

        @pl.loop((c - 1) * pairs, c * pairs)
        def _(pair):
            heads_back(pair)

        col = (c - 1) * stripe
        dqkv_ref[:, width + col : width + col + stripe] = jnp.transpose(dk_t[col : col + stripe, :])
        dqkv_ref[:, 2 * width + col : 2 * width + col + stripe] = jnp.transpose(
            dv_t[col : col + stripe, :]
        )
        for third in range(3):
            here = third * width + col
            part_ref[c, :, :, third * stripe : third * stripe + stripe] = (
                dot_nn(normed_t[...], dqkv_ref[:, here : here + stripe])
                .astype(LOW)
                .reshape(experts, width // experts, stripe)
            )
        pair_send(c)
        plane_send(c - 1)
        if c >= 2:
            group_send(c - 2)
        if c >= 3:
            final_send(c - 3)

    ggain1 = jnp.zeros((8, width), FULL)
    for row0 in range(0, seq_len, tile):
        rows = slice(row0, row0 + tile)
        x = tokens_ref[rows, :].astype(FULL)
        inv = lax.rsqrt(jnp.mean(x * x, axis=1, keepdims=True) + EPS)
        unit = x * inv
        ngrad = dot_nt(dqkv_ref[rows, :], wqkv_ref[...])
        ng = ngrad * unit
        for i in range(tile // 8):
            ggain1 = ggain1 + ng[i * 8 : i * 8 + 8]
        scaled = ngrad * gain1_ref[...][None, :]
        proj = jnp.mean(scaled * unit, axis=1, keepdims=True)
        gtok_ref[rows, :] = (hgrad_ref[rows, :] + inv * (scaled - unit * proj)).astype(LOW)
        if row0 == 0:
            plane_send(chunks - 1)
        if row0 == tile:
            group_send(chunks - 2)
    ggain1 = jnp.sum(ggain1, axis=0, keepdims=True)

    gtable = exact_nt(onehot_ref[...], diag_ref[...])
    shard = width // experts
    per = gtable.shape[0] // experts
    for e in range(experts):
        cols = slice(e * shard, e * shard + shard)
        block = jnp.concatenate([ggain1[:, cols], ggain2[:, cols], grouter[:, cols]], axis=0)
        small_ref[e] = jnp.zeros(small_ref.shape[1:], FULL)
        small_ref[e, 0 : 2 + experts, 0:shard] = block
        small_ref[e, 2 + experts : 2 + experts + per, 0 : gtable.shape[1]] = gtable[
            e * per : e * per + per
        ]
    for mask in range(1, experts):
        other = lax.bitwise_xor(me, mask)
        go(remote(small_ref.at[other], small_in.at[mask], small_sems, (mask,), device(mask)))
    group_send(chunks - 1)
    final_send(chunks - 3)
    total = small_ref[me]
    for mask in range(1, experts):
        remote(
            small_ref.at[0], small_in.at[mask], small_sems, (mask,), device(mask)
        ).wait_recv()
        total = total + small_in[mask]
    small_plane[...] = total
    for step in range(1, groups):
        where = (lax.rem(g + step, groups), me)
        go(remote(small_plane, small_group.at[step], smallz_sems, (step,), where))
    final_send(chunks - 2)
    final_send(chunks - 1)
    for step in range(1, groups):
        remote(
            small_plane, small_group.at[step], smallz_sems, (step,), (lax.rem(g + step, groups), me)
        ).wait_recv()
        total = total + small_group[step]
    small_out[...] = total
    for c in range(chunks):
        finish(c)
    for copy in started:
        copy.wait_send()


def attn_back(
    tokens, cot, hidden, normed2, mixed, qkv, prob, recv, token, gain1, gain2, wqkv, wproj, wrouter, table, groups
):
    seq_len, width = tokens.shape
    buckets, heads = table.shape
    experts = wrouter.shape[1]
    shard = width // experts
    chunks = groups
    chips = experts // 2
    small = (16, 128)
    sds = jax.ShapeDtypeStruct
    dma = pltpu.SemaphoreType.DMA
    return pl.pallas_call(
        attn_back_kernel,
        out_shape=(
            sds((seq_len, width), LOW),
            sds((chunks, shard, width), LOW),
            sds(small, FULL),
        ),
        in_specs=[VM] * 15,
        out_specs=[VM] * 3,
        scratch_shapes=[
            pltpu.VMEM((seq_len, width), FULL),
            pltpu.VMEM((seq_len, width), LOW),
            pltpu.VMEM((width, seq_len), LOW),
            pltpu.VMEM((width, seq_len), LOW),
            pltpu.VMEM((width, seq_len), LOW),
            pltpu.VMEM((2, seq_len, seq_len), LOW),
            pltpu.VMEM((heads, 512), FULL),
            pltpu.VMEM((width, seq_len), LOW),
            pltpu.VMEM((width, seq_len), LOW),
            pltpu.VMEM((seq_len, 3 * width), LOW),
            pltpu.VMEM((chunks, experts, shard, width), LOW),
            pltpu.VMEM((chunks, chips, shard, width), LOW),
            pltpu.VMEM((chunks, chips, shard, width), LOW),
            pltpu.VMEM((chunks, chips - 1, shard, width), LOW),
            pltpu.VMEM((chunks, shard, width), LOW),
            pltpu.VMEM((groups, shard, width), LOW),
            pltpu.VMEM((experts, *small), FULL),
            pltpu.VMEM((experts, *small), FULL),
            pltpu.VMEM(small, FULL),
            pltpu.VMEM((groups, *small), FULL),
            dma((2, chunks, chips)),
            dma((2, chunks, chips - 1)),
            dma((2, groups)),
            dma((2, chunks, groups - 1)),
            dma((2, experts)),
            dma((2, groups)),
        ],
        compiler_params=pltpu.CompilerParams(
            vmem_limit_bytes=60 * MIB, collective_id=1, has_side_effects=True
        ),
        cost_estimate=pl.CostEstimate(
            flops=30_000_000_000, bytes_accessed=30 * MIB, transcendentals=0
        ),
    )(
        tokens,
        cot,
        hidden,
        normed2,
        mixed,
        qkv,
        prob,
        recv,
        token,
        gain1,
        gain2,
        wqkv,
        wproj,
        wrouter.T,
        jnp.asarray(near_onehot(buckets)),
    )


def on_device_fast(
    tokens,
    gain_first,
    w_qkv,
    w_proj,
    bias_table,
    gain_second,
    w_router,
    w_in,
    w_out,
    routes,
    priority,
    span_start,
    cotangent,
):
    experts = w_router.shape[1]
    width = tokens.shape[1]
    qkv, prob, mixed, hidden, normed2, rows, cot_rows, resg, gate_col, token, info = attn_dispatch(
        tokens,
        cotangent,
        gain_first,
        w_qkv,
        w_proj,
        bias_table,
        gain_second,
        w_router,
        routes,
        priority,
        span_start,
    )
    act, slope, grad_outer = expert_first(rows, resg, w_in[0])
    grad_out = lax.psum_scatter(
        grad_outer[None], "group", scatter_dimension=1, tiled=True
    ).astype(FULL)
    ig, packed = expert_second(cot_rows, gate_col, act, slope, w_out[0], w_in[0], info)
    recv = lax.all_to_all(packed, "expert", split_axis=0, concat_axis=0, tiled=True)
    grad_inner = expert_inner(rows, ig)
    grad_in = lax.psum_scatter(
        grad_inner[None], "group", scatter_dimension=1, tiled=True
    ).astype(FULL)
    packed_out = expert_result(act, w_out[0], info)
    back = lax.all_to_all(packed_out, "expert", split_axis=0, concat_axis=0, tiled=True)
    gtok, dense, small = attn_back(
        tokens,
        cotangent,
        hidden,
        normed2,
        mixed,
        qkv,
        prob,
        recv.reshape(-1, width + 128),
        token,
        gain_first,
        gain_second,
        w_qkv,
        w_proj,
        w_router,
        bias_table,
        lax.axis_size("group"),
    )
    block_out = combine(hidden, token, back.reshape(-1, width))
    shard = width // experts
    heads = bias_table.shape[1]
    per = bias_table.shape[0] // experts
    stripe = width // (dense.shape[0] - 1)
    grad_qkv = (
        dense[1:].reshape(-1, shard, 3, stripe).transpose(1, 2, 0, 3).reshape(shard, 3 * width)
    )
    return (
        block_out,
        gtok,
        small[0, :shard],
        grad_qkv.astype(FULL),
        dense[0].astype(FULL),
        small[2 + experts : 2 + experts + per, :heads],
        small[1, :shard],
        small[2 : 2 + experts, :shard].T,
        grad_in,
        grad_out,
    )


def bucket_table(seq_len, buckets):
    half_count = buckets // 2
    exact_count = half_count // 2
    offsets = np.arange(-(seq_len - 1), seq_len)
    upper_half = (offsets > 0).astype(np.int64) * half_count
    distance = np.abs(offsets)
    scaled = (
        np.log(np.maximum(distance, 1) / float(exact_count))
        / np.log(128.0 / exact_count)
        * (half_count - exact_count)
    )
    larger = np.minimum(
        exact_count + np.floor(np.maximum(scaled, 0.0)).astype(np.int64), half_count - 1
    )
    bucket = upper_half + np.where(distance < exact_count, distance, larger)
    places = np.arange(seq_len)
    return bucket[places[None, :] - places[:, None] + seq_len - 1].astype(np.int32)


def allowed_pairs(seq_len, span_begin, span_len):
    places = jnp.arange(seq_len, dtype=jnp.int32)
    causal = places[None, :] <= places[:, None]
    inside = (places >= span_begin) & (places < span_begin + span_len)
    return causal | inside[:, None] & inside[None, :]


def rms_norm(values, norm_gain):
    return values * lax.rsqrt(jnp.mean(values * values, axis=-1, keepdims=True) + 1e-06) * norm_gain


def gate_values(logits, routes, experts):
    probabilities = jax.nn.softmax(logits, axis=-1)
    chosen = (routes[..., None] == jnp.arange(experts, dtype=jnp.int32)).astype(jnp.float32)
    picked = jnp.sum(probabilities[:, None, :] * chosen, axis=-1)
    return picked / jnp.sum(picked, axis=1, keepdims=True)


def local_ranks(choice_hits, priority):
    token_count = priority.shape[0]
    token_order = (
        jnp.zeros((token_count,), jnp.int32)
        .at[priority]
        .set(jnp.arange(token_count, dtype=jnp.int32))
    )
    ordered = choice_hits[token_order]
    running = jnp.cumsum(ordered, axis=0) - ordered
    return jnp.sum(running[priority] * choice_hits, axis=-1)


def contract_rows(left, right):
    return lax.dot_general(
        left, right, (((0,), (0,)), ((), ())), preferred_element_type=jnp.float32
    )


def on_device(
    tokens,
    gain_first,
    w_qkv,
    w_proj,
    bias_table,
    gain_second,
    w_router,
    w_in,
    w_out,
    routes,
    priority,
    span_start,
    cotangent,
):
    seq_len, model_width = tokens.shape
    buckets, head_count = bias_table.shape
    head_dim = model_width // head_count
    experts = w_router.shape[1]
    slot_count = 4 * seq_len // experts
    capacity = 5 * seq_len // 2
    score_scale = 1.0 / math.sqrt(head_dim)
    highest = lax.Precision.HIGHEST
    lowtype = jnp.bfloat16
    fulltype = jnp.float32
    tokens_f = tokens.astype(fulltype)
    normed_one = rms_norm(tokens_f, gain_first).astype(lowtype)
    qkv_rows = jnp.dot(normed_one, w_qkv, preferred_element_type=fulltype).astype(lowtype)
    qkv_rows = qkv_rows.reshape(seq_len, 3, head_count, head_dim)
    queries, key_rows, value_rows = (qkv_rows[:, 0], qkv_rows[:, 1], qkv_rows[:, 2])
    bucket_index = jnp.asarray(bucket_table(seq_len, buckets))
    onehot_table = (bucket_index[:, :, None] == jnp.arange(buckets, dtype=jnp.int32)).astype(
        fulltype
    )
    rel_bias = jnp.einsum("qkb,bh->hqk", onehot_table, bias_table, precision=highest)
    allowed = allowed_pairs(seq_len, span_start[0], PIC)

    def masked_scores():
        raw_scores = (
            jnp.einsum("qhc,khc->hqk", queries, key_rows, preferred_element_type=fulltype)
            * score_scale
            + rel_bias
        )
        return jnp.where(allowed[None], raw_scores, -1e30)

    scores = masked_scores()
    log_total = jax.nn.logsumexp(scores, axis=-1)
    attn_probs = jnp.exp(scores - log_total[..., None]).astype(lowtype)
    mixed_heads = jnp.einsum(
        "hqk,khc->qhc", attn_probs, value_rows, preferred_element_type=fulltype
    )
    mixed_heads = mixed_heads.astype(lowtype).reshape(seq_len, model_width)
    hidden = tokens_f + jnp.dot(mixed_heads, w_proj, preferred_element_type=fulltype)
    normed_two = rms_norm(hidden, gain_second).astype(lowtype)
    logits = jnp.dot(normed_two, w_router, preferred_element_type=fulltype)
    gate_weights = gate_values(logits, routes, experts)
    choice_hits = (routes[..., None] == jnp.arange(experts, dtype=jnp.int32)).astype(jnp.int32)
    counts = jnp.sum(choice_hits, axis=0)
    every_count = lax.all_gather(counts[None], "expert", axis=0, tiled=True)
    pair_ranks = local_ranks(choice_hits, priority[0])
    second_shift = jnp.sum(choice_hits[:, 1] * counts[0], axis=-1)
    slot_index = pair_ranks + jnp.stack([jnp.zeros_like(second_shift), second_shift], axis=-1)
    flat_slot = (routes * slot_count + slot_index).reshape(-1)
    own_expert = (jnp.arange(experts, dtype=jnp.int32) == lax.axis_index("expert")).astype(
        jnp.int32
    )
    own_counts = jnp.sum(every_count * own_expert, axis=-1)
    first_rows, second_rows = (own_counts[:, 0], own_counts[:, 1])
    first_before = jnp.cumsum(first_rows) - first_rows
    second_before = jnp.cumsum(second_rows) - second_rows
    first_total = jnp.sum(first_rows)
    column = jnp.arange(slot_count, dtype=jnp.int32)[None, :]
    position = jnp.where(
        column < first_rows[:, None],
        first_before[:, None] + column,
        first_total + second_before[:, None] + column - first_rows[:, None],
    )
    usable = (column < (first_rows + second_rows)[:, None]) & (position < capacity)
    destination = jnp.where(usable, position, capacity).reshape(-1)

    def pack_pairs(pair_rows):
        packed = jnp.zeros((experts * slot_count, model_width), lowtype)
        packed = packed.at[flat_slot].set(pair_rows.reshape(-1, model_width))
        return packed.reshape(experts, slot_count, model_width)

    def compact_rows(arrived):
        gathered_rows = jnp.zeros((capacity + 1, model_width), lowtype)
        return gathered_rows.at[destination].add(arrived.reshape(-1, model_width))[:capacity]

    def spread_rows(expert_out):
        padded = jnp.concatenate([expert_out, jnp.zeros((1, model_width), lowtype)], axis=0)
        return padded[destination].reshape(-1, slot_count, model_width)

    def unpack_pairs(received):
        return (
            received.reshape(-1, model_width)[flat_slot]
            .reshape(seq_len, 2, model_width)
            .astype(fulltype)
        )

    pair_rows = jnp.broadcast_to(normed_two[:, None, :], (seq_len, 2, model_width))
    arrived = lax.all_to_all(
        pack_pairs(pair_rows), "expert", split_axis=0, concat_axis=0, tiled=True
    )
    expert_rows = compact_rows(arrived)
    inner_pre = jnp.dot(expert_rows, w_in[0], preferred_element_type=fulltype)
    active = jax.nn.gelu(inner_pre).astype(lowtype)
    result = jnp.dot(active, w_out[0], preferred_element_type=fulltype).astype(lowtype)
    returned = unpack_pairs(
        lax.all_to_all(spread_rows(result), "expert", split_axis=0, concat_axis=0, tiled=True)
    )
    block_out = hidden + jnp.sum(gate_weights[..., None] * returned, axis=1)
    upstream = cotangent.astype(fulltype)
    gate_grad = jnp.sum(upstream[:, None, :] * returned, axis=-1)
    result_grad = (gate_weights[..., None] * upstream[:, None, :]).astype(lowtype)
    result_rows = compact_rows(
        lax.all_to_all(pack_pairs(result_grad), "expert", split_axis=0, concat_axis=0, tiled=True)
    )
    grad_outer = contract_rows(active, result_rows)
    hidden_pre_grad = jnp.dot(result_rows, w_out[0].T, preferred_element_type=fulltype)
    inner_grad = jax.vjp(jax.nn.gelu, inner_pre)[1](hidden_pre_grad)[0].astype(lowtype)
    grad_inner = contract_rows(expert_rows, inner_grad)
    rows_grad = jnp.dot(inner_grad, w_in[0].T, preferred_element_type=fulltype).astype(lowtype)
    pair_grad = unpack_pairs(
        lax.all_to_all(spread_rows(rows_grad), "expert", split_axis=0, concat_axis=0, tiled=True)
    )
    logit_grad = jax.vjp(lambda values: gate_values(values, routes, experts), logits)[1](gate_grad)[
        0
    ].astype(lowtype)
    grad_router = contract_rows(normed_two, logit_grad)
    normed_grad = jnp.sum(pair_grad, axis=1) + jnp.dot(
        logit_grad, w_router.T, preferred_element_type=fulltype
    )
    second_back = jax.vjp(rms_norm, hidden, gain_second)[1](normed_grad)
    hidden_grad = upstream + second_back[0]
    branch_grad = hidden_grad.astype(lowtype)
    grad_proj = contract_rows(mixed_heads, branch_grad)
    mixed_grad = jnp.dot(branch_grad, w_proj.T, preferred_element_type=fulltype).astype(lowtype)
    mixed_grad = mixed_grad.reshape(seq_len, head_count, head_dim)
    scores = masked_scores()
    probs_full = jnp.exp(scores - log_total[..., None])
    probs_low = probs_full.astype(lowtype)
    prob_grad = jnp.einsum("qhc,khc->hqk", mixed_grad, value_rows, preferred_element_type=fulltype)
    value_grad = jnp.einsum("hqk,qhc->khc", probs_low, mixed_grad, preferred_element_type=fulltype)
    row_dot = jnp.sum(probs_full * prob_grad, axis=-1, keepdims=True)
    score_grad = (probs_full * (prob_grad - row_dot)).astype(lowtype)
    query_grad = (
        jnp.einsum("hqk,khc->qhc", score_grad, key_rows, preferred_element_type=fulltype)
        * score_scale
    )
    key_grad = (
        jnp.einsum("hqk,qhc->khc", score_grad, queries, preferred_element_type=fulltype)
        * score_scale
    )
    grad_table = jnp.einsum(
        "hqk,qkb->bh", score_grad.astype(fulltype), onehot_table, precision=highest
    )
    qkv_grad = (
        jnp.stack([query_grad, key_grad, value_grad], axis=1)
        .astype(lowtype)
        .reshape(seq_len, 3 * model_width)
    )
    grad_qkv = contract_rows(normed_one, qkv_grad)
    normed_one_grad = jnp.dot(qkv_grad, w_qkv.T, preferred_element_type=fulltype)
    first_back = jax.vjp(rms_norm, tokens_f, gain_first)[1](normed_one_grad)
    grad_tokens = (hidden_grad + first_back[0]).astype(lowtype)
    dense_grads = (first_back[1], grad_qkv, grad_proj, grad_table, second_back[1], grad_router)
    shares = (
        lax.psum_scatter(
            dense_grads[0].astype(jnp.bfloat16), "expert", scatter_dimension=0, tiled=True
        ).astype(jnp.float32),
        lax.psum_scatter(
            dense_grads[1].astype(jnp.bfloat16), "expert", scatter_dimension=0, tiled=True
        ).astype(jnp.float32),
        lax.psum_scatter(
            dense_grads[2].astype(jnp.bfloat16), "expert", scatter_dimension=0, tiled=True
        ).astype(jnp.float32),
        lax.psum_scatter(
            dense_grads[3].astype(jnp.bfloat16), "expert", scatter_dimension=0, tiled=True
        ).astype(jnp.float32),
        lax.psum_scatter(
            dense_grads[4].astype(jnp.bfloat16), "expert", scatter_dimension=0, tiled=True
        ).astype(jnp.float32),
        lax.psum_scatter(
            dense_grads[5].astype(jnp.bfloat16), "expert", scatter_dimension=0, tiled=True
        ).astype(jnp.float32),
    )
    totals = (
        lax.psum(shares[0].astype(jnp.bfloat16), "group").astype(jnp.float32),
        lax.psum(shares[1].astype(jnp.bfloat16), "group").astype(jnp.float32),
        lax.psum(shares[2].astype(jnp.bfloat16), "group").astype(jnp.float32),
        lax.psum(shares[3].astype(jnp.bfloat16), "group").astype(jnp.float32),
        lax.psum(shares[4].astype(jnp.bfloat16), "group").astype(jnp.float32),
        lax.psum(shares[5].astype(jnp.bfloat16), "group").astype(jnp.float32),
    )
    grad_in, grad_out = (
        lax.psum_scatter(
            grad_inner[None].astype(jnp.bfloat16), "group", scatter_dimension=1, tiled=True
        ).astype(jnp.float32),
        lax.psum_scatter(
            grad_outer[None].astype(jnp.bfloat16), "group", scatter_dimension=1, tiled=True
        ).astype(jnp.float32),
    )
    return (
        block_out.astype(lowtype),
        grad_tokens,
        totals[0],
        totals[1],
        totals[2],
        totals[3],
        totals[4],
        totals[5],
        grad_in,
        grad_out,
    )


def solution(mesh):
    fast = (mesh.shape["group"], mesh.shape["expert"]) == (4, 8)
    step = on_device_fast if fast else on_device
    return jax.shard_map(
        step,
        mesh=mesh,
        in_specs=(
            P(("group", "expert"), None),
            P(),
            P(),
            P(),
            P(),
            P(),
            P(),
            P("expert", None, None),
            P("expert", None, None),
            P(("group", "expert"), None),
            P(("group", "expert"), None),
            P(("group", "expert")),
            P(("group", "expert"), None),
        ),
        out_specs=(
            P(("group", "expert"), None),
            P(("group", "expert"), None),
            P("expert"),
            P("expert", None),
            P("expert", None),
            P("expert", None),
            P("expert"),
            P("expert", None),
            P("expert", "group", None),
            P("expert", "group", None),
        ),
        check_vma=False,
    )
```

```python
import functools
import math

import jax
import jax.numpy as jnp
import numpy as np
from jax import lax
from jax.experimental import pallas as pl
from jax.experimental.pallas import tpu as pltpu
from jax.sharding import PartitionSpec as P

PIC = 256
EPS = 1e-6
LOW = jnp.bfloat16
FULL = jnp.float32
VM = pl.BlockSpec(memory_space=pltpu.VMEM)
SM = pl.BlockSpec(memory_space=pltpu.SMEM)
HBM = pl.BlockSpec(memory_space=pl.ANY)
MIB = 1 << 20
ATT_ROWS = 256
ATT_UNROLL = 2
MESH = pl.DeviceIdType.MESH
SECOND = 512.0
SLOTS = 256
ROW_TILE = 256
FF_TILE = 256
THIRDS = 3


def offset_bucket(offsets, buckets):
    half_count = buckets // 2
    exact_count = half_count // 2
    upper_half = (offsets > 0).astype(np.int64) * half_count
    distance = np.abs(offsets)
    scaled = (
        np.log(np.maximum(distance, 1) / float(exact_count))
        / np.log(128.0 / exact_count)
        * (half_count - exact_count)
    )
    larger = np.minimum(
        exact_count + np.floor(np.maximum(scaled, 0.0)).astype(np.int64), half_count - 1
    )
    return upper_half + np.where(distance < exact_count, distance, larger)


def near_onehot(buckets):
    bucket = offset_bucket(np.arange(512) - 256, buckets)
    return (np.arange(buckets)[:, None] == bucket[None, :]).astype(np.float32)


def dot_nn(a, b):
    return lax.dot_general(a, b, (((1,), (0,)), ((), ())), preferred_element_type=FULL)


def dot_nt(a, b):
    return lax.dot_general(a, b, (((1,), (1,)), ((), ())), preferred_element_type=FULL)


def dot_tn(a, b):
    return lax.dot_general(a, b, (((0,), (0,)), ((), ())), preferred_element_type=FULL)


def exact_nn(a, b):
    return lax.dot_general(
        a, b, (((1,), (0,)), ((), ())), precision=lax.Precision.HIGHEST, preferred_element_type=FULL
    )


def exact_nt(a, b):
    return lax.dot_general(
        a, b, (((1,), (1,)), ((), ())), precision=lax.Precision.HIGHEST, preferred_element_type=FULL
    )


def split3(x):
    hi = x.astype(LOW)
    rest = x - hi.astype(FULL)
    mid = rest.astype(LOW)
    low = (rest - mid.astype(FULL)).astype(LOW)
    return hi, mid, low


def half_mask(sub, value, shape=(1, 128)):
    lane = lax.broadcasted_iota(jnp.int32, shape, 1)
    keep = (lane < 64) if sub == 0 else (lane >= 64)
    return jnp.where(keep, value, 0.0).astype(FULL)


def attn_setup(span_ref, table_ref, onehot_ref, near_ref, mask_ref):
    seq_len = mask_ref.shape[0]
    heads = near_ref.shape[0]
    start = span_ref[0]
    qi = lax.broadcasted_iota(jnp.int32, (seq_len, seq_len), 0)
    kj = lax.broadcasted_iota(jnp.int32, (seq_len, seq_len), 1)
    q_in = (qi >= start) & (qi < start + PIC)
    k_in = (kj >= start) & (kj < start + PIC)
    mask_ref[...] = jnp.where((kj <= qi) | (q_in & k_in), 0.0, -1e30).astype(FULL)
    vecs = exact_nn(table_ref[...], onehot_ref[...])
    for h in range(heads):
        rows = jnp.broadcast_to(vecs[h : h + 1, :], (128, 512))
        rolled = pltpu.roll(rows, 0, 1, stride=1, stride_axis=0)
        near_ref[h] = rolled[:, 128:]


def bias_rows(block, blocks, near):
    far_neg = jnp.broadcast_to(near[127:128, 0:1], (128, 128))
    far_pos = jnp.broadcast_to(near[0:1, 383:384], (128, 128))
    pieces = []
    for other in range(blocks):
        d = other - block
        if d <= -2:
            pieces.append(far_neg)
        elif d >= 2:
            pieces.append(far_pos)
        else:
            pieces.append(near[:, (d + 1) * 128 : (d + 2) * 128])
    return jnp.concatenate(pieces, axis=1)


def attn_block(row0, count, qkv_ref, near_ref, mask_ref, prob_ref, mixed_ref):
    seq_len, width3 = qkv_ref.shape
    width = width3 // 3
    blocks = seq_len // 128
    rows = slice(row0, row0 + count)

    @pl.loop(0, width // 128, unroll=ATT_UNROLL)
    def _(pair):
        col = pl.multiple_of(pair * 128, 128)
        qp = qkv_ref[rows, pl.ds(col, 128)].astype(FULL)
        kp = qkv_ref[:, pl.ds(width + col, 128)]
        vp = qkv_ref[:, pl.ds(2 * width + col, 128)]
        qs = jnp.concatenate([qp * half_mask(sub, 0.125) for sub in range(2)], axis=0)
        scores = dot_nt(qs.astype(LOW), kp)
        probs = []
        for sub in range(2):
            h = 2 * pair + sub
            for part in range(count // 128):
                first = sub * count + part * 128
                here = slice(row0 + part * 128, row0 + part * 128 + 128)
                s = scores[first : first + 128]
                bias = bias_rows(row0 // 128 + part, blocks, near_ref[h])
                s = s + bias + mask_ref[here, :]
                top = jnp.max(s, axis=1, keepdims=True)
                e = jnp.exp(s - top)
                total = jnp.sum(e, axis=1, keepdims=True)
                p = (e * (1.0 / total)).astype(LOW)
                prob_ref[h, here, :] = p
                probs.append(p)
        outs = dot_nn(jnp.concatenate(probs, axis=0), vp)
        lane = lax.broadcasted_iota(jnp.int32, (count, 128), 1)
        mixed_ref[rows, pl.ds(col, 128)] = jnp.where(
            lane < 64, outs[:count], outs[count:]
        ).astype(LOW)


def choice_hits(routes, experts):
    who = lax.broadcasted_iota(jnp.int32, (experts, routes.shape[1]), 0)
    return [who == routes[k : k + 1, :] for k in range(2)]


def to_column(row, width):
    return jnp.transpose(jnp.broadcast_to(row, (8, width)))[:, 0:1]


def ranks_by_priority(hits, priority):
    tokens = priority.shape[1]
    prio = priority.astype(FULL)
    less = jnp.where(to_column(prio, tokens) < prio, 1.0, 0.0).astype(LOW)
    return [dot_nn(jnp.where(hit, 1.0, 0.0).astype(LOW), less) for hit in hits]


def attn_dispatch_kernel(
    tokens_ref,
    cot_ref,
    gain1_ref,
    wqkv_ref,
    wproj_ref,
    table_ref,
    onehot_ref,
    gain2_ref,
    wrouter_ref,
    routes_ref,
    prio_ref,
    span_ref,
    win_ref,
    qkv_out,
    prob_out,
    mixed_out,
    hidden_out,
    normed2_out,
    rows_out,
    cotrows_out,
    gatecol_out,
    token_ref,
    info_ref,
    resgt_out,
    act_out,
    slope_out,
    gout_out,
    qkv_ref,
    prob_ref,
    mixed_ref,
    hidden_ref,
    normed2_ref,
    meta_ref,
    gate_ref,
    meta_all,
    gate_all,
    gat_c,
    gat_n,
    acc_g,
    pos_ref,
    win_v,
    rows_ref,
    cotrows_ref,
    gatecol_ref,
    resgt_ref,
    send_sem,
    recv_sem,
    small_send,
    small_recv,
    out_sem,
    in_sem,
    tile_sem,
):
    g = lax.axis_index("group")
    me = lax.axis_index("expert")
    experts = wrouter_ref.shape[0]
    seq_len, width = tokens_ref.shape
    half = seq_len // 2

    def device(mask):
        return (g, lax.bitwise_xor(me, mask))

    barrier = pltpu.get_barrier_semaphore()
    for mask in range(1, experts):
        pl.semaphore_signal(barrier, inc=1, device_id=device(mask), device_id_type=MESH)
    pl.semaphore_wait(barrier, experts - 1)

    gats = (gat_c, gat_n)
    owns = (cot_ref, normed2_ref)

    def send(which, kind, chunk, held, target):
        rows = pl.ds(chunk * half, half)
        slot = lax.bitwise_xor(me, held)
        src = owns[which].at[rows, :] if held == 0 else gats[which].at[slot, rows, :]
        return pltpu.make_async_remote_copy(
            src_ref=src,
            dst_ref=gats[which].at[slot, rows, :],
            send_sem=send_sem.at[which, kind, chunk],
            recv_sem=recv_sem.at[which, held ^ target, chunk],
            device_id=device(target),
            device_id_type=MESH,
        )

    started = []

    def go(*args):
        send(*args).start()
        started.append(functools.partial(send, *args))

    def arrived(which, mask, chunk):
        rows = pl.ds(chunk * half, half)
        here = gats[which].at[lax.bitwise_xor(me, mask), rows, :]
        pltpu.make_async_remote_copy(
            src_ref=here,
            dst_ref=here,
            send_sem=send_sem.at[which, 0, chunk],
            recv_sem=recv_sem.at[which, mask, chunk],
            device_id=device(1),
            device_id_type=MESH,
        ).wait_recv()

    def own_out(which, chunk):
        go(which, 0, chunk, 0, 2)
        go(which, 1, chunk, 0, 4)
        go(which, 2, chunk, 0, 1)

    def own_out_all(which):
        for chunk in range(2):
            go(which, 0, chunk, 0, 2)
            go(which, 1, 1 - chunk, 0, 4)
        for chunk in range(2):
            go(which, 2, chunk, 0, 1)

    def relay(which, chunk, wait=True):
        if wait:
            arrived(which, 4 if chunk else 2, chunk)
        go(which, 3, chunk, 4 if chunk else 2, 2 if chunk else 4)

    def small_copy(src, dst, index, mask):
        return pltpu.make_async_remote_copy(
            src_ref=src,
            dst_ref=dst.at[me],
            send_sem=small_send.at[index, mask],
            recv_sem=small_recv.at[index, mask],
            device_id=device(mask),
            device_id_type=MESH,
        )

    def small(*args):
        for mask in range(1, experts):
            small_copy(*args, mask).start()
            started.append(functools.partial(small_copy, *args, mask))

    def small_arrived(dst, index):
        for mask in range(1, experts):
            here = dst.at[lax.bitwise_xor(me, mask)]
            pltpu.make_async_remote_copy(
                src_ref=here,
                dst_ref=here,
                send_sem=small_send.at[index, mask],
                recv_sem=small_recv.at[index, mask],
                device_id=device(1),
                device_id_type=MESH,
            ).wait_recv()

    own_out_all(0)

    def win_load():
        return pltpu.make_async_copy(win_ref, win_v, in_sem.at[2])

    win_load().start()

    hits = choice_hits(routes_ref[...], experts)
    ranks = ranks_by_priority(hits, prio_ref[...])
    meta = jnp.where(hits[0], ranks[0], jnp.where(hits[1], ranks[1] + SECOND, -1.0))
    meta_ref[...] = meta
    meta_all[me] = meta
    small(meta_ref, meta_all, 0)

    own_pairs = (
        (qkv_ref, qkv_out),
        (prob_ref, prob_out),
        (mixed_ref, mixed_out),
        (hidden_ref, hidden_out),
        (normed2_ref, normed2_out),
        (cotrows_ref, cotrows_out),
        (rows_ref, rows_out),
        (gatecol_ref, gatecol_out),
        (resgt_ref, resgt_out),
    )

    def own_copy(index):
        src, dst = own_pairs[index]
        return pltpu.make_async_copy(src, dst, out_sem.at[index])

    def attention(wqkv_v, wproj_v, near_ref, mask_ref):
        loads = [
            pltpu.make_async_copy(src, dst, in_sem.at[i])
            for i, (src, dst) in enumerate(((wqkv_ref, wqkv_v), (wproj_ref, wproj_v)))
        ]
        for copy in loads:
            copy.start()
        attn_setup(span_ref, table_ref, onehot_ref, near_ref, mask_ref)
        loads[0].wait()
        for row0 in range(0, seq_len, 128):
            rows = slice(row0, row0 + 128)
            x = tokens_ref[rows, :].astype(FULL)
            inv = lax.rsqrt(jnp.mean(x * x, axis=1, keepdims=True) + EPS)
            n1 = (x * inv * gain1_ref[...][None, :]).astype(LOW)
            qkv_ref[rows, :] = dot_nn(n1, wqkv_v[...]).astype(LOW)
        own_copy(0).start()
        loads[1].wait()
        for chunk in range(2):
            row0 = chunk * half
            rows = slice(row0, row0 + half)
            attn_block(row0, half, qkv_ref, near_ref, mask_ref, prob_ref, mixed_ref)
            hidden = tokens_ref[rows, :].astype(FULL) + dot_nn(mixed_ref[rows, :], wproj_v[...])
            hidden_ref[rows, :] = hidden
            inv = lax.rsqrt(jnp.mean(hidden * hidden, axis=1, keepdims=True) + EPS)
            n2 = (hidden * inv * gain2_ref[...][None, :]).astype(LOW)
            normed2_ref[rows, :] = n2
            own_out(1, chunk)

    pl.run_scoped(
        attention,
        pltpu.VMEM(wqkv_ref.shape, LOW),
        pltpu.VMEM(wproj_ref.shape, LOW),
        pltpu.VMEM((table_ref.shape[0], 128, 384), FULL),
        pltpu.VMEM((seq_len, seq_len), FULL),
    )
    for index in range(1, 5):
        own_copy(index).start()

    logits = dot_nt(wrouter_ref[...], normed2_ref[...])
    unnormed = jnp.exp(logits - jnp.max(logits, axis=0, keepdims=True))
    probabilities = unnormed / jnp.sum(unnormed, axis=0, keepdims=True)
    picked = [jnp.sum(jnp.where(hit, probabilities, 0.0), axis=0, keepdims=True) for hit in hits]
    both = picked[0] + picked[1]
    gates = [p / both for p in picked]
    gate = jnp.where(hits[0], gates[0], jnp.where(hits[1], gates[1], 0.0))
    gate_ref[...] = gate
    gate_all[me] = gate
    small(gate_ref, gate_all, 1)

    first_count = jnp.sum(jnp.where(hits[0], 1.0, 0.0), axis=1, keepdims=True)
    who = lax.broadcasted_iota(jnp.int32, hits[0].shape, 0).astype(FULL)
    slots = [
        jnp.sum(jnp.where(hits[0], ranks[0] + who * SLOTS, 0.0), axis=0, keepdims=True),
        jnp.sum(
            jnp.where(hits[1], ranks[1] + first_count + who * SLOTS, 0.0), axis=0, keepdims=True
        ),
    ]
    routes_f = routes_ref[...].astype(FULL)
    token_rows = jnp.concatenate(slots + gates + [routes_f[0:1], routes_f[1:2]] + slots, axis=0)
    token_ref[...] = jnp.transpose(token_rows)

    small_arrived(meta_all, 0)
    value = meta_all[:, me, :]
    is_first = (value >= 0.0) & (value < SECOND)
    is_second = value >= SECOND
    counts = [
        jnp.sum(jnp.where(hit, 1.0, 0.0), axis=1, keepdims=True) for hit in (is_first, is_second)
    ]
    row = lax.broadcasted_iota(jnp.int32, (experts, 128), 0)
    lane = lax.broadcasted_iota(jnp.int32, (experts, 128), 1)
    count_mat = jnp.where(lane == 0, counts[0], jnp.where(lane == 1, counts[1], 0.0))
    before = jnp.zeros((experts, 128), FULL)
    for s in range(experts):
        before = before + jnp.where(row > s, count_mat[s : s + 1, :], 0.0)
    first_total = jnp.sum(counts[0], axis=0, keepdims=True)
    base = [before[:, 0:1], before[:, 1:2] + first_total]
    pos_ref[...] = jnp.where(
        is_first, value + base[0], jnp.where(is_second, value - SECOND + base[1], -1.0)
    )
    info_ref[...] = jnp.where(
        lane == 0,
        counts[0],
        jnp.where(lane == 1, counts[1], jnp.where(lane == 2, base[0], base[1])),
    )

    accs = (cotrows_ref, rows_ref)

    def compact(which, mask):
        slot = lax.bitwise_xor(me, mask)
        acc = accs[which]

        @pl.loop(0, acc.shape[0] // ROW_TILE)
        def _(tile):
            row0 = pl.multiple_of(tile * ROW_TILE, ROW_TILE)
            here = pl.ds(row0, ROW_TILE)
            place = pos_ref[pl.ds(slot, 1), :] - row0.astype(FULL)
            at = lax.broadcasted_iota(jnp.int32, (ROW_TILE, seq_len), 0).astype(FULL)
            hit = at == place
            pick = jnp.where(hit, 1.0, 0.0).astype(LOW)
            data = owns[which][...] if mask == 0 else gats[which][slot]
            got = dot_nn(pick, data).astype(LOW)
            if mask:
                got = got + acc[here, :]
            acc[here, :] = got
            if which == 1:
                gates_here = jnp.where(hit, gate_all[slot, pl.ds(me, 1), :], 0.0)
                part = gates_here[:, 0:128]
                for i in range(1, seq_len // 128):
                    part = part + gates_here[:, i * 128 : i * 128 + 128]
                if mask:
                    part = part + acc_g[here, :]
                acc_g[here, :] = part

    def forward(which, mask, waits=(0, 1)):
        for chunk in waits:
            arrived(which, mask, chunk)
        for chunk in range(2):
            go(which, 3 + mask // 2, chunk, mask, 1)

    def take(which, mask):
        for chunk in range(2):
            arrived(which, mask, chunk)
        compact(which, mask)

    relay(0, 0)
    relay(0, 1)
    forward(0, 2, (1,))
    forward(0, 4, (0,))
    compact(0, 0)
    take(0, 1)
    compact(0, 2)
    compact(0, 4)
    take(0, 3)
    take(0, 5)
    relay(1, 0)
    relay(1, 1)
    small_arrived(gate_all, 1)
    compact(1, 0)
    take(1, 1)
    forward(1, 2, (1,))
    compact(1, 2)
    forward(1, 4, (0,))
    compact(1, 4)
    forward(0, 6)
    compact(0, 6)
    take(0, 7)
    own_copy(5).start()
    take(1, 3)
    take(1, 5)
    forward(1, 6)
    compact(1, 6)
    take(1, 7)
    own_copy(6).start()

    capacity = rows_ref.shape[0]
    tiles = gout_out.shape[0]

    def experts_first(act_v, slope_v, gout_v):
        def tile_copies(tile):
            return [
                pltpu.make_async_copy(src.at[tile], dst, tile_sem.at[kind, tile])
                for kind, (src, dst) in enumerate(
                    (
                        (act_v, act_out.at[tile * THIRDS]),
                        (slope_v, slope_out.at[tile * THIRDS]),
                        (gout_v, gout_out.at[tile]),
                    )
                )
            ]

        win_load().wait()

        def scaled(row0):
            rows = pl.ds(pl.multiple_of(row0, ROW_TILE), ROW_TILE)
            gate_col = jnp.sum(acc_g[rows, :], axis=1, keepdims=True)
            gatecol_ref[rows, :] = jnp.broadcast_to(gate_col, (ROW_TILE, 128))
            resg = gate_col * cotrows_ref[rows, :].astype(FULL)
            resgt_ref[:, rows] = jnp.transpose(resg.astype(LOW))

        parts = capacity // ROW_TILE

        @pl.loop(0, tiles)
        def _(tile):
            cols = pl.ds(pl.multiple_of(tile * THIRDS * FF_TILE, FF_TILE), FF_TILE)
            for row0 in range(0, capacity, ROW_TILE):
                here = slice(row0, row0 + ROW_TILE)
                act, slope = gelu_and_slope(dot_nn(rows_ref[here, :], win_v[:, cols]))
                act_v[tile, here, :] = act.astype(LOW)
                slope_v[tile, here, :] = slope.astype(LOW)
            scaled(tile * ROW_TILE)
            for copy in tile_copies(tile)[:2]:
                copy.start()

        for part in range(tiles, parts):
            scaled(part * ROW_TILE)
        own_copy(7).start()
        own_copy(8).start()

        @pl.loop(0, tiles)
        def _(tile):
            gout_v[tile] = dot_nn(resgt_ref[...], act_v[tile]).astype(LOW)
            tile_copies(tile)[2].start()

        @pl.loop(0, tiles)
        def _(tile):
            for copy in tile_copies(tile):
                copy.wait()

    pl.run_scoped(
        experts_first,
        pltpu.VMEM((tiles, capacity, FF_TILE), LOW),
        pltpu.VMEM((tiles, capacity, FF_TILE), LOW),
        pltpu.VMEM((tiles, width, FF_TILE), LOW),
    )

    for index in range(9):
        own_copy(index).wait()
    for copy in started:
        copy().wait_send()


def attn_dispatch(
    tokens, cot, gain1, wqkv, wproj, table, gain2, wrouter, routes, priority, span, w_in, groups
):
    seq_len, width = tokens.shape
    buckets, heads = table.shape
    experts = wrouter.shape[1]
    capacity = 5 * seq_len // 2
    ff = w_in.shape[1]
    sds = jax.ShapeDtypeStruct
    dma = pltpu.SemaphoreType.DMA
    return pl.pallas_call(
        attn_dispatch_kernel,
        out_shape=(
            sds((seq_len, 3 * width), LOW),
            sds((heads, seq_len, seq_len), LOW),
            sds((seq_len, width), LOW),
            sds((seq_len, width), FULL),
            sds((seq_len, width), LOW),
            sds((capacity, width), LOW),
            sds((capacity, width), LOW),
            sds((capacity, 128), FULL),
            sds((seq_len, 8), FULL),
            sds((experts, 128), FULL),
            sds((width, capacity), LOW),
            sds((ff // FF_TILE, capacity, FF_TILE), LOW),
            sds((ff // FF_TILE, capacity, FF_TILE), LOW),
            sds((groups, width, FF_TILE), LOW),
        ),
        in_specs=[VM] * 3 + [HBM] * 2 + [VM] * 6 + [SM, HBM],
        out_specs=[HBM] * 8 + [VM] * 2 + [HBM] * 4,
        scratch_shapes=[
            pltpu.VMEM((seq_len, 3 * width), LOW),
            pltpu.VMEM((heads, seq_len, seq_len), LOW),
            pltpu.VMEM((seq_len, width), LOW),
            pltpu.VMEM((seq_len, width), FULL),
            pltpu.VMEM((seq_len, width), LOW),
            pltpu.VMEM((experts, seq_len), FULL),
            pltpu.VMEM((experts, seq_len), FULL),
            pltpu.VMEM((experts, experts, seq_len), FULL),
            pltpu.VMEM((experts, experts, seq_len), FULL),
            pltpu.VMEM((experts, seq_len, width), LOW),
            pltpu.VMEM((experts, seq_len, width), LOW),
            pltpu.VMEM((capacity, 128), FULL),
            pltpu.VMEM((experts, seq_len), FULL),
            pltpu.VMEM(w_in.shape, LOW),
            pltpu.VMEM((capacity, width), LOW),
            pltpu.VMEM((capacity, width), LOW),
            pltpu.VMEM((capacity, 128), FULL),
            pltpu.VMEM((width, capacity), LOW),
            dma((2, 7, 2)),
            dma((2, 8, 2)),
            dma((2, 8)),
            dma((2, 8)),
            dma((9,)),
            dma((3,)),
            dma((3, groups)),
        ],
        compiler_params=pltpu.CompilerParams(
            vmem_limit_bytes=60 * MIB, collective_id=0, has_side_effects=True
        ),
    )(
        tokens,
        cot,
        gain1,
        wqkv,
        wproj,
        table.T,
        jnp.asarray(near_onehot(buckets)),
        gain2,
        wrouter.T,
        routes.T,
        priority,
        span,
        w_in,
    )


def gelu_and_slope(x):
    c = math.sqrt(2.0 / math.pi)
    square = x * x
    s = 0.5 * jnp.tanh(x * (c + (c * 0.044715) * square)) + 0.5
    act = x * s
    return act, s + act * (1.0 - s) * (2.0 * c + (6.0 * c * 0.044715) * square)


def pack_rows(source, info_ref, data, slots):
    info = info_ref[pl.ds(source, 1), :]
    slot = lax.broadcasted_iota(jnp.int32, (slots, 1), 0).astype(FULL)
    n0, n1, b0, b1 = [info[:, i : i + 1] for i in range(4)]
    place = jnp.where(slot < n0, b0 + slot, jnp.where(slot < n0 + n1, b1 + slot - n0, -1.0))
    at = lax.broadcasted_iota(jnp.int32, (slots, data.shape[0]), 1).astype(FULL)
    pick = jnp.where(at == place, 1.0, 0.0).astype(LOW)
    return dot_nn(pick, data[...]).astype(LOW)


def expert_first_kernel(rows_ref, resgt_ref, win_ref, act_in, slope_in, act_ref, slope_ref, gout_ref):
    for row0 in range(0, rows_ref.shape[0], ROW_TILE):
        here = slice(row0, row0 + ROW_TILE)
        act, slope = gelu_and_slope(dot_nn(rows_ref[here, :], win_ref[...]))
        act_ref[0, here, :] = act.astype(LOW)
        slope_ref[0, here, :] = slope.astype(LOW)
    gout_ref[0, 0] = dot_nn(resgt_ref[...], act_ref[0]).astype(LOW)


def expert_first(rows, resg_t, w_in, act, slope, groups):
    capacity, width = rows.shape
    rest = THIRDS - 1
    sds = jax.ShapeDtypeStruct

    def tile(i):
        return i // rest * THIRDS + 1 + i % rest

    return pl.pallas_call(
        expert_first_kernel,
        grid=(groups * rest,),
        out_shape=(
            sds(act.shape, LOW),
            sds(slope.shape, LOW),
            sds((groups, rest, width, FF_TILE), LOW),
        ),
        in_specs=[
            pl.BlockSpec((capacity, width), lambda i: (0, 0)),
            pl.BlockSpec((width, capacity), lambda i: (0, 0)),
            pl.BlockSpec((width, FF_TILE), lambda i: (0, tile(i))),
            HBM,
            HBM,
        ],
        out_specs=[
            pl.BlockSpec((1, capacity, FF_TILE), lambda i: (tile(i), 0, 0)),
            pl.BlockSpec((1, capacity, FF_TILE), lambda i: (tile(i), 0, 0)),
            pl.BlockSpec((1, 1, width, FF_TILE), lambda i: (i // rest, i % rest, 0, 0)),
        ],
        input_output_aliases={3: 0, 4: 1},
        compiler_params=pltpu.CompilerParams(vmem_limit_bytes=56 * MIB),
        cost_estimate=pl.CostEstimate(
            flops=4 * capacity * width * FF_TILE * groups * rest,
            bytes_accessed=30 * MIB,
            transcendentals=capacity * FF_TILE * groups * rest,
        ),
    )(rows, resg_t, w_in, act, slope)


def expert_back_kernel(
    cot_ref,
    gate_ref,
    rows_ref,
    info_ref,
    act_ref,
    slope_ref,
    wout_ref,
    win_ref,
    recv_ref,
    packed_ref,
    gin_ref,
    act_v,
    slope_v,
    wout_v,
    win_v,
    ig_v,
    acc_ref,
    gg_ref,
    data_ref,
    send_ref,
    rows_t,
    gin_v,
    load_sem,
    slope_sem,
    gin_sem,
    send_sem,
    recv_sem,
):
    g = lax.axis_index("group")
    me = lax.axis_index("expert")
    experts, slots, wide = send_ref.shape
    tiles, capacity, tile_width = act_v.shape
    width = cot_ref.shape[1]

    def device(mask):
        return (g, lax.bitwise_xor(me, mask))

    def load(index):
        src, dst = ((wout_ref, wout_v), (win_ref, win_v), (act_ref, act_v))[index]
        return pltpu.make_async_copy(src, dst, load_sem.at[index])

    def slope_load(tile):
        slot = lax.rem(tile, 2)
        return pltpu.make_async_copy(slope_ref.at[tile], slope_v.at[slot], slope_sem.at[slot])

    load(0).start()
    slope_load(0).start()
    load(2).start()
    load(1).start()
    barrier = pltpu.get_barrier_semaphore()
    for mask in range(1, experts):
        pl.semaphore_signal(barrier, inc=1, device_id=device(mask), device_id_type=MESH)
    pl.semaphore_wait(barrier, experts - 1)
    acc_ref[...] = jnp.zeros_like(acc_ref)
    gg_ref[...] = jnp.zeros_like(gg_ref)
    for index in range(3):
        load(index).wait()

    def span(tile):
        return pl.ds(pl.multiple_of(tile * tile_width, tile_width), tile_width)

    @pl.loop(0, tiles)
    def _(tile):
        slope_load(tile).wait()

        @pl.when(tile + 1 < tiles)
        def _():
            slope_load(tile + 1).start()

        for row0 in range(0, capacity, ROW_TILE):
            here = slice(row0, row0 + ROW_TILE)
            back = dot_nt(cot_ref[here, :], wout_v[span(tile), :])
            part = act_v[tile, here, :].astype(FULL) * back
            gg_ref[here, :] += part[:, 0:128] + part[:, 128:256]
            slope = slope_v[lax.rem(tile, 2), here, :].astype(FULL)
            ig_v[tile, here, :] = (slope * (gate_ref[here, 0:1] * back)).astype(LOW)
            acc_ref[here, :] += dot_nt(ig_v[tile, here, :], win_v[:, span(tile)])

    data_ref[:, :width] = acc_ref[...].astype(LOW)
    gg = jnp.sum(gg_ref[...], axis=1, keepdims=True)
    hi, mid, low = [t.astype(FULL) for t in split3(gg)]
    lane = lax.broadcasted_iota(jnp.int32, (capacity, 128), 1)
    data_ref[:, width:] = jnp.where(
        lane == 0, hi, jnp.where(lane == 1, mid, jnp.where(lane == 2, low, 0.0))
    ).astype(LOW)

    def exchange(mask):
        return pltpu.make_async_remote_copy(
            src_ref=send_ref.at[lax.bitwise_xor(me, mask)],
            dst_ref=recv_ref.at[me],
            send_sem=send_sem.at[mask],
            recv_sem=recv_sem.at[mask],
            device_id=device(mask),
            device_id_type=MESH,
        )

    for mask in (6, 7, 2, 4, 3, 5, 1):
        other = lax.bitwise_xor(me, mask)
        send_ref[other] = pack_rows(other, info_ref, data_ref, slots)
        exchange(mask).start()
    recv_ref[me] = pack_rows(me, info_ref, data_ref, slots)

    rows_t[...] = jnp.transpose(rows_ref[...])

    def gin_copy(tile):
        slot = lax.rem(tile, 2)
        return pltpu.make_async_copy(gin_v.at[slot], gin_ref.at[:, span(tile)], gin_sem.at[slot])

    @pl.loop(0, tiles)
    def _(tile):
        @pl.when(tile >= 2)
        def _():
            gin_copy(tile).wait()

        gin_v[lax.rem(tile, 2)] = dot_nn(rows_t[...], ig_v[tile]).astype(LOW)
        gin_copy(tile).start()

    acc_ref[...] = jnp.zeros_like(acc_ref)

    @pl.loop(0, tiles)
    def _(tile):
        for row0 in range(0, capacity, ROW_TILE):
            here = slice(row0, row0 + ROW_TILE)
            acc_ref[here, :] += dot_nn(act_v[tile, here, :], wout_v[span(tile), :])

    gin_copy(0).wait()
    gin_copy(1).wait()
    data_ref[:, :width] = acc_ref[...].astype(LOW)

    @pl.loop(0, experts)
    def _(source):
        packed_ref[source] = pack_rows(source, info_ref, data_ref.at[:, 0:width], slots)

    for mask in range(1, experts):
        exchange(mask).wait()


def expert_back(cot_rows, gate_col, rows, info, act, slope, w_out, w_in):
    capacity, width = cot_rows.shape
    tiles, _, tile_width = act.shape
    ff = w_in.shape[1]
    experts = info.shape[0]
    sds = jax.ShapeDtypeStruct
    dma = pltpu.SemaphoreType.DMA
    return pl.pallas_call(
        expert_back_kernel,
        out_shape=(
            sds((experts, SLOTS, width + 128), LOW),
            sds((experts, SLOTS, width), LOW),
            sds((width, ff), LOW),
        ),
        in_specs=[VM] * 4 + [HBM] * 4,
        out_specs=[VM, VM, HBM],
        scratch_shapes=[
            pltpu.VMEM(act.shape, LOW),
            pltpu.VMEM((2, capacity, tile_width), LOW),
            pltpu.VMEM(w_out.shape, LOW),
            pltpu.VMEM(w_in.shape, LOW),
            pltpu.VMEM(act.shape, LOW),
            pltpu.VMEM((capacity, width), FULL),
            pltpu.VMEM((capacity, 128), FULL),
            pltpu.VMEM((capacity, width + 128), LOW),
            pltpu.VMEM((experts, SLOTS, width + 128), LOW),
            pltpu.VMEM((width, capacity), LOW),
            pltpu.VMEM((2, width, tile_width), LOW),
            dma((3,)),
            dma((2,)),
            dma((2,)),
            dma((experts,)),
            dma((experts,)),
        ],
        compiler_params=pltpu.CompilerParams(
            vmem_limit_bytes=60 * MIB, collective_id=2, has_side_effects=True
        ),
        cost_estimate=pl.CostEstimate(
            flops=8 * capacity * width * ff + 30_000_000_000, bytes_accessed=50 * MIB, transcendentals=0
        ),
    )(cot_rows, gate_col, rows, info, act, slope, w_out, w_in)


def attn_back_kernel(
    tokens_ref,
    cot_ref,
    hidden_ref,
    normed2_ref,
    mixed_ref,
    qkv_hbm,
    prob_hbm,
    recv_ref,
    token_ref,
    gain1_ref,
    gain2_ref,
    wqkv_hbm,
    wproj_ref,
    wrouter_ref,
    onehot_ref,
    result_ref,
    block_ref,
    gtok_ref,
    dense_out,
    small_out,
    hgrad_ref,
    mgrad_ref,
    mgrad_t,
    normed_t,
    q_t,
    ds_ref,
    diag_ref,
    dk_t,
    dv_t,
    dqkv_ref,
    part_ref,
    pair_in,
    chip_ref,
    plane_in,
    plane_ref,
    group_in,
    small_ref,
    small_in,
    small_plane,
    small_group,
    qkv_ref,
    prob_ref,
    wqkv_ref,
    back_ref,
    load_sems,
    back_sems,
    pair_sems,
    plane_sems,
    group_sems,
    final_sems,
    small_sems,
    smallz_sems,
):
    seq_len, width = tokens_ref.shape
    experts = wrouter_ref.shape[0]
    chunks = part_ref.shape[0]
    groups = group_in.shape[1]
    tile = 128
    g = lax.axis_index("group")
    me = lax.axis_index("expert")
    parity = lax.rem(me, 2)
    mine = lax.div(me, 2)
    summer = [groups // 2 - 1 + c % 2 for c in range(chunks)]

    def device(mask):
        return (g, lax.bitwise_xor(me, mask))

    def load(index):
        src, dst = ((qkv_hbm, qkv_ref), (prob_hbm, prob_ref), (wqkv_hbm, wqkv_ref))[index]
        return pltpu.make_async_copy(src, dst, load_sems.at[index])

    own_result = pltpu.make_async_copy(result_ref.at[me], back_ref.at[me], load_sems.at[3])
    for index in range(3):
        load(index).start()
    own_result.start()
    barrier = pltpu.get_barrier_semaphore()
    for mask in range(1, experts):
        pl.semaphore_signal(barrier, inc=1, device_id=device(mask), device_id_type=MESH)
    for step in range(1, groups):
        pl.semaphore_signal(
            barrier, inc=1, device_id=(lax.rem(g + step, groups), me), device_id_type=MESH
        )
    pl.semaphore_wait(barrier, experts - 1 + groups - 1)

    def remote(src, dst, sems, at, where):
        return pltpu.make_async_remote_copy(
            src_ref=src,
            dst_ref=dst,
            send_sem=sems.at[(0, *at)],
            recv_sem=sems.at[(1, *at)],
            device_id=where,
            device_id_type=MESH,
        )

    started = []

    def go(copy):
        copy.start()
        started.append(copy)

    def result_copy(mask):
        other = lax.bitwise_xor(me, mask)
        return remote(result_ref.at[other], back_ref.at[me], back_sems, (mask,), device(mask))

    for mask in (2, 4, 3, 5, 1):
        result_copy(mask).start()

    def pair_send(c):
        for chip in range(experts // 2):
            other = 2 * chip + 1 - parity
            go(remote(part_ref.at[c, other], pair_in.at[c, chip], pair_sems, (c, chip), device(1)))

    def plane_send(c):
        for chip in range(experts // 2):
            remote(
                part_ref.at[c, 0], pair_in.at[c, chip], pair_sems, (c, chip), device(1)
            ).wait_recv()
            total = part_ref[c, 2 * chip + parity].astype(FULL) + pair_in[c, chip].astype(FULL)
            chip_ref[c, chip] = total.astype(LOW)
        for other in range(1, experts // 2):
            go(
                remote(
                    chip_ref.at[c, lax.bitwise_xor(mine, other)],
                    plane_in.at[c, other - 1],
                    plane_sems,
                    (c, other - 1),
                    device(2 * other),
                )
            )

    def group_send(c):
        total = chip_ref[c, mine].astype(FULL)
        for other in range(1, experts // 2):
            remote(
                chip_ref.at[c, 0],
                plane_in.at[c, other - 1],
                plane_sems,
                (c, other - 1),
                device(2 * other),
            ).wait_recv()
            total = total + plane_in[c, other - 1].astype(FULL)
        plane_ref[c] = total.astype(LOW)

        @pl.when(g != summer[c])
        def _():
            remote(
                plane_ref.at[c], group_in.at[c, g], group_sems, (c, g), (jnp.int32(summer[c]), me)
            ).start()

    def final_send(c):
        @pl.when(g == summer[c])
        def _():
            total = plane_ref[c].astype(FULL)
            for step in range(1, groups):
                src = lax.rem(g + step, groups)
                remote(
                    plane_ref.at[c], group_in.at[c, src], group_sems, (c, src), (src, me)
                ).wait_recv()
                total = total + group_in[c, src].astype(FULL)
            dense_out[c] = total.astype(LOW)
            for step in range(1, groups):
                where = (lax.rem(g + step, groups), me)
                remote(dense_out.at[c], dense_out.at[c], final_sems, (c, step - 1), where).start()

    def finish(c):
        where = (lax.rem(g + 1, groups), me)
        for step in range(1, groups):
            copy = remote(dense_out.at[c], dense_out.at[c], final_sems, (c, step - 1), where)

            @pl.when(g == summer[c])
            def _():
                copy.wait_send()

            @pl.when(lax.rem(summer[c] + step, groups) == g)
            def _():
                copy.wait_recv()

        @pl.when(g != summer[c])
        def _():
            remote(plane_ref.at[c], group_in.at[c, g], group_sems, (c, g), where).wait_send()

    ggain2 = jnp.zeros((8, width), FULL)
    lg_t = []
    for row0 in range(0, seq_len, tile):
        rows = slice(row0, row0 + tile)
        token = token_ref[rows, :]
        at = lax.broadcasted_iota(jnp.int32, (tile, recv_ref.shape[0]), 1).astype(FULL)
        picks = [jnp.where(at == token[:, k : k + 1], 1.0, 0.0).astype(LOW) for k in range(2)]
        got = dot_nn(jnp.concatenate(picks, axis=0), recv_ref[...])
        gg = [
            jnp.sum(got[k * tile : k * tile + tile, width:], axis=1, keepdims=True) for k in range(2)
        ]
        pull = token[:, 2:3] * token[:, 3:4] * (gg[0] - gg[1])
        expert = lax.broadcasted_iota(jnp.int32, (tile, 128), 1).astype(FULL)
        lg = jnp.where(expert == token[:, 4:5], pull, jnp.where(expert == token[:, 5:6], -pull, 0.0))
        lg_t.append(jnp.transpose(lg)[:experts])
        ngrad = (
            got[:tile, :width]
            + got[tile:, :width]
            + dot_nn(lg[:, :experts].astype(LOW), wrouter_ref[...])
        )
        hidden = hidden_ref[rows, :]
        inv = lax.rsqrt(jnp.mean(hidden * hidden, axis=1, keepdims=True) + EPS)
        unit = hidden * inv
        ng = ngrad * unit
        for i in range(tile // 8):
            ggain2 = ggain2 + ng[i * 8 : i * 8 + 8]
        scaled = ngrad * gain2_ref[...][None, :]
        proj = jnp.mean(scaled * unit, axis=1, keepdims=True)
        hgrad = cot_ref[rows, :].astype(FULL) + inv * (scaled - unit * proj)
        hgrad_ref[rows, :] = hgrad
        mgrad_ref[rows, :] = dot_nt(hgrad.astype(LOW), wproj_ref[...]).astype(LOW)
        x = tokens_ref[rows, :].astype(FULL)
        inv = lax.rsqrt(jnp.mean(x * x, axis=1, keepdims=True) + EPS)
        dqkv_ref[rows, :width] = (x * inv * gain1_ref[...][None, :]).astype(LOW)
    ggain2 = jnp.sum(ggain2, axis=0, keepdims=True)
    logit_grad_t = jnp.concatenate(lg_t, axis=1).astype(LOW)
    grouter = dot_nn(logit_grad_t, normed2_ref[...])
    normed_t[...] = jnp.transpose(dqkv_ref[:, :width])
    part_ref[0] = (
        dot_nn(jnp.transpose(mixed_ref[...]), hgrad_ref[...].astype(LOW))
        .astype(LOW)
        .reshape(experts, width // experts, width)
    )
    pair_send(0)
    mgrad_t[...] = jnp.transpose(mgrad_ref[...])
    load(0).wait()
    q_t[...] = jnp.transpose(qkv_ref[:, :width])
    load(1).wait()
    up = lax.broadcasted_iota(jnp.int32, (128, 128), 0)
    across = lax.broadcasted_iota(jnp.int32, (128, 128), 1)
    flip = jnp.where(up + across == 127, 1.0, 0.0).astype(FULL)

    def heads_back(pair):
        col = pl.multiple_of(pair * 128, 128)
        kp = qkv_ref[:, pl.ds(width + col, 128)]
        vp = qkv_ref[:, pl.ds(2 * width + col, 128)]
        op = mgrad_ref[:, pl.ds(col, 128)].astype(FULL)
        os = jnp.concatenate([(op * half_mask(sub, 1.0)).astype(LOW) for sub in range(2)], axis=0)
        dp = dot_nt(os, vp)
        for sub in range(2):
            h = 2 * pair + sub
            near = jnp.zeros((128, 384), FULL)
            far_neg = jnp.zeros((128, 128), FULL)
            far_pos = jnp.zeros((128, 128), FULL)
            blocks = seq_len // 128
            for block in range(blocks):
                first = sub * seq_len + block * 128
                here = slice(block * 128, block * 128 + 128)
                p = prob_ref[h, here, :].astype(FULL)
                weighted = p * dp[first : first + 128]
                ds = weighted - p * jnp.sum(weighted, axis=1, keepdims=True)
                low = ds.astype(LOW)
                ds_ref[sub, here, :] = low
                ds = low.astype(FULL)
                strip = []
                for d in range(-1, 2):
                    other = block + d
                    if 0 <= other < blocks:
                        strip.append(ds[:, other * 128 : other * 128 + 128])
                    else:
                        strip.append(jnp.zeros((128, 128), FULL))
                near = near + jnp.concatenate(strip, axis=1)
                for other in range(blocks):
                    piece = ds[:, other * 128 : other * 128 + 128]
                    if other - block <= -2:
                        far_neg = far_neg + piece
                    elif other - block >= 2:
                        far_pos = far_pos + piece
            low_sum = jnp.sum(far_neg)
            high_sum = jnp.sum(far_pos)
            padded = jnp.concatenate([exact_nn(flip, near), jnp.zeros((128, 128), FULL)], axis=1)
            turned = pltpu.roll(padded, 1, 1, stride=1, stride_axis=0)
            sums = jnp.sum(turned, axis=0, keepdims=True)
            lane = lax.broadcasted_iota(jnp.int32, (1, 512), 1)
            sums = sums + jnp.where(lane == 1, low_sum, jnp.where(lane == 511, high_sum, 0.0))
            diag_ref[pl.ds(h, 1), :] = sums
        lane = lax.broadcasted_iota(jnp.int32, (seq_len, 128), 1)
        dq = dot_nn(jnp.concatenate([ds_ref[0], ds_ref[1]], axis=0), kp)
        dqkv_ref[:, pl.ds(col, 128)] = (
            jnp.where(lane < 64, dq[:seq_len], dq[seq_len:]) * 0.125
        ).astype(LOW)
        for sub in range(2):
            part = pl.ds(pl.multiple_of(col + sub * 64, 64), 64)
            dk_t[part, :] = (dot_nn(q_t[part, :], ds_ref[sub]) * 0.125).astype(LOW)
            dv_t[part, :] = dot_nn(mgrad_t[part, :], prob_ref[2 * pair + sub]).astype(LOW)

    stripe = width // (chunks - 1)
    for c in range(1, chunks):
        pairs = stripe // 128

        @pl.loop((c - 1) * pairs, c * pairs)
        def _(pair):
            heads_back(pair)

        col = (c - 1) * stripe
        dqkv_ref[:, width + col : width + col + stripe] = jnp.transpose(dk_t[col : col + stripe, :])
        dqkv_ref[:, 2 * width + col : 2 * width + col + stripe] = jnp.transpose(
            dv_t[col : col + stripe, :]
        )
        for third in range(3):
            here = third * width + col
            part_ref[c, :, :, third * stripe : third * stripe + stripe] = (
                dot_nn(normed_t[...], dqkv_ref[:, here : here + stripe])
                .astype(LOW)
                .reshape(experts, width // experts, stripe)
            )
        pair_send(c)
        plane_send(c - 1)
        if c >= 2:
            group_send(c - 2)

    load(2).wait()
    ggain1 = jnp.zeros((8, width), FULL)
    for row0 in range(0, seq_len, tile):
        rows = slice(row0, row0 + tile)
        x = tokens_ref[rows, :].astype(FULL)
        inv = lax.rsqrt(jnp.mean(x * x, axis=1, keepdims=True) + EPS)
        unit = x * inv
        ngrad = dot_nt(dqkv_ref[rows, :], wqkv_ref[...])
        ng = ngrad * unit
        for i in range(tile // 8):
            ggain1 = ggain1 + ng[i * 8 : i * 8 + 8]
        scaled = ngrad * gain1_ref[...][None, :]
        proj = jnp.mean(scaled * unit, axis=1, keepdims=True)
        gtok_ref[rows, :] = (hgrad_ref[rows, :] + inv * (scaled - unit * proj)).astype(LOW)
        if row0 == 0:
            plane_send(chunks - 1)
            for mask in (6, 7):
                result_copy(mask).start()
    ggain1 = jnp.sum(ggain1, axis=0, keepdims=True)

    gtable = exact_nt(onehot_ref[...], diag_ref[...])
    shard = width // experts
    per = gtable.shape[0] // experts
    for e in range(experts):
        cols = slice(e * shard, e * shard + shard)
        block = jnp.concatenate([ggain1[:, cols], ggain2[:, cols], grouter[:, cols]], axis=0)
        small_ref[e] = jnp.zeros(small_ref.shape[1:], FULL)
        small_ref[e, 0 : 2 + experts, 0:shard] = block
        small_ref[e, 2 + experts : 2 + experts + per, 0 : gtable.shape[1]] = gtable[
            e * per : e * per + per
        ]
    for mask in range(1, experts):
        other = lax.bitwise_xor(me, mask)
        go(remote(small_ref.at[other], small_in.at[mask], small_sems, (mask,), device(mask)))
    final_send(0)
    group_send(2)
    total = small_ref[me]
    for mask in range(1, experts):
        remote(
            small_ref.at[0], small_in.at[mask], small_sems, (mask,), device(mask)
        ).wait_recv()
        total = total + small_in[mask]
    small_plane[...] = total
    for step in range(1, groups):
        where = (lax.rem(g + step, groups), me)
        go(remote(small_plane, small_group.at[step], smallz_sems, (step,), where))
    final_send(1)
    group_send(3)
    own_result.wait()
    for mask in range(1, experts):
        result_copy(mask).wait()

    @pl.loop(0, seq_len // tile)
    def _(step):
        rows = pl.ds(pl.multiple_of(step * tile, tile), tile)
        token = token_ref[rows, :]
        at = lax.broadcasted_iota(jnp.int32, (tile, experts * SLOTS), 1).astype(FULL)
        picks = [jnp.where(at == token[:, k : k + 1], 1.0, 0.0).astype(LOW) for k in range(2)]
        got = dot_nn(
            jnp.concatenate(picks, axis=0), back_ref[...].reshape(experts * SLOTS, width)
        )
        block_ref[rows, :] = (
            hidden_ref[rows, :] + token[:, 2:3] * got[:tile] + token[:, 3:4] * got[tile:]
        ).astype(LOW)

    final_send(2)
    final_send(3)
    for step in range(1, groups):
        remote(
            small_plane, small_group.at[step], smallz_sems, (step,), (lax.rem(g + step, groups), me)
        ).wait_recv()
        total = total + small_group[step]
    small_out[...] = total
    for c in range(chunks):
        finish(c)
    for copy in started:
        copy.wait_send()


def attn_back(
    tokens, cot, hidden, normed2, mixed, qkv, prob, recv, token, gain1, gain2, wqkv, wproj, wrouter, table, result, groups
):
    seq_len, width = tokens.shape
    buckets, heads = table.shape
    experts = wrouter.shape[1]
    shard = width // experts
    chunks = groups
    chips = experts // 2
    small = (16, 128)
    sds = jax.ShapeDtypeStruct
    dma = pltpu.SemaphoreType.DMA
    return pl.pallas_call(
        attn_back_kernel,
        out_shape=(
            sds((seq_len, width), LOW),
            sds((seq_len, width), LOW),
            sds((chunks, shard, width), LOW),
            sds(small, FULL),
        ),
        in_specs=[VM] * 5 + [HBM] * 2 + [VM] * 4 + [HBM] + [VM] * 3 + [HBM],
        out_specs=[VM] * 4,
        scratch_shapes=[
            pltpu.VMEM((seq_len, width), FULL),
            pltpu.VMEM((seq_len, width), LOW),
            pltpu.VMEM((width, seq_len), LOW),
            pltpu.VMEM((width, seq_len), LOW),
            pltpu.VMEM((width, seq_len), LOW),
            pltpu.VMEM((2, seq_len, seq_len), LOW),
            pltpu.VMEM((heads, 512), FULL),
            pltpu.VMEM((width, seq_len), LOW),
            pltpu.VMEM((width, seq_len), LOW),
            pltpu.VMEM((seq_len, 3 * width), LOW),
            pltpu.VMEM((chunks, experts, shard, width), LOW),
            pltpu.VMEM((chunks, chips, shard, width), LOW),
            pltpu.VMEM((chunks, chips, shard, width), LOW),
            pltpu.VMEM((chunks, chips - 1, shard, width), LOW),
            pltpu.VMEM((chunks, shard, width), LOW),
            pltpu.VMEM((chunks, groups, shard, width), LOW),
            pltpu.VMEM((experts, *small), FULL),
            pltpu.VMEM((experts, *small), FULL),
            pltpu.VMEM(small, FULL),
            pltpu.VMEM((groups, *small), FULL),
            pltpu.VMEM((seq_len, 3 * width), LOW),
            pltpu.VMEM((heads, seq_len, seq_len), LOW),
            pltpu.VMEM(wqkv.shape, LOW),
            pltpu.VMEM(result.shape, LOW),
            dma((4,)),
            dma((2, experts)),
            dma((2, chunks, chips)),
            dma((2, chunks, chips - 1)),
            dma((2, chunks, groups)),
            dma((2, chunks, groups - 1)),
            dma((2, experts)),
            dma((2, groups)),
        ],
        compiler_params=pltpu.CompilerParams(
            vmem_limit_bytes=60 * MIB, collective_id=1, has_side_effects=True
        ),
        cost_estimate=pl.CostEstimate(
            flops=30_000_000_000, bytes_accessed=30 * MIB, transcendentals=0
        ),
    )(
        tokens,
        cot,
        hidden,
        normed2,
        mixed,
        qkv,
        prob,
        recv,
        token,
        gain1,
        gain2,
        wqkv,
        wproj,
        wrouter.T,
        jnp.asarray(near_onehot(buckets)),
        result,
    )


def on_device_fast(
    tokens,
    gain_first,
    w_qkv,
    w_proj,
    bias_table,
    gain_second,
    w_router,
    w_in,
    w_out,
    routes,
    priority,
    span_start,
    cotangent,
):
    experts = w_router.shape[1]
    width = tokens.shape[1]
    groups = lax.axis_size("group")
    (
        qkv,
        prob,
        mixed,
        hidden,
        normed2,
        rows,
        cot_rows,
        gate_col,
        token,
        info,
        resg_t,
        act,
        slope,
        outer_first,
    ) = attn_dispatch(
        tokens,
        cotangent,
        gain_first,
        w_qkv,
        w_proj,
        bias_table,
        gain_second,
        w_router,
        routes,
        priority,
        span_start,
        w_in[0],
        groups,
    )
    outer_first = lax.psum_scatter(outer_first, "group", scatter_dimension=0, tiled=True)
    act, slope, outer_rest = expert_first(rows, resg_t, w_in[0], act, slope, groups)
    outer_rest = lax.psum_scatter(outer_rest, "group", scatter_dimension=0, tiled=True)
    outer = jnp.concatenate([outer_first[:, None], outer_rest], axis=1)
    grad_out = jnp.swapaxes(outer, 2, 3).reshape(1, -1, width).astype(FULL)
    recv, packed_out, grad_inner = expert_back(
        cot_rows, gate_col, rows, info, act, slope, w_out[0], w_in[0]
    )
    grad_in = lax.psum_scatter(
        grad_inner[None], "group", scatter_dimension=1, tiled=True
    ).astype(FULL)
    block_out, gtok, dense, small = attn_back(
        tokens,
        cotangent,
        hidden,
        normed2,
        mixed,
        qkv,
        prob,
        recv.reshape(-1, width + 128),
        token,
        gain_first,
        gain_second,
        w_qkv,
        w_proj,
        w_router,
        bias_table,
        packed_out,
        groups,
    )
    shard = width // experts
    heads = bias_table.shape[1]
    per = bias_table.shape[0] // experts
    stripe = width // (dense.shape[0] - 1)
    grad_qkv = (
        dense[1:].reshape(-1, shard, 3, stripe).transpose(1, 2, 0, 3).reshape(shard, 3 * width)
    )
    return (
        block_out,
        gtok,
        small[0, :shard],
        grad_qkv.astype(FULL),
        dense[0].astype(FULL),
        small[2 + experts : 2 + experts + per, :heads],
        small[1, :shard],
        small[2 : 2 + experts, :shard].T,
        grad_in,
        grad_out,
    )


def bucket_table(seq_len, buckets):
    half_count = buckets // 2
    exact_count = half_count // 2
    offsets = np.arange(-(seq_len - 1), seq_len)
    upper_half = (offsets > 0).astype(np.int64) * half_count
    distance = np.abs(offsets)
    scaled = (
        np.log(np.maximum(distance, 1) / float(exact_count))
        / np.log(128.0 / exact_count)
        * (half_count - exact_count)
    )
    larger = np.minimum(
        exact_count + np.floor(np.maximum(scaled, 0.0)).astype(np.int64), half_count - 1
    )
    bucket = upper_half + np.where(distance < exact_count, distance, larger)
    places = np.arange(seq_len)
    return bucket[places[None, :] - places[:, None] + seq_len - 1].astype(np.int32)


def allowed_pairs(seq_len, span_begin, span_len):
    places = jnp.arange(seq_len, dtype=jnp.int32)
    causal = places[None, :] <= places[:, None]
    inside = (places >= span_begin) & (places < span_begin + span_len)
    return causal | inside[:, None] & inside[None, :]


def rms_norm(values, norm_gain):
    return values * lax.rsqrt(jnp.mean(values * values, axis=-1, keepdims=True) + 1e-06) * norm_gain


def gate_values(logits, routes, experts):
    probabilities = jax.nn.softmax(logits, axis=-1)
    chosen = (routes[..., None] == jnp.arange(experts, dtype=jnp.int32)).astype(jnp.float32)
    picked = jnp.sum(probabilities[:, None, :] * chosen, axis=-1)
    return picked / jnp.sum(picked, axis=1, keepdims=True)


def local_ranks(choice_hits, priority):
    token_count = priority.shape[0]
    token_order = (
        jnp.zeros((token_count,), jnp.int32)
        .at[priority]
        .set(jnp.arange(token_count, dtype=jnp.int32))
    )
    ordered = choice_hits[token_order]
    running = jnp.cumsum(ordered, axis=0) - ordered
    return jnp.sum(running[priority] * choice_hits, axis=-1)


def contract_rows(left, right):
    return lax.dot_general(
        left, right, (((0,), (0,)), ((), ())), preferred_element_type=jnp.float32
    )


def on_device(
    tokens,
    gain_first,
    w_qkv,
    w_proj,
    bias_table,
    gain_second,
    w_router,
    w_in,
    w_out,
    routes,
    priority,
    span_start,
    cotangent,
):
    seq_len, model_width = tokens.shape
    buckets, head_count = bias_table.shape
    head_dim = model_width // head_count
    experts = w_router.shape[1]
    slot_count = 4 * seq_len // experts
    capacity = 5 * seq_len // 2
    score_scale = 1.0 / math.sqrt(head_dim)
    highest = lax.Precision.HIGHEST
    lowtype = jnp.bfloat16
    fulltype = jnp.float32
    tokens_f = tokens.astype(fulltype)
    normed_one = rms_norm(tokens_f, gain_first).astype(lowtype)
    qkv_rows = jnp.dot(normed_one, w_qkv, preferred_element_type=fulltype).astype(lowtype)
    qkv_rows = qkv_rows.reshape(seq_len, 3, head_count, head_dim)
    queries, key_rows, value_rows = (qkv_rows[:, 0], qkv_rows[:, 1], qkv_rows[:, 2])
    bucket_index = jnp.asarray(bucket_table(seq_len, buckets))
    onehot_table = (bucket_index[:, :, None] == jnp.arange(buckets, dtype=jnp.int32)).astype(
        fulltype
    )
    rel_bias = jnp.einsum("qkb,bh->hqk", onehot_table, bias_table, precision=highest)
    allowed = allowed_pairs(seq_len, span_start[0], PIC)

    def masked_scores():
        raw_scores = (
            jnp.einsum("qhc,khc->hqk", queries, key_rows, preferred_element_type=fulltype)
            * score_scale
            + rel_bias
        )
        return jnp.where(allowed[None], raw_scores, -1e30)

    scores = masked_scores()
    log_total = jax.nn.logsumexp(scores, axis=-1)
    attn_probs = jnp.exp(scores - log_total[..., None]).astype(lowtype)
    mixed_heads = jnp.einsum(
        "hqk,khc->qhc", attn_probs, value_rows, preferred_element_type=fulltype
    )
    mixed_heads = mixed_heads.astype(lowtype).reshape(seq_len, model_width)
    hidden = tokens_f + jnp.dot(mixed_heads, w_proj, preferred_element_type=fulltype)
    normed_two = rms_norm(hidden, gain_second).astype(lowtype)
    logits = jnp.dot(normed_two, w_router, preferred_element_type=fulltype)
    gate_weights = gate_values(logits, routes, experts)
    choice_hits = (routes[..., None] == jnp.arange(experts, dtype=jnp.int32)).astype(jnp.int32)
    counts = jnp.sum(choice_hits, axis=0)
    every_count = lax.all_gather(counts[None], "expert", axis=0, tiled=True)
    pair_ranks = local_ranks(choice_hits, priority[0])
    second_shift = jnp.sum(choice_hits[:, 1] * counts[0], axis=-1)
    slot_index = pair_ranks + jnp.stack([jnp.zeros_like(second_shift), second_shift], axis=-1)
    flat_slot = (routes * slot_count + slot_index).reshape(-1)
    own_expert = (jnp.arange(experts, dtype=jnp.int32) == lax.axis_index("expert")).astype(
        jnp.int32
    )
    own_counts = jnp.sum(every_count * own_expert, axis=-1)
    first_rows, second_rows = (own_counts[:, 0], own_counts[:, 1])
    first_before = jnp.cumsum(first_rows) - first_rows
    second_before = jnp.cumsum(second_rows) - second_rows
    first_total = jnp.sum(first_rows)
    column = jnp.arange(slot_count, dtype=jnp.int32)[None, :]
    position = jnp.where(
        column < first_rows[:, None],
        first_before[:, None] + column,
        first_total + second_before[:, None] + column - first_rows[:, None],
    )
    usable = (column < (first_rows + second_rows)[:, None]) & (position < capacity)
    destination = jnp.where(usable, position, capacity).reshape(-1)

    def pack_pairs(pair_rows):
        packed = jnp.zeros((experts * slot_count, model_width), lowtype)
        packed = packed.at[flat_slot].set(pair_rows.reshape(-1, model_width))
        return packed.reshape(experts, slot_count, model_width)

    def compact_rows(arrived):
        gathered_rows = jnp.zeros((capacity + 1, model_width), lowtype)
        return gathered_rows.at[destination].add(arrived.reshape(-1, model_width))[:capacity]

    def spread_rows(expert_out):
        padded = jnp.concatenate([expert_out, jnp.zeros((1, model_width), lowtype)], axis=0)
        return padded[destination].reshape(-1, slot_count, model_width)

    def unpack_pairs(received):
        return (
            received.reshape(-1, model_width)[flat_slot]
            .reshape(seq_len, 2, model_width)
            .astype(fulltype)
        )

    pair_rows = jnp.broadcast_to(normed_two[:, None, :], (seq_len, 2, model_width))
    arrived = lax.all_to_all(
        pack_pairs(pair_rows), "expert", split_axis=0, concat_axis=0, tiled=True
    )
    expert_rows = compact_rows(arrived)
    inner_pre = jnp.dot(expert_rows, w_in[0], preferred_element_type=fulltype)
    active = jax.nn.gelu(inner_pre).astype(lowtype)
    result = jnp.dot(active, w_out[0], preferred_element_type=fulltype).astype(lowtype)
    returned = unpack_pairs(
        lax.all_to_all(spread_rows(result), "expert", split_axis=0, concat_axis=0, tiled=True)
    )
    block_out = hidden + jnp.sum(gate_weights[..., None] * returned, axis=1)
    upstream = cotangent.astype(fulltype)
    gate_grad = jnp.sum(upstream[:, None, :] * returned, axis=-1)
    result_grad = (gate_weights[..., None] * upstream[:, None, :]).astype(lowtype)
    result_rows = compact_rows(
        lax.all_to_all(pack_pairs(result_grad), "expert", split_axis=0, concat_axis=0, tiled=True)
    )
    grad_outer = contract_rows(active, result_rows)
    hidden_pre_grad = jnp.dot(result_rows, w_out[0].T, preferred_element_type=fulltype)
    inner_grad = jax.vjp(jax.nn.gelu, inner_pre)[1](hidden_pre_grad)[0].astype(lowtype)
    grad_inner = contract_rows(expert_rows, inner_grad)
    rows_grad = jnp.dot(inner_grad, w_in[0].T, preferred_element_type=fulltype).astype(lowtype)
    pair_grad = unpack_pairs(
        lax.all_to_all(spread_rows(rows_grad), "expert", split_axis=0, concat_axis=0, tiled=True)
    )
    logit_grad = jax.vjp(lambda values: gate_values(values, routes, experts), logits)[1](gate_grad)[
        0
    ].astype(lowtype)
    grad_router = contract_rows(normed_two, logit_grad)
    normed_grad = jnp.sum(pair_grad, axis=1) + jnp.dot(
        logit_grad, w_router.T, preferred_element_type=fulltype
    )
    second_back = jax.vjp(rms_norm, hidden, gain_second)[1](normed_grad)
    hidden_grad = upstream + second_back[0]
    branch_grad = hidden_grad.astype(lowtype)
    grad_proj = contract_rows(mixed_heads, branch_grad)
    mixed_grad = jnp.dot(branch_grad, w_proj.T, preferred_element_type=fulltype).astype(lowtype)
    mixed_grad = mixed_grad.reshape(seq_len, head_count, head_dim)
    scores = masked_scores()
    probs_full = jnp.exp(scores - log_total[..., None])
    probs_low = probs_full.astype(lowtype)
    prob_grad = jnp.einsum("qhc,khc->hqk", mixed_grad, value_rows, preferred_element_type=fulltype)
    value_grad = jnp.einsum("hqk,qhc->khc", probs_low, mixed_grad, preferred_element_type=fulltype)
    row_dot = jnp.sum(probs_full * prob_grad, axis=-1, keepdims=True)
    score_grad = (probs_full * (prob_grad - row_dot)).astype(lowtype)
    query_grad = (
        jnp.einsum("hqk,khc->qhc", score_grad, key_rows, preferred_element_type=fulltype)
        * score_scale
    )
    key_grad = (
        jnp.einsum("hqk,qhc->khc", score_grad, queries, preferred_element_type=fulltype)
        * score_scale
    )
    grad_table = jnp.einsum(
        "hqk,qkb->bh", score_grad.astype(fulltype), onehot_table, precision=highest
    )
    qkv_grad = (
        jnp.stack([query_grad, key_grad, value_grad], axis=1)
        .astype(lowtype)
        .reshape(seq_len, 3 * model_width)
    )
    grad_qkv = contract_rows(normed_one, qkv_grad)
    normed_one_grad = jnp.dot(qkv_grad, w_qkv.T, preferred_element_type=fulltype)
    first_back = jax.vjp(rms_norm, tokens_f, gain_first)[1](normed_one_grad)
    grad_tokens = (hidden_grad + first_back[0]).astype(lowtype)
    dense_grads = (first_back[1], grad_qkv, grad_proj, grad_table, second_back[1], grad_router)
    shares = (
        lax.psum_scatter(
            dense_grads[0].astype(jnp.bfloat16), "expert", scatter_dimension=0, tiled=True
        ).astype(jnp.float32),
        lax.psum_scatter(
            dense_grads[1].astype(jnp.bfloat16), "expert", scatter_dimension=0, tiled=True
        ).astype(jnp.float32),
        lax.psum_scatter(
            dense_grads[2].astype(jnp.bfloat16), "expert", scatter_dimension=0, tiled=True
        ).astype(jnp.float32),
        lax.psum_scatter(
            dense_grads[3].astype(jnp.bfloat16), "expert", scatter_dimension=0, tiled=True
        ).astype(jnp.float32),
        lax.psum_scatter(
            dense_grads[4].astype(jnp.bfloat16), "expert", scatter_dimension=0, tiled=True
        ).astype(jnp.float32),
        lax.psum_scatter(
            dense_grads[5].astype(jnp.bfloat16), "expert", scatter_dimension=0, tiled=True
        ).astype(jnp.float32),
    )
    totals = (
        lax.psum(shares[0].astype(jnp.bfloat16), "group").astype(jnp.float32),
        lax.psum(shares[1].astype(jnp.bfloat16), "group").astype(jnp.float32),
        lax.psum(shares[2].astype(jnp.bfloat16), "group").astype(jnp.float32),
        lax.psum(shares[3].astype(jnp.bfloat16), "group").astype(jnp.float32),
        lax.psum(shares[4].astype(jnp.bfloat16), "group").astype(jnp.float32),
        lax.psum(shares[5].astype(jnp.bfloat16), "group").astype(jnp.float32),
    )
    grad_in, grad_out = (
        lax.psum_scatter(
            grad_inner[None].astype(jnp.bfloat16), "group", scatter_dimension=1, tiled=True
        ).astype(jnp.float32),
        lax.psum_scatter(
            grad_outer[None].astype(jnp.bfloat16), "group", scatter_dimension=1, tiled=True
        ).astype(jnp.float32),
    )
    return (
        block_out.astype(lowtype),
        grad_tokens,
        totals[0],
        totals[1],
        totals[2],
        totals[3],
        totals[4],
        totals[5],
        grad_in,
        grad_out,
    )


def solution(mesh):
    fast = (mesh.shape["group"], mesh.shape["expert"]) == (4, 8)
    step = on_device_fast if fast else on_device
    return jax.shard_map(
        step,
        mesh=mesh,
        in_specs=(
            P(("group", "expert"), None),
            P(),
            P(),
            P(),
            P(),
            P(),
            P(),
            P("expert", None, None),
            P("expert", None, None),
            P(("group", "expert"), None),
            P(("group", "expert"), None),
            P(("group", "expert")),
            P(("group", "expert"), None),
        ),
        out_specs=(
            P(("group", "expert"), None),
            P(("group", "expert"), None),
            P("expert"),
            P("expert", None),
            P("expert", None),
            P("expert", None),
            P("expert"),
            P("expert", None),
            P("expert", "group", None),
            P("expert", "group", None),
        ),
        check_vma=False,
    )
```

```python
import functools
import math

import jax
import jax.numpy as jnp
import numpy as np
from jax import lax
from jax.experimental import pallas as pl
from jax.experimental.pallas import tpu as pltpu
from jax.sharding import PartitionSpec as P

PIC = 256
EPS = 1e-6
LOW = jnp.bfloat16
FULL = jnp.float32
VM = pl.BlockSpec(memory_space=pltpu.VMEM)
SM = pl.BlockSpec(memory_space=pltpu.SMEM)
HBM = pl.BlockSpec(memory_space=pl.ANY)
MIB = 1 << 20
ATT_ROWS = 256
ATT_UNROLL = 2
MESH = pl.DeviceIdType.MESH
SECOND = 512.0
SLOTS = 256
ROW_TILE = 256
FF_TILE = 256
THIRDS = 3


def offset_bucket(offsets, buckets):
    half_count = buckets // 2
    exact_count = half_count // 2
    upper_half = (offsets > 0).astype(np.int64) * half_count
    distance = np.abs(offsets)
    scaled = (
        np.log(np.maximum(distance, 1) / float(exact_count))
        / np.log(128.0 / exact_count)
        * (half_count - exact_count)
    )
    larger = np.minimum(
        exact_count + np.floor(np.maximum(scaled, 0.0)).astype(np.int64), half_count - 1
    )
    return upper_half + np.where(distance < exact_count, distance, larger)


def near_onehot(buckets):
    bucket = offset_bucket(np.arange(512) - 256, buckets)
    return (np.arange(buckets)[:, None] == bucket[None, :]).astype(np.float32)


def dot_nn(a, b):
    return lax.dot_general(a, b, (((1,), (0,)), ((), ())), preferred_element_type=FULL)


def dot_nt(a, b):
    return lax.dot_general(a, b, (((1,), (1,)), ((), ())), preferred_element_type=FULL)


def dot_tn(a, b):
    return lax.dot_general(a, b, (((0,), (0,)), ((), ())), preferred_element_type=FULL)


def exact_nn(a, b):
    return lax.dot_general(
        a, b, (((1,), (0,)), ((), ())), precision=lax.Precision.HIGHEST, preferred_element_type=FULL
    )


def exact_nt(a, b):
    return lax.dot_general(
        a, b, (((1,), (1,)), ((), ())), precision=lax.Precision.HIGHEST, preferred_element_type=FULL
    )


def split3(x):
    hi = x.astype(LOW)
    rest = x - hi.astype(FULL)
    mid = rest.astype(LOW)
    low = (rest - mid.astype(FULL)).astype(LOW)
    return hi, mid, low


def half_mask(sub, value, shape=(1, 128)):
    lane = lax.broadcasted_iota(jnp.int32, shape, 1)
    keep = (lane < 64) if sub == 0 else (lane >= 64)
    return jnp.where(keep, value, 0.0).astype(FULL)


def attn_setup(span_ref, table_ref, onehot_ref, near_ref, mask_ref):
    seq_len = mask_ref.shape[0]
    heads = near_ref.shape[0]
    start = span_ref[0]
    qi = lax.broadcasted_iota(jnp.int32, (seq_len, seq_len), 0)
    kj = lax.broadcasted_iota(jnp.int32, (seq_len, seq_len), 1)
    q_in = (qi >= start) & (qi < start + PIC)
    k_in = (kj >= start) & (kj < start + PIC)
    mask_ref[...] = jnp.where((kj <= qi) | (q_in & k_in), 0.0, -1e30).astype(FULL)
    vecs = exact_nn(table_ref[...], onehot_ref[...])
    for h in range(heads):
        rows = jnp.broadcast_to(vecs[h : h + 1, :], (128, 512))
        rolled = pltpu.roll(rows, 0, 1, stride=1, stride_axis=0)
        near_ref[h] = rolled[:, 128:]


def bias_rows(block, blocks, near):
    far_neg = jnp.broadcast_to(near[127:128, 0:1], (128, 128))
    far_pos = jnp.broadcast_to(near[0:1, 383:384], (128, 128))
    pieces = []
    for other in range(blocks):
        d = other - block
        if d <= -2:
            pieces.append(far_neg)
        elif d >= 2:
            pieces.append(far_pos)
        else:
            pieces.append(near[:, (d + 1) * 128 : (d + 2) * 128])
    return jnp.concatenate(pieces, axis=1)


def attn_block(row0, count, qkv_ref, near_ref, mask_ref, prob_ref, mixed_ref):
    seq_len, width3 = qkv_ref.shape
    width = width3 // 3
    blocks = seq_len // 128
    rows = slice(row0, row0 + count)

    @pl.loop(0, width // 128, unroll=ATT_UNROLL)
    def _(pair):
        col = pl.multiple_of(pair * 128, 128)
        qp = qkv_ref[rows, pl.ds(col, 128)].astype(FULL)
        kp = qkv_ref[:, pl.ds(width + col, 128)]
        vp = qkv_ref[:, pl.ds(2 * width + col, 128)]
        qs = jnp.concatenate([qp * half_mask(sub, 0.125) for sub in range(2)], axis=0)
        scores = dot_nt(qs.astype(LOW), kp)
        probs = []
        for sub in range(2):
            h = 2 * pair + sub
            for part in range(count // 128):
                first = sub * count + part * 128
                here = slice(row0 + part * 128, row0 + part * 128 + 128)
                s = scores[first : first + 128]
                bias = bias_rows(row0 // 128 + part, blocks, near_ref[h])
                s = s + bias + mask_ref[here, :]
                top = jnp.max(s, axis=1, keepdims=True)
                e = jnp.exp(s - top)
                total = jnp.sum(e, axis=1, keepdims=True)
                p = (e * (1.0 / total)).astype(LOW)
                prob_ref[h, here, :] = p
                probs.append(p)
        outs = dot_nn(jnp.concatenate(probs, axis=0), vp)
        lane = lax.broadcasted_iota(jnp.int32, (count, 128), 1)
        mixed_ref[rows, pl.ds(col, 128)] = jnp.where(
            lane < 64, outs[:count], outs[count:]
        ).astype(LOW)


def choice_hits(routes, experts):
    who = lax.broadcasted_iota(jnp.int32, (experts, routes.shape[1]), 0)
    return [who == routes[k : k + 1, :] for k in range(2)]


def to_column(row, width):
    return jnp.transpose(jnp.broadcast_to(row, (8, width)))[:, 0:1]


def ranks_by_priority(hits, priority):
    tokens = priority.shape[1]
    prio = priority.astype(FULL)
    less = jnp.where(to_column(prio, tokens) < prio, 1.0, 0.0).astype(LOW)
    return [dot_nn(jnp.where(hit, 1.0, 0.0).astype(LOW), less) for hit in hits]


def attn_dispatch_kernel(
    tokens_ref,
    cot_ref,
    gain1_ref,
    wqkv_ref,
    wproj_ref,
    table_ref,
    onehot_ref,
    gain2_ref,
    wrouter_ref,
    routes_ref,
    prio_ref,
    span_ref,
    win_ref,
    qkv_out,
    prob_out,
    mixed_out,
    hidden_out,
    normed2_out,
    rows_out,
    cotrows_out,
    gatecol_out,
    token_ref,
    info_ref,
    resgt_out,
    act_out,
    slope_out,
    gout_out,
    qkv_ref,
    prob_ref,
    mixed_ref,
    hidden_ref,
    normed2_ref,
    meta_ref,
    gate_ref,
    meta_all,
    gate_all,
    gat_c,
    gat_n,
    acc_g,
    pos_ref,
    win_v,
    rows_ref,
    cotrows_ref,
    gatecol_ref,
    resgt_ref,
    send_sem,
    recv_sem,
    small_send,
    small_recv,
    out_sem,
    in_sem,
    tile_sem,
):
    g = lax.axis_index("group")
    me = lax.axis_index("expert")
    experts = wrouter_ref.shape[0]
    seq_len, width = tokens_ref.shape
    half = seq_len // 2

    def device(mask):
        return (g, lax.bitwise_xor(me, mask))

    barrier = pltpu.get_barrier_semaphore()
    for mask in range(1, experts):
        pl.semaphore_signal(barrier, inc=1, device_id=device(mask), device_id_type=MESH)
    pl.semaphore_wait(barrier, experts - 1)

    gats = (gat_c, gat_n)
    owns = (cot_ref, normed2_ref)

    def send(which, kind, chunk, held, target):
        rows = pl.ds(chunk * half, half)
        slot = lax.bitwise_xor(me, held)
        src = owns[which].at[rows, :] if held == 0 else gats[which].at[slot, rows, :]
        return pltpu.make_async_remote_copy(
            src_ref=src,
            dst_ref=gats[which].at[slot, rows, :],
            send_sem=send_sem.at[which, kind, chunk],
            recv_sem=recv_sem.at[which, held ^ target, chunk],
            device_id=device(target),
            device_id_type=MESH,
        )

    started = []

    def go(*args):
        send(*args).start()
        started.append(functools.partial(send, *args))

    def arrived(which, mask, chunk):
        rows = pl.ds(chunk * half, half)
        here = gats[which].at[lax.bitwise_xor(me, mask), rows, :]
        pltpu.make_async_remote_copy(
            src_ref=here,
            dst_ref=here,
            send_sem=send_sem.at[which, 0, chunk],
            recv_sem=recv_sem.at[which, mask, chunk],
            device_id=device(1),
            device_id_type=MESH,
        ).wait_recv()

    def own_out(which, chunk):
        go(which, 0, chunk, 0, 2)
        go(which, 1, chunk, 0, 4)
        go(which, 2, chunk, 0, 1)

    def own_out_all(which):
        for chunk in range(2):
            go(which, 0, chunk, 0, 2)
            go(which, 1, 1 - chunk, 0, 4)
        for chunk in range(2):
            go(which, 2, chunk, 0, 1)

    def relay(which, chunk, wait=True):
        if wait:
            arrived(which, 4 if chunk else 2, chunk)
        go(which, 3, chunk, 4 if chunk else 2, 2 if chunk else 4)

    def small_copy(src, dst, index, mask):
        return pltpu.make_async_remote_copy(
            src_ref=src,
            dst_ref=dst.at[me],
            send_sem=small_send.at[index, mask],
            recv_sem=small_recv.at[index, mask],
            device_id=device(mask),
            device_id_type=MESH,
        )

    def small(*args):
        for mask in range(1, experts):
            small_copy(*args, mask).start()
            started.append(functools.partial(small_copy, *args, mask))

    def small_arrived(dst, index):
        for mask in range(1, experts):
            here = dst.at[lax.bitwise_xor(me, mask)]
            pltpu.make_async_remote_copy(
                src_ref=here,
                dst_ref=here,
                send_sem=small_send.at[index, mask],
                recv_sem=small_recv.at[index, mask],
                device_id=device(1),
                device_id_type=MESH,
            ).wait_recv()

    own_out_all(0)

    def win_load():
        return pltpu.make_async_copy(win_ref, win_v, in_sem.at[2])

    win_load().start()

    hits = choice_hits(routes_ref[...], experts)
    ranks = ranks_by_priority(hits, prio_ref[...])
    meta = jnp.where(hits[0], ranks[0], jnp.where(hits[1], ranks[1] + SECOND, -1.0))
    meta_ref[...] = meta
    meta_all[me] = meta
    small(meta_ref, meta_all, 0)

    own_pairs = (
        (qkv_ref, qkv_out),
        (prob_ref, prob_out),
        (mixed_ref, mixed_out),
        (hidden_ref, hidden_out),
        (normed2_ref, normed2_out),
        (cotrows_ref, cotrows_out),
        (rows_ref, rows_out),
        (gatecol_ref, gatecol_out),
        (resgt_ref, resgt_out),
    )

    def own_copy(index):
        src, dst = own_pairs[index]
        return pltpu.make_async_copy(src, dst, out_sem.at[index])

    def attention(wqkv_v, wproj_v, near_ref, mask_ref):
        loads = [
            pltpu.make_async_copy(src, dst, in_sem.at[i])
            for i, (src, dst) in enumerate(((wqkv_ref, wqkv_v), (wproj_ref, wproj_v)))
        ]
        for copy in loads:
            copy.start()
        attn_setup(span_ref, table_ref, onehot_ref, near_ref, mask_ref)
        loads[0].wait()
        for row0 in range(0, seq_len, 128):
            rows = slice(row0, row0 + 128)
            x = tokens_ref[rows, :].astype(FULL)
            inv = lax.rsqrt(jnp.mean(x * x, axis=1, keepdims=True) + EPS)
            n1 = (x * inv * gain1_ref[...][None, :]).astype(LOW)
            qkv_ref[rows, :] = dot_nn(n1, wqkv_v[...]).astype(LOW)
        own_copy(0).start()
        loads[1].wait()
        for chunk in range(2):
            row0 = chunk * half
            rows = slice(row0, row0 + half)
            attn_block(row0, half, qkv_ref, near_ref, mask_ref, prob_ref, mixed_ref)
            hidden = tokens_ref[rows, :].astype(FULL) + dot_nn(mixed_ref[rows, :], wproj_v[...])
            hidden_ref[rows, :] = hidden
            inv = lax.rsqrt(jnp.mean(hidden * hidden, axis=1, keepdims=True) + EPS)
            n2 = (hidden * inv * gain2_ref[...][None, :]).astype(LOW)
            normed2_ref[rows, :] = n2
            own_out(1, chunk)

    pl.run_scoped(
        attention,
        pltpu.VMEM(wqkv_ref.shape, LOW),
        pltpu.VMEM(wproj_ref.shape, LOW),
        pltpu.VMEM((table_ref.shape[0], 128, 384), FULL),
        pltpu.VMEM((seq_len, seq_len), FULL),
    )
    for index in range(1, 5):
        own_copy(index).start()

    logits = dot_nt(wrouter_ref[...], normed2_ref[...])
    unnormed = jnp.exp(logits - jnp.max(logits, axis=0, keepdims=True))
    probabilities = unnormed / jnp.sum(unnormed, axis=0, keepdims=True)
    picked = [jnp.sum(jnp.where(hit, probabilities, 0.0), axis=0, keepdims=True) for hit in hits]
    both = picked[0] + picked[1]
    gates = [p / both for p in picked]
    gate = jnp.where(hits[0], gates[0], jnp.where(hits[1], gates[1], 0.0))
    gate_ref[...] = gate
    gate_all[me] = gate
    small(gate_ref, gate_all, 1)

    first_count = jnp.sum(jnp.where(hits[0], 1.0, 0.0), axis=1, keepdims=True)
    who = lax.broadcasted_iota(jnp.int32, hits[0].shape, 0).astype(FULL)
    slots = [
        jnp.sum(jnp.where(hits[0], ranks[0] + who * SLOTS, 0.0), axis=0, keepdims=True),
        jnp.sum(
            jnp.where(hits[1], ranks[1] + first_count + who * SLOTS, 0.0), axis=0, keepdims=True
        ),
    ]
    routes_f = routes_ref[...].astype(FULL)
    token_rows = jnp.concatenate(slots + gates + [routes_f[0:1], routes_f[1:2]] + slots, axis=0)
    token_ref[...] = jnp.transpose(token_rows)

    small_arrived(meta_all, 0)
    value = meta_all[:, me, :]
    is_first = (value >= 0.0) & (value < SECOND)
    is_second = value >= SECOND
    counts = [
        jnp.sum(jnp.where(hit, 1.0, 0.0), axis=1, keepdims=True) for hit in (is_first, is_second)
    ]
    row = lax.broadcasted_iota(jnp.int32, (experts, 128), 0)
    lane = lax.broadcasted_iota(jnp.int32, (experts, 128), 1)
    count_mat = jnp.where(lane == 0, counts[0], jnp.where(lane == 1, counts[1], 0.0))
    before = jnp.zeros((experts, 128), FULL)
    for s in range(experts):
        before = before + jnp.where(row > s, count_mat[s : s + 1, :], 0.0)
    first_total = jnp.sum(counts[0], axis=0, keepdims=True)
    base = [before[:, 0:1], before[:, 1:2] + first_total]
    pos_ref[...] = jnp.where(
        is_first, value + base[0], jnp.where(is_second, value - SECOND + base[1], -1.0)
    )
    info_ref[...] = jnp.where(
        lane == 0,
        counts[0],
        jnp.where(lane == 1, counts[1], jnp.where(lane == 2, base[0], base[1])),
    )

    accs = (cotrows_ref, rows_ref)

    def compact(which, mask):
        slot = lax.bitwise_xor(me, mask)
        acc = accs[which]

        @pl.loop(0, acc.shape[0] // ROW_TILE)
        def _(tile):
            row0 = pl.multiple_of(tile * ROW_TILE, ROW_TILE)
            here = pl.ds(row0, ROW_TILE)
            place = pos_ref[pl.ds(slot, 1), :] - row0.astype(FULL)
            at = lax.broadcasted_iota(jnp.int32, (ROW_TILE, seq_len), 0).astype(FULL)
            hit = at == place
            pick = jnp.where(hit, 1.0, 0.0).astype(LOW)
            data = owns[which][...] if mask == 0 else gats[which][slot]
            got = dot_nn(pick, data).astype(LOW)
            if mask:
                got = got + acc[here, :]
            acc[here, :] = got
            if which == 1:
                gates_here = jnp.where(hit, gate_all[slot, pl.ds(me, 1), :], 0.0)
                part = gates_here[:, 0:128]
                for i in range(1, seq_len // 128):
                    part = part + gates_here[:, i * 128 : i * 128 + 128]
                if mask:
                    part = part + acc_g[here, :]
                acc_g[here, :] = part

    def forward(which, mask, waits=(0, 1)):
        for chunk in waits:
            arrived(which, mask, chunk)
        for chunk in range(2):
            go(which, 3 + mask // 2, chunk, mask, 1)

    def take(which, mask):
        for chunk in range(2):
            arrived(which, mask, chunk)
        compact(which, mask)

    relay(0, 0)
    relay(0, 1)
    forward(0, 2, (1,))
    forward(0, 4, (0,))
    compact(0, 0)
    take(0, 1)
    compact(0, 2)
    compact(0, 4)
    take(0, 3)
    take(0, 5)
    relay(1, 0)
    relay(1, 1)
    small_arrived(gate_all, 1)
    compact(1, 0)
    take(1, 1)
    forward(1, 2, (1,))
    compact(1, 2)
    forward(1, 4, (0,))
    compact(1, 4)
    forward(0, 6)
    compact(0, 6)
    take(0, 7)
    own_copy(5).start()
    take(1, 3)
    take(1, 5)
    forward(1, 6)
    compact(1, 6)
    take(1, 7)
    own_copy(6).start()

    capacity = rows_ref.shape[0]
    tiles = gout_out.shape[0]

    def experts_first(act_v, slope_v, gout_v):
        def tile_copies(tile):
            return [
                pltpu.make_async_copy(src.at[tile], dst, tile_sem.at[kind, tile])
                for kind, (src, dst) in enumerate(
                    (
                        (act_v, act_out.at[tile]),
                        (slope_v, slope_out.at[tile]),
                        (gout_v, gout_out.at[tile]),
                    )
                )
            ]

        win_load().wait()

        def scaled(row0):
            rows = pl.ds(pl.multiple_of(row0, ROW_TILE), ROW_TILE)
            gate_col = jnp.sum(acc_g[rows, :], axis=1, keepdims=True)
            gatecol_ref[rows, :] = jnp.broadcast_to(gate_col, (ROW_TILE, 128))
            resg = gate_col * cotrows_ref[rows, :].astype(FULL)
            resgt_ref[:, rows] = jnp.transpose(resg.astype(LOW))

        parts = capacity // ROW_TILE

        @pl.loop(0, tiles)
        def _(tile):
            cols = pl.ds(pl.multiple_of(tile * THIRDS * FF_TILE, FF_TILE), FF_TILE)
            for row0 in range(0, capacity, ROW_TILE):
                here = slice(row0, row0 + ROW_TILE)
                act, slope = gelu_and_slope(dot_nn(rows_ref[here, :], win_v[:, cols]))
                act_v[tile, here, :] = act.astype(LOW)
                slope_v[tile, here, :] = slope.astype(LOW)
            scaled(tile * ROW_TILE)
            for copy in tile_copies(tile)[:2]:
                copy.start()

        for part in range(tiles, parts):
            scaled(part * ROW_TILE)
        own_copy(7).start()
        own_copy(8).start()

        @pl.loop(0, tiles)
        def _(tile):
            gout_v[tile] = dot_nn(resgt_ref[...], act_v[tile]).astype(LOW)
            tile_copies(tile)[2].start()

        @pl.loop(0, tiles)
        def _(tile):
            for copy in tile_copies(tile):
                copy.wait()

    pl.run_scoped(
        experts_first,
        pltpu.VMEM((tiles, capacity, FF_TILE), LOW),
        pltpu.VMEM((tiles, capacity, FF_TILE), LOW),
        pltpu.VMEM((tiles, width, FF_TILE), LOW),
    )

    for index in range(9):
        own_copy(index).wait()
    for copy in started:
        copy().wait_send()


def attn_dispatch(
    tokens, cot, gain1, wqkv, wproj, table, gain2, wrouter, routes, priority, span, w_in, groups
):
    seq_len, width = tokens.shape
    buckets, heads = table.shape
    experts = wrouter.shape[1]
    capacity = 5 * seq_len // 2
    ff = w_in.shape[1]
    sds = jax.ShapeDtypeStruct
    dma = pltpu.SemaphoreType.DMA
    return pl.pallas_call(
        attn_dispatch_kernel,
        out_shape=(
            sds((seq_len, 3 * width), LOW),
            sds((heads, seq_len, seq_len), LOW),
            sds((seq_len, width), LOW),
            sds((seq_len, width), FULL),
            sds((seq_len, width), LOW),
            sds((capacity, width), LOW),
            sds((capacity, width), LOW),
            sds((capacity, 128), FULL),
            sds((seq_len, 8), FULL),
            sds((experts, 128), FULL),
            sds((width, capacity), LOW),
            sds((groups, capacity, FF_TILE), LOW),
            sds((groups, capacity, FF_TILE), LOW),
            sds((groups, width, FF_TILE), LOW),
        ),
        in_specs=[VM] * 3 + [HBM] * 2 + [VM] * 6 + [SM, HBM],
        out_specs=[HBM] * 8 + [VM] * 2 + [HBM] * 4,
        scratch_shapes=[
            pltpu.VMEM((seq_len, 3 * width), LOW),
            pltpu.VMEM((heads, seq_len, seq_len), LOW),
            pltpu.VMEM((seq_len, width), LOW),
            pltpu.VMEM((seq_len, width), FULL),
            pltpu.VMEM((seq_len, width), LOW),
            pltpu.VMEM((experts, seq_len), FULL),
            pltpu.VMEM((experts, seq_len), FULL),
            pltpu.VMEM((experts, experts, seq_len), FULL),
            pltpu.VMEM((experts, experts, seq_len), FULL),
            pltpu.VMEM((experts, seq_len, width), LOW),
            pltpu.VMEM((experts, seq_len, width), LOW),
            pltpu.VMEM((capacity, 128), FULL),
            pltpu.VMEM((experts, seq_len), FULL),
            pltpu.VMEM(w_in.shape, LOW),
            pltpu.VMEM((capacity, width), LOW),
            pltpu.VMEM((capacity, width), LOW),
            pltpu.VMEM((capacity, 128), FULL),
            pltpu.VMEM((width, capacity), LOW),
            dma((2, 7, 2)),
            dma((2, 8, 2)),
            dma((2, 8)),
            dma((2, 8)),
            dma((9,)),
            dma((3,)),
            dma((3, groups)),
        ],
        compiler_params=pltpu.CompilerParams(
            vmem_limit_bytes=60 * MIB, collective_id=0, has_side_effects=True
        ),
    )(
        tokens,
        cot,
        gain1,
        wqkv,
        wproj,
        table.T,
        jnp.asarray(near_onehot(buckets)),
        gain2,
        wrouter.T,
        routes.T,
        priority,
        span,
        w_in,
    )


def gelu_and_slope(x):
    c = math.sqrt(2.0 / math.pi)
    square = x * x
    s = 0.5 * jnp.tanh(x * (c + (c * 0.044715) * square)) + 0.5
    act = x * s
    return act, s + act * (1.0 - s) * (2.0 * c + (6.0 * c * 0.044715) * square)


def pack_rows(source, info_ref, data, slots):
    info = info_ref[pl.ds(source, 1), :]
    slot = lax.broadcasted_iota(jnp.int32, (slots, 1), 0).astype(FULL)
    n0, n1, b0, b1 = [info[:, i : i + 1] for i in range(4)]
    place = jnp.where(slot < n0, b0 + slot, jnp.where(slot < n0 + n1, b1 + slot - n0, -1.0))
    at = lax.broadcasted_iota(jnp.int32, (slots, data.shape[0]), 1).astype(FULL)
    pick = jnp.where(at == place, 1.0, 0.0).astype(LOW)
    return dot_nn(pick, data[...]).astype(LOW)


def expert_kernel(
    cot_ref,
    gate_ref,
    rows_ref,
    info_ref,
    resgt_hbm,
    act_ref,
    slope_ref,
    outer_ref,
    wout_ref,
    win_ref,
    recv_ref,
    packed_ref,
    gin_ref,
    gout_ref,
    up_in,
    down_in,
    act_v,
    slope_v,
    wout_v,
    win_v,
    ig_v,
    acc_ref,
    gg_ref,
    data_ref,
    send_ref,
    turned,
    gin_v,
    outer_v,
    fold_ref,
    took_ref,
    total_ref,
    packed_v,
    gout_v,
    load_sem,
    act_sem,
    slope_sem,
    outer_sem,
    gin_sem,
    own_sem,
    took_sem,
    total_sem,
    send_sem,
    recv_sem,
    fold_sems,
):
    g = lax.axis_index("group")
    me = lax.axis_index("expert")
    experts, slots, wide = send_ref.shape
    tiles, capacity, tile_width = act_v.shape
    width = cot_ref.shape[1]
    groups = act_ref.shape[0]
    thirds = tiles // groups
    last = groups - 1
    copies = last * thirds
    arrivals = (up_in, down_in)

    def device(mask):
        return (g, lax.bitwise_xor(me, mask))

    def load(index):
        src, dst = ((wout_ref, wout_v), (win_ref, win_v), (resgt_hbm, turned))[index]
        return pltpu.make_async_copy(src, dst, load_sem.at[index])

    def act_load(tile):
        return pltpu.make_async_copy(act_ref.at[tile], act_v.at[tile], act_sem.at[tile])

    def slope_load(tile):
        slot = lax.rem(tile, 2)
        return pltpu.make_async_copy(slope_ref.at[tile], slope_v.at[slot], slope_sem.at[slot])

    def outer_load(tile):
        return pltpu.make_async_copy(outer_ref.at[tile], outer_v.at[tile], outer_sem.at[tile])

    for tile in range(groups):
        outer_load(tile).start()
    load(0).start()
    slope_load(0).start()
    act_load(0).start()
    load(1).start()
    for tile in range(1, groups):
        act_load(tile).start()
    load(2).start()
    barrier = pltpu.get_barrier_semaphore()
    for mask in range(1, experts):
        pl.semaphore_signal(barrier, inc=1, device_id=device(mask), device_id_type=MESH)
    for step in range(1, groups):
        pl.semaphore_signal(
            barrier, inc=1, device_id=(lax.rem(g + step, groups), me), device_id_type=MESH
        )
    pl.semaphore_wait(barrier, experts - 1 + groups - 1)
    for tile in range(groups):
        outer_load(tile).wait()

    def fold_tile(way, k):
        return (k % last if way else last - k % last), k // last

    def fold_copy(way, k, src):
        shard_at, third = fold_tile(way, k)
        there = arrivals[way].at[shard_at, third]
        return pltpu.make_async_remote_copy(
            src_ref=there if src is None else src,
            dst_ref=there,
            send_sem=fold_sems.at[0, way, k],
            recv_sem=fold_sems.at[1, way, k],
            device_id=(lax.rem(g + (last if way else 1), groups), me),
            device_id_type=MESH,
        )

    def take_tile(way, src):
        return pltpu.make_async_copy(src, took_ref.at[way], took_sem.at[way])

    def fold_source(*which):
        for k in which:
            for way in range(2):
                shard_at, third = fold_tile(way, k)

                @pl.when(g == way * last)
                def _():
                    fold_copy(way, k, outer_v.at[third * groups + shard_at]).start()

    def passed(way, here):
        return [
            k
            for k in range(copies)
            if ((fold_tile(way, k)[0] < here) if way else (fold_tile(way, k)[0] > here))
        ]

    def fold_role(hop, k, act):
        for way in range(2):
            here = last - hop if way else hop
            order = passed(way, here)
            if k in order:
                pl.when(g == here)(functools.partial(act, way, k, order, order.index(k)))

    def fold_fetch(hop, k):
        def act(way, k, order, nth):
            shard_at, third = fold_tile(way, k)
            fold_copy(way, k, None).wait_recv()
            take_tile(way, arrivals[way].at[shard_at, third]).start()

        fold_role(hop, k, act)

    def fold_push(hop, k):
        def act(way, k, order, nth):
            shard_at, third = fold_tile(way, k)
            if nth >= 2:
                fold_copy(way, order[nth - 2], None).wait_send()
            take_tile(way, arrivals[way].at[shard_at, third]).wait()
            own = outer_v[third * groups + shard_at].astype(FULL)
            fold_ref[way, nth % 2] = (own + took_ref[way].astype(FULL)).astype(LOW)
            fold_copy(way, k, fold_ref.at[way, nth % 2]).start()

        fold_role(hop, k, act)

    def fold_final(third):
        total_ref[...] = outer_v[third * groups + g].astype(FULL)
        for way, (some, at) in enumerate(((g > 0, last - g), (g < last, g))):

            @pl.when(some)
            def _():
                here = arrivals[way].at[g, third]
                k = third * last + at
                pltpu.make_async_remote_copy(
                    src_ref=here,
                    dst_ref=here,
                    send_sem=fold_sems.at[0, way, k],
                    recv_sem=fold_sems.at[1, way, k],
                    device_id=(lax.rem(g + 1, groups), me),
                    device_id_type=MESH,
                ).wait_recv()
                take_tile(way, here).start()
                take_tile(way, here).wait()
                total_ref[...] += took_ref[way].astype(FULL)

        gout_v[third * tile_width : (third + 1) * tile_width, :] = jnp.transpose(total_ref[...])
        gout_copy(third).start()

    def gout_copy(third):
        here = pl.ds(third * tile_width, tile_width)
        return pltpu.make_async_copy(gout_v.at[here, :], gout_ref.at[here, :], total_sem.at[third])

    def fold_sent():
        for way in range(2):
            for k in range(copies):

                @pl.when(g == way * last)
                def _():
                    fold_copy(way, k, None).wait_send()

            for hop in range(1, last):
                here = last - hop if way else hop
                for k in passed(way, here)[-2:]:

                    @pl.when(g == here)
                    def _():
                        fold_copy(way, k, None).wait_send()

    fold_source(*range(last))
    acc_ref[...] = jnp.zeros_like(acc_ref)
    gg_ref[...] = jnp.zeros_like(gg_ref)
    for index in range(2):
        load(index).wait()

    def span(tile):
        at = lax.rem(tile, groups) * thirds + lax.div(tile, groups)
        return pl.ds(pl.multiple_of(at * tile_width, tile_width), tile_width)

    def back_tile(tile, slope_slot):
        for row0 in range(0, capacity, ROW_TILE):
            here = slice(row0, row0 + ROW_TILE)
            back = dot_nt(cot_ref[here, :], wout_v[span(tile), :])
            part = act_v[tile, here, :].astype(FULL) * back
            gg_ref[here, :] += part[:, 0:128] + part[:, 128:256]
            slope = slope_v[slope_slot, here, :].astype(FULL)
            ig_v[tile, here, :] = (slope * (gate_ref[here, 0:1] * back)).astype(LOW)
            acc_ref[here, :] += dot_nt(ig_v[tile, here, :], win_v[:, span(tile)])

    @pl.loop(0, groups)
    def _(tile):
        slope_load(tile).wait()
        act_load(tile).wait()

        @pl.when(tile + 1 < groups)
        def _():
            slope_load(tile + 1).start()

        back_tile(tile, lax.rem(tile, 2))

    load(2).wait()
    fold_fetch(1, 0)

    def own_tiles(first, count):
        @pl.loop(first, first + count)
        def _(tile):
            for row0 in range(0, capacity, ROW_TILE):
                here = slice(row0, row0 + ROW_TILE)
                act, slope = gelu_and_slope(dot_nn(rows_ref[here, :], win_v[:, span(tile)]))
                act_v[tile, here, :] = act.astype(LOW)
                slope_v[0, here, :] = slope.astype(LOW)
            outer_v[tile] = dot_nn(turned[...], act_v[tile]).astype(LOW)
            back_tile(tile, 0)

    own_tiles(groups, 2)
    fold_push(1, 0)
    own_tiles(groups + 2, groups - 2)
    fold_source(*range(last, 2 * last))
    fold_fetch(1, 1)
    own_tiles(2 * groups, 2)
    fold_push(1, 1)
    fold_fetch(1, 2)
    fold_fetch(2, 0)
    own_tiles(2 * groups + 2, groups - 2)
    fold_source(*range(2 * last, 3 * last))
    fold_push(1, 2)
    fold_push(2, 0)

    data_ref[:, :width] = acc_ref[...].astype(LOW)
    gg = jnp.sum(gg_ref[...], axis=1, keepdims=True)
    hi, mid, low = [t.astype(FULL) for t in split3(gg)]
    lane = lax.broadcasted_iota(jnp.int32, (capacity, 128), 1)
    data_ref[:, width:] = jnp.where(
        lane == 0, hi, jnp.where(lane == 1, mid, jnp.where(lane == 2, low, 0.0))
    ).astype(LOW)

    def exchange(mask):
        return pltpu.make_async_remote_copy(
            src_ref=send_ref.at[lax.bitwise_xor(me, mask)],
            dst_ref=recv_ref.at[me],
            send_sem=send_sem.at[mask],
            recv_sem=recv_sem.at[mask],
            device_id=device(mask),
            device_id_type=MESH,
        )

    for mask in (6, 7, 2, 4, 3, 5, 1):
        other = lax.bitwise_xor(me, mask)
        send_ref[other] = pack_rows(other, info_ref, data_ref, slots)
        exchange(mask).start()
        if mask == 4:
            fold_fetch(1, 3)
    send_ref[me] = pack_rows(me, info_ref, data_ref, slots)
    own_rows = pltpu.make_async_copy(send_ref.at[me], recv_ref.at[me], own_sem)
    own_rows.start()
    fold_push(1, 3)
    fold_fetch(1, 4)

    turned[...] = jnp.transpose(rows_ref[...])

    def gin_copy(tile):
        slot = lax.rem(tile, 2)
        cols = pl.ds(pl.multiple_of(lax.div(tile, groups) * tile_width, tile_width), tile_width)
        return pltpu.make_async_copy(
            gin_v.at[slot], gin_ref.at[:, lax.rem(tile, groups), :, cols], gin_sem.at[slot]
        )

    def gin_tiles(first, count):
        @pl.loop(first, first + count)
        def _(tile):
            @pl.when(tile >= 2)
            def _():
                gin_copy(tile).wait()

            got = dot_nn(turned[...], ig_v[tile]).astype(LOW)
            gin_v[lax.rem(tile, 2)] = got.reshape(gin_v.shape[1:])
            gin_copy(tile).start()

    gin_tiles(0, tiles // 2)
    fold_push(1, 4)
    gin_tiles(tiles // 2, tiles // 2)
    fold_fetch(1, 5)
    fold_fetch(2, 3)

    acc_ref[...] = jnp.zeros_like(acc_ref)

    def result_tiles(first, count):
        @pl.loop(first, first + count)
        def _(tile):
            for row0 in range(0, capacity, ROW_TILE):
                here = slice(row0, row0 + ROW_TILE)
                acc_ref[here, :] += dot_nn(act_v[tile, here, :], wout_v[span(tile), :])

    result_tiles(0, tiles // 2)
    fold_push(1, 5)
    fold_push(2, 3)
    result_tiles(tiles // 2, tiles // 2)
    fold_fetch(1, 6)
    gin_copy(0).wait()
    gin_copy(1).wait()
    data_ref[:, :width] = acc_ref[...].astype(LOW)

    @pl.loop(0, experts)
    def _(source):
        packed_v[source] = pack_rows(source, info_ref, data_ref.at[:, 0:width], slots)

    packed_copy = pltpu.make_async_copy(packed_v, packed_ref, total_sem.at[thirds])
    packed_copy.start()
    fold_push(1, 6)
    fold_final(0)
    fold_fetch(1, 7)
    fold_push(1, 7)
    fold_fetch(2, 6)
    fold_push(2, 6)
    fold_final(1)
    fold_fetch(1, 8)
    fold_push(1, 8)
    fold_final(2)
    packed_copy.wait()
    for third in range(thirds):
        gout_copy(third).wait()
    own_rows.wait()
    for mask in range(1, experts):
        exchange(mask).wait()
    fold_sent()


def expert_call(cot_rows, gate_col, rows, info, resg_t, act, slope, outer, w_out, w_in):
    capacity, width = cot_rows.shape
    groups, _, tile_width = act.shape
    ff = w_in.shape[1]
    tiles = ff // tile_width
    experts = info.shape[0]
    sds = jax.ShapeDtypeStruct
    dma = pltpu.SemaphoreType.DMA
    arrival = sds((groups, tiles // groups, width, tile_width), LOW)
    outs = pl.pallas_call(
        expert_kernel,
        out_shape=(
            sds((experts, SLOTS, width + 128), LOW),
            sds((experts, SLOTS, width), LOW),
            sds((groups, groups, width // groups, ff // groups), LOW),
            sds((ff // groups, width), FULL),
            arrival,
            arrival,
        ),
        in_specs=[VM] * 4 + [HBM] * 6,
        out_specs=[HBM] * 6,
        scratch_shapes=[
            pltpu.VMEM((tiles, capacity, tile_width), LOW),
            pltpu.VMEM((2, capacity, tile_width), LOW),
            pltpu.VMEM(w_out.shape, LOW),
            pltpu.VMEM(w_in.shape, LOW),
            pltpu.VMEM((tiles, capacity, tile_width), LOW),
            pltpu.VMEM((capacity, width), FULL),
            pltpu.VMEM((capacity, 128), FULL),
            pltpu.VMEM((capacity, width + 128), LOW),
            pltpu.VMEM((experts, SLOTS, width + 128), LOW),
            pltpu.VMEM((width, capacity), LOW),
            pltpu.VMEM((2, groups, width // groups, tile_width), LOW),
            pltpu.VMEM((tiles, width, tile_width), LOW),
            pltpu.VMEM((2, 2, width, tile_width), LOW),
            pltpu.VMEM((2, width, tile_width), LOW),
            pltpu.VMEM((width, tile_width), FULL),
            pltpu.VMEM((experts, SLOTS, width), LOW),
            pltpu.VMEM((ff // groups, width), FULL),
            dma((3,)),
            dma((groups,)),
            dma((2,)),
            dma((groups,)),
            dma((2,)),
            dma,
            dma((2,)),
            dma((tiles // groups + 1,)),
            dma((experts,)),
            dma((experts,)),
            dma((2, 2, (groups - 1) * (tiles // groups))),
        ],
        compiler_params=pltpu.CompilerParams(
            vmem_limit_bytes=62 * MIB, collective_id=2, has_side_effects=True
        ),
        cost_estimate=pl.CostEstimate(
            flops=12 * capacity * width * ff, bytes_accessed=50 * MIB, transcendentals=0
        ),
    )(cot_rows, gate_col, rows, info, resg_t, act, slope, outer, w_out, w_in)
    return outs[:4]


def attn_back_kernel(
    tokens_ref,
    cot_ref,
    hidden_ref,
    normed2_ref,
    mixed_ref,
    qkv_hbm,
    prob_hbm,
    recv_ref,
    token_ref,
    gain1_ref,
    gain2_ref,
    wqkv_hbm,
    wproj_ref,
    wrouter_ref,
    onehot_ref,
    result_ref,
    gin_ref,
    block_ref,
    gtok_ref,
    dense_out,
    small_out,
    gin_out,
    up_in,
    down_in,
    hgrad_ref,
    mgrad_ref,
    mgrad_t,
    normed_t,
    q_t,
    ds_ref,
    diag_ref,
    dk_t,
    dv_t,
    dqkv_ref,
    part_ref,
    pair_in,
    chip_ref,
    plane_in,
    plane_ref,
    group_in,
    small_ref,
    small_in,
    small_plane,
    small_group,
    qkv_ref,
    prob_ref,
    wqkv_ref,
    back_ref,
    fold_ref,
    took_ref,
    total_ref,
    fold_sems,
    took_sems,
    total_sems,
    load_sems,
    back_sems,
    pair_sems,
    plane_sems,
    group_sems,
    final_sems,
    small_sems,
    smallz_sems,
):
    seq_len, width = tokens_ref.shape
    experts = wrouter_ref.shape[0]
    chunks = part_ref.shape[0]
    groups = group_in.shape[1]
    tile = 128
    g = lax.axis_index("group")
    me = lax.axis_index("expert")
    parity = lax.rem(me, 2)
    mine = lax.div(me, 2)
    summer = [groups // 2 - 1 + c % 2 for c in range(chunks)]

    def device(mask):
        return (g, lax.bitwise_xor(me, mask))

    def load(index):
        src, dst = ((qkv_hbm, qkv_ref), (prob_hbm, prob_ref), (wqkv_hbm, wqkv_ref))[index]
        return pltpu.make_async_copy(src, dst, load_sems.at[index])

    own_result = pltpu.make_async_copy(result_ref.at[me], back_ref.at[me], load_sems.at[3])
    for index in range(3):
        load(index).start()
    own_result.start()
    barrier = pltpu.get_barrier_semaphore()
    for mask in range(1, experts):
        pl.semaphore_signal(barrier, inc=1, device_id=device(mask), device_id_type=MESH)
    for step in range(1, groups):
        pl.semaphore_signal(
            barrier, inc=1, device_id=(lax.rem(g + step, groups), me), device_id_type=MESH
        )
    pl.semaphore_wait(barrier, experts - 1 + groups - 1)

    def remote(src, dst, sems, at, where):
        return pltpu.make_async_remote_copy(
            src_ref=src,
            dst_ref=dst,
            send_sem=sems.at[(0, *at)],
            recv_sem=sems.at[(1, *at)],
            device_id=where,
            device_id_type=MESH,
        )

    started = []

    def go(copy):
        copy.start()
        started.append(copy)

    def result_copy(mask):
        other = lax.bitwise_xor(me, mask)
        return remote(result_ref.at[other], back_ref.at[me], back_sems, (mask,), device(mask))

    for mask in (2, 4, 3, 5, 1):
        result_copy(mask).start()

    def pair_send(c):
        for chip in range(experts // 2):
            other = 2 * chip + 1 - parity
            go(remote(part_ref.at[c, other], pair_in.at[c, chip], pair_sems, (c, chip), device(1)))

    def plane_send(c):
        for chip in range(experts // 2):
            remote(
                part_ref.at[c, 0], pair_in.at[c, chip], pair_sems, (c, chip), device(1)
            ).wait_recv()
            total = part_ref[c, 2 * chip + parity].astype(FULL) + pair_in[c, chip].astype(FULL)
            chip_ref[c, chip] = total.astype(LOW)
        for other in range(1, experts // 2):
            go(
                remote(
                    chip_ref.at[c, lax.bitwise_xor(mine, other)],
                    plane_in.at[c, other - 1],
                    plane_sems,
                    (c, other - 1),
                    device(2 * other),
                )
            )

    def group_send(c):
        total = chip_ref[c, mine].astype(FULL)
        for other in range(1, experts // 2):
            remote(
                chip_ref.at[c, 0],
                plane_in.at[c, other - 1],
                plane_sems,
                (c, other - 1),
                device(2 * other),
            ).wait_recv()
            total = total + plane_in[c, other - 1].astype(FULL)
        plane_ref[c] = total.astype(LOW)

        @pl.when(g != summer[c])
        def _():
            remote(
                plane_ref.at[c], group_in.at[c, g], group_sems, (c, g), (jnp.int32(summer[c]), me)
            ).start()

    def final_send(c):
        @pl.when(g == summer[c])
        def _():
            total = plane_ref[c].astype(FULL)
            for step in range(1, groups):
                src = lax.rem(g + step, groups)
                remote(
                    plane_ref.at[c], group_in.at[c, src], group_sems, (c, src), (src, me)
                ).wait_recv()
                total = total + group_in[c, src].astype(FULL)
            dense_out[c] = total.astype(LOW)
            for step in range(1, groups):
                where = (lax.rem(g + step, groups), me)
                remote(dense_out.at[c], dense_out.at[c], final_sems, (c, step - 1), where).start()

    def finish(c):
        where = (lax.rem(g + 1, groups), me)
        for step in range(1, groups):
            copy = remote(dense_out.at[c], dense_out.at[c], final_sems, (c, step - 1), where)

            @pl.when(g == summer[c])
            def _():
                copy.wait_send()

            @pl.when(lax.rem(summer[c] + step, groups) == g)
            def _():
                copy.wait_recv()

        @pl.when(g != summer[c])
        def _():
            remote(plane_ref.at[c], group_in.at[c, g], group_sems, (c, g), where).wait_send()

    parts = gin_ref.shape[1]
    last = groups - 1
    copies = last * parts
    arrivals = (up_in, down_in)

    def fold_tile(way, k):
        return (k // parts if way else last - k // parts), k % parts

    def fold_copy(way, k, src):
        shard_at, tile_at = fold_tile(way, k)
        there = arrivals[way].at[shard_at, tile_at]
        step = last if way else 1
        where = (lax.rem(g + step, groups), me)
        return pltpu.make_async_remote_copy(
            src_ref=there if src is None else src,
            dst_ref=there,
            send_sem=fold_sems.at[0, way, k],
            recv_sem=fold_sems.at[1, way, k],
            device_id=where,
            device_id_type=MESH,
        )

    def take_tile(way, which, src):
        return pltpu.make_async_copy(src, took_ref.at[way, which], took_sems.at[way, which])

    def fold_source(k):
        for way in range(2):

            @pl.when(g == way * last)
            def _():
                fold_copy(way, k, gin_ref.at[fold_tile(way, k)]).start()

    def fold_place(way, k):
        main = (g == 1) if way == 0 else (g == last - 1)
        return jnp.where(main, k, (last - 1) * parts + k)

    def fold_role(hop, k, act):
        for way in range(2):
            shard_at, tile_at = fold_tile(way, k)
            here = last - hop if way else hop
            if (shard_at < here) if way else (shard_at > here):
                pl.when(g == here)(functools.partial(act, way, k, shard_at, tile_at))

    def fold_fetch(hop, k):
        def act(way, k, shard_at, tile_at):
            take_tile(way, 0, gin_ref.at[shard_at, tile_at]).start()
            fold_copy(way, k, None).wait_recv()
            take_tile(way, 1, arrivals[way].at[shard_at, tile_at]).start()

        fold_role(hop, k, act)

    def fold_push(hop, k):
        def act(way, k, shard_at, tile_at):
            take_tile(way, 0, gin_ref.at[shard_at, tile_at]).wait()
            take_tile(way, 1, arrivals[way].at[shard_at, tile_at]).wait()
            place = fold_place(way, k)
            total = took_ref[way, 0].astype(FULL) + took_ref[way, 1].astype(FULL)
            fold_ref[place] = total.astype(LOW)
            fold_copy(way, k, fold_ref.at[place]).start()

        fold_role(hop, k, act)

    def fold_final(tile_at):
        own = take_tile(0, 0, gin_ref.at[g, tile_at])
        own.start()
        cases = ((g > 0, up_in, (last - g) * parts + tile_at), (g < last, down_in, g * parts + tile_at))
        for way, (some, arrival, k) in enumerate(cases):

            @pl.when(some)
            def _():
                here = arrival.at[g, tile_at]
                pltpu.make_async_remote_copy(
                    src_ref=here,
                    dst_ref=here,
                    send_sem=fold_sems.at[0, way, k],
                    recv_sem=fold_sems.at[1, way, k],
                    device_id=(lax.rem(g + 1, groups), me),
                    device_id_type=MESH,
                ).wait_recv()
                take_tile(way, 1, here).start()

        own.wait()
        if tile_at >= 2:
            final_copy(tile_at - 2).wait()
        total_ref[tile_at % 2] = took_ref[0, 0].astype(FULL)
        for way, (some, arrival, k) in enumerate(cases):

            @pl.when(some)
            def _():
                take_tile(way, 1, arrival.at[g, tile_at]).wait()
                total_ref[tile_at % 2] += took_ref[way, 1].astype(FULL)

        final_copy(tile_at).start()

    def final_copy(tile_at):
        cols = pl.ds(tile_at * total_ref.shape[2], total_ref.shape[2])
        return pltpu.make_async_copy(
            total_ref.at[tile_at % 2], gin_out.at[:, cols], total_sems.at[tile_at % 2]
        )

    def fold_sent():
        for way in range(2):
            for k in range(copies):
                shard_at, _ = fold_tile(way, k)

                @pl.when((g > shard_at) if way else (g < shard_at))
                def _():
                    fold_copy(way, k, None).wait_send()

    for k in range(3):
        fold_source(k)
    ggain2 = jnp.zeros((8, width), FULL)
    lg_t = []
    for row0 in range(0, seq_len, tile):
        rows = slice(row0, row0 + tile)
        token = token_ref[rows, :]
        at = lax.broadcasted_iota(jnp.int32, (tile, recv_ref.shape[0]), 1).astype(FULL)
        picks = [jnp.where(at == token[:, k : k + 1], 1.0, 0.0).astype(LOW) for k in range(2)]
        got = dot_nn(jnp.concatenate(picks, axis=0), recv_ref[...])
        gg = [
            jnp.sum(got[k * tile : k * tile + tile, width:], axis=1, keepdims=True) for k in range(2)
        ]
        pull = token[:, 2:3] * token[:, 3:4] * (gg[0] - gg[1])
        expert = lax.broadcasted_iota(jnp.int32, (tile, 128), 1).astype(FULL)
        lg = jnp.where(expert == token[:, 4:5], pull, jnp.where(expert == token[:, 5:6], -pull, 0.0))
        lg_t.append(jnp.transpose(lg)[:experts])
        ngrad = (
            got[:tile, :width]
            + got[tile:, :width]
            + dot_nn(lg[:, :experts].astype(LOW), wrouter_ref[...])
        )
        hidden = hidden_ref[rows, :]
        inv = lax.rsqrt(jnp.mean(hidden * hidden, axis=1, keepdims=True) + EPS)
        unit = hidden * inv
        ng = ngrad * unit
        for i in range(tile // 8):
            ggain2 = ggain2 + ng[i * 8 : i * 8 + 8]
        scaled = ngrad * gain2_ref[...][None, :]
        proj = jnp.mean(scaled * unit, axis=1, keepdims=True)
        hgrad = cot_ref[rows, :].astype(FULL) + inv * (scaled - unit * proj)
        hgrad_ref[rows, :] = hgrad
        mgrad_ref[rows, :] = dot_nt(hgrad.astype(LOW), wproj_ref[...]).astype(LOW)
        x = tokens_ref[rows, :].astype(FULL)
        inv = lax.rsqrt(jnp.mean(x * x, axis=1, keepdims=True) + EPS)
        dqkv_ref[rows, :width] = (x * inv * gain1_ref[...][None, :]).astype(LOW)
        if row0 == tile:
            fold_source(3)
        if row0 == 3 * tile:
            fold_fetch(1, 0)
            fold_source(4)
    ggain2 = jnp.sum(ggain2, axis=0, keepdims=True)
    logit_grad_t = jnp.concatenate(lg_t, axis=1).astype(LOW)
    grouter = dot_nn(logit_grad_t, normed2_ref[...])
    normed_t[...] = jnp.transpose(dqkv_ref[:, :width])
    part_ref[0] = (
        dot_nn(jnp.transpose(mixed_ref[...]), hgrad_ref[...].astype(LOW))
        .astype(LOW)
        .reshape(experts, width // experts, width)
    )
    pair_send(0)
    fold_push(1, 0)
    fold_fetch(1, 1)
    mgrad_t[...] = jnp.transpose(mgrad_ref[...])
    load(0).wait()
    q_t[...] = jnp.transpose(qkv_ref[:, :width])
    load(1).wait()
    up = lax.broadcasted_iota(jnp.int32, (128, 128), 0)
    across = lax.broadcasted_iota(jnp.int32, (128, 128), 1)
    flip = jnp.where(up + across == 127, 1.0, 0.0).astype(FULL)

    def heads_back(pair):
        col = pl.multiple_of(pair * 128, 128)
        kp = qkv_ref[:, pl.ds(width + col, 128)]
        vp = qkv_ref[:, pl.ds(2 * width + col, 128)]
        op = mgrad_ref[:, pl.ds(col, 128)].astype(FULL)
        os = jnp.concatenate([(op * half_mask(sub, 1.0)).astype(LOW) for sub in range(2)], axis=0)
        dp = dot_nt(os, vp)
        for sub in range(2):
            h = 2 * pair + sub
            near = jnp.zeros((128, 384), FULL)
            far_neg = jnp.zeros((128, 128), FULL)
            far_pos = jnp.zeros((128, 128), FULL)
            blocks = seq_len // 128
            for block in range(blocks):
                first = sub * seq_len + block * 128
                here = slice(block * 128, block * 128 + 128)
                p = prob_ref[h, here, :].astype(FULL)
                weighted = p * dp[first : first + 128]
                ds = weighted - p * jnp.sum(weighted, axis=1, keepdims=True)
                low = ds.astype(LOW)
                ds_ref[sub, here, :] = low
                ds = low.astype(FULL)
                strip = []
                for d in range(-1, 2):
                    other = block + d
                    if 0 <= other < blocks:
                        strip.append(ds[:, other * 128 : other * 128 + 128])
                    else:
                        strip.append(jnp.zeros((128, 128), FULL))
                near = near + jnp.concatenate(strip, axis=1)
                for other in range(blocks):
                    piece = ds[:, other * 128 : other * 128 + 128]
                    if other - block <= -2:
                        far_neg = far_neg + piece
                    elif other - block >= 2:
                        far_pos = far_pos + piece
            low_sum = jnp.sum(far_neg)
            high_sum = jnp.sum(far_pos)
            padded = jnp.concatenate([exact_nn(flip, near), jnp.zeros((128, 128), FULL)], axis=1)
            turned = pltpu.roll(padded, 1, 1, stride=1, stride_axis=0)
            sums = jnp.sum(turned, axis=0, keepdims=True)
            lane = lax.broadcasted_iota(jnp.int32, (1, 512), 1)
            sums = sums + jnp.where(lane == 1, low_sum, jnp.where(lane == 511, high_sum, 0.0))
            diag_ref[pl.ds(h, 1), :] = sums
        lane = lax.broadcasted_iota(jnp.int32, (seq_len, 128), 1)
        dq = dot_nn(jnp.concatenate([ds_ref[0], ds_ref[1]], axis=0), kp)
        dqkv_ref[:, pl.ds(col, 128)] = (
            jnp.where(lane < 64, dq[:seq_len], dq[seq_len:]) * 0.125
        ).astype(LOW)
        for sub in range(2):
            part = pl.ds(pl.multiple_of(col + sub * 64, 64), 64)
            dk_t[part, :] = (dot_nn(q_t[part, :], ds_ref[sub]) * 0.125).astype(LOW)
            dv_t[part, :] = dot_nn(mgrad_t[part, :], prob_ref[2 * pair + sub]).astype(LOW)

    stripe = width // (chunks - 1)
    for c in range(1, chunks):
        pairs = stripe // 128

        @pl.loop((c - 1) * pairs, c * pairs)
        def _(pair):
            heads_back(pair)

        col = (c - 1) * stripe
        dqkv_ref[:, width + col : width + col + stripe] = jnp.transpose(dk_t[col : col + stripe, :])
        dqkv_ref[:, 2 * width + col : 2 * width + col + stripe] = jnp.transpose(
            dv_t[col : col + stripe, :]
        )
        for third in range(3):
            here = third * width + col
            part_ref[c, :, :, third * stripe : third * stripe + stripe] = (
                dot_nn(normed_t[...], dqkv_ref[:, here : here + stripe])
                .astype(LOW)
                .reshape(experts, width // experts, stripe)
            )
        pair_send(c)
        plane_send(c - 1)
        if c >= 2:
            group_send(c - 2)
        fold_push(1, c)
        fold_source(c + 4)
        if c < chunks - 1:
            fold_fetch(1, c + 1)
        if c == 2:
            fold_fetch(2, 0)
        if c == 3:
            fold_push(2, 0)
            fold_fetch(2, 1)

    load(2).wait()
    ggain1 = jnp.zeros((8, width), FULL)
    for row0 in range(0, seq_len, tile):
        rows = slice(row0, row0 + tile)
        x = tokens_ref[rows, :].astype(FULL)
        inv = lax.rsqrt(jnp.mean(x * x, axis=1, keepdims=True) + EPS)
        unit = x * inv
        ngrad = dot_nt(dqkv_ref[rows, :], wqkv_ref[...])
        ng = ngrad * unit
        for i in range(tile // 8):
            ggain1 = ggain1 + ng[i * 8 : i * 8 + 8]
        scaled = ngrad * gain1_ref[...][None, :]
        proj = jnp.mean(scaled * unit, axis=1, keepdims=True)
        gtok_ref[rows, :] = (hgrad_ref[rows, :] + inv * (scaled - unit * proj)).astype(LOW)
        if row0 == 0:
            plane_send(chunks - 1)
            for mask in (6, 7):
                result_copy(mask).start()
            fold_fetch(1, 4)
            fold_push(2, 1)
        if row0 == 2 * tile:
            fold_push(1, 4)
            fold_fetch(2, 2)
            fold_source(8)
    ggain1 = jnp.sum(ggain1, axis=0, keepdims=True)

    gtable = exact_nt(onehot_ref[...], diag_ref[...])
    shard = width // experts
    per = gtable.shape[0] // experts
    for e in range(experts):
        cols = slice(e * shard, e * shard + shard)
        block = jnp.concatenate([ggain1[:, cols], ggain2[:, cols], grouter[:, cols]], axis=0)
        small_ref[e] = jnp.zeros(small_ref.shape[1:], FULL)
        small_ref[e, 0 : 2 + experts, 0:shard] = block
        small_ref[e, 2 + experts : 2 + experts + per, 0 : gtable.shape[1]] = gtable[
            e * per : e * per + per
        ]
    for mask in range(1, experts):
        other = lax.bitwise_xor(me, mask)
        go(remote(small_ref.at[other], small_in.at[mask], small_sems, (mask,), device(mask)))
    fold_source(9)
    fold_fetch(1, 5)
    fold_push(2, 2)
    final_send(0)
    group_send(2)
    fold_push(1, 5)
    fold_fetch(2, 3)
    total = small_ref[me]
    for mask in range(1, experts):
        remote(
            small_ref.at[0], small_in.at[mask], small_sems, (mask,), device(mask)
        ).wait_recv()
        total = total + small_in[mask]
    small_plane[...] = total
    for step in range(1, groups):
        where = (lax.rem(g + step, groups), me)
        go(remote(small_plane, small_group.at[step], smallz_sems, (step,), where))
    fold_fetch(1, 6)
    fold_push(2, 3)
    final_send(1)
    group_send(3)
    fold_source(10)
    fold_source(11)
    fold_push(1, 6)
    fold_fetch(1, 7)
    own_result.wait()
    for mask in range(1, experts):
        result_copy(mask).wait()

    fold_push(1, 7)

    @pl.loop(0, seq_len // tile)
    def _(step):
        rows = pl.ds(pl.multiple_of(step * tile, tile), tile)
        token = token_ref[rows, :]
        at = lax.broadcasted_iota(jnp.int32, (tile, experts * SLOTS), 1).astype(FULL)
        picks = [jnp.where(at == token[:, k : k + 1], 1.0, 0.0).astype(LOW) for k in range(2)]
        got = dot_nn(
            jnp.concatenate(picks, axis=0), back_ref[...].reshape(experts * SLOTS, width)
        )
        block_ref[rows, :] = (
            hidden_ref[rows, :] + token[:, 2:3] * got[:tile] + token[:, 3:4] * got[tile:]
        ).astype(LOW)

    fold_final(0)
    final_send(2)
    fold_final(1)
    final_send(3)
    for tile_at in range(2, parts):
        fold_final(tile_at)
    for tile_at in range(parts - 2, parts):
        final_copy(tile_at).wait()
    for step in range(1, groups):
        remote(
            small_plane, small_group.at[step], smallz_sems, (step,), (lax.rem(g + step, groups), me)
        ).wait_recv()
        total = total + small_group[step]
    small_out[...] = total
    for c in range(chunks):
        finish(c)
    fold_sent()
    for copy in started:
        copy.wait_send()


def attn_back(
    tokens, cot, hidden, normed2, mixed, qkv, prob, recv, token, gain1, gain2, wqkv, wproj, wrouter, table, result, gin, groups
):
    seq_len, width = tokens.shape
    buckets, heads = table.shape
    experts = wrouter.shape[1]
    shard = width // experts
    chunks = groups
    chips = experts // 2
    small = (16, 128)
    sds = jax.ShapeDtypeStruct
    dma = pltpu.SemaphoreType.DMA
    outs = pl.pallas_call(
        attn_back_kernel,
        out_shape=(
            sds((seq_len, width), LOW),
            sds((seq_len, width), LOW),
            sds((chunks, shard, width), LOW),
            sds(small, FULL),
            sds((gin.shape[2], gin.shape[1] * gin.shape[3]), FULL),
            sds(gin.shape, LOW),
            sds(gin.shape, LOW),
        ),
        in_specs=[VM] * 5 + [HBM] * 2 + [VM] * 4 + [HBM] + [VM] * 3 + [HBM] * 2,
        out_specs=[VM] * 4 + [HBM] * 3,
        scratch_shapes=[
            pltpu.VMEM((seq_len, width), FULL),
            pltpu.VMEM((seq_len, width), LOW),
            pltpu.VMEM((width, seq_len), LOW),
            pltpu.VMEM((width, seq_len), LOW),
            pltpu.VMEM((width, seq_len), LOW),
            pltpu.VMEM((2, seq_len, seq_len), LOW),
            pltpu.VMEM((heads, 512), FULL),
            pltpu.VMEM((width, seq_len), LOW),
            pltpu.VMEM((width, seq_len), LOW),
            pltpu.VMEM((seq_len, 3 * width), LOW),
            pltpu.VMEM((chunks, experts, shard, width), LOW),
            pltpu.VMEM((chunks, chips, shard, width), LOW),
            pltpu.VMEM((chunks, chips, shard, width), LOW),
            pltpu.VMEM((chunks, chips - 1, shard, width), LOW),
            pltpu.VMEM((chunks, shard, width), LOW),
            pltpu.VMEM((chunks, groups, shard, width), LOW),
            pltpu.VMEM((experts, *small), FULL),
            pltpu.VMEM((experts, *small), FULL),
            pltpu.VMEM(small, FULL),
            pltpu.VMEM((groups, *small), FULL),
            pltpu.VMEM((seq_len, 3 * width), LOW),
            pltpu.VMEM((heads, seq_len, seq_len), LOW),
            pltpu.VMEM(wqkv.shape, LOW),
            pltpu.VMEM(result.shape, LOW),
            pltpu.VMEM((groups * (groups - 1), *gin.shape[2:]), LOW),
            pltpu.VMEM((2, 2, *gin.shape[2:]), LOW),
            pltpu.VMEM((2, *gin.shape[2:]), FULL),
            dma((2, 2, (groups - 1) * gin.shape[1])),
            dma((2, 2)),
            dma((2,)),
            dma((4,)),
            dma((2, experts)),
            dma((2, chunks, chips)),
            dma((2, chunks, chips - 1)),
            dma((2, chunks, groups)),
            dma((2, chunks, groups - 1)),
            dma((2, experts)),
            dma((2, groups)),
        ],
        compiler_params=pltpu.CompilerParams(
            vmem_limit_bytes=60 * MIB, collective_id=1, has_side_effects=True
        ),
        cost_estimate=pl.CostEstimate(
            flops=30_000_000_000, bytes_accessed=30 * MIB, transcendentals=0
        ),
    )(
        tokens,
        cot,
        hidden,
        normed2,
        mixed,
        qkv,
        prob,
        recv,
        token,
        gain1,
        gain2,
        wqkv,
        wproj,
        wrouter.T,
        jnp.asarray(near_onehot(buckets)),
        result,
        gin,
    )
    return outs[:5]


def outputs_kernel(
    block_in,
    gtok_in,
    gin_in,
    gout_in,
    dense_ref,
    small_ref,
    block_ref,
    gtok_ref,
    gain1_ref,
    qkv_ref,
    proj_ref,
    table_ref,
    gain2_ref,
    router_ref,
    gin_ref,
    gout_ref,
    gin_v,
    gout_v,
    block_v,
    gtok_v,
    sems,
):
    passed = (
        (gin_in, gin_v, gin_ref.at[0]),
        (gout_in, gout_v, gout_ref.at[0]),
        (block_in, block_v, block_ref),
        (gtok_in, gtok_v, gtok_ref),
    )
    pieces = 4
    copies = []
    for i, (src, mid, dst) in enumerate(passed):
        rows = src.shape[0] // pieces
        for piece in range(pieces):
            here = pl.ds(piece * rows, rows)
            copies.append(
                [
                    pltpu.make_async_copy(a.at[here, :], b.at[here, :], sems.at[way, i, piece])
                    for way, (a, b) in enumerate(((src, mid), (mid, dst)))
                ]
            )
    for copy_in, _ in copies:
        copy_in.start()
    chunks, shard, width = dense_ref.shape
    experts = router_ref.shape[0]
    stripe = width // (chunks - 1)
    proj_ref[...] = dense_ref[0].astype(FULL)
    for c in range(1, chunks):
        for third in range(3):
            col = third * width + (c - 1) * stripe
            qkv_ref[:, col : col + stripe] = dense_ref[
                c, :, third * stripe : third * stripe + stripe
            ].astype(FULL)
    gain1_ref[...] = small_ref[0:1, 0:shard]
    gain2_ref[...] = small_ref[1:2, 0:shard]
    router_ref[...] = small_ref[2 : 2 + experts, 0:shard]
    per, heads = table_ref.shape
    table_ref[...] = small_ref[2 + experts : 2 + experts + per, 0:heads]
    for copy_in, copy_out in copies:
        copy_in.wait()
        copy_out.start()
    for _, copy_out in copies:
        copy_out.wait()


def outputs(block, gtok, gin, gout, dense, small, experts, table_shape):
    chunks, shard, width = dense.shape
    buckets, heads = table_shape
    sds = jax.ShapeDtypeStruct
    return pl.pallas_call(
        outputs_kernel,
        out_shape=(
            sds(block.shape, LOW),
            sds(gtok.shape, LOW),
            sds((1, shard), FULL),
            sds((shard, 3 * width), FULL),
            sds((shard, width), FULL),
            sds((buckets // experts, heads), FULL),
            sds((1, shard), FULL),
            sds((experts, shard), FULL),
            sds((1, *gin.shape), FULL),
            sds((1, *gout.shape), FULL),
        ),
        in_specs=[HBM] * 4 + [VM] * 2,
        out_specs=[HBM] * 2 + [VM] * 6 + [HBM] * 2,
        scratch_shapes=[
            pltpu.VMEM(gin.shape, FULL),
            pltpu.VMEM(gout.shape, FULL),
            pltpu.VMEM(block.shape, LOW),
            pltpu.VMEM(gtok.shape, LOW),
            pltpu.SemaphoreType.DMA((2, 4, 4)),
        ],
        compiler_params=pltpu.CompilerParams(vmem_limit_bytes=32 * MIB),
    )(block, gtok, gin, gout, dense, small)


def on_device_fast(
    tokens,
    gain_first,
    w_qkv,
    w_proj,
    bias_table,
    gain_second,
    w_router,
    w_in,
    w_out,
    routes,
    priority,
    span_start,
    cotangent,
):
    experts = w_router.shape[1]
    width = tokens.shape[1]
    groups = lax.axis_size("group")
    (
        qkv,
        prob,
        mixed,
        hidden,
        normed2,
        rows,
        cot_rows,
        gate_col,
        token,
        info,
        resg_t,
        act,
        slope,
        outer_first,
    ) = attn_dispatch(
        tokens,
        cotangent,
        gain_first,
        w_qkv,
        w_proj,
        bias_table,
        gain_second,
        w_router,
        routes,
        priority,
        span_start,
        w_in[0],
        groups,
    )
    recv, packed_out, grad_inner, grad_out = expert_call(
        cot_rows, gate_col, rows, info, resg_t, act, slope, outer_first, w_out[0], w_in[0]
    )
    block_out, gtok, dense, small, grad_in = attn_back(
        tokens,
        cotangent,
        hidden,
        normed2,
        mixed,
        qkv,
        prob,
        recv.reshape(-1, width + 128),
        token,
        gain_first,
        gain_second,
        w_qkv,
        w_proj,
        w_router,
        bias_table,
        packed_out,
        grad_inner,
        groups,
    )
    final = list(
        outputs(block_out, gtok, grad_in, grad_out, dense, small, experts, bias_table.shape)
    )
    final[2] = final[2].reshape(-1)
    final[6] = final[6].reshape(-1)
    final[7] = final[7].T
    return tuple(final)


def bucket_table(seq_len, buckets):
    half_count = buckets // 2
    exact_count = half_count // 2
    offsets = np.arange(-(seq_len - 1), seq_len)
    upper_half = (offsets > 0).astype(np.int64) * half_count
    distance = np.abs(offsets)
    scaled = (
        np.log(np.maximum(distance, 1) / float(exact_count))
        / np.log(128.0 / exact_count)
        * (half_count - exact_count)
    )
    larger = np.minimum(
        exact_count + np.floor(np.maximum(scaled, 0.0)).astype(np.int64), half_count - 1
    )
    bucket = upper_half + np.where(distance < exact_count, distance, larger)
    places = np.arange(seq_len)
    return bucket[places[None, :] - places[:, None] + seq_len - 1].astype(np.int32)


def allowed_pairs(seq_len, span_begin, span_len):
    places = jnp.arange(seq_len, dtype=jnp.int32)
    causal = places[None, :] <= places[:, None]
    inside = (places >= span_begin) & (places < span_begin + span_len)
    return causal | inside[:, None] & inside[None, :]


def rms_norm(values, norm_gain):
    return values * lax.rsqrt(jnp.mean(values * values, axis=-1, keepdims=True) + 1e-06) * norm_gain


def gate_values(logits, routes, experts):
    probabilities = jax.nn.softmax(logits, axis=-1)
    chosen = (routes[..., None] == jnp.arange(experts, dtype=jnp.int32)).astype(jnp.float32)
    picked = jnp.sum(probabilities[:, None, :] * chosen, axis=-1)
    return picked / jnp.sum(picked, axis=1, keepdims=True)


def local_ranks(choice_hits, priority):
    token_count = priority.shape[0]
    token_order = (
        jnp.zeros((token_count,), jnp.int32)
        .at[priority]
        .set(jnp.arange(token_count, dtype=jnp.int32))
    )
    ordered = choice_hits[token_order]
    running = jnp.cumsum(ordered, axis=0) - ordered
    return jnp.sum(running[priority] * choice_hits, axis=-1)


def contract_rows(left, right):
    return lax.dot_general(
        left, right, (((0,), (0,)), ((), ())), preferred_element_type=jnp.float32
    )


def on_device(
    tokens,
    gain_first,
    w_qkv,
    w_proj,
    bias_table,
    gain_second,
    w_router,
    w_in,
    w_out,
    routes,
    priority,
    span_start,
    cotangent,
):
    seq_len, model_width = tokens.shape
    buckets, head_count = bias_table.shape
    head_dim = model_width // head_count
    experts = w_router.shape[1]
    slot_count = 4 * seq_len // experts
    capacity = 5 * seq_len // 2
    score_scale = 1.0 / math.sqrt(head_dim)
    highest = lax.Precision.HIGHEST
    lowtype = jnp.bfloat16
    fulltype = jnp.float32
    tokens_f = tokens.astype(fulltype)
    normed_one = rms_norm(tokens_f, gain_first).astype(lowtype)
    qkv_rows = jnp.dot(normed_one, w_qkv, preferred_element_type=fulltype).astype(lowtype)
    qkv_rows = qkv_rows.reshape(seq_len, 3, head_count, head_dim)
    queries, key_rows, value_rows = (qkv_rows[:, 0], qkv_rows[:, 1], qkv_rows[:, 2])
    bucket_index = jnp.asarray(bucket_table(seq_len, buckets))
    onehot_table = (bucket_index[:, :, None] == jnp.arange(buckets, dtype=jnp.int32)).astype(
        fulltype
    )
    rel_bias = jnp.einsum("qkb,bh->hqk", onehot_table, bias_table, precision=highest)
    allowed = allowed_pairs(seq_len, span_start[0], PIC)

    def masked_scores():
        raw_scores = (
            jnp.einsum("qhc,khc->hqk", queries, key_rows, preferred_element_type=fulltype)
            * score_scale
            + rel_bias
        )
        return jnp.where(allowed[None], raw_scores, -1e30)

    scores = masked_scores()
    log_total = jax.nn.logsumexp(scores, axis=-1)
    attn_probs = jnp.exp(scores - log_total[..., None]).astype(lowtype)
    mixed_heads = jnp.einsum(
        "hqk,khc->qhc", attn_probs, value_rows, preferred_element_type=fulltype
    )
    mixed_heads = mixed_heads.astype(lowtype).reshape(seq_len, model_width)
    hidden = tokens_f + jnp.dot(mixed_heads, w_proj, preferred_element_type=fulltype)
    normed_two = rms_norm(hidden, gain_second).astype(lowtype)
    logits = jnp.dot(normed_two, w_router, preferred_element_type=fulltype)
    gate_weights = gate_values(logits, routes, experts)
    choice_hits = (routes[..., None] == jnp.arange(experts, dtype=jnp.int32)).astype(jnp.int32)
    counts = jnp.sum(choice_hits, axis=0)
    every_count = lax.all_gather(counts[None], "expert", axis=0, tiled=True)
    pair_ranks = local_ranks(choice_hits, priority[0])
    second_shift = jnp.sum(choice_hits[:, 1] * counts[0], axis=-1)
    slot_index = pair_ranks + jnp.stack([jnp.zeros_like(second_shift), second_shift], axis=-1)
    flat_slot = (routes * slot_count + slot_index).reshape(-1)
    own_expert = (jnp.arange(experts, dtype=jnp.int32) == lax.axis_index("expert")).astype(
        jnp.int32
    )
    own_counts = jnp.sum(every_count * own_expert, axis=-1)
    first_rows, second_rows = (own_counts[:, 0], own_counts[:, 1])
    first_before = jnp.cumsum(first_rows) - first_rows
    second_before = jnp.cumsum(second_rows) - second_rows
    first_total = jnp.sum(first_rows)
    column = jnp.arange(slot_count, dtype=jnp.int32)[None, :]
    position = jnp.where(
        column < first_rows[:, None],
        first_before[:, None] + column,
        first_total + second_before[:, None] + column - first_rows[:, None],
    )
    usable = (column < (first_rows + second_rows)[:, None]) & (position < capacity)
    destination = jnp.where(usable, position, capacity).reshape(-1)

    def pack_pairs(pair_rows):
        packed = jnp.zeros((experts * slot_count, model_width), lowtype)
        packed = packed.at[flat_slot].set(pair_rows.reshape(-1, model_width))
        return packed.reshape(experts, slot_count, model_width)

    def compact_rows(arrived):
        gathered_rows = jnp.zeros((capacity + 1, model_width), lowtype)
        return gathered_rows.at[destination].add(arrived.reshape(-1, model_width))[:capacity]

    def spread_rows(expert_out):
        padded = jnp.concatenate([expert_out, jnp.zeros((1, model_width), lowtype)], axis=0)
        return padded[destination].reshape(-1, slot_count, model_width)

    def unpack_pairs(received):
        return (
            received.reshape(-1, model_width)[flat_slot]
            .reshape(seq_len, 2, model_width)
            .astype(fulltype)
        )

    pair_rows = jnp.broadcast_to(normed_two[:, None, :], (seq_len, 2, model_width))
    arrived = lax.all_to_all(
        pack_pairs(pair_rows), "expert", split_axis=0, concat_axis=0, tiled=True
    )
    expert_rows = compact_rows(arrived)
    inner_pre = jnp.dot(expert_rows, w_in[0], preferred_element_type=fulltype)
    active = jax.nn.gelu(inner_pre).astype(lowtype)
    result = jnp.dot(active, w_out[0], preferred_element_type=fulltype).astype(lowtype)
    returned = unpack_pairs(
        lax.all_to_all(spread_rows(result), "expert", split_axis=0, concat_axis=0, tiled=True)
    )
    block_out = hidden + jnp.sum(gate_weights[..., None] * returned, axis=1)
    upstream = cotangent.astype(fulltype)
    gate_grad = jnp.sum(upstream[:, None, :] * returned, axis=-1)
    result_grad = (gate_weights[..., None] * upstream[:, None, :]).astype(lowtype)
    result_rows = compact_rows(
        lax.all_to_all(pack_pairs(result_grad), "expert", split_axis=0, concat_axis=0, tiled=True)
    )
    grad_outer = contract_rows(active, result_rows)
    hidden_pre_grad = jnp.dot(result_rows, w_out[0].T, preferred_element_type=fulltype)
    inner_grad = jax.vjp(jax.nn.gelu, inner_pre)[1](hidden_pre_grad)[0].astype(lowtype)
    grad_inner = contract_rows(expert_rows, inner_grad)
    rows_grad = jnp.dot(inner_grad, w_in[0].T, preferred_element_type=fulltype).astype(lowtype)
    pair_grad = unpack_pairs(
        lax.all_to_all(spread_rows(rows_grad), "expert", split_axis=0, concat_axis=0, tiled=True)
    )
    logit_grad = jax.vjp(lambda values: gate_values(values, routes, experts), logits)[1](gate_grad)[
        0
    ].astype(lowtype)
    grad_router = contract_rows(normed_two, logit_grad)
    normed_grad = jnp.sum(pair_grad, axis=1) + jnp.dot(
        logit_grad, w_router.T, preferred_element_type=fulltype
    )
    second_back = jax.vjp(rms_norm, hidden, gain_second)[1](normed_grad)
    hidden_grad = upstream + second_back[0]
    branch_grad = hidden_grad.astype(lowtype)
    grad_proj = contract_rows(mixed_heads, branch_grad)
    mixed_grad = jnp.dot(branch_grad, w_proj.T, preferred_element_type=fulltype).astype(lowtype)
    mixed_grad = mixed_grad.reshape(seq_len, head_count, head_dim)
    scores = masked_scores()
    probs_full = jnp.exp(scores - log_total[..., None])
    probs_low = probs_full.astype(lowtype)
    prob_grad = jnp.einsum("qhc,khc->hqk", mixed_grad, value_rows, preferred_element_type=fulltype)
    value_grad = jnp.einsum("hqk,qhc->khc", probs_low, mixed_grad, preferred_element_type=fulltype)
    row_dot = jnp.sum(probs_full * prob_grad, axis=-1, keepdims=True)
    score_grad = (probs_full * (prob_grad - row_dot)).astype(lowtype)
    query_grad = (
        jnp.einsum("hqk,khc->qhc", score_grad, key_rows, preferred_element_type=fulltype)
        * score_scale
    )
    key_grad = (
        jnp.einsum("hqk,qhc->khc", score_grad, queries, preferred_element_type=fulltype)
        * score_scale
    )
    grad_table = jnp.einsum(
        "hqk,qkb->bh", score_grad.astype(fulltype), onehot_table, precision=highest
    )
    qkv_grad = (
        jnp.stack([query_grad, key_grad, value_grad], axis=1)
        .astype(lowtype)
        .reshape(seq_len, 3 * model_width)
    )
    grad_qkv = contract_rows(normed_one, qkv_grad)
    normed_one_grad = jnp.dot(qkv_grad, w_qkv.T, preferred_element_type=fulltype)
    first_back = jax.vjp(rms_norm, tokens_f, gain_first)[1](normed_one_grad)
    grad_tokens = (hidden_grad + first_back[0]).astype(lowtype)
    dense_grads = (first_back[1], grad_qkv, grad_proj, grad_table, second_back[1], grad_router)
    shares = (
        lax.psum_scatter(
            dense_grads[0].astype(jnp.bfloat16), "expert", scatter_dimension=0, tiled=True
        ).astype(jnp.float32),
        lax.psum_scatter(
            dense_grads[1].astype(jnp.bfloat16), "expert", scatter_dimension=0, tiled=True
        ).astype(jnp.float32),
        lax.psum_scatter(
            dense_grads[2].astype(jnp.bfloat16), "expert", scatter_dimension=0, tiled=True
        ).astype(jnp.float32),
        lax.psum_scatter(
            dense_grads[3].astype(jnp.bfloat16), "expert", scatter_dimension=0, tiled=True
        ).astype(jnp.float32),
        lax.psum_scatter(
            dense_grads[4].astype(jnp.bfloat16), "expert", scatter_dimension=0, tiled=True
        ).astype(jnp.float32),
        lax.psum_scatter(
            dense_grads[5].astype(jnp.bfloat16), "expert", scatter_dimension=0, tiled=True
        ).astype(jnp.float32),
    )
    totals = (
        lax.psum(shares[0].astype(jnp.bfloat16), "group").astype(jnp.float32),
        lax.psum(shares[1].astype(jnp.bfloat16), "group").astype(jnp.float32),
        lax.psum(shares[2].astype(jnp.bfloat16), "group").astype(jnp.float32),
        lax.psum(shares[3].astype(jnp.bfloat16), "group").astype(jnp.float32),
        lax.psum(shares[4].astype(jnp.bfloat16), "group").astype(jnp.float32),
        lax.psum(shares[5].astype(jnp.bfloat16), "group").astype(jnp.float32),
    )
    grad_in, grad_out = (
        lax.psum_scatter(
            grad_inner[None].astype(jnp.bfloat16), "group", scatter_dimension=1, tiled=True
        ).astype(jnp.float32),
        lax.psum_scatter(
            grad_outer[None].astype(jnp.bfloat16), "group", scatter_dimension=1, tiled=True
        ).astype(jnp.float32),
    )
    return (
        block_out.astype(lowtype),
        grad_tokens,
        totals[0],
        totals[1],
        totals[2],
        totals[3],
        totals[4],
        totals[5],
        grad_in,
        grad_out,
    )


def solution(mesh):
    fast = (mesh.shape["group"], mesh.shape["expert"]) == (4, 8)
    step = on_device_fast if fast else on_device
    return jax.shard_map(
        step,
        mesh=mesh,
        in_specs=(
            P(("group", "expert"), None),
            P(),
            P(),
            P(),
            P(),
            P(),
            P(),
            P("expert", None, None),
            P("expert", None, None),
            P(("group", "expert"), None),
            P(("group", "expert"), None),
            P(("group", "expert")),
            P(("group", "expert"), None),
        ),
        out_specs=(
            P(("group", "expert"), None),
            P(("group", "expert"), None),
            P("expert"),
            P("expert", None),
            P("expert", None),
            P("expert", None),
            P("expert"),
            P("expert", None),
            P("expert", "group", None),
            P("expert", "group", None),
        ),
        check_vma=False,
    )
```

```python
import functools
import math

import jax
import jax.numpy as jnp
import numpy as np
from jax import lax
from jax.experimental import pallas as pl
from jax.experimental.pallas import tpu as pltpu
from jax.sharding import PartitionSpec as P

PIC = 256
EPS = 1e-6
LOW = jnp.bfloat16
FULL = jnp.float32
VM = pl.BlockSpec(memory_space=pltpu.VMEM)
SM = pl.BlockSpec(memory_space=pltpu.SMEM)
HBM = pl.BlockSpec(memory_space=pl.ANY)
MIB = 1 << 20
ATT_ROWS = 256
ATT_UNROLL = 2
MESH = pl.DeviceIdType.MESH
SECOND = 512.0
SLOTS = 256
ROW_TILE = 256
EARLY = 2
FF_TILE = 256
THIRDS = 3


def offset_bucket(offsets, buckets):
    half_count = buckets // 2
    exact_count = half_count // 2
    upper_half = (offsets > 0).astype(np.int64) * half_count
    distance = np.abs(offsets)
    scaled = (
        np.log(np.maximum(distance, 1) / float(exact_count))
        / np.log(128.0 / exact_count)
        * (half_count - exact_count)
    )
    larger = np.minimum(
        exact_count + np.floor(np.maximum(scaled, 0.0)).astype(np.int64), half_count - 1
    )
    return upper_half + np.where(distance < exact_count, distance, larger)


def near_onehot(buckets):
    bucket = offset_bucket(np.arange(512) - 256, buckets)
    return (np.arange(buckets)[:, None] == bucket[None, :]).astype(np.float32)


def dot_nn(a, b):
    return lax.dot_general(a, b, (((1,), (0,)), ((), ())), preferred_element_type=FULL)


def dot_nt(a, b):
    return lax.dot_general(a, b, (((1,), (1,)), ((), ())), preferred_element_type=FULL)


def dot_tn(a, b):
    return lax.dot_general(a, b, (((0,), (0,)), ((), ())), preferred_element_type=FULL)


def exact_nn(a, b):
    return lax.dot_general(
        a, b, (((1,), (0,)), ((), ())), precision=lax.Precision.HIGHEST, preferred_element_type=FULL
    )


def exact_nt(a, b):
    return lax.dot_general(
        a, b, (((1,), (1,)), ((), ())), precision=lax.Precision.HIGHEST, preferred_element_type=FULL
    )


def split3(x):
    hi = x.astype(LOW)
    rest = x - hi.astype(FULL)
    mid = rest.astype(LOW)
    low = (rest - mid.astype(FULL)).astype(LOW)
    return hi, mid, low


def half_mask(sub, value, shape=(1, 128)):
    lane = lax.broadcasted_iota(jnp.int32, shape, 1)
    keep = (lane < 64) if sub == 0 else (lane >= 64)
    return jnp.where(keep, value, 0.0).astype(FULL)


def attn_setup(span_ref, table_ref, onehot_ref, near_ref, mask_ref):
    seq_len = mask_ref.shape[0]
    heads = near_ref.shape[0]
    start = span_ref[0]
    qi = lax.broadcasted_iota(jnp.int32, (seq_len, seq_len), 0)
    kj = lax.broadcasted_iota(jnp.int32, (seq_len, seq_len), 1)
    q_in = (qi >= start) & (qi < start + PIC)
    k_in = (kj >= start) & (kj < start + PIC)
    mask_ref[...] = jnp.where((kj <= qi) | (q_in & k_in), 0.0, -1e30).astype(FULL)
    vecs = exact_nn(table_ref[...], onehot_ref[...])
    for h in range(heads):
        rows = jnp.broadcast_to(vecs[h : h + 1, :], (128, 512))
        rolled = pltpu.roll(rows, 0, 1, stride=1, stride_axis=0)
        near_ref[h] = rolled[:, 128:]


def bias_rows(block, blocks, near):
    far_neg = jnp.broadcast_to(near[127:128, 0:1], (128, 128))
    far_pos = jnp.broadcast_to(near[0:1, 383:384], (128, 128))
    pieces = []
    for other in range(blocks):
        d = other - block
        if d <= -2:
            pieces.append(far_neg)
        elif d >= 2:
            pieces.append(far_pos)
        else:
            pieces.append(near[:, (d + 1) * 128 : (d + 2) * 128])
    return jnp.concatenate(pieces, axis=1)


def attn_block(row0, count, qkv_ref, near_ref, mask_ref, prob_ref, mixed_ref):
    seq_len, width3 = qkv_ref.shape
    width = width3 // 3
    blocks = seq_len // 128
    rows = slice(row0, row0 + count)

    @pl.loop(0, width // 128, unroll=ATT_UNROLL)
    def _(pair):
        col = pl.multiple_of(pair * 128, 128)
        qp = qkv_ref[rows, pl.ds(col, 128)].astype(FULL)
        kp = qkv_ref[:, pl.ds(width + col, 128)]
        vp = qkv_ref[:, pl.ds(2 * width + col, 128)]
        qs = jnp.concatenate([qp * half_mask(sub, 0.125) for sub in range(2)], axis=0)
        scores = dot_nt(qs.astype(LOW), kp)
        probs = []
        for sub in range(2):
            h = 2 * pair + sub
            for part in range(count // 128):
                first = sub * count + part * 128
                here = slice(row0 + part * 128, row0 + part * 128 + 128)
                s = scores[first : first + 128]
                bias = bias_rows(row0 // 128 + part, blocks, near_ref[h])
                s = s + bias + mask_ref[here, :]
                top = jnp.max(s, axis=1, keepdims=True)
                e = jnp.exp(s - top)
                total = jnp.sum(e, axis=1, keepdims=True)
                p = (e * (1.0 / total)).astype(LOW)
                prob_ref[h, here, :] = p
                probs.append(p)
        outs = dot_nn(jnp.concatenate(probs, axis=0), vp)
        lane = lax.broadcasted_iota(jnp.int32, (count, 128), 1)
        mixed_ref[rows, pl.ds(col, 128)] = jnp.where(
            lane < 64, outs[:count], outs[count:]
        ).astype(LOW)


def choice_hits(routes, experts):
    who = lax.broadcasted_iota(jnp.int32, (experts, routes.shape[1]), 0)
    return [who == routes[k : k + 1, :] for k in range(2)]


def to_column(row, width):
    return jnp.transpose(jnp.broadcast_to(row, (8, width)))[:, 0:1]


def ranks_by_priority(hits, priority):
    tokens = priority.shape[1]
    prio = priority.astype(FULL)
    less = jnp.where(to_column(prio, tokens) < prio, 1.0, 0.0).astype(LOW)
    return [dot_nn(jnp.where(hit, 1.0, 0.0).astype(LOW), less) for hit in hits]


def attn_dispatch_kernel(
    tokens_ref,
    cot_ref,
    gain1_ref,
    wqkv_ref,
    wproj_ref,
    table_ref,
    onehot_ref,
    gain2_ref,
    wrouter_ref,
    routes_ref,
    prio_ref,
    span_ref,
    win_ref,
    qkv_out,
    prob_out,
    mixed_out,
    hidden_out,
    normed2_out,
    rows_out,
    cotrows_out,
    gatecol_out,
    token_ref,
    info_ref,
    resgt_out,
    act_out,
    slope_out,
    gout_out,
    qkv_ref,
    prob_ref,
    mixed_ref,
    hidden_ref,
    normed2_ref,
    meta_ref,
    gate_ref,
    meta_all,
    gate_all,
    gat_c,
    gat_n,
    acc_g,
    pos_ref,
    win_v,
    rows_ref,
    cotrows_ref,
    gatecol_ref,
    resgt_ref,
    send_sem,
    recv_sem,
    small_send,
    small_recv,
    out_sem,
    in_sem,
    tile_sem,
):
    g = lax.axis_index("group")
    me = lax.axis_index("expert")
    experts = wrouter_ref.shape[0]
    seq_len, width = tokens_ref.shape
    half = seq_len // 2

    def device(mask):
        return (g, lax.bitwise_xor(me, mask))

    barrier = pltpu.get_barrier_semaphore()
    for mask in range(1, experts):
        pl.semaphore_signal(barrier, inc=1, device_id=device(mask), device_id_type=MESH)
    pl.semaphore_wait(barrier, experts - 1)

    gats = (gat_c, gat_n)
    owns = (cot_ref, normed2_ref)

    def send(which, kind, chunk, held, target):
        rows = pl.ds(chunk * half, half)
        slot = lax.bitwise_xor(me, held)
        src = owns[which].at[rows, :] if held == 0 else gats[which].at[slot, rows, :]
        return pltpu.make_async_remote_copy(
            src_ref=src,
            dst_ref=gats[which].at[slot, rows, :],
            send_sem=send_sem.at[which, kind, chunk],
            recv_sem=recv_sem.at[which, held ^ target, chunk],
            device_id=device(target),
            device_id_type=MESH,
        )

    started = []

    def go(*args):
        send(*args).start()
        started.append(functools.partial(send, *args))

    def arrived(which, mask, chunk):
        rows = pl.ds(chunk * half, half)
        here = gats[which].at[lax.bitwise_xor(me, mask), rows, :]
        pltpu.make_async_remote_copy(
            src_ref=here,
            dst_ref=here,
            send_sem=send_sem.at[which, 0, chunk],
            recv_sem=recv_sem.at[which, mask, chunk],
            device_id=device(1),
            device_id_type=MESH,
        ).wait_recv()

    def own_out(which, chunk):
        go(which, 0, chunk, 0, 2)
        go(which, 1, chunk, 0, 4)
        go(which, 2, chunk, 0, 1)

    def own_out_all(which):
        for chunk in range(2):
            go(which, 0, chunk, 0, 2)
            go(which, 1, 1 - chunk, 0, 4)
        for chunk in range(2):
            go(which, 2, chunk, 0, 1)

    def relay(which, chunk, wait=True):
        if wait:
            arrived(which, 4 if chunk else 2, chunk)
        go(which, 3, chunk, 4 if chunk else 2, 2 if chunk else 4)

    def small_copy(src, dst, index, mask):
        return pltpu.make_async_remote_copy(
            src_ref=src,
            dst_ref=dst.at[me],
            send_sem=small_send.at[index, mask],
            recv_sem=small_recv.at[index, mask],
            device_id=device(mask),
            device_id_type=MESH,
        )

    def small(*args):
        for mask in range(1, experts):
            small_copy(*args, mask).start()
            started.append(functools.partial(small_copy, *args, mask))

    def small_arrived(dst, index):
        for mask in range(1, experts):
            here = dst.at[lax.bitwise_xor(me, mask)]
            pltpu.make_async_remote_copy(
                src_ref=here,
                dst_ref=here,
                send_sem=small_send.at[index, mask],
                recv_sem=small_recv.at[index, mask],
                device_id=device(1),
                device_id_type=MESH,
            ).wait_recv()

    own_out_all(0)

    def win_load():
        return pltpu.make_async_copy(win_ref, win_v, in_sem.at[2])

    win_load().start()

    hits = choice_hits(routes_ref[...], experts)
    ranks = ranks_by_priority(hits, prio_ref[...])
    meta = jnp.where(hits[0], ranks[0], jnp.where(hits[1], ranks[1] + SECOND, -1.0))
    meta_ref[...] = meta
    meta_all[me] = meta
    small(meta_ref, meta_all, 0)

    own_pairs = (
        (qkv_ref, qkv_out),
        (prob_ref, prob_out),
        (mixed_ref, mixed_out),
        (hidden_ref, hidden_out),
        (normed2_ref, normed2_out),
        (cotrows_ref, cotrows_out),
        (rows_ref, rows_out),
        (gatecol_ref, gatecol_out),
        (resgt_ref, resgt_out),
    )

    def own_copy(index):
        src, dst = own_pairs[index]
        return pltpu.make_async_copy(src, dst, out_sem.at[index])

    def attention(wqkv_v, wproj_v, near_ref, mask_ref):
        loads = [
            pltpu.make_async_copy(src, dst, in_sem.at[i])
            for i, (src, dst) in enumerate(((wqkv_ref, wqkv_v), (wproj_ref, wproj_v)))
        ]
        for copy in loads:
            copy.start()
        attn_setup(span_ref, table_ref, onehot_ref, near_ref, mask_ref)
        loads[0].wait()
        for row0 in range(0, seq_len, 128):
            rows = slice(row0, row0 + 128)
            x = tokens_ref[rows, :].astype(FULL)
            inv = lax.rsqrt(jnp.mean(x * x, axis=1, keepdims=True) + EPS)
            n1 = (x * inv * gain1_ref[...][None, :]).astype(LOW)
            qkv_ref[rows, :] = dot_nn(n1, wqkv_v[...]).astype(LOW)
        own_copy(0).start()
        loads[1].wait()
        for chunk in range(2):
            row0 = chunk * half
            rows = slice(row0, row0 + half)
            attn_block(row0, half, qkv_ref, near_ref, mask_ref, prob_ref, mixed_ref)
            hidden = tokens_ref[rows, :].astype(FULL) + dot_nn(mixed_ref[rows, :], wproj_v[...])
            hidden_ref[rows, :] = hidden
            inv = lax.rsqrt(jnp.mean(hidden * hidden, axis=1, keepdims=True) + EPS)
            n2 = (hidden * inv * gain2_ref[...][None, :]).astype(LOW)
            normed2_ref[rows, :] = n2
            own_out(1, chunk)

    pl.run_scoped(
        attention,
        pltpu.VMEM(wqkv_ref.shape, LOW),
        pltpu.VMEM(wproj_ref.shape, LOW),
        pltpu.VMEM((table_ref.shape[0], 128, 384), FULL),
        pltpu.VMEM((seq_len, seq_len), FULL),
    )
    for index in range(1, 5):
        own_copy(index).start()

    logits = dot_nt(wrouter_ref[...], normed2_ref[...])
    unnormed = jnp.exp(logits - jnp.max(logits, axis=0, keepdims=True))
    probabilities = unnormed / jnp.sum(unnormed, axis=0, keepdims=True)
    picked = [jnp.sum(jnp.where(hit, probabilities, 0.0), axis=0, keepdims=True) for hit in hits]
    both = picked[0] + picked[1]
    gates = [p / both for p in picked]
    gate = jnp.where(hits[0], gates[0], jnp.where(hits[1], gates[1], 0.0))
    gate_ref[...] = gate
    gate_all[me] = gate
    small(gate_ref, gate_all, 1)

    first_count = jnp.sum(jnp.where(hits[0], 1.0, 0.0), axis=1, keepdims=True)
    who = lax.broadcasted_iota(jnp.int32, hits[0].shape, 0).astype(FULL)
    slots = [
        jnp.sum(jnp.where(hits[0], ranks[0] + who * SLOTS, 0.0), axis=0, keepdims=True),
        jnp.sum(
            jnp.where(hits[1], ranks[1] + first_count + who * SLOTS, 0.0), axis=0, keepdims=True
        ),
    ]
    routes_f = routes_ref[...].astype(FULL)
    token_rows = jnp.concatenate(slots + gates + [routes_f[0:1], routes_f[1:2]] + slots, axis=0)
    token_ref[...] = jnp.transpose(token_rows)

    small_arrived(meta_all, 0)
    value = meta_all[:, me, :]
    is_first = (value >= 0.0) & (value < SECOND)
    is_second = value >= SECOND
    counts = [
        jnp.sum(jnp.where(hit, 1.0, 0.0), axis=1, keepdims=True) for hit in (is_first, is_second)
    ]
    row = lax.broadcasted_iota(jnp.int32, (experts, 128), 0)
    lane = lax.broadcasted_iota(jnp.int32, (experts, 128), 1)
    count_mat = jnp.where(lane == 0, counts[0], jnp.where(lane == 1, counts[1], 0.0))
    before = jnp.zeros((experts, 128), FULL)
    for s in range(experts):
        before = before + jnp.where(row > s, count_mat[s : s + 1, :], 0.0)
    first_total = jnp.sum(counts[0], axis=0, keepdims=True)
    base = [before[:, 0:1], before[:, 1:2] + first_total]
    pos_ref[...] = jnp.where(
        is_first, value + base[0], jnp.where(is_second, value - SECOND + base[1], -1.0)
    )
    info_ref[...] = jnp.where(
        lane == 0,
        counts[0],
        jnp.where(lane == 1, counts[1], jnp.where(lane == 2, base[0], base[1])),
    )

    accs = (cotrows_ref, rows_ref)

    def compact(which, mask):
        slot = lax.bitwise_xor(me, mask)
        acc = accs[which]

        @pl.loop(0, acc.shape[0] // ROW_TILE)
        def _(tile):
            row0 = pl.multiple_of(tile * ROW_TILE, ROW_TILE)
            here = pl.ds(row0, ROW_TILE)
            place = pos_ref[pl.ds(slot, 1), :] - row0.astype(FULL)
            at = lax.broadcasted_iota(jnp.int32, (ROW_TILE, seq_len), 0).astype(FULL)
            hit = at == place
            pick = jnp.where(hit, 1.0, 0.0).astype(LOW)
            data = owns[which][...] if mask == 0 else gats[which][slot]
            got = dot_nn(pick, data).astype(LOW)
            if mask:
                got = got + acc[here, :]
            acc[here, :] = got
            if which == 1:
                gates_here = jnp.where(hit, gate_all[slot, pl.ds(me, 1), :], 0.0)
                part = gates_here[:, 0:128]
                for i in range(1, seq_len // 128):
                    part = part + gates_here[:, i * 128 : i * 128 + 128]
                if mask:
                    part = part + acc_g[here, :]
                acc_g[here, :] = part

    def forward(which, mask, waits=(0, 1)):
        for chunk in waits:
            arrived(which, mask, chunk)
        for chunk in range(2):
            go(which, 3 + mask // 2, chunk, mask, 1)

    def take(which, mask):
        for chunk in range(2):
            arrived(which, mask, chunk)
        compact(which, mask)

    relay(0, 0)
    relay(0, 1)
    forward(0, 2, (1,))
    forward(0, 4, (0,))
    compact(0, 0)
    take(0, 1)
    compact(0, 2)
    compact(0, 4)
    take(0, 3)
    take(0, 5)
    relay(1, 0)
    relay(1, 1)
    small_arrived(gate_all, 1)
    compact(1, 0)
    take(1, 1)
    forward(1, 2, (1,))
    compact(1, 2)
    forward(1, 4, (0,))
    compact(1, 4)
    forward(0, 6)
    compact(0, 6)
    take(0, 7)
    own_copy(5).start()
    take(1, 3)
    take(1, 5)
    forward(1, 6)
    compact(1, 6)
    take(1, 7)
    own_copy(6).start()

    capacity = rows_ref.shape[0]
    tiles = gout_out.shape[0]

    def experts_first(act_v, slope_v, gout_v):
        def tile_copies(tile):
            return [
                pltpu.make_async_copy(src.at[tile], dst, tile_sem.at[kind, tile])
                for kind, (src, dst) in enumerate(
                    (
                        (act_v, act_out.at[tile]),
                        (slope_v, slope_out.at[tile]),
                        (gout_v, gout_out.at[tile]),
                    )
                )
            ]

        win_load().wait()

        def scaled(row0):
            rows = pl.ds(pl.multiple_of(row0, ROW_TILE), ROW_TILE)
            gate_col = jnp.sum(acc_g[rows, :], axis=1, keepdims=True)
            gatecol_ref[rows, :] = jnp.broadcast_to(gate_col, (ROW_TILE, 128))
            resg = gate_col * cotrows_ref[rows, :].astype(FULL)
            resgt_ref[:, rows] = jnp.transpose(resg.astype(LOW))

        parts = capacity // ROW_TILE

        @pl.loop(0, tiles)
        def _(tile):
            cols = pl.ds(pl.multiple_of(tile * THIRDS * FF_TILE, FF_TILE), FF_TILE)
            for row0 in range(0, capacity, ROW_TILE):
                here = slice(row0, row0 + ROW_TILE)
                act, slope = gelu_and_slope(dot_nn(rows_ref[here, :], win_v[:, cols]))
                act_v[tile, here, :] = act.astype(LOW)
                slope_v[tile, here, :] = slope.astype(LOW)
            scaled(tile * ROW_TILE)
            for copy in tile_copies(tile)[:2]:
                copy.start()

        for part in range(tiles, parts):
            scaled(part * ROW_TILE)
        own_copy(7).start()
        own_copy(8).start()

        @pl.loop(0, tiles)
        def _(tile):
            gout_v[tile] = dot_nn(resgt_ref[...], act_v[tile]).astype(LOW)
            tile_copies(tile)[2].start()

        @pl.loop(0, tiles)
        def _(tile):
            for copy in tile_copies(tile):
                copy.wait()

    pl.run_scoped(
        experts_first,
        pltpu.VMEM((tiles, capacity, FF_TILE), LOW),
        pltpu.VMEM((tiles, capacity, FF_TILE), LOW),
        pltpu.VMEM((tiles, width, FF_TILE), LOW),
    )

    for index in range(9):
        own_copy(index).wait()
    for copy in started:
        copy().wait_send()


def attn_dispatch(
    tokens, cot, gain1, wqkv, wproj, table, gain2, wrouter, routes, priority, span, w_in, groups
):
    seq_len, width = tokens.shape
    buckets, heads = table.shape
    experts = wrouter.shape[1]
    capacity = 5 * seq_len // 2
    ff = w_in.shape[1]
    sds = jax.ShapeDtypeStruct
    dma = pltpu.SemaphoreType.DMA
    return pl.pallas_call(
        attn_dispatch_kernel,
        out_shape=(
            sds((seq_len, 3 * width), LOW),
            sds((heads, seq_len, seq_len), LOW),
            sds((seq_len, width), LOW),
            sds((seq_len, width), FULL),
            sds((seq_len, width), LOW),
            sds((capacity, width), LOW),
            sds((capacity, width), LOW),
            sds((capacity, 128), FULL),
            sds((seq_len, 8), FULL),
            sds((experts, 128), FULL),
            sds((width, capacity), LOW),
            sds((groups, capacity, FF_TILE), LOW),
            sds((groups, capacity, FF_TILE), LOW),
            sds((groups, width, FF_TILE), LOW),
        ),
        in_specs=[VM] * 3 + [HBM] * 2 + [VM] * 6 + [SM, HBM],
        out_specs=[HBM] * 8 + [VM] * 2 + [HBM] * 4,
        scratch_shapes=[
            pltpu.VMEM((seq_len, 3 * width), LOW),
            pltpu.VMEM((heads, seq_len, seq_len), LOW),
            pltpu.VMEM((seq_len, width), LOW),
            pltpu.VMEM((seq_len, width), FULL),
            pltpu.VMEM((seq_len, width), LOW),
            pltpu.VMEM((experts, seq_len), FULL),
            pltpu.VMEM((experts, seq_len), FULL),
            pltpu.VMEM((experts, experts, seq_len), FULL),
            pltpu.VMEM((experts, experts, seq_len), FULL),
            pltpu.VMEM((experts, seq_len, width), LOW),
            pltpu.VMEM((experts, seq_len, width), LOW),
            pltpu.VMEM((capacity, 128), FULL),
            pltpu.VMEM((experts, seq_len), FULL),
            pltpu.VMEM(w_in.shape, LOW),
            pltpu.VMEM((capacity, width), LOW),
            pltpu.VMEM((capacity, width), LOW),
            pltpu.VMEM((capacity, 128), FULL),
            pltpu.VMEM((width, capacity), LOW),
            dma((2, 7, 2)),
            dma((2, 8, 2)),
            dma((2, 8)),
            dma((2, 8)),
            dma((9,)),
            dma((3,)),
            dma((3, groups)),
        ],
        compiler_params=pltpu.CompilerParams(
            vmem_limit_bytes=60 * MIB, collective_id=0, has_side_effects=True
        ),
    )(
        tokens,
        cot,
        gain1,
        wqkv,
        wproj,
        table.T,
        jnp.asarray(near_onehot(buckets)),
        gain2,
        wrouter.T,
        routes.T,
        priority,
        span,
        w_in,
    )


def gelu_and_slope(x):
    c = math.sqrt(2.0 / math.pi)
    square = x * x
    s = 0.5 * jnp.tanh(x * (c + (c * 0.044715) * square)) + 0.5
    act = x * s
    return act, s + act * (1.0 - s) * (2.0 * c + (6.0 * c * 0.044715) * square)


def pack_rows(source, info_ref, data, slots):
    info = info_ref[pl.ds(source, 1), :]
    slot = lax.broadcasted_iota(jnp.int32, (slots, 1), 0).astype(FULL)
    n0, n1, b0, b1 = [info[:, i : i + 1] for i in range(4)]
    place = jnp.where(slot < n0, b0 + slot, jnp.where(slot < n0 + n1, b1 + slot - n0, -1.0))
    at = lax.broadcasted_iota(jnp.int32, (slots, data.shape[0]), 1).astype(FULL)
    pick = jnp.where(at == place, 1.0, 0.0).astype(LOW)
    return dot_nn(pick, data[...]).astype(LOW)


def expert_kernel(
    cot_ref,
    gate_ref,
    rows_ref,
    info_ref,
    resgt_hbm,
    act_ref,
    slope_ref,
    outer_ref,
    wout_ref,
    win_ref,
    recv_ref,
    packed_ref,
    gin_ref,
    gout_ref,
    early_up,
    early_down,
    up_in,
    down_in,
    act_v,
    slope_v,
    wout_v,
    win_v,
    ig_v,
    acc_ref,
    gg_ref,
    data_ref,
    send_ref,
    turned,
    gin_v,
    outer_v,
    fold_ref,
    took_ref,
    total_ref,
    packed_v,
    gout_v,
    load_sem,
    act_sem,
    slope_sem,
    outer_sem,
    gin_sem,
    own_sem,
    took_sem,
    total_sem,
    send_sem,
    recv_sem,
    fold_sems,
    early_sems,
):
    g = lax.axis_index("group")
    me = lax.axis_index("expert")
    experts, slots, wide = send_ref.shape
    tiles, capacity, tile_width = act_v.shape
    width = cot_ref.shape[1]
    groups = act_ref.shape[0]
    thirds = tiles // groups
    last = groups - 1
    copies = last * thirds
    arrivals = (up_in, down_in)

    def device(mask):
        return (g, lax.bitwise_xor(me, mask))

    def load(index):
        src, dst = ((wout_ref, wout_v), (win_ref, win_v), (resgt_hbm, turned))[index]
        return pltpu.make_async_copy(src, dst, load_sem.at[index])

    def act_load(tile):
        return pltpu.make_async_copy(act_ref.at[tile], act_v.at[tile], act_sem.at[tile])

    def slope_load(tile):
        slot = lax.rem(tile, 2)
        return pltpu.make_async_copy(slope_ref.at[tile], slope_v.at[slot], slope_sem.at[slot])

    def outer_load(tile):
        return pltpu.make_async_copy(outer_ref.at[tile], outer_v.at[tile], outer_sem.at[tile])

    for tile in range(groups):
        outer_load(tile).start()
    load(0).start()
    slope_load(0).start()
    act_load(0).start()
    load(1).start()
    for tile in range(1, groups):
        act_load(tile).start()
    load(2).start()
    barrier = pltpu.get_barrier_semaphore()
    for mask in range(1, experts):
        pl.semaphore_signal(barrier, inc=1, device_id=device(mask), device_id_type=MESH)
    for step in range(1, groups):
        pl.semaphore_signal(
            barrier, inc=1, device_id=(lax.rem(g + step, groups), me), device_id_type=MESH
        )
    pl.semaphore_wait(barrier, experts - 1 + groups - 1)
    for tile in range(groups):
        outer_load(tile).wait()

    def fold_tile(way, k):
        return (k % last if way else last - k % last), k // last

    def fold_copy(way, k, src):
        shard_at, third = fold_tile(way, k)
        there = arrivals[way].at[shard_at, third]
        return pltpu.make_async_remote_copy(
            src_ref=there if src is None else src,
            dst_ref=there,
            send_sem=fold_sems.at[0, way, k],
            recv_sem=fold_sems.at[1, way, k],
            device_id=(lax.rem(g + (last if way else 1), groups), me),
            device_id_type=MESH,
        )

    def take_tile(way, src):
        return pltpu.make_async_copy(src, took_ref.at[way], took_sem.at[way])

    def fold_source(*which):
        for k in which:
            for way in range(2):
                shard_at, third = fold_tile(way, k)

                @pl.when(g == way * last)
                def _():
                    fold_copy(way, k, outer_v.at[third * groups + shard_at]).start()

    def passed(way, here):
        return [
            k
            for k in range(copies)
            if ((fold_tile(way, k)[0] < here) if way else (fold_tile(way, k)[0] > here))
        ]

    def fold_role(hop, k, act):
        for way in range(2):
            here = last - hop if way else hop
            order = passed(way, here)
            if k in order:
                pl.when(g == here)(functools.partial(act, way, k, order, order.index(k)))

    def fold_fetch(hop, k):
        def act(way, k, order, nth):
            shard_at, third = fold_tile(way, k)
            fold_copy(way, k, None).wait_recv()
            take_tile(way, arrivals[way].at[shard_at, third]).start()

        fold_role(hop, k, act)

    def fold_push(hop, k):
        def act(way, k, order, nth):
            shard_at, third = fold_tile(way, k)
            if nth >= 2:
                fold_copy(way, order[nth - 2], None).wait_send()
            take_tile(way, arrivals[way].at[shard_at, third]).wait()
            own = outer_v[third * groups + shard_at].astype(FULL)
            fold_ref[way, nth % 2] = (own + took_ref[way].astype(FULL)).astype(LOW)
            fold_copy(way, k, fold_ref.at[way, nth % 2]).start()

        fold_role(hop, k, act)

    def fold_final(third):
        total_ref[...] = outer_v[third * groups + g].astype(FULL)
        for way, (some, at) in enumerate(((g > 0, last - g), (g < last, g))):

            @pl.when(some)
            def _():
                here = arrivals[way].at[g, third]
                k = third * last + at
                pltpu.make_async_remote_copy(
                    src_ref=here,
                    dst_ref=here,
                    send_sem=fold_sems.at[0, way, k],
                    recv_sem=fold_sems.at[1, way, k],
                    device_id=(lax.rem(g + 1, groups), me),
                    device_id_type=MESH,
                ).wait_recv()
                take_tile(way, here).start()
                take_tile(way, here).wait()
                total_ref[...] += took_ref[way].astype(FULL)

        gout_v[third * tile_width : (third + 1) * tile_width, :] = jnp.transpose(total_ref[...])
        gout_copy(third).start()

    def gout_copy(third):
        here = pl.ds(third * tile_width, tile_width)
        return pltpu.make_async_copy(gout_v.at[here, :], gout_ref.at[here, :], total_sem.at[third])

    def fold_sent():
        for way in range(2):
            for k in range(copies):

                @pl.when(g == way * last)
                def _():
                    fold_copy(way, k, None).wait_send()

            for hop in range(1, last):
                here = last - hop if way else hop
                for k in passed(way, here)[-2:]:

                    @pl.when(g == here)
                    def _():
                        fold_copy(way, k, None).wait_send()

    fold_source(*range(last))
    acc_ref[...] = jnp.zeros_like(acc_ref)
    gg_ref[...] = jnp.zeros_like(gg_ref)
    for index in range(2):
        load(index).wait()

    def span(tile):
        at = lax.rem(tile, groups) * thirds + lax.div(tile, groups)
        return pl.ds(pl.multiple_of(at * tile_width, tile_width), tile_width)

    def back_tile(tile, slope_slot):
        for row0 in range(0, capacity, ROW_TILE):
            here = slice(row0, row0 + ROW_TILE)
            back = dot_nt(cot_ref[here, :], wout_v[span(tile), :])
            part = act_v[tile, here, :].astype(FULL) * back
            gg_ref[here, :] += part[:, 0:128] + part[:, 128:256]
            slope = slope_v[slope_slot, here, :].astype(FULL)
            ig_v[tile, here, :] = (slope * (gate_ref[here, 0:1] * back)).astype(LOW)
            acc_ref[here, :] += dot_nt(ig_v[tile, here, :], win_v[:, span(tile)])

    @pl.loop(0, groups)
    def _(tile):
        slope_load(tile).wait()
        act_load(tile).wait()

        @pl.when(tile + 1 < groups)
        def _():
            slope_load(tile + 1).start()

        back_tile(tile, lax.rem(tile, 2))

    load(2).wait()
    fold_fetch(1, 0)

    def own_tiles(first, count):
        @pl.loop(first, first + count)
        def _(tile):
            for row0 in range(0, capacity, ROW_TILE):
                here = slice(row0, row0 + ROW_TILE)
                act, slope = gelu_and_slope(dot_nn(rows_ref[here, :], win_v[:, span(tile)]))
                act_v[tile, here, :] = act.astype(LOW)
                slope_v[0, here, :] = slope.astype(LOW)
            outer_v[tile] = dot_nn(turned[...], act_v[tile]).astype(LOW)
            back_tile(tile, 0)

    own_tiles(groups, 2)
    fold_push(1, 0)
    own_tiles(groups + 2, groups - 2)
    fold_source(*range(last, 2 * last))
    fold_fetch(1, 1)
    own_tiles(2 * groups, 2)
    fold_push(1, 1)
    fold_fetch(1, 2)
    fold_fetch(2, 0)
    own_tiles(2 * groups + 2, groups - 2)
    fold_source(*range(2 * last, 3 * last))
    fold_push(1, 2)
    fold_push(2, 0)

    data_ref[:, :width] = acc_ref[...].astype(LOW)
    gg = jnp.sum(gg_ref[...], axis=1, keepdims=True)
    hi, mid, low = [t.astype(FULL) for t in split3(gg)]
    lane = lax.broadcasted_iota(jnp.int32, (capacity, 128), 1)
    data_ref[:, width:] = jnp.where(
        lane == 0, hi, jnp.where(lane == 1, mid, jnp.where(lane == 2, low, 0.0))
    ).astype(LOW)

    def exchange(mask):
        return pltpu.make_async_remote_copy(
            src_ref=send_ref.at[lax.bitwise_xor(me, mask)],
            dst_ref=recv_ref.at[me],
            send_sem=send_sem.at[mask],
            recv_sem=recv_sem.at[mask],
            device_id=device(mask),
            device_id_type=MESH,
        )

    for mask in (6, 7, 2, 4, 3, 5, 1):
        other = lax.bitwise_xor(me, mask)
        send_ref[other] = pack_rows(other, info_ref, data_ref, slots)
        exchange(mask).start()
        if mask == 4:
            fold_fetch(1, 3)
    send_ref[me] = pack_rows(me, info_ref, data_ref, slots)
    own_rows = pltpu.make_async_copy(send_ref.at[me], recv_ref.at[me], own_sem)
    own_rows.start()
    fold_push(1, 3)
    fold_fetch(1, 4)

    turned[...] = jnp.transpose(rows_ref[...])

    def gin_copy(tile):
        slot = lax.rem(tile, 2)
        cols = pl.ds(pl.multiple_of(lax.div(tile, groups) * tile_width, tile_width), tile_width)
        return pltpu.make_async_copy(
            gin_v.at[slot], gin_ref.at[:, lax.rem(tile, groups), :, cols], gin_sem.at[slot]
        )

    def gin_tiles(first, count):
        @pl.loop(first, first + count)
        def _(tile):
            @pl.when(tile >= 2)
            def _():
                gin_copy(tile).wait()

            got = dot_nn(turned[...], ig_v[tile]).astype(LOW)
            gin_v[lax.rem(tile, 2)] = got.reshape(gin_v.shape[1:])
            gin_copy(tile).start()

    gin_tiles(0, tiles // 2)
    fold_push(1, 4)
    gin_tiles(tiles // 2, tiles // 2)
    fold_fetch(1, 5)
    fold_fetch(2, 3)

    acc_ref[...] = jnp.zeros_like(acc_ref)

    def result_tiles(first, count):
        @pl.loop(first, first + count)
        def _(tile):
            for row0 in range(0, capacity, ROW_TILE):
                here = slice(row0, row0 + ROW_TILE)
                acc_ref[here, :] += dot_nn(act_v[tile, here, :], wout_v[span(tile), :])

    result_tiles(0, tiles // 2)
    fold_push(1, 5)
    fold_push(2, 3)
    result_tiles(tiles // 2, tiles // 2)
    fold_fetch(1, 6)
    gin_copy(0).wait()
    gin_copy(1).wait()

    def early_copy(way, k):
        return pltpu.make_async_remote_copy(
            src_ref=gin_ref.at[0 if way else last, k],
            dst_ref=(early_up, early_down)[way].at[k],
            send_sem=early_sems.at[0, way, k],
            recv_sem=early_sems.at[1, way, k],
            device_id=(lax.rem(g + (last if way else 1), groups), me),
            device_id_type=MESH,
        )

    def early_each(act):
        for way in range(2):
            for k in range(EARLY):
                act(way, k)

    def early_start(way, k):
        @pl.when(g == way * last)
        def _():
            early_copy(way, k).start()

    def early_end(way, k):
        @pl.when(g == way * last)
        def _():
            early_copy(way, k).wait_send()

        @pl.when(g == (last - 1 if way else 1))
        def _():
            early_copy(way, k).wait_recv()

    early_each(early_start)
    data_ref[:, :width] = acc_ref[...].astype(LOW)

    @pl.loop(0, experts)
    def _(source):
        packed_v[source] = pack_rows(source, info_ref, data_ref.at[:, 0:width], slots)

    packed_copy = pltpu.make_async_copy(packed_v, packed_ref, total_sem.at[thirds])
    packed_copy.start()
    fold_push(1, 6)
    fold_final(0)
    fold_fetch(1, 7)
    fold_push(1, 7)
    fold_fetch(2, 6)
    fold_push(2, 6)
    fold_final(1)
    fold_fetch(1, 8)
    fold_push(1, 8)
    fold_final(2)
    packed_copy.wait()
    for third in range(thirds):
        gout_copy(third).wait()
    own_rows.wait()
    for mask in range(1, experts):
        exchange(mask).wait()
    fold_sent()
    early_each(early_end)


def expert_call(cot_rows, gate_col, rows, info, resg_t, act, slope, outer, w_out, w_in):
    capacity, width = cot_rows.shape
    groups, _, tile_width = act.shape
    ff = w_in.shape[1]
    tiles = ff // tile_width
    experts = info.shape[0]
    sds = jax.ShapeDtypeStruct
    dma = pltpu.SemaphoreType.DMA
    early = sds((EARLY, width // groups, ff // groups), LOW)
    arrival = sds((groups, tiles // groups, width, tile_width), LOW)
    outs = pl.pallas_call(
        expert_kernel,
        out_shape=(
            sds((experts, SLOTS, width + 128), LOW),
            sds((experts, SLOTS, width), LOW),
            sds((groups, groups, width // groups, ff // groups), LOW),
            sds((ff // groups, width), FULL),
            early,
            early,
            arrival,
            arrival,
        ),
        in_specs=[VM] * 4 + [HBM] * 6,
        out_specs=[HBM] * 8,
        scratch_shapes=[
            pltpu.VMEM((tiles, capacity, tile_width), LOW),
            pltpu.VMEM((2, capacity, tile_width), LOW),
            pltpu.VMEM(w_out.shape, LOW),
            pltpu.VMEM(w_in.shape, LOW),
            pltpu.VMEM((tiles, capacity, tile_width), LOW),
            pltpu.VMEM((capacity, width), FULL),
            pltpu.VMEM((capacity, 128), FULL),
            pltpu.VMEM((capacity, width + 128), LOW),
            pltpu.VMEM((experts, SLOTS, width + 128), LOW),
            pltpu.VMEM((width, capacity), LOW),
            pltpu.VMEM((2, groups, width // groups, tile_width), LOW),
            pltpu.VMEM((tiles, width, tile_width), LOW),
            pltpu.VMEM((2, 2, width, tile_width), LOW),
            pltpu.VMEM((2, width, tile_width), LOW),
            pltpu.VMEM((width, tile_width), FULL),
            pltpu.VMEM((experts, SLOTS, width), LOW),
            pltpu.VMEM((ff // groups, width), FULL),
            dma((3,)),
            dma((groups,)),
            dma((2,)),
            dma((groups,)),
            dma((2,)),
            dma,
            dma((2,)),
            dma((tiles // groups + 1,)),
            dma((experts,)),
            dma((experts,)),
            dma((2, 2, (groups - 1) * (tiles // groups))),
            dma((2, 2, EARLY)),
        ],
        compiler_params=pltpu.CompilerParams(
            vmem_limit_bytes=62 * MIB, collective_id=2, has_side_effects=True
        ),
        cost_estimate=pl.CostEstimate(
            flops=12 * capacity * width * ff, bytes_accessed=50 * MIB, transcendentals=0
        ),
    )(cot_rows, gate_col, rows, info, resg_t, act, slope, outer, w_out, w_in)
    return outs[:6]


def attn_back_kernel(
    tokens_ref,
    cot_ref,
    hidden_ref,
    normed2_ref,
    mixed_ref,
    qkv_hbm,
    prob_hbm,
    recv_ref,
    token_ref,
    gain1_ref,
    gain2_ref,
    wqkv_hbm,
    wproj_ref,
    wrouter_ref,
    onehot_ref,
    result_ref,
    gin_ref,
    early_up,
    early_down,
    block_ref,
    gtok_ref,
    dense_out,
    small_out,
    gin_out,
    up_in,
    down_in,
    hgrad_ref,
    mgrad_ref,
    mgrad_t,
    normed_t,
    q_t,
    ds_ref,
    diag_ref,
    dk_t,
    dv_t,
    dqkv_ref,
    part_ref,
    pair_in,
    chip_ref,
    plane_in,
    plane_ref,
    group_in,
    small_ref,
    small_in,
    small_plane,
    small_group,
    qkv_ref,
    prob_ref,
    wqkv_ref,
    back_ref,
    fold_ref,
    took_ref,
    total_ref,
    fold_sems,
    took_sems,
    total_sems,
    load_sems,
    back_sems,
    pair_sems,
    plane_sems,
    group_sems,
    final_sems,
    small_sems,
    smallz_sems,
):
    seq_len, width = tokens_ref.shape
    experts = wrouter_ref.shape[0]
    chunks = part_ref.shape[0]
    groups = group_in.shape[1]
    tile = 128
    g = lax.axis_index("group")
    me = lax.axis_index("expert")
    parity = lax.rem(me, 2)
    mine = lax.div(me, 2)
    summer = [groups // 2 - 1 + c % 2 for c in range(chunks)]

    def device(mask):
        return (g, lax.bitwise_xor(me, mask))

    def load(index):
        src, dst = ((qkv_hbm, qkv_ref), (prob_hbm, prob_ref), (wqkv_hbm, wqkv_ref))[index]
        return pltpu.make_async_copy(src, dst, load_sems.at[index])

    own_result = pltpu.make_async_copy(result_ref.at[me], back_ref.at[me], load_sems.at[3])
    for index in range(3):
        load(index).start()
    own_result.start()
    barrier = pltpu.get_barrier_semaphore()
    for mask in range(1, experts):
        pl.semaphore_signal(barrier, inc=1, device_id=device(mask), device_id_type=MESH)
    for step in range(1, groups):
        pl.semaphore_signal(
            barrier, inc=1, device_id=(lax.rem(g + step, groups), me), device_id_type=MESH
        )
    pl.semaphore_wait(barrier, experts - 1 + groups - 1)

    def remote(src, dst, sems, at, where):
        return pltpu.make_async_remote_copy(
            src_ref=src,
            dst_ref=dst,
            send_sem=sems.at[(0, *at)],
            recv_sem=sems.at[(1, *at)],
            device_id=where,
            device_id_type=MESH,
        )

    started = []

    def go(copy):
        copy.start()
        started.append(copy)

    def result_copy(mask):
        other = lax.bitwise_xor(me, mask)
        return remote(result_ref.at[other], back_ref.at[me], back_sems, (mask,), device(mask))

    for mask in (2, 4, 3, 5, 1):
        result_copy(mask).start()

    def pair_send(c):
        for chip in range(experts // 2):
            other = 2 * chip + 1 - parity
            go(remote(part_ref.at[c, other], pair_in.at[c, chip], pair_sems, (c, chip), device(1)))

    def plane_send(c):
        for chip in range(experts // 2):
            remote(
                part_ref.at[c, 0], pair_in.at[c, chip], pair_sems, (c, chip), device(1)
            ).wait_recv()
            total = part_ref[c, 2 * chip + parity].astype(FULL) + pair_in[c, chip].astype(FULL)
            chip_ref[c, chip] = total.astype(LOW)
        for other in range(1, experts // 2):
            go(
                remote(
                    chip_ref.at[c, lax.bitwise_xor(mine, other)],
                    plane_in.at[c, other - 1],
                    plane_sems,
                    (c, other - 1),
                    device(2 * other),
                )
            )

    def group_send(c):
        total = chip_ref[c, mine].astype(FULL)
        for other in range(1, experts // 2):
            remote(
                chip_ref.at[c, 0],
                plane_in.at[c, other - 1],
                plane_sems,
                (c, other - 1),
                device(2 * other),
            ).wait_recv()
            total = total + plane_in[c, other - 1].astype(FULL)
        plane_ref[c] = total.astype(LOW)

        @pl.when(g != summer[c])
        def _():
            remote(
                plane_ref.at[c], group_in.at[c, g], group_sems, (c, g), (jnp.int32(summer[c]), me)
            ).start()

    def final_send(c):
        @pl.when(g == summer[c])
        def _():
            total = plane_ref[c].astype(FULL)
            for step in range(1, groups):
                src = lax.rem(g + step, groups)
                remote(
                    plane_ref.at[c], group_in.at[c, src], group_sems, (c, src), (src, me)
                ).wait_recv()
                total = total + group_in[c, src].astype(FULL)
            dense_out[c] = total.astype(LOW)
            for step in range(1, groups):
                where = (lax.rem(g + step, groups), me)
                remote(dense_out.at[c], dense_out.at[c], final_sems, (c, step - 1), where).start()

    def finish(c):
        where = (lax.rem(g + 1, groups), me)
        for step in range(1, groups):
            copy = remote(dense_out.at[c], dense_out.at[c], final_sems, (c, step - 1), where)

            @pl.when(g == summer[c])
            def _():
                copy.wait_send()

            @pl.when(lax.rem(summer[c] + step, groups) == g)
            def _():
                copy.wait_recv()

        @pl.when(g != summer[c])
        def _():
            remote(plane_ref.at[c], group_in.at[c, g], group_sems, (c, g), where).wait_send()

    parts = gin_ref.shape[1]
    last = groups - 1
    copies = last * parts
    arrivals = (up_in, down_in)

    def fold_tile(way, k):
        return (k // parts if way else last - k // parts), k % parts

    def fold_copy(way, k, src):
        shard_at, tile_at = fold_tile(way, k)
        there = arrivals[way].at[shard_at, tile_at]
        step = last if way else 1
        where = (lax.rem(g + step, groups), me)
        return pltpu.make_async_remote_copy(
            src_ref=there if src is None else src,
            dst_ref=there,
            send_sem=fold_sems.at[0, way, k],
            recv_sem=fold_sems.at[1, way, k],
            device_id=where,
            device_id_type=MESH,
        )

    def take_tile(way, which, src):
        return pltpu.make_async_copy(src, took_ref.at[way, which], took_sems.at[way, which])

    def fold_source(k):
        for way in range(2):

            @pl.when(g == way * last)
            def _():
                fold_copy(way, k, gin_ref.at[fold_tile(way, k)]).start()

    def fold_place(way, k):
        main = (g == 1) if way == 0 else (g == last - 1)
        return jnp.where(main, k, (last - 1) * parts + k)

    def fold_role(hop, k, act):
        for way in range(2):
            shard_at, tile_at = fold_tile(way, k)
            here = last - hop if way else hop
            if (shard_at < here) if way else (shard_at > here):
                pl.when(g == here)(functools.partial(act, way, k, shard_at, tile_at))

    def arrived(hop, way, k):
        if hop == 1 and k < EARLY:
            return (early_up, early_down)[way].at[k]
        return arrivals[way].at[fold_tile(way, k)]

    def fold_fetch(hop, k):
        def act(way, k, shard_at, tile_at):
            take_tile(way, 0, gin_ref.at[shard_at, tile_at]).start()
            if not (hop == 1 and k < EARLY):
                fold_copy(way, k, None).wait_recv()
            take_tile(way, 1, arrived(hop, way, k)).start()

        fold_role(hop, k, act)

    def fold_push(hop, k):
        def act(way, k, shard_at, tile_at):
            take_tile(way, 0, gin_ref.at[shard_at, tile_at]).wait()
            take_tile(way, 1, arrived(hop, way, k)).wait()
            place = fold_place(way, k)
            total = took_ref[way, 0].astype(FULL) + took_ref[way, 1].astype(FULL)
            fold_ref[place] = total.astype(LOW)
            fold_copy(way, k, fold_ref.at[place]).start()

        fold_role(hop, k, act)

    def fold_final(tile_at):
        own = take_tile(0, 0, gin_ref.at[g, tile_at])
        own.start()
        cases = ((g > 0, up_in, (last - g) * parts + tile_at), (g < last, down_in, g * parts + tile_at))
        for way, (some, arrival, k) in enumerate(cases):

            @pl.when(some)
            def _():
                here = arrival.at[g, tile_at]
                pltpu.make_async_remote_copy(
                    src_ref=here,
                    dst_ref=here,
                    send_sem=fold_sems.at[0, way, k],
                    recv_sem=fold_sems.at[1, way, k],
                    device_id=(lax.rem(g + 1, groups), me),
                    device_id_type=MESH,
                ).wait_recv()
                take_tile(way, 1, here).start()

        own.wait()
        if tile_at >= 2:
            final_copy(tile_at - 2).wait()
        total_ref[tile_at % 2] = took_ref[0, 0].astype(FULL)
        for way, (some, arrival, k) in enumerate(cases):

            @pl.when(some)
            def _():
                take_tile(way, 1, arrival.at[g, tile_at]).wait()
                total_ref[tile_at % 2] += took_ref[way, 1].astype(FULL)

        final_copy(tile_at).start()

    def final_copy(tile_at):
        cols = pl.ds(tile_at * total_ref.shape[2], total_ref.shape[2])
        return pltpu.make_async_copy(
            total_ref.at[tile_at % 2], gin_out.at[:, cols], total_sems.at[tile_at % 2]
        )

    def fold_sent():
        for way in range(2):
            for k in range(copies):
                shard_at, _ = fold_tile(way, k)
                sends = (g > shard_at) if way else (g < shard_at)
                if k < EARLY:
                    sends = sends & (g != way * last)

                @pl.when(sends)
                def _():
                    fold_copy(way, k, None).wait_send()

    for k in range(EARLY, EARLY + 3):
        fold_source(k)
    fold_fetch(1, 0)
    ggain2 = jnp.zeros((8, width), FULL)
    lg_t = []
    for row0 in range(0, seq_len, tile):
        rows = slice(row0, row0 + tile)
        token = token_ref[rows, :]
        at = lax.broadcasted_iota(jnp.int32, (tile, recv_ref.shape[0]), 1).astype(FULL)
        picks = [jnp.where(at == token[:, k : k + 1], 1.0, 0.0).astype(LOW) for k in range(2)]
        got = dot_nn(jnp.concatenate(picks, axis=0), recv_ref[...])
        gg = [
            jnp.sum(got[k * tile : k * tile + tile, width:], axis=1, keepdims=True) for k in range(2)
        ]
        pull = token[:, 2:3] * token[:, 3:4] * (gg[0] - gg[1])
        expert = lax.broadcasted_iota(jnp.int32, (tile, 128), 1).astype(FULL)
        lg = jnp.where(expert == token[:, 4:5], pull, jnp.where(expert == token[:, 5:6], -pull, 0.0))
        lg_t.append(jnp.transpose(lg)[:experts])
        ngrad = (
            got[:tile, :width]
            + got[tile:, :width]
            + dot_nn(lg[:, :experts].astype(LOW), wrouter_ref[...])
        )
        hidden = hidden_ref[rows, :]
        inv = lax.rsqrt(jnp.mean(hidden * hidden, axis=1, keepdims=True) + EPS)
        unit = hidden * inv
        ng = ngrad * unit
        for i in range(tile // 8):
            ggain2 = ggain2 + ng[i * 8 : i * 8 + 8]
        scaled = ngrad * gain2_ref[...][None, :]
        proj = jnp.mean(scaled * unit, axis=1, keepdims=True)
        hgrad = cot_ref[rows, :].astype(FULL) + inv * (scaled - unit * proj)
        hgrad_ref[rows, :] = hgrad
        mgrad_ref[rows, :] = dot_nt(hgrad.astype(LOW), wproj_ref[...]).astype(LOW)
        x = tokens_ref[rows, :].astype(FULL)
        inv = lax.rsqrt(jnp.mean(x * x, axis=1, keepdims=True) + EPS)
        dqkv_ref[rows, :width] = (x * inv * gain1_ref[...][None, :]).astype(LOW)
        if row0 == tile:
            fold_source(5)
            fold_push(1, 0)
            fold_fetch(1, 1)
        if row0 == 3 * tile:
            fold_source(6)
            fold_push(1, 1)
            fold_fetch(1, 2)
    ggain2 = jnp.sum(ggain2, axis=0, keepdims=True)
    logit_grad_t = jnp.concatenate(lg_t, axis=1).astype(LOW)
    grouter = dot_nn(logit_grad_t, normed2_ref[...])
    normed_t[...] = jnp.transpose(dqkv_ref[:, :width])
    part_ref[0] = (
        dot_nn(jnp.transpose(mixed_ref[...]), hgrad_ref[...].astype(LOW))
        .astype(LOW)
        .reshape(experts, width // experts, width)
    )
    pair_send(0)
    fold_push(1, 2)
    fold_fetch(1, 3)
    fold_fetch(2, 0)
    mgrad_t[...] = jnp.transpose(mgrad_ref[...])
    load(0).wait()
    q_t[...] = jnp.transpose(qkv_ref[:, :width])
    load(1).wait()
    up = lax.broadcasted_iota(jnp.int32, (128, 128), 0)
    across = lax.broadcasted_iota(jnp.int32, (128, 128), 1)
    flip = jnp.where(up + across == 127, 1.0, 0.0).astype(FULL)

    def heads_back(pair):
        col = pl.multiple_of(pair * 128, 128)
        kp = qkv_ref[:, pl.ds(width + col, 128)]
        vp = qkv_ref[:, pl.ds(2 * width + col, 128)]
        op = mgrad_ref[:, pl.ds(col, 128)].astype(FULL)
        os = jnp.concatenate([(op * half_mask(sub, 1.0)).astype(LOW) for sub in range(2)], axis=0)
        dp = dot_nt(os, vp)
        for sub in range(2):
            h = 2 * pair + sub
            near = jnp.zeros((128, 384), FULL)
            far_neg = jnp.zeros((128, 128), FULL)
            far_pos = jnp.zeros((128, 128), FULL)
            blocks = seq_len // 128
            for block in range(blocks):
                first = sub * seq_len + block * 128
                here = slice(block * 128, block * 128 + 128)
                p = prob_ref[h, here, :].astype(FULL)
                weighted = p * dp[first : first + 128]
                ds = weighted - p * jnp.sum(weighted, axis=1, keepdims=True)
                low = ds.astype(LOW)
                ds_ref[sub, here, :] = low
                ds = low.astype(FULL)
                strip = []
                for d in range(-1, 2):
                    other = block + d
                    if 0 <= other < blocks:
                        strip.append(ds[:, other * 128 : other * 128 + 128])
                    else:
                        strip.append(jnp.zeros((128, 128), FULL))
                near = near + jnp.concatenate(strip, axis=1)
                for other in range(blocks):
                    piece = ds[:, other * 128 : other * 128 + 128]
                    if other - block <= -2:
                        far_neg = far_neg + piece
                    elif other - block >= 2:
                        far_pos = far_pos + piece
            low_sum = jnp.sum(far_neg)
            high_sum = jnp.sum(far_pos)
            padded = jnp.concatenate([exact_nn(flip, near), jnp.zeros((128, 128), FULL)], axis=1)
            turned = pltpu.roll(padded, 1, 1, stride=1, stride_axis=0)
            sums = jnp.sum(turned, axis=0, keepdims=True)
            lane = lax.broadcasted_iota(jnp.int32, (1, 512), 1)
            sums = sums + jnp.where(lane == 1, low_sum, jnp.where(lane == 511, high_sum, 0.0))
            diag_ref[pl.ds(h, 1), :] = sums
        lane = lax.broadcasted_iota(jnp.int32, (seq_len, 128), 1)
        dq = dot_nn(jnp.concatenate([ds_ref[0], ds_ref[1]], axis=0), kp)
        dqkv_ref[:, pl.ds(col, 128)] = (
            jnp.where(lane < 64, dq[:seq_len], dq[seq_len:]) * 0.125
        ).astype(LOW)
        for sub in range(2):
            part = pl.ds(pl.multiple_of(col + sub * 64, 64), 64)
            dk_t[part, :] = (dot_nn(q_t[part, :], ds_ref[sub]) * 0.125).astype(LOW)
            dv_t[part, :] = dot_nn(mgrad_t[part, :], prob_ref[2 * pair + sub]).astype(LOW)

    stripe = width // (chunks - 1)
    for c in range(1, chunks):
        pairs = stripe // 128

        @pl.loop((c - 1) * pairs, c * pairs)
        def _(pair):
            heads_back(pair)

        col = (c - 1) * stripe
        dqkv_ref[:, width + col : width + col + stripe] = jnp.transpose(dk_t[col : col + stripe, :])
        dqkv_ref[:, 2 * width + col : 2 * width + col + stripe] = jnp.transpose(
            dv_t[col : col + stripe, :]
        )
        for third in range(3):
            here = third * width + col
            part_ref[c, :, :, third * stripe : third * stripe + stripe] = (
                dot_nn(normed_t[...], dqkv_ref[:, here : here + stripe])
                .astype(LOW)
                .reshape(experts, width // experts, stripe)
            )
        pair_send(c)
        plane_send(c - 1)
        if c >= 2:
            group_send(c - 2)
        fold_push(1, c + 2)
        fold_push(2, c - 1)
        fold_source(c + 6)
        fold_fetch(1, c + 3)
        fold_fetch(2, c)

    load(2).wait()
    ggain1 = jnp.zeros((8, width), FULL)
    for row0 in range(0, seq_len, tile):
        rows = slice(row0, row0 + tile)
        x = tokens_ref[rows, :].astype(FULL)
        inv = lax.rsqrt(jnp.mean(x * x, axis=1, keepdims=True) + EPS)
        unit = x * inv
        ngrad = dot_nt(dqkv_ref[rows, :], wqkv_ref[...])
        ng = ngrad * unit
        for i in range(tile // 8):
            ggain1 = ggain1 + ng[i * 8 : i * 8 + 8]
        scaled = ngrad * gain1_ref[...][None, :]
        proj = jnp.mean(scaled * unit, axis=1, keepdims=True)
        gtok_ref[rows, :] = (hgrad_ref[rows, :] + inv * (scaled - unit * proj)).astype(LOW)
        if row0 == 0:
            plane_send(chunks - 1)
            for mask in (6, 7):
                result_copy(mask).start()
            fold_push(2, 3)
        if row0 == 2 * tile:
            fold_push(1, 6)
    ggain1 = jnp.sum(ggain1, axis=0, keepdims=True)

    gtable = exact_nt(onehot_ref[...], diag_ref[...])
    shard = width // experts
    per = gtable.shape[0] // experts
    for e in range(experts):
        cols = slice(e * shard, e * shard + shard)
        block = jnp.concatenate([ggain1[:, cols], ggain2[:, cols], grouter[:, cols]], axis=0)
        small_ref[e] = jnp.zeros(small_ref.shape[1:], FULL)
        small_ref[e, 0 : 2 + experts, 0:shard] = block
        small_ref[e, 2 + experts : 2 + experts + per, 0 : gtable.shape[1]] = gtable[
            e * per : e * per + per
        ]
    for mask in range(1, experts):
        other = lax.bitwise_xor(me, mask)
        go(remote(small_ref.at[other], small_in.at[mask], small_sems, (mask,), device(mask)))
    final_send(0)
    group_send(2)
    fold_fetch(1, 7)
    total = small_ref[me]
    for mask in range(1, experts):
        remote(
            small_ref.at[0], small_in.at[mask], small_sems, (mask,), device(mask)
        ).wait_recv()
        total = total + small_in[mask]
    small_plane[...] = total
    for step in range(1, groups):
        where = (lax.rem(g + step, groups), me)
        go(remote(small_plane, small_group.at[step], smallz_sems, (step,), where))
    fold_push(1, 7)
    final_send(1)
    group_send(3)
    fold_source(10)
    fold_source(11)
    own_result.wait()
    for mask in range(1, experts):
        result_copy(mask).wait()

    @pl.loop(0, seq_len // tile)
    def _(step):
        rows = pl.ds(pl.multiple_of(step * tile, tile), tile)
        token = token_ref[rows, :]
        at = lax.broadcasted_iota(jnp.int32, (tile, experts * SLOTS), 1).astype(FULL)
        picks = [jnp.where(at == token[:, k : k + 1], 1.0, 0.0).astype(LOW) for k in range(2)]
        got = dot_nn(
            jnp.concatenate(picks, axis=0), back_ref[...].reshape(experts * SLOTS, width)
        )
        block_ref[rows, :] = (
            hidden_ref[rows, :] + token[:, 2:3] * got[:tile] + token[:, 3:4] * got[tile:]
        ).astype(LOW)

    fold_final(0)
    final_send(2)
    fold_final(1)
    final_send(3)
    for tile_at in range(2, parts):
        fold_final(tile_at)
    for tile_at in range(parts - 2, parts):
        final_copy(tile_at).wait()
    for step in range(1, groups):
        remote(
            small_plane, small_group.at[step], smallz_sems, (step,), (lax.rem(g + step, groups), me)
        ).wait_recv()
        total = total + small_group[step]
    small_out[...] = total
    for c in range(chunks):
        finish(c)
    fold_sent()
    for copy in started:
        copy.wait_send()


def attn_back(
    tokens, cot, hidden, normed2, mixed, qkv, prob, recv, token, gain1, gain2, wqkv, wproj, wrouter, table, result, gin, early_up, early_down, groups
):
    seq_len, width = tokens.shape
    buckets, heads = table.shape
    experts = wrouter.shape[1]
    shard = width // experts
    chunks = groups
    chips = experts // 2
    small = (16, 128)
    sds = jax.ShapeDtypeStruct
    dma = pltpu.SemaphoreType.DMA
    outs = pl.pallas_call(
        attn_back_kernel,
        out_shape=(
            sds((seq_len, width), LOW),
            sds((seq_len, width), LOW),
            sds((chunks, shard, width), LOW),
            sds(small, FULL),
            sds((gin.shape[2], gin.shape[1] * gin.shape[3]), FULL),
            sds(gin.shape, LOW),
            sds(gin.shape, LOW),
        ),
        in_specs=[VM] * 5 + [HBM] * 2 + [VM] * 4 + [HBM] + [VM] * 3 + [HBM] * 4,
        out_specs=[VM] * 4 + [HBM] * 3,
        scratch_shapes=[
            pltpu.VMEM((seq_len, width), FULL),
            pltpu.VMEM((seq_len, width), LOW),
            pltpu.VMEM((width, seq_len), LOW),
            pltpu.VMEM((width, seq_len), LOW),
            pltpu.VMEM((width, seq_len), LOW),
            pltpu.VMEM((2, seq_len, seq_len), LOW),
            pltpu.VMEM((heads, 512), FULL),
            pltpu.VMEM((width, seq_len), LOW),
            pltpu.VMEM((width, seq_len), LOW),
            pltpu.VMEM((seq_len, 3 * width), LOW),
            pltpu.VMEM((chunks, experts, shard, width), LOW),
            pltpu.VMEM((chunks, chips, shard, width), LOW),
            pltpu.VMEM((chunks, chips, shard, width), LOW),
            pltpu.VMEM((chunks, chips - 1, shard, width), LOW),
            pltpu.VMEM((chunks, shard, width), LOW),
            pltpu.VMEM((chunks, groups, shard, width), LOW),
            pltpu.VMEM((experts, *small), FULL),
            pltpu.VMEM((experts, *small), FULL),
            pltpu.VMEM(small, FULL),
            pltpu.VMEM((groups, *small), FULL),
            pltpu.VMEM((seq_len, 3 * width), LOW),
            pltpu.VMEM((heads, seq_len, seq_len), LOW),
            pltpu.VMEM(wqkv.shape, LOW),
            pltpu.VMEM(result.shape, LOW),
            pltpu.VMEM((groups * (groups - 1), *gin.shape[2:]), LOW),
            pltpu.VMEM((2, 2, *gin.shape[2:]), LOW),
            pltpu.VMEM((2, *gin.shape[2:]), FULL),
            dma((2, 2, (groups - 1) * gin.shape[1])),
            dma((2, 2)),
            dma((2,)),
            dma((4,)),
            dma((2, experts)),
            dma((2, chunks, chips)),
            dma((2, chunks, chips - 1)),
            dma((2, chunks, groups)),
            dma((2, chunks, groups - 1)),
            dma((2, experts)),
            dma((2, groups)),
        ],
        compiler_params=pltpu.CompilerParams(
            vmem_limit_bytes=60 * MIB, collective_id=1, has_side_effects=True
        ),
        cost_estimate=pl.CostEstimate(
            flops=30_000_000_000, bytes_accessed=30 * MIB, transcendentals=0
        ),
    )(
        tokens,
        cot,
        hidden,
        normed2,
        mixed,
        qkv,
        prob,
        recv,
        token,
        gain1,
        gain2,
        wqkv,
        wproj,
        wrouter.T,
        jnp.asarray(near_onehot(buckets)),
        result,
        gin,
        early_up,
        early_down,
    )
    return outs[:5]


def outputs_kernel(
    block_in,
    gtok_in,
    gin_in,
    gout_in,
    dense_ref,
    small_ref,
    block_ref,
    gtok_ref,
    gain1_ref,
    qkv_ref,
    proj_ref,
    table_ref,
    gain2_ref,
    router_ref,
    gin_ref,
    gout_ref,
    gin_v,
    gout_v,
    block_v,
    gtok_v,
    sems,
):
    passed = (
        (gin_in, gin_v, gin_ref.at[0]),
        (gout_in, gout_v, gout_ref.at[0]),
        (block_in, block_v, block_ref),
        (gtok_in, gtok_v, gtok_ref),
    )
    pieces = 4
    copies = []
    for i, (src, mid, dst) in enumerate(passed):
        rows = src.shape[0] // pieces
        for piece in range(pieces):
            here = pl.ds(piece * rows, rows)
            copies.append(
                [
                    pltpu.make_async_copy(a.at[here, :], b.at[here, :], sems.at[way, i, piece])
                    for way, (a, b) in enumerate(((src, mid), (mid, dst)))
                ]
            )
    for copy_in, _ in copies:
        copy_in.start()
    chunks, shard, width = dense_ref.shape
    experts = router_ref.shape[0]
    stripe = width // (chunks - 1)
    proj_ref[...] = dense_ref[0].astype(FULL)
    for c in range(1, chunks):
        for third in range(3):
            col = third * width + (c - 1) * stripe
            qkv_ref[:, col : col + stripe] = dense_ref[
                c, :, third * stripe : third * stripe + stripe
            ].astype(FULL)
    gain1_ref[...] = small_ref[0:1, 0:shard]
    gain2_ref[...] = small_ref[1:2, 0:shard]
    router_ref[...] = small_ref[2 : 2 + experts, 0:shard]
    per, heads = table_ref.shape
    table_ref[...] = small_ref[2 + experts : 2 + experts + per, 0:heads]
    for copy_in, copy_out in copies:
        copy_in.wait()
        copy_out.start()
    for _, copy_out in copies:
        copy_out.wait()


def outputs(block, gtok, gin, gout, dense, small, experts, table_shape):
    chunks, shard, width = dense.shape
    buckets, heads = table_shape
    sds = jax.ShapeDtypeStruct
    return pl.pallas_call(
        outputs_kernel,
        out_shape=(
            sds(block.shape, LOW),
            sds(gtok.shape, LOW),
            sds((1, shard), FULL),
            sds((shard, 3 * width), FULL),
            sds((shard, width), FULL),
            sds((buckets // experts, heads), FULL),
            sds((1, shard), FULL),
            sds((experts, shard), FULL),
            sds((1, *gin.shape), FULL),
            sds((1, *gout.shape), FULL),
        ),
        in_specs=[HBM] * 4 + [VM] * 2,
        out_specs=[HBM] * 2 + [VM] * 6 + [HBM] * 2,
        scratch_shapes=[
            pltpu.VMEM(gin.shape, FULL),
            pltpu.VMEM(gout.shape, FULL),
            pltpu.VMEM(block.shape, LOW),
            pltpu.VMEM(gtok.shape, LOW),
            pltpu.SemaphoreType.DMA((2, 4, 4)),
        ],
        compiler_params=pltpu.CompilerParams(vmem_limit_bytes=60 * MIB),
    )(block, gtok, gin, gout, dense, small)


def on_device_fast(
    tokens,
    gain_first,
    w_qkv,
    w_proj,
    bias_table,
    gain_second,
    w_router,
    w_in,
    w_out,
    routes,
    priority,
    span_start,
    cotangent,
):
    experts = w_router.shape[1]
    width = tokens.shape[1]
    groups = lax.axis_size("group")
    (
        qkv,
        prob,
        mixed,
        hidden,
        normed2,
        rows,
        cot_rows,
        gate_col,
        token,
        info,
        resg_t,
        act,
        slope,
        outer_first,
    ) = attn_dispatch(
        tokens,
        cotangent,
        gain_first,
        w_qkv,
        w_proj,
        bias_table,
        gain_second,
        w_router,
        routes,
        priority,
        span_start,
        w_in[0],
        groups,
    )
    recv, packed_out, grad_inner, grad_out, early_up, early_down = expert_call(
        cot_rows, gate_col, rows, info, resg_t, act, slope, outer_first, w_out[0], w_in[0]
    )
    block_out, gtok, dense, small, grad_in = attn_back(
        tokens,
        cotangent,
        hidden,
        normed2,
        mixed,
        qkv,
        prob,
        recv.reshape(-1, width + 128),
        token,
        gain_first,
        gain_second,
        w_qkv,
        w_proj,
        w_router,
        bias_table,
        packed_out,
        grad_inner,
        early_up,
        early_down,
        groups,
    )
    final = list(
        outputs(block_out, gtok, grad_in, grad_out, dense, small, experts, bias_table.shape)
    )
    final[2] = final[2].reshape(-1)
    final[6] = final[6].reshape(-1)
    final[7] = final[7].T
    return tuple(final)


def bucket_table(seq_len, buckets):
    half_count = buckets // 2
    exact_count = half_count // 2
    offsets = np.arange(-(seq_len - 1), seq_len)
    upper_half = (offsets > 0).astype(np.int64) * half_count
    distance = np.abs(offsets)
    scaled = (
        np.log(np.maximum(distance, 1) / float(exact_count))
        / np.log(128.0 / exact_count)
        * (half_count - exact_count)
    )
    larger = np.minimum(
        exact_count + np.floor(np.maximum(scaled, 0.0)).astype(np.int64), half_count - 1
    )
    bucket = upper_half + np.where(distance < exact_count, distance, larger)
    places = np.arange(seq_len)
    return bucket[places[None, :] - places[:, None] + seq_len - 1].astype(np.int32)


def allowed_pairs(seq_len, span_begin, span_len):
    places = jnp.arange(seq_len, dtype=jnp.int32)
    causal = places[None, :] <= places[:, None]
    inside = (places >= span_begin) & (places < span_begin + span_len)
    return causal | inside[:, None] & inside[None, :]


def rms_norm(values, norm_gain):
    return values * lax.rsqrt(jnp.mean(values * values, axis=-1, keepdims=True) + 1e-06) * norm_gain


def gate_values(logits, routes, experts):
    probabilities = jax.nn.softmax(logits, axis=-1)
    chosen = (routes[..., None] == jnp.arange(experts, dtype=jnp.int32)).astype(jnp.float32)
    picked = jnp.sum(probabilities[:, None, :] * chosen, axis=-1)
    return picked / jnp.sum(picked, axis=1, keepdims=True)


def local_ranks(choice_hits, priority):
    token_count = priority.shape[0]
    token_order = (
        jnp.zeros((token_count,), jnp.int32)
        .at[priority]
        .set(jnp.arange(token_count, dtype=jnp.int32))
    )
    ordered = choice_hits[token_order]
    running = jnp.cumsum(ordered, axis=0) - ordered
    return jnp.sum(running[priority] * choice_hits, axis=-1)


def contract_rows(left, right):
    return lax.dot_general(
        left, right, (((0,), (0,)), ((), ())), preferred_element_type=jnp.float32
    )


def on_device(
    tokens,
    gain_first,
    w_qkv,
    w_proj,
    bias_table,
    gain_second,
    w_router,
    w_in,
    w_out,
    routes,
    priority,
    span_start,
    cotangent,
):
    seq_len, model_width = tokens.shape
    buckets, head_count = bias_table.shape
    head_dim = model_width // head_count
    experts = w_router.shape[1]
    slot_count = 4 * seq_len // experts
    capacity = 5 * seq_len // 2
    score_scale = 1.0 / math.sqrt(head_dim)
    highest = lax.Precision.HIGHEST
    lowtype = jnp.bfloat16
    fulltype = jnp.float32
    tokens_f = tokens.astype(fulltype)
    normed_one = rms_norm(tokens_f, gain_first).astype(lowtype)
    qkv_rows = jnp.dot(normed_one, w_qkv, preferred_element_type=fulltype).astype(lowtype)
    qkv_rows = qkv_rows.reshape(seq_len, 3, head_count, head_dim)
    queries, key_rows, value_rows = (qkv_rows[:, 0], qkv_rows[:, 1], qkv_rows[:, 2])
    bucket_index = jnp.asarray(bucket_table(seq_len, buckets))
    onehot_table = (bucket_index[:, :, None] == jnp.arange(buckets, dtype=jnp.int32)).astype(
        fulltype
    )
    rel_bias = jnp.einsum("qkb,bh->hqk", onehot_table, bias_table, precision=highest)
    allowed = allowed_pairs(seq_len, span_start[0], PIC)

    def masked_scores():
        raw_scores = (
            jnp.einsum("qhc,khc->hqk", queries, key_rows, preferred_element_type=fulltype)
            * score_scale
            + rel_bias
        )
        return jnp.where(allowed[None], raw_scores, -1e30)

    scores = masked_scores()
    log_total = jax.nn.logsumexp(scores, axis=-1)
    attn_probs = jnp.exp(scores - log_total[..., None]).astype(lowtype)
    mixed_heads = jnp.einsum(
        "hqk,khc->qhc", attn_probs, value_rows, preferred_element_type=fulltype
    )
    mixed_heads = mixed_heads.astype(lowtype).reshape(seq_len, model_width)
    hidden = tokens_f + jnp.dot(mixed_heads, w_proj, preferred_element_type=fulltype)
    normed_two = rms_norm(hidden, gain_second).astype(lowtype)
    logits = jnp.dot(normed_two, w_router, preferred_element_type=fulltype)
    gate_weights = gate_values(logits, routes, experts)
    choice_hits = (routes[..., None] == jnp.arange(experts, dtype=jnp.int32)).astype(jnp.int32)
    counts = jnp.sum(choice_hits, axis=0)
    every_count = lax.all_gather(counts[None], "expert", axis=0, tiled=True)
    pair_ranks = local_ranks(choice_hits, priority[0])
    second_shift = jnp.sum(choice_hits[:, 1] * counts[0], axis=-1)
    slot_index = pair_ranks + jnp.stack([jnp.zeros_like(second_shift), second_shift], axis=-1)
    flat_slot = (routes * slot_count + slot_index).reshape(-1)
    own_expert = (jnp.arange(experts, dtype=jnp.int32) == lax.axis_index("expert")).astype(
        jnp.int32
    )
    own_counts = jnp.sum(every_count * own_expert, axis=-1)
    first_rows, second_rows = (own_counts[:, 0], own_counts[:, 1])
    first_before = jnp.cumsum(first_rows) - first_rows
    second_before = jnp.cumsum(second_rows) - second_rows
    first_total = jnp.sum(first_rows)
    column = jnp.arange(slot_count, dtype=jnp.int32)[None, :]
    position = jnp.where(
        column < first_rows[:, None],
        first_before[:, None] + column,
        first_total + second_before[:, None] + column - first_rows[:, None],
    )
    usable = (column < (first_rows + second_rows)[:, None]) & (position < capacity)
    destination = jnp.where(usable, position, capacity).reshape(-1)

    def pack_pairs(pair_rows):
        packed = jnp.zeros((experts * slot_count, model_width), lowtype)
        packed = packed.at[flat_slot].set(pair_rows.reshape(-1, model_width))
        return packed.reshape(experts, slot_count, model_width)

    def compact_rows(arrived):
        gathered_rows = jnp.zeros((capacity + 1, model_width), lowtype)
        return gathered_rows.at[destination].add(arrived.reshape(-1, model_width))[:capacity]

    def spread_rows(expert_out):
        padded = jnp.concatenate([expert_out, jnp.zeros((1, model_width), lowtype)], axis=0)
        return padded[destination].reshape(-1, slot_count, model_width)

    def unpack_pairs(received):
        return (
            received.reshape(-1, model_width)[flat_slot]
            .reshape(seq_len, 2, model_width)
            .astype(fulltype)
        )

    pair_rows = jnp.broadcast_to(normed_two[:, None, :], (seq_len, 2, model_width))
    arrived = lax.all_to_all(
        pack_pairs(pair_rows), "expert", split_axis=0, concat_axis=0, tiled=True
    )
    expert_rows = compact_rows(arrived)
    inner_pre = jnp.dot(expert_rows, w_in[0], preferred_element_type=fulltype)
    active = jax.nn.gelu(inner_pre).astype(lowtype)
    result = jnp.dot(active, w_out[0], preferred_element_type=fulltype).astype(lowtype)
    returned = unpack_pairs(
        lax.all_to_all(spread_rows(result), "expert", split_axis=0, concat_axis=0, tiled=True)
    )
    block_out = hidden + jnp.sum(gate_weights[..., None] * returned, axis=1)
    upstream = cotangent.astype(fulltype)
    gate_grad = jnp.sum(upstream[:, None, :] * returned, axis=-1)
    result_grad = (gate_weights[..., None] * upstream[:, None, :]).astype(lowtype)
    result_rows = compact_rows(
        lax.all_to_all(pack_pairs(result_grad), "expert", split_axis=0, concat_axis=0, tiled=True)
    )
    grad_outer = contract_rows(active, result_rows)
    hidden_pre_grad = jnp.dot(result_rows, w_out[0].T, preferred_element_type=fulltype)
    inner_grad = jax.vjp(jax.nn.gelu, inner_pre)[1](hidden_pre_grad)[0].astype(lowtype)
    grad_inner = contract_rows(expert_rows, inner_grad)
    rows_grad = jnp.dot(inner_grad, w_in[0].T, preferred_element_type=fulltype).astype(lowtype)
    pair_grad = unpack_pairs(
        lax.all_to_all(spread_rows(rows_grad), "expert", split_axis=0, concat_axis=0, tiled=True)
    )
    logit_grad = jax.vjp(lambda values: gate_values(values, routes, experts), logits)[1](gate_grad)[
        0
    ].astype(lowtype)
    grad_router = contract_rows(normed_two, logit_grad)
    normed_grad = jnp.sum(pair_grad, axis=1) + jnp.dot(
        logit_grad, w_router.T, preferred_element_type=fulltype
    )
    second_back = jax.vjp(rms_norm, hidden, gain_second)[1](normed_grad)
    hidden_grad = upstream + second_back[0]
    branch_grad = hidden_grad.astype(lowtype)
    grad_proj = contract_rows(mixed_heads, branch_grad)
    mixed_grad = jnp.dot(branch_grad, w_proj.T, preferred_element_type=fulltype).astype(lowtype)
    mixed_grad = mixed_grad.reshape(seq_len, head_count, head_dim)
    scores = masked_scores()
    probs_full = jnp.exp(scores - log_total[..., None])
    probs_low = probs_full.astype(lowtype)
    prob_grad = jnp.einsum("qhc,khc->hqk", mixed_grad, value_rows, preferred_element_type=fulltype)
    value_grad = jnp.einsum("hqk,qhc->khc", probs_low, mixed_grad, preferred_element_type=fulltype)
    row_dot = jnp.sum(probs_full * prob_grad, axis=-1, keepdims=True)
    score_grad = (probs_full * (prob_grad - row_dot)).astype(lowtype)
    query_grad = (
        jnp.einsum("hqk,khc->qhc", score_grad, key_rows, preferred_element_type=fulltype)
        * score_scale
    )
    key_grad = (
        jnp.einsum("hqk,qhc->khc", score_grad, queries, preferred_element_type=fulltype)
        * score_scale
    )
    grad_table = jnp.einsum(
        "hqk,qkb->bh", score_grad.astype(fulltype), onehot_table, precision=highest
    )
    qkv_grad = (
        jnp.stack([query_grad, key_grad, value_grad], axis=1)
        .astype(lowtype)
        .reshape(seq_len, 3 * model_width)
    )
    grad_qkv = contract_rows(normed_one, qkv_grad)
    normed_one_grad = jnp.dot(qkv_grad, w_qkv.T, preferred_element_type=fulltype)
    first_back = jax.vjp(rms_norm, tokens_f, gain_first)[1](normed_one_grad)
    grad_tokens = (hidden_grad + first_back[0]).astype(lowtype)
    dense_grads = (first_back[1], grad_qkv, grad_proj, grad_table, second_back[1], grad_router)
    shares = (
        lax.psum_scatter(
            dense_grads[0].astype(jnp.bfloat16), "expert", scatter_dimension=0, tiled=True
        ).astype(jnp.float32),
        lax.psum_scatter(
            dense_grads[1].astype(jnp.bfloat16), "expert", scatter_dimension=0, tiled=True
        ).astype(jnp.float32),
        lax.psum_scatter(
            dense_grads[2].astype(jnp.bfloat16), "expert", scatter_dimension=0, tiled=True
        ).astype(jnp.float32),
        lax.psum_scatter(
            dense_grads[3].astype(jnp.bfloat16), "expert", scatter_dimension=0, tiled=True
        ).astype(jnp.float32),
        lax.psum_scatter(
            dense_grads[4].astype(jnp.bfloat16), "expert", scatter_dimension=0, tiled=True
        ).astype(jnp.float32),
        lax.psum_scatter(
            dense_grads[5].astype(jnp.bfloat16), "expert", scatter_dimension=0, tiled=True
        ).astype(jnp.float32),
    )
    totals = (
        lax.psum(shares[0].astype(jnp.bfloat16), "group").astype(jnp.float32),
        lax.psum(shares[1].astype(jnp.bfloat16), "group").astype(jnp.float32),
        lax.psum(shares[2].astype(jnp.bfloat16), "group").astype(jnp.float32),
        lax.psum(shares[3].astype(jnp.bfloat16), "group").astype(jnp.float32),
        lax.psum(shares[4].astype(jnp.bfloat16), "group").astype(jnp.float32),
        lax.psum(shares[5].astype(jnp.bfloat16), "group").astype(jnp.float32),
    )
    grad_in, grad_out = (
        lax.psum_scatter(
            grad_inner[None].astype(jnp.bfloat16), "group", scatter_dimension=1, tiled=True
        ).astype(jnp.float32),
        lax.psum_scatter(
            grad_outer[None].astype(jnp.bfloat16), "group", scatter_dimension=1, tiled=True
        ).astype(jnp.float32),
    )
    return (
        block_out.astype(lowtype),
        grad_tokens,
        totals[0],
        totals[1],
        totals[2],
        totals[3],
        totals[4],
        totals[5],
        grad_in,
        grad_out,
    )


def solution(mesh):
    fast = (mesh.shape["group"], mesh.shape["expert"]) == (4, 8)
    step = on_device_fast if fast else on_device
    return jax.shard_map(
        step,
        mesh=mesh,
        in_specs=(
            P(("group", "expert"), None),
            P(),
            P(),
            P(),
            P(),
            P(),
            P(),
            P("expert", None, None),
            P("expert", None, None),
            P(("group", "expert"), None),
            P(("group", "expert"), None),
            P(("group", "expert")),
            P(("group", "expert"), None),
        ),
        out_specs=(
            P(("group", "expert"), None),
            P(("group", "expert"), None),
            P("expert"),
            P("expert", None),
            P("expert", None),
            P("expert", None),
            P("expert"),
            P("expert", None),
            P("expert", "group", None),
            P("expert", "group", None),
        ),
        check_vma=False,
    )
```

```python
import functools
import math

import jax
import jax.numpy as jnp
import numpy as np
from jax import lax
from jax.experimental import pallas as pl
from jax.experimental.pallas import tpu as pltpu
from jax.sharding import PartitionSpec as P

PIC = 256
EPS = 1e-6
LOW = jnp.bfloat16
FULL = jnp.float32
VM = pl.BlockSpec(memory_space=pltpu.VMEM)
SM = pl.BlockSpec(memory_space=pltpu.SMEM)
HBM = pl.BlockSpec(memory_space=pl.ANY)
MIB = 1 << 20
ATT_ROWS = 256
ATT_UNROLL = 2
MESH = pl.DeviceIdType.MESH
SECOND = 512.0
SLOTS = 256
ROW_TILE = 256
EARLY = 2
FF_TILE = 256
THIRDS = 3


def offset_bucket(offsets, buckets):
    half_count = buckets // 2
    exact_count = half_count // 2
    upper_half = (offsets > 0).astype(np.int64) * half_count
    distance = np.abs(offsets)
    scaled = (
        np.log(np.maximum(distance, 1) / float(exact_count))
        / np.log(128.0 / exact_count)
        * (half_count - exact_count)
    )
    larger = np.minimum(
        exact_count + np.floor(np.maximum(scaled, 0.0)).astype(np.int64), half_count - 1
    )
    return upper_half + np.where(distance < exact_count, distance, larger)


def near_onehot(buckets):
    bucket = offset_bucket(np.arange(512) - 256, buckets)
    return (np.arange(buckets)[:, None] == bucket[None, :]).astype(np.float32)


def dot_nn(a, b):
    return lax.dot_general(a, b, (((1,), (0,)), ((), ())), preferred_element_type=FULL)


def dot_nt(a, b):
    return lax.dot_general(a, b, (((1,), (1,)), ((), ())), preferred_element_type=FULL)


def dot_tn(a, b):
    return lax.dot_general(a, b, (((0,), (0,)), ((), ())), preferred_element_type=FULL)


def exact_nn(a, b):
    return lax.dot_general(
        a, b, (((1,), (0,)), ((), ())), precision=lax.Precision.HIGHEST, preferred_element_type=FULL
    )


def exact_nt(a, b):
    return lax.dot_general(
        a, b, (((1,), (1,)), ((), ())), precision=lax.Precision.HIGHEST, preferred_element_type=FULL
    )


def split3(x):
    hi = x.astype(LOW)
    rest = x - hi.astype(FULL)
    mid = rest.astype(LOW)
    low = (rest - mid.astype(FULL)).astype(LOW)
    return hi, mid, low


def half_mask(sub, value, shape=(1, 128)):
    lane = lax.broadcasted_iota(jnp.int32, shape, 1)
    keep = (lane < 64) if sub == 0 else (lane >= 64)
    return jnp.where(keep, value, 0.0).astype(FULL)


def attn_setup(span_ref, table_ref, onehot_ref, near_ref, mask_ref):
    seq_len = mask_ref.shape[0]
    heads = near_ref.shape[0]
    start = span_ref[0]
    qi = lax.broadcasted_iota(jnp.int32, (seq_len, seq_len), 0)
    kj = lax.broadcasted_iota(jnp.int32, (seq_len, seq_len), 1)
    q_in = (qi >= start) & (qi < start + PIC)
    k_in = (kj >= start) & (kj < start + PIC)
    mask_ref[...] = jnp.where((kj <= qi) | (q_in & k_in), 0.0, -1e30).astype(FULL)
    vecs = exact_nn(table_ref[...], onehot_ref[...])
    for h in range(heads):
        rows = jnp.broadcast_to(vecs[h : h + 1, :], (128, 512))
        rolled = pltpu.roll(rows, 0, 1, stride=1, stride_axis=0)
        near_ref[h] = rolled[:, 128:]


def bias_rows(block, blocks, near):
    far_neg = jnp.broadcast_to(near[127:128, 0:1], (128, 128))
    far_pos = jnp.broadcast_to(near[0:1, 383:384], (128, 128))
    pieces = []
    for other in range(blocks):
        d = other - block
        if d <= -2:
            pieces.append(far_neg)
        elif d >= 2:
            pieces.append(far_pos)
        else:
            pieces.append(near[:, (d + 1) * 128 : (d + 2) * 128])
    return jnp.concatenate(pieces, axis=1)


def attn_block(row0, count, qkv_ref, near_ref, mask_ref, prob_ref, mixed_ref):
    seq_len, width3 = qkv_ref.shape
    width = width3 // 3
    blocks = seq_len // 128
    rows = slice(row0, row0 + count)

    @pl.loop(0, width // 128, unroll=ATT_UNROLL)
    def _(pair):
        col = pl.multiple_of(pair * 128, 128)
        qp = qkv_ref[rows, pl.ds(col, 128)].astype(FULL)
        kp = qkv_ref[:, pl.ds(width + col, 128)]
        vp = qkv_ref[:, pl.ds(2 * width + col, 128)]
        qs = jnp.concatenate([qp * half_mask(sub, 0.125) for sub in range(2)], axis=0)
        scores = dot_nt(qs.astype(LOW), kp)
        probs = []
        for sub in range(2):
            h = 2 * pair + sub
            for part in range(count // 128):
                first = sub * count + part * 128
                here = slice(row0 + part * 128, row0 + part * 128 + 128)
                s = scores[first : first + 128]
                bias = bias_rows(row0 // 128 + part, blocks, near_ref[h])
                s = s + bias + mask_ref[here, :]
                top = jnp.max(s, axis=1, keepdims=True)
                e = jnp.exp(s - top)
                total = jnp.sum(e, axis=1, keepdims=True)
                p = (e * (1.0 / total)).astype(LOW)
                prob_ref[h, here, :] = p
                probs.append(p)
        outs = dot_nn(jnp.concatenate(probs, axis=0), vp)
        lane = lax.broadcasted_iota(jnp.int32, (count, 128), 1)
        mixed_ref[rows, pl.ds(col, 128)] = jnp.where(
            lane < 64, outs[:count], outs[count:]
        ).astype(LOW)


def choice_hits(routes, experts):
    who = lax.broadcasted_iota(jnp.int32, (experts, routes.shape[1]), 0)
    return [who == routes[k : k + 1, :] for k in range(2)]


def to_column(row, width):
    return jnp.transpose(jnp.broadcast_to(row, (8, width)))[:, 0:1]


def ranks_by_priority(hits, priority):
    tokens = priority.shape[1]
    prio = priority.astype(FULL)
    less = jnp.where(to_column(prio, tokens) < prio, 1.0, 0.0).astype(LOW)
    return [dot_nn(jnp.where(hit, 1.0, 0.0).astype(LOW), less) for hit in hits]


def attn_dispatch_kernel(
    tokens_ref,
    cot_ref,
    gain1_ref,
    wqkv_ref,
    wproj_ref,
    table_ref,
    onehot_ref,
    gain2_ref,
    wrouter_ref,
    routes_ref,
    prio_ref,
    span_ref,
    win_ref,
    qkv_out,
    prob_out,
    mixed_out,
    hidden_out,
    normed2_out,
    rows_out,
    cotrows_out,
    gatecol_out,
    token_ref,
    info_ref,
    resgt_out,
    act_out,
    slope_out,
    gout_out,
    qkv_ref,
    prob_ref,
    mixed_ref,
    hidden_ref,
    normed2_ref,
    meta_ref,
    gate_ref,
    meta_all,
    gate_all,
    gat_c,
    gat_n,
    acc_g,
    pos_ref,
    win_v,
    rows_ref,
    cotrows_ref,
    gatecol_ref,
    resgt_ref,
    send_sem,
    recv_sem,
    small_send,
    small_recv,
    out_sem,
    in_sem,
    tile_sem,
):
    g = lax.axis_index("group")
    me = lax.axis_index("expert")
    experts = wrouter_ref.shape[0]
    seq_len, width = tokens_ref.shape
    half = seq_len // 2

    def device(mask):
        return (g, lax.bitwise_xor(me, mask))

    barrier = pltpu.get_barrier_semaphore()
    for mask in range(1, experts):
        pl.semaphore_signal(barrier, inc=1, device_id=device(mask), device_id_type=MESH)
    pl.semaphore_wait(barrier, experts - 1)

    gats = (gat_c, gat_n)
    owns = (cot_ref, normed2_ref)

    def send(which, kind, chunk, held, target):
        rows = pl.ds(chunk * half, half)
        slot = lax.bitwise_xor(me, held)
        src = owns[which].at[rows, :] if held == 0 else gats[which].at[slot, rows, :]
        return pltpu.make_async_remote_copy(
            src_ref=src,
            dst_ref=gats[which].at[slot, rows, :],
            send_sem=send_sem.at[which, kind, chunk],
            recv_sem=recv_sem.at[which, held ^ target, chunk],
            device_id=device(target),
            device_id_type=MESH,
        )

    started = []

    def go(*args):
        send(*args).start()
        started.append(functools.partial(send, *args))

    def arrived(which, mask, chunk):
        rows = pl.ds(chunk * half, half)
        here = gats[which].at[lax.bitwise_xor(me, mask), rows, :]
        pltpu.make_async_remote_copy(
            src_ref=here,
            dst_ref=here,
            send_sem=send_sem.at[which, 0, chunk],
            recv_sem=recv_sem.at[which, mask, chunk],
            device_id=device(1),
            device_id_type=MESH,
        ).wait_recv()

    def own_out(which, chunk):
        go(which, 0, chunk, 0, 2)
        go(which, 1, chunk, 0, 4)
        go(which, 2, chunk, 0, 1)

    def own_out_all(which):
        for chunk in range(2):
            go(which, 0, chunk, 0, 2)
            go(which, 1, 1 - chunk, 0, 4)
        for chunk in range(2):
            go(which, 2, chunk, 0, 1)

    def relay(which, chunk, wait=True):
        if wait:
            arrived(which, 4 if chunk else 2, chunk)
        go(which, 3, chunk, 4 if chunk else 2, 2 if chunk else 4)

    def small_copy(src, dst, index, mask):
        return pltpu.make_async_remote_copy(
            src_ref=src,
            dst_ref=dst.at[me],
            send_sem=small_send.at[index, mask],
            recv_sem=small_recv.at[index, mask],
            device_id=device(mask),
            device_id_type=MESH,
        )

    def small(*args):
        for mask in range(1, experts):
            small_copy(*args, mask).start()
            started.append(functools.partial(small_copy, *args, mask))

    def small_arrived(dst, index):
        for mask in range(1, experts):
            here = dst.at[lax.bitwise_xor(me, mask)]
            pltpu.make_async_remote_copy(
                src_ref=here,
                dst_ref=here,
                send_sem=small_send.at[index, mask],
                recv_sem=small_recv.at[index, mask],
                device_id=device(1),
                device_id_type=MESH,
            ).wait_recv()

    own_out_all(0)

    def win_load():
        return pltpu.make_async_copy(win_ref, win_v, in_sem.at[2])

    win_load().start()

    hits = choice_hits(routes_ref[...], experts)
    ranks = ranks_by_priority(hits, prio_ref[...])
    meta = jnp.where(hits[0], ranks[0], jnp.where(hits[1], ranks[1] + SECOND, -1.0))
    meta_ref[...] = meta
    meta_all[me] = meta
    small(meta_ref, meta_all, 0)

    own_pairs = (
        (qkv_ref, qkv_out),
        (prob_ref, prob_out),
        (mixed_ref, mixed_out),
        (hidden_ref, hidden_out),
        (normed2_ref, normed2_out),
        (cotrows_ref, cotrows_out),
        (rows_ref, rows_out),
        (gatecol_ref, gatecol_out),
        (resgt_ref, resgt_out),
    )

    def own_copy(index):
        src, dst = own_pairs[index]
        return pltpu.make_async_copy(src, dst, out_sem.at[index])

    def attention(wqkv_v, wproj_v, near_ref, mask_ref):
        loads = [
            pltpu.make_async_copy(src, dst, in_sem.at[i])
            for i, (src, dst) in enumerate(((wqkv_ref, wqkv_v), (wproj_ref, wproj_v)))
        ]
        for copy in loads:
            copy.start()
        attn_setup(span_ref, table_ref, onehot_ref, near_ref, mask_ref)
        loads[0].wait()
        for row0 in range(0, seq_len, 128):
            rows = slice(row0, row0 + 128)
            x = tokens_ref[rows, :].astype(FULL)
            inv = lax.rsqrt(jnp.mean(x * x, axis=1, keepdims=True) + EPS)
            n1 = (x * inv * gain1_ref[...][None, :]).astype(LOW)
            qkv_ref[rows, :] = dot_nn(n1, wqkv_v[...]).astype(LOW)
        own_copy(0).start()
        loads[1].wait()
        for chunk in range(2):
            row0 = chunk * half
            rows = slice(row0, row0 + half)
            attn_block(row0, half, qkv_ref, near_ref, mask_ref, prob_ref, mixed_ref)
            hidden = tokens_ref[rows, :].astype(FULL) + dot_nn(mixed_ref[rows, :], wproj_v[...])
            hidden_ref[rows, :] = hidden
            inv = lax.rsqrt(jnp.mean(hidden * hidden, axis=1, keepdims=True) + EPS)
            n2 = (hidden * inv * gain2_ref[...][None, :]).astype(LOW)
            normed2_ref[rows, :] = n2
            own_out(1, chunk)

    pl.run_scoped(
        attention,
        pltpu.VMEM(wqkv_ref.shape, LOW),
        pltpu.VMEM(wproj_ref.shape, LOW),
        pltpu.VMEM((table_ref.shape[0], 128, 384), FULL),
        pltpu.VMEM((seq_len, seq_len), FULL),
    )
    for index in range(1, 5):
        own_copy(index).start()

    logits = dot_nt(wrouter_ref[...], normed2_ref[...])
    unnormed = jnp.exp(logits - jnp.max(logits, axis=0, keepdims=True))
    probabilities = unnormed / jnp.sum(unnormed, axis=0, keepdims=True)
    picked = [jnp.sum(jnp.where(hit, probabilities, 0.0), axis=0, keepdims=True) for hit in hits]
    both = picked[0] + picked[1]
    gates = [p / both for p in picked]
    gate = jnp.where(hits[0], gates[0], jnp.where(hits[1], gates[1], 0.0))
    gate_ref[...] = gate
    gate_all[me] = gate
    small(gate_ref, gate_all, 1)

    first_count = jnp.sum(jnp.where(hits[0], 1.0, 0.0), axis=1, keepdims=True)
    who = lax.broadcasted_iota(jnp.int32, hits[0].shape, 0).astype(FULL)
    slots = [
        jnp.sum(jnp.where(hits[0], ranks[0] + who * SLOTS, 0.0), axis=0, keepdims=True),
        jnp.sum(
            jnp.where(hits[1], ranks[1] + first_count + who * SLOTS, 0.0), axis=0, keepdims=True
        ),
    ]
    routes_f = routes_ref[...].astype(FULL)
    token_rows = jnp.concatenate(slots + gates + [routes_f[0:1], routes_f[1:2]] + slots, axis=0)
    token_ref[...] = jnp.transpose(token_rows)

    small_arrived(meta_all, 0)
    value = meta_all[:, me, :]
    is_first = (value >= 0.0) & (value < SECOND)
    is_second = value >= SECOND
    counts = [
        jnp.sum(jnp.where(hit, 1.0, 0.0), axis=1, keepdims=True) for hit in (is_first, is_second)
    ]
    row = lax.broadcasted_iota(jnp.int32, (experts, 128), 0)
    lane = lax.broadcasted_iota(jnp.int32, (experts, 128), 1)
    count_mat = jnp.where(lane == 0, counts[0], jnp.where(lane == 1, counts[1], 0.0))
    before = jnp.zeros((experts, 128), FULL)
    for s in range(experts):
        before = before + jnp.where(row > s, count_mat[s : s + 1, :], 0.0)
    first_total = jnp.sum(counts[0], axis=0, keepdims=True)
    base = [before[:, 0:1], before[:, 1:2] + first_total]
    pos_ref[...] = jnp.where(
        is_first, value + base[0], jnp.where(is_second, value - SECOND + base[1], -1.0)
    )
    info_ref[...] = jnp.where(
        lane == 0,
        counts[0],
        jnp.where(lane == 1, counts[1], jnp.where(lane == 2, base[0], base[1])),
    )

    accs = (cotrows_ref, rows_ref)

    def compact(which, mask):
        slot = lax.bitwise_xor(me, mask)
        acc = accs[which]

        @pl.loop(0, acc.shape[0] // ROW_TILE)
        def _(tile):
            row0 = pl.multiple_of(tile * ROW_TILE, ROW_TILE)
            here = pl.ds(row0, ROW_TILE)
            place = pos_ref[pl.ds(slot, 1), :] - row0.astype(FULL)
            at = lax.broadcasted_iota(jnp.int32, (ROW_TILE, seq_len), 0).astype(FULL)
            hit = at == place
            pick = jnp.where(hit, 1.0, 0.0).astype(LOW)
            data = owns[which][...] if mask == 0 else gats[which][slot]
            got = dot_nn(pick, data).astype(LOW)
            if mask:
                got = got + acc[here, :]
            acc[here, :] = got
            if which == 1:
                gates_here = jnp.where(hit, gate_all[slot, pl.ds(me, 1), :], 0.0)
                part = gates_here[:, 0:128]
                for i in range(1, seq_len // 128):
                    part = part + gates_here[:, i * 128 : i * 128 + 128]
                if mask:
                    part = part + acc_g[here, :]
                acc_g[here, :] = part

    def forward(which, mask, waits=(0, 1)):
        for chunk in waits:
            arrived(which, mask, chunk)
        for chunk in range(2):
            go(which, 3 + mask // 2, chunk, mask, 1)

    def take(which, mask):
        for chunk in range(2):
            arrived(which, mask, chunk)
        compact(which, mask)

    relay(0, 0)
    relay(0, 1)
    forward(0, 2, (1,))
    forward(0, 4, (0,))
    compact(0, 0)
    take(0, 1)
    compact(0, 2)
    compact(0, 4)
    take(0, 3)
    take(0, 5)
    relay(1, 0)
    relay(1, 1)
    small_arrived(gate_all, 1)
    compact(1, 0)
    take(1, 1)
    forward(1, 2, (1,))
    compact(1, 2)
    forward(1, 4, (0,))
    compact(1, 4)
    forward(0, 6)
    compact(0, 6)
    take(0, 7)
    own_copy(5).start()
    take(1, 3)
    take(1, 5)
    forward(1, 6)
    compact(1, 6)
    take(1, 7)
    own_copy(6).start()

    capacity = rows_ref.shape[0]
    tiles = gout_out.shape[0]

    def experts_first(act_v, slope_v, gout_v):
        def tile_copies(tile):
            return [
                pltpu.make_async_copy(src.at[tile], dst, tile_sem.at[kind, tile])
                for kind, (src, dst) in enumerate(
                    (
                        (act_v, act_out.at[tile]),
                        (slope_v, slope_out.at[tile]),
                        (gout_v, gout_out.at[tile]),
                    )
                )
            ]

        win_load().wait()

        def scaled(row0):
            rows = pl.ds(pl.multiple_of(row0, ROW_TILE), ROW_TILE)
            gate_col = jnp.sum(acc_g[rows, :], axis=1, keepdims=True)
            gatecol_ref[rows, :] = jnp.broadcast_to(gate_col, (ROW_TILE, 128))
            resg = gate_col * cotrows_ref[rows, :].astype(FULL)
            resgt_ref[:, rows] = jnp.transpose(resg.astype(LOW))

        parts = capacity // ROW_TILE

        @pl.loop(0, tiles)
        def _(tile):
            cols = pl.ds(pl.multiple_of(tile * THIRDS * FF_TILE, FF_TILE), FF_TILE)
            for row0 in range(0, capacity, ROW_TILE):
                here = slice(row0, row0 + ROW_TILE)
                act, slope = gelu_and_slope(dot_nn(rows_ref[here, :], win_v[:, cols]))
                act_v[tile, here, :] = act.astype(LOW)
                slope_v[tile, here, :] = slope.astype(LOW)
            scaled(tile * ROW_TILE)
            for copy in tile_copies(tile)[:2]:
                copy.start()

        for part in range(tiles, parts):
            scaled(part * ROW_TILE)
        own_copy(7).start()
        own_copy(8).start()

        @pl.loop(0, tiles)
        def _(tile):
            gout_v[tile] = dot_nn(resgt_ref[...], act_v[tile]).astype(LOW)
            tile_copies(tile)[2].start()

        @pl.loop(0, tiles)
        def _(tile):
            for copy in tile_copies(tile):
                copy.wait()

    pl.run_scoped(
        experts_first,
        pltpu.VMEM((tiles, capacity, FF_TILE), LOW),
        pltpu.VMEM((tiles, capacity, FF_TILE), LOW),
        pltpu.VMEM((tiles, width, FF_TILE), LOW),
    )

    for index in range(9):
        own_copy(index).wait()
    for copy in started:
        copy().wait_send()


def attn_dispatch(
    tokens, cot, gain1, wqkv, wproj, table, gain2, wrouter, routes, priority, span, w_in, groups
):
    seq_len, width = tokens.shape
    buckets, heads = table.shape
    experts = wrouter.shape[1]
    capacity = 5 * seq_len // 2
    ff = w_in.shape[1]
    sds = jax.ShapeDtypeStruct
    dma = pltpu.SemaphoreType.DMA
    return pl.pallas_call(
        attn_dispatch_kernel,
        out_shape=(
            sds((seq_len, 3 * width), LOW),
            sds((heads, seq_len, seq_len), LOW),
            sds((seq_len, width), LOW),
            sds((seq_len, width), FULL),
            sds((seq_len, width), LOW),
            sds((capacity, width), LOW),
            sds((capacity, width), LOW),
            sds((capacity, 128), FULL),
            sds((seq_len, 8), FULL),
            sds((experts, 128), FULL),
            sds((width, capacity), LOW),
            sds((groups, capacity, FF_TILE), LOW),
            sds((groups, capacity, FF_TILE), LOW),
            sds((groups, width, FF_TILE), LOW),
        ),
        in_specs=[VM] * 3 + [HBM] * 2 + [VM] * 6 + [SM, HBM],
        out_specs=[HBM] * 8 + [VM] * 2 + [HBM] * 4,
        scratch_shapes=[
            pltpu.VMEM((seq_len, 3 * width), LOW),
            pltpu.VMEM((heads, seq_len, seq_len), LOW),
            pltpu.VMEM((seq_len, width), LOW),
            pltpu.VMEM((seq_len, width), FULL),
            pltpu.VMEM((seq_len, width), LOW),
            pltpu.VMEM((experts, seq_len), FULL),
            pltpu.VMEM((experts, seq_len), FULL),
            pltpu.VMEM((experts, experts, seq_len), FULL),
            pltpu.VMEM((experts, experts, seq_len), FULL),
            pltpu.VMEM((experts, seq_len, width), LOW),
            pltpu.VMEM((experts, seq_len, width), LOW),
            pltpu.VMEM((capacity, 128), FULL),
            pltpu.VMEM((experts, seq_len), FULL),
            pltpu.VMEM(w_in.shape, LOW),
            pltpu.VMEM((capacity, width), LOW),
            pltpu.VMEM((capacity, width), LOW),
            pltpu.VMEM((capacity, 128), FULL),
            pltpu.VMEM((width, capacity), LOW),
            dma((2, 7, 2)),
            dma((2, 8, 2)),
            dma((2, 8)),
            dma((2, 8)),
            dma((9,)),
            dma((3,)),
            dma((3, groups)),
        ],
        compiler_params=pltpu.CompilerParams(
            vmem_limit_bytes=60 * MIB, collective_id=0, has_side_effects=True
        ),
    )(
        tokens,
        cot,
        gain1,
        wqkv,
        wproj,
        table.T,
        jnp.asarray(near_onehot(buckets)),
        gain2,
        wrouter.T,
        routes.T,
        priority,
        span,
        w_in,
    )


def gelu_and_slope(x):
    c = math.sqrt(2.0 / math.pi)
    square = x * x
    s = 0.5 * jnp.tanh(x * (c + (c * 0.044715) * square)) + 0.5
    act = x * s
    return act, s + act * (1.0 - s) * (2.0 * c + (6.0 * c * 0.044715) * square)


def pack_rows(source, info_ref, data, slots):
    info = info_ref[pl.ds(source, 1), :]
    slot = lax.broadcasted_iota(jnp.int32, (slots, 1), 0).astype(FULL)
    n0, n1, b0, b1 = [info[:, i : i + 1] for i in range(4)]
    place = jnp.where(slot < n0, b0 + slot, jnp.where(slot < n0 + n1, b1 + slot - n0, -1.0))
    at = lax.broadcasted_iota(jnp.int32, (slots, data.shape[0]), 1).astype(FULL)
    pick = jnp.where(at == place, 1.0, 0.0).astype(LOW)
    return dot_nn(pick, data[...]).astype(LOW)


def expert_kernel(
    cot_hbm,
    gate_hbm,
    rows_hbm,
    info_ref,
    resgt_hbm,
    act_ref,
    slope_ref,
    outer_ref,
    wout_ref,
    win_ref,
    recv_ref,
    packed_ref,
    gin_ref,
    gout_ref,
    early_up,
    early_down,
    up_in,
    down_in,
    cot_ref,
    gate_ref,
    rows_ref,
    act_v,
    slope_v,
    wout_v,
    win_v,
    ig_v,
    acc_ref,
    gg_ref,
    data_ref,
    send_ref,
    turned,
    gin_v,
    outer_v,
    fold_ref,
    took_ref,
    total_ref,
    packed_v,
    gout_v,
    load_sem,
    act_sem,
    slope_sem,
    outer_sem,
    gin_sem,
    own_sem,
    took_sem,
    total_sem,
    send_sem,
    recv_sem,
    fold_sems,
    early_sems,
):
    g = lax.axis_index("group")
    me = lax.axis_index("expert")
    experts, slots, wide = send_ref.shape
    tiles, capacity, tile_width = act_v.shape
    width = cot_ref.shape[1]
    groups = act_ref.shape[0]
    thirds = tiles // groups
    last = groups - 1
    copies = last * thirds
    arrivals = (up_in, down_in)

    def device(mask):
        return (g, lax.bitwise_xor(me, mask))

    def load(index):
        src, dst = (
            (wout_ref, wout_v),
            (win_ref, win_v),
            (resgt_hbm, turned),
            (cot_hbm, cot_ref),
            (gate_hbm, gate_ref),
            (rows_hbm, rows_ref),
        )[index]
        return pltpu.make_async_copy(src, dst, load_sem.at[index])

    def act_load(tile):
        return pltpu.make_async_copy(act_ref.at[tile], act_v.at[tile], act_sem.at[tile])

    def slope_load(tile):
        slot = lax.rem(tile, 2)
        return pltpu.make_async_copy(slope_ref.at[tile], slope_v.at[slot], slope_sem.at[slot])

    def outer_load(tile):
        return pltpu.make_async_copy(outer_ref.at[tile], outer_v.at[tile], outer_sem.at[tile])

    for tile in range(groups):
        outer_load(tile).start()
    load(3).start()
    load(4).start()
    load(0).start()
    slope_load(0).start()
    act_load(0).start()
    load(1).start()
    for tile in range(1, groups):
        act_load(tile).start()
    load(5).start()
    load(2).start()
    barrier = pltpu.get_barrier_semaphore()
    for mask in range(1, experts):
        pl.semaphore_signal(barrier, inc=1, device_id=device(mask), device_id_type=MESH)
    for step in range(1, groups):
        pl.semaphore_signal(
            barrier, inc=1, device_id=(lax.rem(g + step, groups), me), device_id_type=MESH
        )
    pl.semaphore_wait(barrier, experts - 1 + groups - 1)
    for tile in range(groups):
        outer_load(tile).wait()

    def fold_tile(way, k):
        return (k % last if way else last - k % last), k // last

    def fold_copy(way, k, src):
        shard_at, third = fold_tile(way, k)
        there = arrivals[way].at[shard_at, third]
        return pltpu.make_async_remote_copy(
            src_ref=there if src is None else src,
            dst_ref=there,
            send_sem=fold_sems.at[0, way, k],
            recv_sem=fold_sems.at[1, way, k],
            device_id=(lax.rem(g + (last if way else 1), groups), me),
            device_id_type=MESH,
        )

    def take_tile(way, src):
        return pltpu.make_async_copy(src, took_ref.at[way], took_sem.at[way])

    def fold_source(*which):
        for k in which:
            for way in range(2):
                shard_at, third = fold_tile(way, k)

                @pl.when(g == way * last)
                def _():
                    fold_copy(way, k, outer_v.at[third * groups + shard_at]).start()

    def passed(way, here):
        return [
            k
            for k in range(copies)
            if ((fold_tile(way, k)[0] < here) if way else (fold_tile(way, k)[0] > here))
        ]

    def fold_role(hop, k, act):
        for way in range(2):
            here = last - hop if way else hop
            order = passed(way, here)
            if k in order:
                pl.when(g == here)(functools.partial(act, way, k, order, order.index(k)))

    def fold_fetch(hop, k):
        def act(way, k, order, nth):
            shard_at, third = fold_tile(way, k)
            fold_copy(way, k, None).wait_recv()
            take_tile(way, arrivals[way].at[shard_at, third]).start()

        fold_role(hop, k, act)

    def fold_push(hop, k):
        def act(way, k, order, nth):
            shard_at, third = fold_tile(way, k)
            if nth >= 2:
                fold_copy(way, order[nth - 2], None).wait_send()
            take_tile(way, arrivals[way].at[shard_at, third]).wait()
            own = outer_v[third * groups + shard_at].astype(FULL)
            fold_ref[way, nth % 2] = (own + took_ref[way].astype(FULL)).astype(LOW)
            fold_copy(way, k, fold_ref.at[way, nth % 2]).start()

        fold_role(hop, k, act)

    def fold_final(third):
        total_ref[...] = outer_v[third * groups + g].astype(FULL)
        for way, (some, at) in enumerate(((g > 0, last - g), (g < last, g))):

            @pl.when(some)
            def _():
                here = arrivals[way].at[g, third]
                k = third * last + at
                pltpu.make_async_remote_copy(
                    src_ref=here,
                    dst_ref=here,
                    send_sem=fold_sems.at[0, way, k],
                    recv_sem=fold_sems.at[1, way, k],
                    device_id=(lax.rem(g + 1, groups), me),
                    device_id_type=MESH,
                ).wait_recv()
                take_tile(way, here).start()
                take_tile(way, here).wait()
                total_ref[...] += took_ref[way].astype(FULL)

        gout_v[third * tile_width : (third + 1) * tile_width, :] = jnp.transpose(total_ref[...])
        gout_copy(third).start()

    def gout_copy(third):
        here = pl.ds(third * tile_width, tile_width)
        return pltpu.make_async_copy(gout_v.at[here, :], gout_ref.at[here, :], total_sem.at[third])

    def fold_sent():
        for way in range(2):
            for k in range(copies):

                @pl.when(g == way * last)
                def _():
                    fold_copy(way, k, None).wait_send()

            for hop in range(1, last):
                here = last - hop if way else hop
                for k in passed(way, here)[-2:]:

                    @pl.when(g == here)
                    def _():
                        fold_copy(way, k, None).wait_send()

    fold_source(*range(last))
    acc_ref[...] = jnp.zeros_like(acc_ref)
    gg_ref[...] = jnp.zeros_like(gg_ref)
    for index in (0, 1, 3, 4, 5):
        load(index).wait()

    def span(tile):
        at = lax.rem(tile, groups) * thirds + lax.div(tile, groups)
        return pl.ds(pl.multiple_of(at * tile_width, tile_width), tile_width)

    def back_tile(tile, slope_slot):
        for row0 in range(0, capacity, ROW_TILE):
            here = slice(row0, row0 + ROW_TILE)
            back = dot_nt(cot_ref[here, :], wout_v[span(tile), :])
            part = act_v[tile, here, :].astype(FULL) * back
            gg_ref[here, :] += part[:, 0:128] + part[:, 128:256]
            slope = slope_v[slope_slot, here, :].astype(FULL)
            ig_v[tile, here, :] = (slope * (gate_ref[here, 0:1] * back)).astype(LOW)
            acc_ref[here, :] += dot_nt(ig_v[tile, here, :], win_v[:, span(tile)])

    @pl.loop(0, groups)
    def _(tile):
        slope_load(tile).wait()
        act_load(tile).wait()

        @pl.when(tile + 1 < groups)
        def _():
            slope_load(tile + 1).start()

        back_tile(tile, lax.rem(tile, 2))

    load(2).wait()
    fold_fetch(1, 0)

    def own_tiles(first, count):
        @pl.loop(first, first + count)
        def _(tile):
            for row0 in range(0, capacity, ROW_TILE):
                here = slice(row0, row0 + ROW_TILE)
                act, slope = gelu_and_slope(dot_nn(rows_ref[here, :], win_v[:, span(tile)]))
                act_v[tile, here, :] = act.astype(LOW)
                slope_v[0, here, :] = slope.astype(LOW)
            outer_v[tile] = dot_nn(turned[...], act_v[tile]).astype(LOW)
            back_tile(tile, 0)

    own_tiles(groups, 2)
    fold_push(1, 0)
    own_tiles(groups + 2, groups - 2)
    fold_source(*range(last, 2 * last))
    fold_fetch(1, 1)
    own_tiles(2 * groups, 2)
    fold_push(1, 1)
    fold_fetch(1, 2)
    fold_fetch(2, 0)
    own_tiles(2 * groups + 2, groups - 2)
    fold_source(*range(2 * last, 3 * last))
    fold_push(1, 2)
    fold_push(2, 0)

    data_ref[:, :width] = acc_ref[...].astype(LOW)
    gg = jnp.sum(gg_ref[...], axis=1, keepdims=True)
    hi, mid, low = [t.astype(FULL) for t in split3(gg)]
    lane = lax.broadcasted_iota(jnp.int32, (capacity, 128), 1)
    data_ref[:, width:] = jnp.where(
        lane == 0, hi, jnp.where(lane == 1, mid, jnp.where(lane == 2, low, 0.0))
    ).astype(LOW)

    def exchange(mask):
        return pltpu.make_async_remote_copy(
            src_ref=send_ref.at[lax.bitwise_xor(me, mask)],
            dst_ref=recv_ref.at[me],
            send_sem=send_sem.at[mask],
            recv_sem=recv_sem.at[mask],
            device_id=device(mask),
            device_id_type=MESH,
        )

    for mask in (6, 7, 2, 4, 3, 5, 1):
        other = lax.bitwise_xor(me, mask)
        send_ref[other] = pack_rows(other, info_ref, data_ref, slots)
        exchange(mask).start()
        if mask == 4:
            fold_fetch(1, 3)
    send_ref[me] = pack_rows(me, info_ref, data_ref, slots)
    own_rows = pltpu.make_async_copy(send_ref.at[me], recv_ref.at[me], own_sem)
    own_rows.start()
    fold_push(1, 3)
    fold_fetch(1, 4)

    turned[...] = jnp.transpose(rows_ref[...])

    def gin_copy(tile):
        slot = lax.rem(tile, 2)
        cols = pl.ds(pl.multiple_of(lax.div(tile, groups) * tile_width, tile_width), tile_width)
        return pltpu.make_async_copy(
            gin_v.at[slot], gin_ref.at[:, lax.rem(tile, groups), :, cols], gin_sem.at[slot]
        )

    def gin_tiles(first, count):
        @pl.loop(first, first + count)
        def _(tile):
            @pl.when(tile >= 2)
            def _():
                gin_copy(tile).wait()

            got = dot_nn(turned[...], ig_v[tile]).astype(LOW)
            gin_v[lax.rem(tile, 2)] = got.reshape(gin_v.shape[1:])
            gin_copy(tile).start()

    gin_tiles(0, tiles // 2)
    fold_push(1, 4)
    gin_tiles(tiles // 2, tiles // 2)
    fold_fetch(1, 5)
    fold_fetch(2, 3)

    acc_ref[...] = jnp.zeros_like(acc_ref)

    def result_tiles(first, count):
        @pl.loop(first, first + count)
        def _(tile):
            for row0 in range(0, capacity, ROW_TILE):
                here = slice(row0, row0 + ROW_TILE)
                acc_ref[here, :] += dot_nn(act_v[tile, here, :], wout_v[span(tile), :])

    result_tiles(0, tiles // 2)
    fold_push(1, 5)
    fold_push(2, 3)
    result_tiles(tiles // 2, tiles // 2)
    fold_fetch(1, 6)
    gin_copy(0).wait()
    gin_copy(1).wait()

    def early_copy(way, k):
        return pltpu.make_async_remote_copy(
            src_ref=gin_ref.at[0 if way else last, k],
            dst_ref=(early_up, early_down)[way].at[k],
            send_sem=early_sems.at[0, way, k],
            recv_sem=early_sems.at[1, way, k],
            device_id=(lax.rem(g + (last if way else 1), groups), me),
            device_id_type=MESH,
        )

    def early_each(act):
        for way in range(2):
            for k in range(EARLY):
                act(way, k)

    def early_start(way, k):
        @pl.when(g == way * last)
        def _():
            early_copy(way, k).start()

    def early_end(way, k):
        @pl.when(g == way * last)
        def _():
            early_copy(way, k).wait_send()

        @pl.when(g == (last - 1 if way else 1))
        def _():
            early_copy(way, k).wait_recv()

    early_each(early_start)
    data_ref[:, :width] = acc_ref[...].astype(LOW)

    @pl.loop(0, experts)
    def _(source):
        packed_v[source] = pack_rows(source, info_ref, data_ref.at[:, 0:width], slots)

    packed_copy = pltpu.make_async_copy(packed_v, packed_ref, total_sem.at[thirds])
    packed_copy.start()
    fold_push(1, 6)
    fold_final(0)
    fold_fetch(1, 7)
    fold_push(1, 7)
    fold_fetch(2, 6)
    fold_push(2, 6)
    fold_final(1)
    fold_fetch(1, 8)
    fold_push(1, 8)
    fold_final(2)
    packed_copy.wait()
    for third in range(thirds):
        gout_copy(third).wait()
    own_rows.wait()
    for mask in range(1, experts):
        exchange(mask).wait()
    fold_sent()
    early_each(early_end)


def expert_call(cot_rows, gate_col, rows, info, resg_t, act, slope, outer, w_out, w_in):
    capacity, width = cot_rows.shape
    groups, _, tile_width = act.shape
    ff = w_in.shape[1]
    tiles = ff // tile_width
    experts = info.shape[0]
    sds = jax.ShapeDtypeStruct
    dma = pltpu.SemaphoreType.DMA
    early = sds((EARLY, width // groups, ff // groups), LOW)
    arrival = sds((groups, tiles // groups, width, tile_width), LOW)
    outs = pl.pallas_call(
        expert_kernel,
        out_shape=(
            sds((experts, SLOTS, width + 128), LOW),
            sds((experts, SLOTS, width), LOW),
            sds((groups, groups, width // groups, ff // groups), LOW),
            sds((ff // groups, width), FULL),
            early,
            early,
            arrival,
            arrival,
        ),
        in_specs=[HBM] * 3 + [VM] + [HBM] * 6,
        out_specs=[HBM] * 8,
        scratch_shapes=[
            pltpu.VMEM(cot_rows.shape, LOW),
            pltpu.VMEM(gate_col.shape, FULL),
            pltpu.VMEM(rows.shape, LOW),
            pltpu.VMEM((tiles, capacity, tile_width), LOW),
            pltpu.VMEM((2, capacity, tile_width), LOW),
            pltpu.VMEM(w_out.shape, LOW),
            pltpu.VMEM(w_in.shape, LOW),
            pltpu.VMEM((tiles, capacity, tile_width), LOW),
            pltpu.VMEM((capacity, width), FULL),
            pltpu.VMEM((capacity, 128), FULL),
            pltpu.VMEM((capacity, width + 128), LOW),
            pltpu.VMEM((experts, SLOTS, width + 128), LOW),
            pltpu.VMEM((width, capacity), LOW),
            pltpu.VMEM((2, groups, width // groups, tile_width), LOW),
            pltpu.VMEM((tiles, width, tile_width), LOW),
            pltpu.VMEM((2, 2, width, tile_width), LOW),
            pltpu.VMEM((2, width, tile_width), LOW),
            pltpu.VMEM((width, tile_width), FULL),
            pltpu.VMEM((experts, SLOTS, width), LOW),
            pltpu.VMEM((ff // groups, width), FULL),
            dma((6,)),
            dma((groups,)),
            dma((2,)),
            dma((groups,)),
            dma((2,)),
            dma,
            dma((2,)),
            dma((tiles // groups + 1,)),
            dma((experts,)),
            dma((experts,)),
            dma((2, 2, (groups - 1) * (tiles // groups))),
            dma((2, 2, EARLY)),
        ],
        compiler_params=pltpu.CompilerParams(
            vmem_limit_bytes=62 * MIB, collective_id=2, has_side_effects=True
        ),
        cost_estimate=pl.CostEstimate(
            flops=12 * capacity * width * ff, bytes_accessed=50 * MIB, transcendentals=0
        ),
    )(cot_rows, gate_col, rows, info, resg_t, act, slope, outer, w_out, w_in)
    return outs[:6]


def attn_back_kernel(
    tokens_hbm,
    cot_hbm,
    hidden_hbm,
    normed2_hbm,
    mixed_hbm,
    qkv_hbm,
    prob_hbm,
    recv_hbm,
    token_ref,
    gain1_ref,
    gain2_ref,
    wqkv_hbm,
    wproj_hbm,
    wrouter_ref,
    onehot_ref,
    result_ref,
    gin_ref,
    early_up,
    early_down,
    block_ref,
    gtok_ref,
    dense_out,
    small_out,
    gin_out,
    up_in,
    down_in,
    tokens_ref,
    cot_ref,
    hidden_ref,
    normed2_ref,
    mixed_ref,
    recv_ref,
    wproj_ref,
    hgrad_ref,
    mgrad_ref,
    mgrad_t,
    normed_t,
    q_t,
    ds_ref,
    diag_ref,
    dk_t,
    dv_t,
    dqkv_ref,
    part_ref,
    pair_in,
    chip_ref,
    plane_in,
    plane_ref,
    group_in,
    small_ref,
    small_in,
    small_plane,
    small_group,
    qkv_ref,
    prob_ref,
    wqkv_ref,
    back_ref,
    fold_ref,
    took_ref,
    total_ref,
    fold_sems,
    took_sems,
    total_sems,
    load_sems,
    back_sems,
    pair_sems,
    plane_sems,
    group_sems,
    final_sems,
    small_sems,
    smallz_sems,
):
    seq_len, width = tokens_hbm.shape
    experts = wrouter_ref.shape[0]
    chunks = part_ref.shape[0]
    groups = group_in.shape[1]
    tile = 128
    g = lax.axis_index("group")
    me = lax.axis_index("expert")
    parity = lax.rem(me, 2)
    mine = lax.div(me, 2)
    summer = [groups // 2 - 1 + c % 2 for c in range(chunks)]

    def device(mask):
        return (g, lax.bitwise_xor(me, mask))

    def load(index):
        src, dst = (
            (qkv_hbm, qkv_ref),
            (prob_hbm, prob_ref),
            (wqkv_hbm, wqkv_ref),
            None,
            (recv_hbm, recv_ref),
            (hidden_hbm, hidden_ref),
            (cot_hbm, cot_ref),
            (tokens_hbm, tokens_ref),
            (wproj_hbm, wproj_ref),
            (normed2_hbm, normed2_ref),
            (mixed_hbm, mixed_ref),
        )[index]
        return pltpu.make_async_copy(src, dst, load_sems.at[index])

    own_result = pltpu.make_async_copy(result_ref.at[me], back_ref.at[me], load_sems.at[3])
    for index in (4, 5, 6, 7, 8, 9, 10, 0, 1, 2):
        load(index).start()
    own_result.start()
    barrier = pltpu.get_barrier_semaphore()
    for mask in range(1, experts):
        pl.semaphore_signal(barrier, inc=1, device_id=device(mask), device_id_type=MESH)
    for step in range(1, groups):
        pl.semaphore_signal(
            barrier, inc=1, device_id=(lax.rem(g + step, groups), me), device_id_type=MESH
        )
    pl.semaphore_wait(barrier, experts - 1 + groups - 1)

    def remote(src, dst, sems, at, where):
        return pltpu.make_async_remote_copy(
            src_ref=src,
            dst_ref=dst,
            send_sem=sems.at[(0, *at)],
            recv_sem=sems.at[(1, *at)],
            device_id=where,
            device_id_type=MESH,
        )

    started = []

    def go(copy):
        copy.start()
        started.append(copy)

    def result_copy(mask):
        other = lax.bitwise_xor(me, mask)
        return remote(result_ref.at[other], back_ref.at[me], back_sems, (mask,), device(mask))

    for mask in (2, 4, 3, 5, 1):
        result_copy(mask).start()

    def pair_send(c):
        for chip in range(experts // 2):
            other = 2 * chip + 1 - parity
            go(remote(part_ref.at[c, other], pair_in.at[c, chip], pair_sems, (c, chip), device(1)))

    def plane_send(c):
        for chip in range(experts // 2):
            remote(
                part_ref.at[c, 0], pair_in.at[c, chip], pair_sems, (c, chip), device(1)
            ).wait_recv()
            total = part_ref[c, 2 * chip + parity].astype(FULL) + pair_in[c, chip].astype(FULL)
            chip_ref[c, chip] = total.astype(LOW)
        for other in range(1, experts // 2):
            go(
                remote(
                    chip_ref.at[c, lax.bitwise_xor(mine, other)],
                    plane_in.at[c, other - 1],
                    plane_sems,
                    (c, other - 1),
                    device(2 * other),
                )
            )

    def group_send(c):
        total = chip_ref[c, mine].astype(FULL)
        for other in range(1, experts // 2):
            remote(
                chip_ref.at[c, 0],
                plane_in.at[c, other - 1],
                plane_sems,
                (c, other - 1),
                device(2 * other),
            ).wait_recv()
            total = total + plane_in[c, other - 1].astype(FULL)
        plane_ref[c] = total.astype(LOW)

        @pl.when(g != summer[c])
        def _():
            remote(
                plane_ref.at[c], group_in.at[c, g], group_sems, (c, g), (jnp.int32(summer[c]), me)
            ).start()

    def final_send(c):
        @pl.when(g == summer[c])
        def _():
            total = plane_ref[c].astype(FULL)
            for step in range(1, groups):
                src = lax.rem(g + step, groups)
                remote(
                    plane_ref.at[c], group_in.at[c, src], group_sems, (c, src), (src, me)
                ).wait_recv()
                total = total + group_in[c, src].astype(FULL)
            dense_out[c] = total.astype(LOW)
            for step in range(1, groups):
                where = (lax.rem(g + step, groups), me)
                remote(dense_out.at[c], dense_out.at[c], final_sems, (c, step - 1), where).start()

    def finish(c):
        where = (lax.rem(g + 1, groups), me)
        for step in range(1, groups):
            copy = remote(dense_out.at[c], dense_out.at[c], final_sems, (c, step - 1), where)

            @pl.when(g == summer[c])
            def _():
                copy.wait_send()

            @pl.when(lax.rem(summer[c] + step, groups) == g)
            def _():
                copy.wait_recv()

        @pl.when(g != summer[c])
        def _():
            remote(plane_ref.at[c], group_in.at[c, g], group_sems, (c, g), where).wait_send()

    parts = gin_ref.shape[1]
    last = groups - 1
    copies = last * parts
    arrivals = (up_in, down_in)

    def fold_tile(way, k):
        return (k // parts if way else last - k // parts), k % parts

    def fold_copy(way, k, src):
        shard_at, tile_at = fold_tile(way, k)
        there = arrivals[way].at[shard_at, tile_at]
        step = last if way else 1
        where = (lax.rem(g + step, groups), me)
        return pltpu.make_async_remote_copy(
            src_ref=there if src is None else src,
            dst_ref=there,
            send_sem=fold_sems.at[0, way, k],
            recv_sem=fold_sems.at[1, way, k],
            device_id=where,
            device_id_type=MESH,
        )

    def take_tile(way, which, src):
        return pltpu.make_async_copy(src, took_ref.at[way, which], took_sems.at[way, which])

    def fold_source(k):
        for way in range(2):

            @pl.when(g == way * last)
            def _():
                fold_copy(way, k, gin_ref.at[fold_tile(way, k)]).start()

    def fold_place(way, k):
        main = (g == 1) if way == 0 else (g == last - 1)
        return jnp.where(main, k, (last - 1) * parts + k)

    def fold_role(hop, k, act):
        for way in range(2):
            shard_at, tile_at = fold_tile(way, k)
            here = last - hop if way else hop
            if (shard_at < here) if way else (shard_at > here):
                pl.when(g == here)(functools.partial(act, way, k, shard_at, tile_at))

    def arrived(hop, way, k):
        if hop == 1 and k < EARLY:
            return (early_up, early_down)[way].at[k]
        return arrivals[way].at[fold_tile(way, k)]

    def fold_fetch(hop, k):
        def act(way, k, shard_at, tile_at):
            take_tile(way, 0, gin_ref.at[shard_at, tile_at]).start()
            if not (hop == 1 and k < EARLY):
                fold_copy(way, k, None).wait_recv()
            take_tile(way, 1, arrived(hop, way, k)).start()

        fold_role(hop, k, act)

    def fold_push(hop, k):
        def act(way, k, shard_at, tile_at):
            take_tile(way, 0, gin_ref.at[shard_at, tile_at]).wait()
            take_tile(way, 1, arrived(hop, way, k)).wait()
            place = fold_place(way, k)
            total = took_ref[way, 0].astype(FULL) + took_ref[way, 1].astype(FULL)
            fold_ref[place] = total.astype(LOW)
            fold_copy(way, k, fold_ref.at[place]).start()

        fold_role(hop, k, act)

    def fold_final(tile_at):
        own = take_tile(0, 0, gin_ref.at[g, tile_at])
        own.start()
        cases = ((g > 0, up_in, (last - g) * parts + tile_at), (g < last, down_in, g * parts + tile_at))
        for way, (some, arrival, k) in enumerate(cases):

            @pl.when(some)
            def _():
                here = arrival.at[g, tile_at]
                pltpu.make_async_remote_copy(
                    src_ref=here,
                    dst_ref=here,
                    send_sem=fold_sems.at[0, way, k],
                    recv_sem=fold_sems.at[1, way, k],
                    device_id=(lax.rem(g + 1, groups), me),
                    device_id_type=MESH,
                ).wait_recv()
                take_tile(way, 1, here).start()

        own.wait()
        if tile_at >= 2:
            final_copy(tile_at - 2).wait()
        total_ref[tile_at % 2] = took_ref[0, 0].astype(FULL)
        for way, (some, arrival, k) in enumerate(cases):

            @pl.when(some)
            def _():
                take_tile(way, 1, arrival.at[g, tile_at]).wait()
                total_ref[tile_at % 2] += took_ref[way, 1].astype(FULL)

        final_copy(tile_at).start()

    def final_copy(tile_at):
        cols = pl.ds(tile_at * total_ref.shape[2], total_ref.shape[2])
        return pltpu.make_async_copy(
            total_ref.at[tile_at % 2], gin_out.at[:, cols], total_sems.at[tile_at % 2]
        )

    def fold_sent():
        for way in range(2):
            for k in range(copies):
                shard_at, _ = fold_tile(way, k)
                sends = (g > shard_at) if way else (g < shard_at)
                if k < EARLY:
                    sends = sends & (g != way * last)

                @pl.when(sends)
                def _():
                    fold_copy(way, k, None).wait_send()

    for k in range(EARLY, EARLY + 3):
        fold_source(k)
    fold_fetch(1, 0)
    for index in range(4, 11):
        load(index).wait()
    ggain2 = jnp.zeros((8, width), FULL)
    lg_t = []
    for row0 in range(0, seq_len, tile):
        rows = slice(row0, row0 + tile)
        token = token_ref[rows, :]
        at = lax.broadcasted_iota(jnp.int32, (tile, recv_ref.shape[0]), 1).astype(FULL)
        picks = [jnp.where(at == token[:, k : k + 1], 1.0, 0.0).astype(LOW) for k in range(2)]
        got = dot_nn(jnp.concatenate(picks, axis=0), recv_ref[...])
        gg = [
            jnp.sum(got[k * tile : k * tile + tile, width:], axis=1, keepdims=True) for k in range(2)
        ]
        pull = token[:, 2:3] * token[:, 3:4] * (gg[0] - gg[1])
        expert = lax.broadcasted_iota(jnp.int32, (tile, 128), 1).astype(FULL)
        lg = jnp.where(expert == token[:, 4:5], pull, jnp.where(expert == token[:, 5:6], -pull, 0.0))
        lg_t.append(jnp.transpose(lg)[:experts])
        ngrad = (
            got[:tile, :width]
            + got[tile:, :width]
            + dot_nn(lg[:, :experts].astype(LOW), wrouter_ref[...])
        )
        hidden = hidden_ref[rows, :]
        inv = lax.rsqrt(jnp.mean(hidden * hidden, axis=1, keepdims=True) + EPS)
        unit = hidden * inv
        ng = ngrad * unit
        for i in range(tile // 8):
            ggain2 = ggain2 + ng[i * 8 : i * 8 + 8]
        scaled = ngrad * gain2_ref[...][None, :]
        proj = jnp.mean(scaled * unit, axis=1, keepdims=True)
        hgrad = cot_ref[rows, :].astype(FULL) + inv * (scaled - unit * proj)
        hgrad_ref[rows, :] = hgrad
        mgrad_ref[rows, :] = dot_nt(hgrad.astype(LOW), wproj_ref[...]).astype(LOW)
        x = tokens_ref[rows, :].astype(FULL)
        inv = lax.rsqrt(jnp.mean(x * x, axis=1, keepdims=True) + EPS)
        dqkv_ref[rows, :width] = (x * inv * gain1_ref[...][None, :]).astype(LOW)
        if row0 == tile:
            fold_source(5)
            fold_push(1, 0)
            fold_fetch(1, 1)
        if row0 == 3 * tile:
            fold_source(6)
            fold_push(1, 1)
            fold_fetch(1, 2)
    ggain2 = jnp.sum(ggain2, axis=0, keepdims=True)
    logit_grad_t = jnp.concatenate(lg_t, axis=1).astype(LOW)
    grouter = dot_nn(logit_grad_t, normed2_ref[...])
    normed_t[...] = jnp.transpose(dqkv_ref[:, :width])
    part_ref[0] = (
        dot_nn(jnp.transpose(mixed_ref[...]), hgrad_ref[...].astype(LOW))
        .astype(LOW)
        .reshape(experts, width // experts, width)
    )
    pair_send(0)
    fold_push(1, 2)
    fold_fetch(1, 3)
    fold_fetch(2, 0)
    mgrad_t[...] = jnp.transpose(mgrad_ref[...])
    load(0).wait()
    q_t[...] = jnp.transpose(qkv_ref[:, :width])
    load(1).wait()
    up = lax.broadcasted_iota(jnp.int32, (128, 128), 0)
    across = lax.broadcasted_iota(jnp.int32, (128, 128), 1)
    flip = jnp.where(up + across == 127, 1.0, 0.0).astype(FULL)

    def heads_back(pair):
        col = pl.multiple_of(pair * 128, 128)
        kp = qkv_ref[:, pl.ds(width + col, 128)]
        vp = qkv_ref[:, pl.ds(2 * width + col, 128)]
        op = mgrad_ref[:, pl.ds(col, 128)].astype(FULL)
        os = jnp.concatenate([(op * half_mask(sub, 1.0)).astype(LOW) for sub in range(2)], axis=0)
        dp = dot_nt(os, vp)
        for sub in range(2):
            h = 2 * pair + sub
            near = jnp.zeros((128, 384), FULL)
            far_neg = jnp.zeros((128, 128), FULL)
            far_pos = jnp.zeros((128, 128), FULL)
            blocks = seq_len // 128
            for block in range(blocks):
                first = sub * seq_len + block * 128
                here = slice(block * 128, block * 128 + 128)
                p = prob_ref[h, here, :].astype(FULL)
                weighted = p * dp[first : first + 128]
                ds = weighted - p * jnp.sum(weighted, axis=1, keepdims=True)
                low = ds.astype(LOW)
                ds_ref[sub, here, :] = low
                ds = low.astype(FULL)
                strip = []
                for d in range(-1, 2):
                    other = block + d
                    if 0 <= other < blocks:
                        strip.append(ds[:, other * 128 : other * 128 + 128])
                    else:
                        strip.append(jnp.zeros((128, 128), FULL))
                near = near + jnp.concatenate(strip, axis=1)
                for other in range(blocks):
                    piece = ds[:, other * 128 : other * 128 + 128]
                    if other - block <= -2:
                        far_neg = far_neg + piece
                    elif other - block >= 2:
                        far_pos = far_pos + piece
            low_sum = jnp.sum(far_neg)
            high_sum = jnp.sum(far_pos)
            padded = jnp.concatenate([exact_nn(flip, near), jnp.zeros((128, 128), FULL)], axis=1)
            turned = pltpu.roll(padded, 1, 1, stride=1, stride_axis=0)
            sums = jnp.sum(turned, axis=0, keepdims=True)
            lane = lax.broadcasted_iota(jnp.int32, (1, 512), 1)
            sums = sums + jnp.where(lane == 1, low_sum, jnp.where(lane == 511, high_sum, 0.0))
            diag_ref[pl.ds(h, 1), :] = sums
        lane = lax.broadcasted_iota(jnp.int32, (seq_len, 128), 1)
        dq = dot_nn(jnp.concatenate([ds_ref[0], ds_ref[1]], axis=0), kp)
        dqkv_ref[:, pl.ds(col, 128)] = (
            jnp.where(lane < 64, dq[:seq_len], dq[seq_len:]) * 0.125
        ).astype(LOW)
        for sub in range(2):
            part = pl.ds(pl.multiple_of(col + sub * 64, 64), 64)
            dk_t[part, :] = (dot_nn(q_t[part, :], ds_ref[sub]) * 0.125).astype(LOW)
            dv_t[part, :] = dot_nn(mgrad_t[part, :], prob_ref[2 * pair + sub]).astype(LOW)

    stripe = width // (chunks - 1)
    for c in range(1, chunks):
        pairs = stripe // 128

        @pl.loop((c - 1) * pairs, c * pairs)
        def _(pair):
            heads_back(pair)

        col = (c - 1) * stripe
        dqkv_ref[:, width + col : width + col + stripe] = jnp.transpose(dk_t[col : col + stripe, :])
        dqkv_ref[:, 2 * width + col : 2 * width + col + stripe] = jnp.transpose(
            dv_t[col : col + stripe, :]
        )
        for third in range(3):
            here = third * width + col
            part_ref[c, :, :, third * stripe : third * stripe + stripe] = (
                dot_nn(normed_t[...], dqkv_ref[:, here : here + stripe])
                .astype(LOW)
                .reshape(experts, width // experts, stripe)
            )
        pair_send(c)
        plane_send(c - 1)
        if c >= 2:
            group_send(c - 2)
        fold_push(1, c + 2)
        fold_push(2, c - 1)
        fold_source(c + 6)
        fold_fetch(1, c + 3)
        fold_fetch(2, c)

    load(2).wait()
    ggain1 = jnp.zeros((8, width), FULL)
    for row0 in range(0, seq_len, tile):
        rows = slice(row0, row0 + tile)
        x = tokens_ref[rows, :].astype(FULL)
        inv = lax.rsqrt(jnp.mean(x * x, axis=1, keepdims=True) + EPS)
        unit = x * inv
        ngrad = dot_nt(dqkv_ref[rows, :], wqkv_ref[...])
        ng = ngrad * unit
        for i in range(tile // 8):
            ggain1 = ggain1 + ng[i * 8 : i * 8 + 8]
        scaled = ngrad * gain1_ref[...][None, :]
        proj = jnp.mean(scaled * unit, axis=1, keepdims=True)
        gtok_ref[rows, :] = (hgrad_ref[rows, :] + inv * (scaled - unit * proj)).astype(LOW)
        if row0 == 0:
            plane_send(chunks - 1)
            for mask in (6, 7):
                result_copy(mask).start()
            fold_push(2, 3)
        if row0 == 2 * tile:
            fold_push(1, 6)
    ggain1 = jnp.sum(ggain1, axis=0, keepdims=True)

    gtable = exact_nt(onehot_ref[...], diag_ref[...])
    shard = width // experts
    per = gtable.shape[0] // experts
    for e in range(experts):
        cols = slice(e * shard, e * shard + shard)
        block = jnp.concatenate([ggain1[:, cols], ggain2[:, cols], grouter[:, cols]], axis=0)
        small_ref[e] = jnp.zeros(small_ref.shape[1:], FULL)
        small_ref[e, 0 : 2 + experts, 0:shard] = block
        small_ref[e, 2 + experts : 2 + experts + per, 0 : gtable.shape[1]] = gtable[
            e * per : e * per + per
        ]
    for mask in range(1, experts):
        other = lax.bitwise_xor(me, mask)
        go(remote(small_ref.at[other], small_in.at[mask], small_sems, (mask,), device(mask)))
    final_send(0)
    group_send(2)
    fold_fetch(1, 7)
    total = small_ref[me]
    for mask in range(1, experts):
        remote(
            small_ref.at[0], small_in.at[mask], small_sems, (mask,), device(mask)
        ).wait_recv()
        total = total + small_in[mask]
    small_plane[...] = total
    for step in range(1, groups):
        where = (lax.rem(g + step, groups), me)
        go(remote(small_plane, small_group.at[step], smallz_sems, (step,), where))
    fold_push(1, 7)
    final_send(1)
    group_send(3)
    fold_source(10)
    fold_source(11)
    own_result.wait()
    for mask in range(1, experts):
        result_copy(mask).wait()

    @pl.loop(0, seq_len // tile)
    def _(step):
        rows = pl.ds(pl.multiple_of(step * tile, tile), tile)
        token = token_ref[rows, :]
        at = lax.broadcasted_iota(jnp.int32, (tile, experts * SLOTS), 1).astype(FULL)
        picks = [jnp.where(at == token[:, k : k + 1], 1.0, 0.0).astype(LOW) for k in range(2)]
        got = dot_nn(
            jnp.concatenate(picks, axis=0), back_ref[...].reshape(experts * SLOTS, width)
        )
        block_ref[rows, :] = (
            hidden_ref[rows, :] + token[:, 2:3] * got[:tile] + token[:, 3:4] * got[tile:]
        ).astype(LOW)

    fold_final(0)
    final_send(2)
    fold_final(1)
    final_send(3)
    for tile_at in range(2, parts):
        fold_final(tile_at)
    for tile_at in range(parts - 2, parts):
        final_copy(tile_at).wait()
    for step in range(1, groups):
        remote(
            small_plane, small_group.at[step], smallz_sems, (step,), (lax.rem(g + step, groups), me)
        ).wait_recv()
        total = total + small_group[step]
    small_out[...] = total
    for c in range(chunks):
        finish(c)
    fold_sent()
    for copy in started:
        copy.wait_send()


def attn_back(
    tokens, cot, hidden, normed2, mixed, qkv, prob, recv, token, gain1, gain2, wqkv, wproj, wrouter, table, result, gin, early_up, early_down, groups
):
    seq_len, width = tokens.shape
    buckets, heads = table.shape
    experts = wrouter.shape[1]
    shard = width // experts
    chunks = groups
    chips = experts // 2
    small = (16, 128)
    sds = jax.ShapeDtypeStruct
    dma = pltpu.SemaphoreType.DMA
    outs = pl.pallas_call(
        attn_back_kernel,
        out_shape=(
            sds((seq_len, width), LOW),
            sds((seq_len, width), LOW),
            sds((chunks, shard, width), LOW),
            sds(small, FULL),
            sds((gin.shape[2], gin.shape[1] * gin.shape[3]), FULL),
            sds(gin.shape, LOW),
            sds(gin.shape, LOW),
        ),
        in_specs=[HBM] * 8 + [VM] * 3 + [HBM] * 2 + [VM] * 2 + [HBM] * 4,
        out_specs=[VM] * 4 + [HBM] * 3,
        scratch_shapes=[
            pltpu.VMEM(tokens.shape, LOW),
            pltpu.VMEM(cot.shape, LOW),
            pltpu.VMEM(hidden.shape, FULL),
            pltpu.VMEM(normed2.shape, LOW),
            pltpu.VMEM(mixed.shape, LOW),
            pltpu.VMEM(recv.shape, LOW),
            pltpu.VMEM(wproj.shape, LOW),
            pltpu.VMEM((seq_len, width), FULL),
            pltpu.VMEM((seq_len, width), LOW),
            pltpu.VMEM((width, seq_len), LOW),
            pltpu.VMEM((width, seq_len), LOW),
            pltpu.VMEM((width, seq_len), LOW),
            pltpu.VMEM((2, seq_len, seq_len), LOW),
            pltpu.VMEM((heads, 512), FULL),
            pltpu.VMEM((width, seq_len), LOW),
            pltpu.VMEM((width, seq_len), LOW),
            pltpu.VMEM((seq_len, 3 * width), LOW),
            pltpu.VMEM((chunks, experts, shard, width), LOW),
            pltpu.VMEM((chunks, chips, shard, width), LOW),
            pltpu.VMEM((chunks, chips, shard, width), LOW),
            pltpu.VMEM((chunks, chips - 1, shard, width), LOW),
            pltpu.VMEM((chunks, shard, width), LOW),
            pltpu.VMEM((chunks, groups, shard, width), LOW),
            pltpu.VMEM((experts, *small), FULL),
            pltpu.VMEM((experts, *small), FULL),
            pltpu.VMEM(small, FULL),
            pltpu.VMEM((groups, *small), FULL),
            pltpu.VMEM((seq_len, 3 * width), LOW),
            pltpu.VMEM((heads, seq_len, seq_len), LOW),
            pltpu.VMEM(wqkv.shape, LOW),
            pltpu.VMEM(result.shape, LOW),
            pltpu.VMEM((groups * (groups - 1), *gin.shape[2:]), LOW),
            pltpu.VMEM((2, 2, *gin.shape[2:]), LOW),
            pltpu.VMEM((2, *gin.shape[2:]), FULL),
            dma((2, 2, (groups - 1) * gin.shape[1])),
            dma((2, 2)),
            dma((2,)),
            dma((11,)),
            dma((2, experts)),
            dma((2, chunks, chips)),
            dma((2, chunks, chips - 1)),
            dma((2, chunks, groups)),
            dma((2, chunks, groups - 1)),
            dma((2, experts)),
            dma((2, groups)),
        ],
        compiler_params=pltpu.CompilerParams(
            vmem_limit_bytes=60 * MIB, collective_id=1, has_side_effects=True
        ),
        cost_estimate=pl.CostEstimate(
            flops=30_000_000_000, bytes_accessed=30 * MIB, transcendentals=0
        ),
    )(
        tokens,
        cot,
        hidden,
        normed2,
        mixed,
        qkv,
        prob,
        recv,
        token,
        gain1,
        gain2,
        wqkv,
        wproj,
        wrouter.T,
        jnp.asarray(near_onehot(buckets)),
        result,
        gin,
        early_up,
        early_down,
    )
    return outs[:5]


def outputs_kernel(
    block_in,
    gtok_in,
    gin_in,
    gout_in,
    dense_ref,
    small_ref,
    block_ref,
    gtok_ref,
    gain1_ref,
    qkv_ref,
    proj_ref,
    table_ref,
    gain2_ref,
    router_ref,
    gin_ref,
    gout_ref,
    gin_v,
    gout_v,
    block_v,
    gtok_v,
    sems,
):
    passed = (
        (gin_in, gin_v, gin_ref.at[0]),
        (gout_in, gout_v, gout_ref.at[0]),
        (block_in, block_v, block_ref),
        (gtok_in, gtok_v, gtok_ref),
    )
    pieces = 4
    copies = []
    for i, (src, mid, dst) in enumerate(passed):
        rows = src.shape[0] // pieces
        for piece in range(pieces):
            here = pl.ds(piece * rows, rows)
            copies.append(
                [
                    pltpu.make_async_copy(a.at[here, :], b.at[here, :], sems.at[way, i, piece])
                    for way, (a, b) in enumerate(((src, mid), (mid, dst)))
                ]
            )
    for copy_in, _ in copies:
        copy_in.start()
    chunks, shard, width = dense_ref.shape
    experts = router_ref.shape[0]
    stripe = width // (chunks - 1)
    proj_ref[...] = dense_ref[0].astype(FULL)
    for c in range(1, chunks):
        for third in range(3):
            col = third * width + (c - 1) * stripe
            qkv_ref[:, col : col + stripe] = dense_ref[
                c, :, third * stripe : third * stripe + stripe
            ].astype(FULL)
    gain1_ref[...] = small_ref[0:1, 0:shard]
    gain2_ref[...] = small_ref[1:2, 0:shard]
    router_ref[...] = small_ref[2 : 2 + experts, 0:shard]
    per, heads = table_ref.shape
    table_ref[...] = small_ref[2 + experts : 2 + experts + per, 0:heads]
    for copy_in, copy_out in copies:
        copy_in.wait()
        copy_out.start()
    for _, copy_out in copies:
        copy_out.wait()


def outputs(block, gtok, gin, gout, dense, small, experts, table_shape):
    chunks, shard, width = dense.shape
    buckets, heads = table_shape
    sds = jax.ShapeDtypeStruct
    return pl.pallas_call(
        outputs_kernel,
        out_shape=(
            sds(block.shape, LOW),
            sds(gtok.shape, LOW),
            sds((1, shard), FULL),
            sds((shard, 3 * width), FULL),
            sds((shard, width), FULL),
            sds((buckets // experts, heads), FULL),
            sds((1, shard), FULL),
            sds((experts, shard), FULL),
            sds((1, *gin.shape), FULL),
            sds((1, *gout.shape), FULL),
        ),
        in_specs=[HBM] * 4 + [VM] * 2,
        out_specs=[HBM] * 2 + [VM] * 6 + [HBM] * 2,
        scratch_shapes=[
            pltpu.VMEM(gin.shape, FULL),
            pltpu.VMEM(gout.shape, FULL),
            pltpu.VMEM(block.shape, LOW),
            pltpu.VMEM(gtok.shape, LOW),
            pltpu.SemaphoreType.DMA((2, 4, 4)),
        ],
        compiler_params=pltpu.CompilerParams(vmem_limit_bytes=60 * MIB),
    )(block, gtok, gin, gout, dense, small)


def on_device_fast(
    tokens,
    gain_first,
    w_qkv,
    w_proj,
    bias_table,
    gain_second,
    w_router,
    w_in,
    w_out,
    routes,
    priority,
    span_start,
    cotangent,
):
    experts = w_router.shape[1]
    width = tokens.shape[1]
    groups = lax.axis_size("group")
    (
        qkv,
        prob,
        mixed,
        hidden,
        normed2,
        rows,
        cot_rows,
        gate_col,
        token,
        info,
        resg_t,
        act,
        slope,
        outer_first,
    ) = attn_dispatch(
        tokens,
        cotangent,
        gain_first,
        w_qkv,
        w_proj,
        bias_table,
        gain_second,
        w_router,
        routes,
        priority,
        span_start,
        w_in[0],
        groups,
    )
    recv, packed_out, grad_inner, grad_out, early_up, early_down = expert_call(
        cot_rows, gate_col, rows, info, resg_t, act, slope, outer_first, w_out[0], w_in[0]
    )
    block_out, gtok, dense, small, grad_in = attn_back(
        tokens,
        cotangent,
        hidden,
        normed2,
        mixed,
        qkv,
        prob,
        recv.reshape(-1, width + 128),
        token,
        gain_first,
        gain_second,
        w_qkv,
        w_proj,
        w_router,
        bias_table,
        packed_out,
        grad_inner,
        early_up,
        early_down,
        groups,
    )
    final = list(
        outputs(block_out, gtok, grad_in, grad_out, dense, small, experts, bias_table.shape)
    )
    final[2] = final[2].reshape(-1)
    final[6] = final[6].reshape(-1)
    final[7] = final[7].T
    return tuple(final)


def bucket_table(seq_len, buckets):
    half_count = buckets // 2
    exact_count = half_count // 2
    offsets = np.arange(-(seq_len - 1), seq_len)
    upper_half = (offsets > 0).astype(np.int64) * half_count
    distance = np.abs(offsets)
    scaled = (
        np.log(np.maximum(distance, 1) / float(exact_count))
        / np.log(128.0 / exact_count)
        * (half_count - exact_count)
    )
    larger = np.minimum(
        exact_count + np.floor(np.maximum(scaled, 0.0)).astype(np.int64), half_count - 1
    )
    bucket = upper_half + np.where(distance < exact_count, distance, larger)
    places = np.arange(seq_len)
    return bucket[places[None, :] - places[:, None] + seq_len - 1].astype(np.int32)


def allowed_pairs(seq_len, span_begin, span_len):
    places = jnp.arange(seq_len, dtype=jnp.int32)
    causal = places[None, :] <= places[:, None]
    inside = (places >= span_begin) & (places < span_begin + span_len)
    return causal | inside[:, None] & inside[None, :]


def rms_norm(values, norm_gain):
    return values * lax.rsqrt(jnp.mean(values * values, axis=-1, keepdims=True) + 1e-06) * norm_gain


def gate_values(logits, routes, experts):
    probabilities = jax.nn.softmax(logits, axis=-1)
    chosen = (routes[..., None] == jnp.arange(experts, dtype=jnp.int32)).astype(jnp.float32)
    picked = jnp.sum(probabilities[:, None, :] * chosen, axis=-1)
    return picked / jnp.sum(picked, axis=1, keepdims=True)


def local_ranks(choice_hits, priority):
    token_count = priority.shape[0]
    token_order = (
        jnp.zeros((token_count,), jnp.int32)
        .at[priority]
        .set(jnp.arange(token_count, dtype=jnp.int32))
    )
    ordered = choice_hits[token_order]
    running = jnp.cumsum(ordered, axis=0) - ordered
    return jnp.sum(running[priority] * choice_hits, axis=-1)


def contract_rows(left, right):
    return lax.dot_general(
        left, right, (((0,), (0,)), ((), ())), preferred_element_type=jnp.float32
    )


def on_device(
    tokens,
    gain_first,
    w_qkv,
    w_proj,
    bias_table,
    gain_second,
    w_router,
    w_in,
    w_out,
    routes,
    priority,
    span_start,
    cotangent,
):
    seq_len, model_width = tokens.shape
    buckets, head_count = bias_table.shape
    head_dim = model_width // head_count
    experts = w_router.shape[1]
    slot_count = 4 * seq_len // experts
    capacity = 5 * seq_len // 2
    score_scale = 1.0 / math.sqrt(head_dim)
    highest = lax.Precision.HIGHEST
    lowtype = jnp.bfloat16
    fulltype = jnp.float32
    tokens_f = tokens.astype(fulltype)
    normed_one = rms_norm(tokens_f, gain_first).astype(lowtype)
    qkv_rows = jnp.dot(normed_one, w_qkv, preferred_element_type=fulltype).astype(lowtype)
    qkv_rows = qkv_rows.reshape(seq_len, 3, head_count, head_dim)
    queries, key_rows, value_rows = (qkv_rows[:, 0], qkv_rows[:, 1], qkv_rows[:, 2])
    bucket_index = jnp.asarray(bucket_table(seq_len, buckets))
    onehot_table = (bucket_index[:, :, None] == jnp.arange(buckets, dtype=jnp.int32)).astype(
        fulltype
    )
    rel_bias = jnp.einsum("qkb,bh->hqk", onehot_table, bias_table, precision=highest)
    allowed = allowed_pairs(seq_len, span_start[0], PIC)

    def masked_scores():
        raw_scores = (
            jnp.einsum("qhc,khc->hqk", queries, key_rows, preferred_element_type=fulltype)
            * score_scale
            + rel_bias
        )
        return jnp.where(allowed[None], raw_scores, -1e30)

    scores = masked_scores()
    log_total = jax.nn.logsumexp(scores, axis=-1)
    attn_probs = jnp.exp(scores - log_total[..., None]).astype(lowtype)
    mixed_heads = jnp.einsum(
        "hqk,khc->qhc", attn_probs, value_rows, preferred_element_type=fulltype
    )
    mixed_heads = mixed_heads.astype(lowtype).reshape(seq_len, model_width)
    hidden = tokens_f + jnp.dot(mixed_heads, w_proj, preferred_element_type=fulltype)
    normed_two = rms_norm(hidden, gain_second).astype(lowtype)
    logits = jnp.dot(normed_two, w_router, preferred_element_type=fulltype)
    gate_weights = gate_values(logits, routes, experts)
    choice_hits = (routes[..., None] == jnp.arange(experts, dtype=jnp.int32)).astype(jnp.int32)
    counts = jnp.sum(choice_hits, axis=0)
    every_count = lax.all_gather(counts[None], "expert", axis=0, tiled=True)
    pair_ranks = local_ranks(choice_hits, priority[0])
    second_shift = jnp.sum(choice_hits[:, 1] * counts[0], axis=-1)
    slot_index = pair_ranks + jnp.stack([jnp.zeros_like(second_shift), second_shift], axis=-1)
    flat_slot = (routes * slot_count + slot_index).reshape(-1)
    own_expert = (jnp.arange(experts, dtype=jnp.int32) == lax.axis_index("expert")).astype(
        jnp.int32
    )
    own_counts = jnp.sum(every_count * own_expert, axis=-1)
    first_rows, second_rows = (own_counts[:, 0], own_counts[:, 1])
    first_before = jnp.cumsum(first_rows) - first_rows
    second_before = jnp.cumsum(second_rows) - second_rows
    first_total = jnp.sum(first_rows)
    column = jnp.arange(slot_count, dtype=jnp.int32)[None, :]
    position = jnp.where(
        column < first_rows[:, None],
        first_before[:, None] + column,
        first_total + second_before[:, None] + column - first_rows[:, None],
    )
    usable = (column < (first_rows + second_rows)[:, None]) & (position < capacity)
    destination = jnp.where(usable, position, capacity).reshape(-1)

    def pack_pairs(pair_rows):
        packed = jnp.zeros((experts * slot_count, model_width), lowtype)
        packed = packed.at[flat_slot].set(pair_rows.reshape(-1, model_width))
        return packed.reshape(experts, slot_count, model_width)

    def compact_rows(arrived):
        gathered_rows = jnp.zeros((capacity + 1, model_width), lowtype)
        return gathered_rows.at[destination].add(arrived.reshape(-1, model_width))[:capacity]

    def spread_rows(expert_out):
        padded = jnp.concatenate([expert_out, jnp.zeros((1, model_width), lowtype)], axis=0)
        return padded[destination].reshape(-1, slot_count, model_width)

    def unpack_pairs(received):
        return (
            received.reshape(-1, model_width)[flat_slot]
            .reshape(seq_len, 2, model_width)
            .astype(fulltype)
        )

    pair_rows = jnp.broadcast_to(normed_two[:, None, :], (seq_len, 2, model_width))
    arrived = lax.all_to_all(
        pack_pairs(pair_rows), "expert", split_axis=0, concat_axis=0, tiled=True
    )
    expert_rows = compact_rows(arrived)
    inner_pre = jnp.dot(expert_rows, w_in[0], preferred_element_type=fulltype)
    active = jax.nn.gelu(inner_pre).astype(lowtype)
    result = jnp.dot(active, w_out[0], preferred_element_type=fulltype).astype(lowtype)
    returned = unpack_pairs(
        lax.all_to_all(spread_rows(result), "expert", split_axis=0, concat_axis=0, tiled=True)
    )
    block_out = hidden + jnp.sum(gate_weights[..., None] * returned, axis=1)
    upstream = cotangent.astype(fulltype)
    gate_grad = jnp.sum(upstream[:, None, :] * returned, axis=-1)
    result_grad = (gate_weights[..., None] * upstream[:, None, :]).astype(lowtype)
    result_rows = compact_rows(
        lax.all_to_all(pack_pairs(result_grad), "expert", split_axis=0, concat_axis=0, tiled=True)
    )
    grad_outer = contract_rows(active, result_rows)
    hidden_pre_grad = jnp.dot(result_rows, w_out[0].T, preferred_element_type=fulltype)
    inner_grad = jax.vjp(jax.nn.gelu, inner_pre)[1](hidden_pre_grad)[0].astype(lowtype)
    grad_inner = contract_rows(expert_rows, inner_grad)
    rows_grad = jnp.dot(inner_grad, w_in[0].T, preferred_element_type=fulltype).astype(lowtype)
    pair_grad = unpack_pairs(
        lax.all_to_all(spread_rows(rows_grad), "expert", split_axis=0, concat_axis=0, tiled=True)
    )
    logit_grad = jax.vjp(lambda values: gate_values(values, routes, experts), logits)[1](gate_grad)[
        0
    ].astype(lowtype)
    grad_router = contract_rows(normed_two, logit_grad)
    normed_grad = jnp.sum(pair_grad, axis=1) + jnp.dot(
        logit_grad, w_router.T, preferred_element_type=fulltype
    )
    second_back = jax.vjp(rms_norm, hidden, gain_second)[1](normed_grad)
    hidden_grad = upstream + second_back[0]
    branch_grad = hidden_grad.astype(lowtype)
    grad_proj = contract_rows(mixed_heads, branch_grad)
    mixed_grad = jnp.dot(branch_grad, w_proj.T, preferred_element_type=fulltype).astype(lowtype)
    mixed_grad = mixed_grad.reshape(seq_len, head_count, head_dim)
    scores = masked_scores()
    probs_full = jnp.exp(scores - log_total[..., None])
    probs_low = probs_full.astype(lowtype)
    prob_grad = jnp.einsum("qhc,khc->hqk", mixed_grad, value_rows, preferred_element_type=fulltype)
    value_grad = jnp.einsum("hqk,qhc->khc", probs_low, mixed_grad, preferred_element_type=fulltype)
    row_dot = jnp.sum(probs_full * prob_grad, axis=-1, keepdims=True)
    score_grad = (probs_full * (prob_grad - row_dot)).astype(lowtype)
    query_grad = (
        jnp.einsum("hqk,khc->qhc", score_grad, key_rows, preferred_element_type=fulltype)
        * score_scale
    )
    key_grad = (
        jnp.einsum("hqk,qhc->khc", score_grad, queries, preferred_element_type=fulltype)
        * score_scale
    )
    grad_table = jnp.einsum(
        "hqk,qkb->bh", score_grad.astype(fulltype), onehot_table, precision=highest
    )
    qkv_grad = (
        jnp.stack([query_grad, key_grad, value_grad], axis=1)
        .astype(lowtype)
        .reshape(seq_len, 3 * model_width)
    )
    grad_qkv = contract_rows(normed_one, qkv_grad)
    normed_one_grad = jnp.dot(qkv_grad, w_qkv.T, preferred_element_type=fulltype)
    first_back = jax.vjp(rms_norm, tokens_f, gain_first)[1](normed_one_grad)
    grad_tokens = (hidden_grad + first_back[0]).astype(lowtype)
    dense_grads = (first_back[1], grad_qkv, grad_proj, grad_table, second_back[1], grad_router)
    shares = (
        lax.psum_scatter(
            dense_grads[0].astype(jnp.bfloat16), "expert", scatter_dimension=0, tiled=True
        ).astype(jnp.float32),
        lax.psum_scatter(
            dense_grads[1].astype(jnp.bfloat16), "expert", scatter_dimension=0, tiled=True
        ).astype(jnp.float32),
        lax.psum_scatter(
            dense_grads[2].astype(jnp.bfloat16), "expert", scatter_dimension=0, tiled=True
        ).astype(jnp.float32),
        lax.psum_scatter(
            dense_grads[3].astype(jnp.bfloat16), "expert", scatter_dimension=0, tiled=True
        ).astype(jnp.float32),
        lax.psum_scatter(
            dense_grads[4].astype(jnp.bfloat16), "expert", scatter_dimension=0, tiled=True
        ).astype(jnp.float32),
        lax.psum_scatter(
            dense_grads[5].astype(jnp.bfloat16), "expert", scatter_dimension=0, tiled=True
        ).astype(jnp.float32),
    )
    totals = (
        lax.psum(shares[0].astype(jnp.bfloat16), "group").astype(jnp.float32),
        lax.psum(shares[1].astype(jnp.bfloat16), "group").astype(jnp.float32),
        lax.psum(shares[2].astype(jnp.bfloat16), "group").astype(jnp.float32),
        lax.psum(shares[3].astype(jnp.bfloat16), "group").astype(jnp.float32),
        lax.psum(shares[4].astype(jnp.bfloat16), "group").astype(jnp.float32),
        lax.psum(shares[5].astype(jnp.bfloat16), "group").astype(jnp.float32),
    )
    grad_in, grad_out = (
        lax.psum_scatter(
            grad_inner[None].astype(jnp.bfloat16), "group", scatter_dimension=1, tiled=True
        ).astype(jnp.float32),
        lax.psum_scatter(
            grad_outer[None].astype(jnp.bfloat16), "group", scatter_dimension=1, tiled=True
        ).astype(jnp.float32),
    )
    return (
        block_out.astype(lowtype),
        grad_tokens,
        totals[0],
        totals[1],
        totals[2],
        totals[3],
        totals[4],
        totals[5],
        grad_in,
        grad_out,
    )


def solution(mesh):
    fast = (mesh.shape["group"], mesh.shape["expert"]) == (4, 8)
    step = on_device_fast if fast else on_device
    return jax.shard_map(
        step,
        mesh=mesh,
        in_specs=(
            P(("group", "expert"), None),
            P(),
            P(),
            P(),
            P(),
            P(),
            P(),
            P("expert", None, None),
            P("expert", None, None),
            P(("group", "expert"), None),
            P(("group", "expert"), None),
            P(("group", "expert")),
            P(("group", "expert"), None),
        ),
        out_specs=(
            P(("group", "expert"), None),
            P(("group", "expert"), None),
            P("expert"),
            P("expert", None),
            P("expert", None),
            P("expert", None),
            P("expert"),
            P("expert", None),
            P("expert", "group", None),
            P("expert", "group", None),
        ),
        check_vma=False,
    )
```
